32 devices in a mesh: role: 2 (over x), seq: 4 (over z), rep: 4 (over y, core).
Axes of the slice: x: 2, y: 2, z: 4, core: 2. Of those that a mesh axis runs over, the one named last changes fastest.
Arguments:
- hidden_in: bfloat16 [2, 1024, 2048], P('role', ('seq', 'rep')), may hold values from -6 to 6
- attn_gain: float32 [2048], replicated, may hold values from 0.25 to 1.75
- w_query: bfloat16 [2048, 2048], P(None, 'rep'), may hold values from -0.125 to 0.125
- w_keyval: bfloat16 [2, 2048, 256], replicated, may hold values from -0.125 to 0.125
- q_gain: float32 [128], replicated, may hold values from 1.2 to 14
- k_gain: float32 [128], replicated, may hold values from 1.2 to 14
- w_out: bfloat16 [2048, 2048], P('rep'), may hold values from -0.25 to 0.25
- moe_gain: float32 [2048], replicated, may hold values from 0.25 to 1.75
- expert_ids: int32 [2, 1024, 8], P('role', ('seq', 'rep')), may hold values from 0 to 31, all different within a row; in each aligned block of 64 rows (0 to 63, 64 to 127, ..., all dimensions but the last counted through in order) at most 28 rows name the same one
- gate_fixed: int32 [2, 1024, 8], P('role', ('seq', 'rep')), may hold values from 1 to 4095
- w_gateup: bfloat16 [32, 2048, 1536], P(('role', 'seq', 'rep')), may hold values from -0.125 to 0.125
- w_down: bfloat16 [32, 768, 2048], P(('role', 'seq', 'rep')), may hold values from -0.21875 to 0.21875
Outputs:
- layer_out: bfloat16 [2, 1024, 2048], P('role', ('seq', 'rep'))
The draws below stay inside these ranges and needn't reach their ends.
Inputs may be any that keep to these rules, and one draw needn't show every extreme that they name: `expert_ids`: each row names 8 different experts; the 64 tokens of one device name no expert more than 28 times, and some device names some expert exactly 28 times.
All inputs are finite; a program needn't handle non-finite values.
Results may differ from the reference program's by a relative error of at most 0.015.
The reference program's roundings to bfloat16 on the way (of `normed`, `probs`, `context`, `moe_in`, `expert_hidden` and `expert_out`) count: a program that leaves them out, or rounds other values in their place, can miss the bound.
Values may be sent and summed in bfloat16 or wider, within the bound.
No kernel may reach another device: no remote copies, remote signals or barrier semaphores. Data moves between devices by JAX's collectives and lax.ppermute only.
A program may use at most 128 MiB of HBM per device.

```python
import math
import jax
import jax.numpy as jnp
import numpy as np
from jax import lax

D = 2048
HQ = 16
HK = 2
HD = 128
FFE = 768
TOP = 8
ROWS = 64
LENGTH = 1024
MB = 2
EXPERTS = 32
MOST = 28


def base_gains(key):
    return jnp.exp(jax.random.uniform(key, (HD,), jnp.float32, math.log(1.2), math.log(2.5)))


def draw_q_gain(key, part):
    key = jax.random.fold_in(key, 1)
    gains = base_gains(key)
    return gains


def draw_k_gain(key, part):
    key = jax.random.fold_in(key, 2)
    gains = base_gains(key)
    return gains


def plant(array, key, least, largest):
    longest = array.shape.index(max(array.shape))
    spots = []
    for shift in (0, 1):
        where = [jax.random.randint(jax.random.fold_in(key, axis), (), 0, length) for axis, length in enumerate(array.shape)]
        where[longest] = (where[longest] + shift) % array.shape[longest]
        spots.append(tuple(where))
    return array.at[spots[0]].set(least).at[spots[1]].set(largest)


def block_levels(key, extent, pieces, least, largest):
    def one(dim, parts):
        draws = jax.random.uniform(jax.random.fold_in(jax.random.fold_in(key, 6), dim), (parts,), jnp.float32, least / len(pieces), largest / len(pieces))
        return jnp.repeat(jnp.exp(draws), extent[dim] // parts).reshape((-1,) + (1,) * (len(extent) - dim - 1))

    loudness = one(*pieces[0])
    for cut in pieces[1:]:
        loudness = loudness * one(*cut)
    return loudness


def routed_block(rng, own, number, rows, count, top, reach, skew):
    order = jax.random.permutation(rng, count)
    crowded, common = load_shares(count, rows * top, reach, skew, True), load_shares(count, rows * top, reach, skew, False)
    places = jnp.arange(count)

    def named(sizes, turn):
        used = int((sizes > 0).sum())
        fixed = max(1, used // 4)
        shifted = fixed + (places - fixed + turn * (used - fixed)) % max(1, count - fixed)
        return jnp.zeros((count,), jnp.int32).at[order[jnp.where(places < fixed, places, shifted)]].set(jnp.asarray(sizes, jnp.int32))

    sizes = jnp.where(number % 4 == 0, named(crowded, number // 4), named(common, number - number // 4 - 1))
    mixed = jax.random.permutation(jax.random.fold_in(own, 3), count)
    donor, sink = mixed[0:count // 2 * 2:2], mixed[1:count // 2 * 2:2]
    margin = jnp.minimum(sizes[donor] - 1, reach - sizes[sink]) // 2
    margin = jnp.where((donor == order[0]) | (sink == order[0]) | (sizes[sink] == 0), 0, jnp.maximum(margin, 0))
    shifted = jax.random.randint(jax.random.fold_in(own, 4), (count // 2,), 0, 1 << 20) % (margin + 1)
    sizes = sizes.at[donor].add(-shifted).at[sink].add(shifted)
    members = jnp.searchsorted(jnp.cumsum(sizes), jnp.arange(rows * top), side="right").astype(jnp.int32)
    table = members.reshape(top, rows).T
    table = table[jax.random.permutation(jax.random.fold_in(own, 1), rows)]
    turn = jax.random.randint(jax.random.fold_in(own, 2), (rows, 1), 0, top)
    return jnp.take_along_axis(table, (jnp.arange(top)[None, :] + turn) % top, axis=1)


def load_shares(number_of, total, most, skew, full):
    loads = [(1 << 20) // math.isqrt(standing ** skew) + 1 for standing in range(1, number_of + 1)]
    largest = most if full else min(most, max(-(-total // number_of), total * loads[0] // sum(loads)))
    least = 1 if total - largest >= number_of - 1 else 0
    holding, spare = [largest] + [least] * (number_of - 1), total - largest - least * (number_of - 1)
    while spare > 0:
        free = [i for i in range(1, number_of) if holding[i] < largest] or [i for i in range(1, number_of) if holding[i] < most]
        pool, remaining = sum([loads[i] for i in free]), spare
        for i in free:
            addition = min(most - holding[i], max(1, remaining * loads[i] // pool), spare)
            holding[i] = holding[i] + addition
            spare = spare - addition
    return np.array(holding)


def centred(stream_key, extent, spread, reach, split=(), kind=jnp.bfloat16):
    result = spread * jax.random.normal(stream_key, extent, jnp.float32)
    if split:
        result = result * block_levels(stream_key, extent, split, -0.22, 0.18)
    return jnp.clip(result, -reach, reach).astype(kind)


def setup_inputs(seed: int = 0) -> dict:
    key_of = jax.random.split(jax.random.key(seed), 13)
    hidden_in = centred(key_of[0], (MB, LENGTH, D), 1.0, 6.0, ((0, 2), (1, 16)))
    attn_gain = jnp.clip(1.0 + 0.15 * jax.random.normal(key_of[1], (D,), jnp.float32), 0.25, 1.75)
    w_query = centred(key_of[2], (D, HQ * HD), D ** -0.5, 0.125, ((1, 4),))
    w_keyval = centred(key_of[3], (2, D, HK * HD), D ** -0.5, 0.125)
    q_gain = draw_q_gain(jax.random.fold_in(key_of[12], 71), 0)
    k_gain = draw_k_gain(jax.random.fold_in(key_of[12], 71), 0)
    w_out = centred(key_of[6], (HQ * HD, D), (HQ * HD // 4) ** -0.5, 0.25, ((0, 4),))
    moe_gain = jnp.clip(1.0 + 0.15 * jax.random.normal(key_of[7], (D,), jnp.float32), 0.25, 1.75)
    expert_ids_keys = jax.random.split(jax.random.fold_in(key_of[8], 1), MB * LENGTH // ROWS)
    expert_ids_turns = jax.random.permutation(jax.random.fold_in(key_of[8], 3), MB * LENGTH // ROWS)
    expert_ids = jax.vmap(lambda own, number: routed_block(jax.random.fold_in(key_of[8], 2), own, number, ROWS, EXPERTS, TOP, MOST, 2))(expert_ids_keys, expert_ids_turns).reshape((MB, LENGTH, TOP))
    gate_fixed = plant(jax.random.randint(key_of[9], (MB, LENGTH, TOP), 1, 4096), jax.random.fold_in(key_of[9], 1), 1, 4095).astype(jnp.int32)
    w_gateup = centred(key_of[10], (EXPERTS, D, 2 * FFE), D ** -0.5, 0.125, ((0, 32),))
    w_down = centred(key_of[11], (EXPERTS, FFE, D), FFE ** -0.5, 0.21875, ((0, 32),))
    return {"hidden_in": hidden_in, "attn_gain": attn_gain, "w_query": w_query, "w_keyval": w_keyval, "q_gain": q_gain, "k_gain": k_gain, "w_out": w_out, "moe_gain": moe_gain, "expert_ids": expert_ids, "gate_fixed": gate_fixed, "w_gateup": w_gateup, "w_down": w_down}


def rms_rows(values_in, gain_vec):
    return values_in * lax.rsqrt(lax.optimization_barrier(jnp.mean(values_in * values_in, axis=-1, keepdims=True)) + 1e-06) * gain_vec

def attend_head(packed):
    query_head, key_head, value_head = packed
    block_size = math.gcd(LENGTH, 1024)
    query_blocks = query_head.reshape(LENGTH // block_size, block_size, HD)

    def one_block(query_block):
        scores = jnp.dot(query_block, key_head.T, preferred_element_type=jnp.float32) * HD ** (-0.5)
        row_max = lax.optimization_barrier(jnp.max(scores, axis=1, keepdims=True))
        expo = jnp.exp(scores - row_max)
        denom = lax.optimization_barrier(jnp.sum(expo, axis=1, keepdims=True))
        probs = expo.astype(jnp.bfloat16)
        return (jnp.dot(probs, value_head, preferred_element_type=jnp.float32) / denom).astype(jnp.bfloat16)
    return lax.map(one_block, query_blocks).reshape(LENGTH, HD)

def reference(hidden_in, attn_gain, w_query, w_keyval, q_gain, k_gain, w_out, moe_gain, expert_ids, gate_fixed, w_gateup, w_down):
    mixed_parts = []
    group_size = HQ // HK
    for micro in range(MB):
        tokens = hidden_in[micro].astype(jnp.float32)
        normed = rms_rows(tokens, attn_gain).astype(jnp.bfloat16)
        query_raw = jnp.dot(normed, w_query, preferred_element_type=jnp.float32).reshape(LENGTH, HQ, HD)
        key_raw = jnp.dot(normed, w_keyval[0], preferred_element_type=jnp.float32).reshape(LENGTH, HK, HD)
        value_raw = jnp.dot(normed, w_keyval[1], preferred_element_type=jnp.float32).reshape(LENGTH, HK, HD)
        queries = rms_rows(query_raw, q_gain).astype(jnp.bfloat16)
        key_rows = rms_rows(key_raw, k_gain).astype(jnp.bfloat16)
        value_rows = value_raw.astype(jnp.bfloat16)
        query_heads = jnp.transpose(queries, (1, 0, 2))
        key_heads = jnp.repeat(jnp.transpose(key_rows, (1, 0, 2)), group_size, axis=0)
        value_heads = jnp.repeat(jnp.transpose(value_rows, (1, 0, 2)), group_size, axis=0)
        context_heads = lax.map(attend_head, (query_heads, key_heads, value_heads))
        context = jnp.transpose(context_heads, (1, 0, 2)).reshape(LENGTH, HQ * HD)
        mixed_parts.append(tokens + jnp.dot(context, w_out, preferred_element_type=jnp.float32))
    mixed = jnp.concatenate(mixed_parts, axis=0)
    moe_in = rms_rows(mixed, moe_gain).astype(jnp.bfloat16)
    total_rows = MB * LENGTH
    block_count = total_rows // ROWS
    expert_flat = expert_ids.reshape(block_count, ROWS * TOP).astype(jnp.int32)
    onehot = (expert_flat[:, :, None] == jnp.arange(EXPERTS, dtype=jnp.int32)[None, None, :]).astype(jnp.int32)
    ranking = lax.optimization_barrier(jnp.sum((jnp.cumsum(onehot, axis=1) - onehot) * onehot, axis=2))
    capacity = block_count * MOST
    block_index = jnp.arange(block_count, dtype=jnp.int32)[:, None]
    slot_index = (expert_flat * capacity + block_index * MOST + ranking).reshape(-1).astype(jnp.int32)
    owner_row = (jnp.arange(total_rows * TOP, dtype=jnp.int32) // TOP).astype(jnp.int32)
    fixed_gates = gate_fixed.reshape(total_rows, TOP).astype(jnp.float32)
    gate_share = (fixed_gates / lax.optimization_barrier(jnp.sum(fixed_gates, axis=1, keepdims=True))).reshape(-1)
    table = jnp.full((EXPERTS * capacity,), total_rows, jnp.int32).at[slot_index].set(owner_row)
    weight_table = jnp.zeros((EXPERTS * capacity,), jnp.float32).at[slot_index].set(gate_share)
    source = jnp.concatenate([moe_in, jnp.zeros((1, D), jnp.bfloat16)], axis=0)

    def one_expert(running, packed):
        index_rows, weight_rows, gateup_weight, down_weight = packed
        chosen = source[index_rows]
        gate_up = jnp.dot(chosen, gateup_weight, preferred_element_type=jnp.float32)
        expert_hidden = (jax.nn.silu(gate_up[:, :FFE]) * gate_up[:, FFE:]).astype(jnp.bfloat16)
        expert_out = jnp.dot(expert_hidden, down_weight, preferred_element_type=jnp.float32).astype(jnp.bfloat16)
        expert_out = lax.optimization_barrier(expert_out)
        return (running.at[index_rows].add(expert_out.astype(jnp.float32) * weight_rows[:, None]), None)
    routed, _ = lax.scan(one_expert, jnp.zeros((total_rows + 1, D), jnp.float32), (table.reshape(EXPERTS, capacity), weight_table.reshape(EXPERTS, capacity), w_gateup, w_down))
    return (mixed + routed[:total_rows]).astype(jnp.bfloat16).reshape(MB, LENGTH, D)
```

```python
import math

import jax
import jax.numpy as jnp
from jax import lax
from jax.sharding import PartitionSpec as P


EVERY = ("role", "seq", "rep")


def rms_rows(values_in, gain_vec):
    return (
        values_in
        * lax.rsqrt(jnp.mean(values_in * values_in, axis=-1, keepdims=True) + 1e-06)
        * gain_vec
    )


def per_device(
    hidden_in,
    attn_gain,
    w_query,
    w_keyval,
    q_gain,
    k_gain,
    w_out,
    moe_gain,
    expert_ids,
    gate_fixed,
    w_gateup,
    w_down,
):
    tokens = hidden_in[0]
    row_count, model_width = tokens.shape
    head_dim = q_gain.shape[0]
    local_heads = w_query.shape[1] // head_dim
    kv_heads = w_keyval.shape[2] // head_dim
    all_heads = local_heads * lax.axis_size("rep")
    group_size = all_heads // kv_heads
    kv_index = lax.axis_index("rep") * local_heads // group_size
    kv_width = kv_heads * head_dim
    top_count = expert_ids.shape[2]
    routes = lax.all_gather(
        jnp.concatenate([expert_ids[0], gate_fixed[0]], axis=1), EVERY, axis=0, tiled=True
    )
    normed = rms_rows(tokens.astype(jnp.float32), attn_gain).astype(jnp.bfloat16)
    gathered = lax.all_gather(normed, "rep", axis=0, tiled=True)
    own_keys = jnp.dot(normed, w_keyval[0], preferred_element_type=jnp.float32)
    own_values = jnp.dot(normed, w_keyval[1], preferred_element_type=jnp.float32)
    own_keys = rms_rows(own_keys.reshape(row_count, kv_heads, head_dim), k_gain)
    own_kv = jnp.concatenate([own_keys.reshape(row_count, kv_width), own_values], axis=1)
    all_kv = lax.all_gather(own_kv.astype(jnp.bfloat16), ("seq", "rep"), axis=0, tiled=True)
    key_piece = lax.dynamic_slice_in_dim(all_kv, kv_index * head_dim, head_dim, 1)
    value_piece = lax.dynamic_slice_in_dim(all_kv, kv_width + kv_index * head_dim, head_dim, 1)
    projected = jnp.dot(gathered, w_query, preferred_element_type=jnp.float32)
    query_span = projected.shape[0]
    query_part = projected.reshape(query_span, local_heads, head_dim)
    queries = rms_rows(query_part, q_gain).astype(jnp.bfloat16)
    score_scale = head_dim ** (-0.5)
    initial = (
        jnp.full((query_span, local_heads), -1e30, jnp.float32),
        jnp.zeros((query_span, local_heads), jnp.float32),
        jnp.zeros((query_span, local_heads, head_dim), jnp.float32),
    )
    key_count = key_piece.shape[0]
    block_size = math.gcd(key_count, 1024)
    key_blocks = key_piece.reshape(key_count // block_size, block_size, head_dim)
    value_blocks = value_piece.reshape(key_count // block_size, block_size, head_dim)

    def one_block(state, blocks):
        run_max, run_sum, run_acc = state
        key_block, value_block = blocks
        scores = (
            jnp.einsum("qhd,kd->qhk", queries, key_block, preferred_element_type=jnp.float32)
            * score_scale
        )
        new_max = jnp.maximum(run_max, jnp.max(scores, axis=2))
        rescale = jnp.exp(run_max - new_max)
        weights = jnp.exp(scores - new_max[:, :, None])
        run_sum = run_sum * rescale + jnp.sum(weights, axis=2)
        run_acc = run_acc * rescale[:, :, None] + jnp.einsum(
            "qhk,kd->qhd",
            weights.astype(jnp.bfloat16),
            value_block,
            preferred_element_type=jnp.float32,
        )
        return ((new_max, run_sum, run_acc), None)

    final_state, _ = lax.scan(one_block, initial, (key_blocks, value_blocks))
    run_max, run_sum, run_acc = final_state
    context = (
        (run_acc / run_sum[:, :, None])
        .astype(jnp.bfloat16)
        .reshape(query_span, local_heads * head_dim)
    )
    attended = lax.psum_scatter(
        jnp.dot(context, w_out, preferred_element_type=jnp.float32).astype(jnp.bfloat16),
        "rep",
        scatter_dimension=0,
        tiled=True,
    ).astype(jnp.float32)
    mixed = tokens.astype(jnp.float32) + attended
    moe_in = rms_rows(mixed, moe_gain).astype(jnp.bfloat16)
    everyone = moe_in
    for axis in reversed(EVERY) if lax.axis_size(EVERY) > 32 else (EVERY,):
        everyone = lax.all_gather(everyone, axis, axis=0, tiled=True)
    hidden_width = w_down.shape[1]
    my_expert = lax.axis_index(EVERY)
    gates = routes[:, top_count:].astype(jnp.float32)
    mine = jnp.sum(jnp.where(routes[:, :top_count] == my_expert, gates, 0.0), axis=1)
    share = mine / jnp.sum(gates, axis=1)
    span = math.gcd(everyone.shape[0], 2048)

    def one_span(packed):
        span_rows, span_share = packed
        gate_up = jnp.dot(span_rows, w_gateup[0], preferred_element_type=jnp.float32)
        expert_hidden = (
            jax.nn.silu(gate_up[:, :hidden_width]) * gate_up[:, hidden_width:]
        ).astype(jnp.bfloat16)
        served = jnp.dot(expert_hidden, w_down[0], preferred_element_type=jnp.float32)
        served = served.astype(jnp.bfloat16).astype(jnp.float32)
        return (served * span_share[:, None]).astype(jnp.bfloat16)

    weighted = lax.map(
        one_span, (everyone.reshape(-1, span, model_width), share.reshape(-1, span))
    ).reshape(-1, model_width)
    routed = lax.psum_scatter(weighted, EVERY, scatter_dimension=0, tiled=True).astype(jnp.float32)
    return (mixed + routed).astype(jnp.bfloat16)[None]


def solution(mesh):
    placed = (
        P("role", ("seq", "rep"), None),
        P(),
        P(None, "rep"),
        P(),
        P(),
        P(),
        P("rep", None),
        P(),
        P("role", ("seq", "rep"), None),
        P("role", ("seq", "rep"), None),
        P(("role", "seq", "rep"), None, None),
        P(("role", "seq", "rep"), None, None),
    )
    return jax.shard_map(
        per_device,
        mesh=mesh,
        in_specs=placed,
        out_specs=P("role", ("seq", "rep"), None),
        check_vma=False,
    )
```

```python
import jax
import jax.numpy as jnp
from jax import lax
from jax.experimental import pallas as pl
from jax.experimental.pallas import tpu as pltpu
from jax.sharding import PartitionSpec as P

EVERY = ("role", "seq", "rep")
PAIR = 1
ACROSS = 2
TILE = 256


def rms_rows(values_in, gain_vec):
    return (
        values_in
        * lax.rsqrt(jnp.mean(values_in * values_in, axis=-1, keepdims=True) + 1e-06)
        * gain_vec
    )


def swap(block, axis, bits):
    size = lax.axis_size(axis)
    return lax.ppermute(block, axis, [(i, i ^ bits) for i in range(size)])


def along_seq(block):
    return [swap(block, "seq", bits) for bits in range(1, lax.axis_size("seq"))]


def spread_routes(own):
    near = jnp.concatenate([own] + along_seq(own), axis=0)
    by_rep = swap(near, "rep", ACROSS)
    both = jnp.stack([near, by_rep])
    return jnp.concatenate([both, swap(both, "role", 1)], axis=0)


def spread_rows(own):
    half = own.shape[1] // 2
    parts = [own, jnp.concatenate(along_seq(own), axis=0)]
    pieces = []
    for part in parts:
        by_rep = swap(part, "rep", ACROSS)
        by_role = swap(part, "role", 1)
        corner_low = swap(by_rep[:, :half], "role", 1)
        corner_high = swap(by_role[:, half:], "rep", ACROSS)
        pieces.append((part, by_rep, by_role, corner_low, corner_high))
    return pieces


def added(first, second):
    return (first.astype(jnp.float32) + second.astype(jnp.float32)).astype(jnp.bfloat16)


def collect_rows(parts, row_count):
    lows, highs = parts
    corner_low = swap(lows[3], "role", 1)
    corner_high = swap(highs[3], "rep", ACROSS)
    straight_low = swap(lows[2], "role", 1)
    straight_high = swap(highs[1], "rep", ACROSS)
    turned_low = swap(added(lows[1], corner_low), "rep", ACROSS)
    turned_high = swap(added(highs[2], corner_high), "role", 1)
    totals = []
    for base, first, second in (
        (lows[0], straight_low, turned_low),
        (highs[0], straight_high, turned_high),
    ):
        near = base.astype(jnp.float32) + first.astype(jnp.float32) + second.astype(jnp.float32)
        total = near[:row_count]
        rounded = near.astype(jnp.bfloat16)
        for bits in range(1, lax.axis_size("seq")):
            block = rounded[bits * row_count : (bits + 1) * row_count]
            total = total + swap(block, "seq", bits).astype(jnp.float32)
        totals.append(total)
    return jnp.concatenate(totals, axis=1)


def expert_kernel(
    row_count,
    pick_ref,
    place_ref,
    share_ref,
    own_gu_ref,
    far_gu_ref,
    own_dn_ref,
    far_dn_ref,
    *refs,
):
    piece_refs, out_refs = refs[:10], refs[10:18]
    x_buf, xs_buf, gu_buf, dn_buf, hid_buf, served_buf, y_buf, x_sem, w_sem, y_sem = refs[18:]
    groups, group_rows = place_ref.shape[1], place_ref.shape[2]
    slots = place_ref.shape[3]
    width = x_buf.shape[2]
    half = width // 2
    hidden = own_dn_ref.shape[0]
    tiles = hidden // TILE
    depth = x_buf.shape[0]

    def row_copies(group):
        copies = []
        for which in range(2):
            start = which * row_count
            rows = pl.ds(start, row_count if which == 0 else group_rows - row_count)
            base = piece_refs[5 * which : 5 * which + 5]
            slot = group % depth
            if group < 3:
                copies.append((base[group], x_buf.at[slot, rows]))
            else:
                copies.append((base[3], x_buf.at[slot, rows, pl.ds(0, half)]))
                copies.append((base[4], x_buf.at[slot, rows, pl.ds(half, half)]))
        return [
            pltpu.make_async_copy(src, dst, x_sem.at[group, number])
            for number, (src, dst) in enumerate(copies)
        ]

    weight_copies = []
    for expert, (gu_ref, dn_ref) in enumerate(((own_gu_ref, own_dn_ref), (far_gu_ref, far_dn_ref))):
        mine = []
        for tile in range(tiles):
            for side in range(2):
                mine.append(
                    pltpu.make_async_copy(
                        gu_ref.at[:, pl.ds(side * hidden + tile * TILE, TILE)],
                        gu_buf.at[expert, tile, side],
                        w_sem.at[expert, 2 * tile + side],
                    )
                )
        mine.append(pltpu.make_async_copy(dn_ref, dn_buf.at[expert], w_sem.at[expert, 2 * tiles]))
        weight_copies.append(mine)

    for group in range(min(depth, groups)):
        for copy in row_copies(group):
            copy.start()
    for mine in weight_copies:
        for copy in mine:
            copy.start()

    for group in range(groups):
        for copy in row_copies(group):
            copy.wait()
        chosen = jnp.dot(
            pick_ref[group], x_buf[group % depth], preferred_element_type=jnp.float32
        ).astype(jnp.bfloat16)
        xs_buf[0, pl.ds(group * slots, slots)] = chosen[:slots]
        xs_buf[1, pl.ds(group * slots, slots)] = chosen[slots:]
        if group + depth < groups:
            for copy in row_copies(group + depth):
                copy.start()

    for expert in range(2):
        for tile in range(tiles):
            weight_copies[expert][2 * tile].wait()
            weight_copies[expert][2 * tile + 1].wait()
            gate = jnp.dot(
                xs_buf[expert], gu_buf[expert, tile, 0], preferred_element_type=jnp.float32
            )
            up = jnp.dot(
                xs_buf[expert], gu_buf[expert, tile, 1], preferred_element_type=jnp.float32
            )
            value = gate / (1.0 + jnp.exp(-gate)) * up
            hid_buf[:, tile * TILE : (tile + 1) * TILE] = value.astype(jnp.bfloat16)
        weight_copies[expert][2 * tiles].wait()
        for column in range(0, width, 2 * TILE):
            served_buf[expert, :, column : column + 2 * TILE] = jnp.dot(
                hid_buf[...],
                dn_buf[expert, :, column : column + 2 * TILE],
                preferred_element_type=jnp.float32,
            ).astype(jnp.bfloat16)

    def out_copies(group):
        return [
            pltpu.make_async_copy(
                y_buf.at[group % depth, :, pl.ds(side * half, half)],
                out_refs[2 * group + side],
                y_sem.at[group, side],
            )
            for side in range(2)
        ]

    for number, group in enumerate(reversed(range(groups))):
        if number >= depth:
            for copy in out_copies(group + depth):
                copy.wait()
        for column in range(0, width, 2 * TILE):
            total = None
            for expert in range(2):
                placed = jnp.dot(
                    place_ref[expert, group],
                    served_buf[expert, pl.ds(group * slots, slots), column : column + 2 * TILE],
                    preferred_element_type=jnp.float32,
                )
                term = placed * share_ref[group, :, expert : expert + 1]
                total = term if total is None else total + term
            y_buf[group % depth, :, column : column + 2 * TILE] = total.astype(jnp.bfloat16)
        for copy in out_copies(group):
            copy.start()
    for group in range(min(depth, groups)):
        for copy in out_copies(group):
            copy.wait()


def run_experts(pieces, pick, place, share, own_gu, far_gu, own_dn, far_dn):
    row_count, width = pieces[0][0].shape
    groups, group_rows, slots = place.shape[1:]
    hidden = own_dn.shape[0]
    tiles = hidden // TILE
    depth = groups if groups * group_rows * width <= 1 << 22 else 2
    anywhere = pl.BlockSpec(memory_space=pl.ANY)
    inside = pl.BlockSpec(memory_space=pltpu.VMEM)
    outs = pl.pallas_call(
        lambda *refs: expert_kernel(row_count, *refs),
        out_shape=[jax.ShapeDtypeStruct((group_rows, width // 2), jnp.bfloat16)] * (2 * groups),
        in_specs=[inside] * 3 + [anywhere] * 14,
        out_specs=[anywhere] * (2 * groups),
        scratch_shapes=[
            pltpu.VMEM((depth, group_rows, width), jnp.bfloat16),
            pltpu.VMEM((2, groups * slots, width), jnp.bfloat16),
            pltpu.VMEM((2, tiles, 2, width, TILE), jnp.bfloat16),
            pltpu.VMEM((2, hidden, width), jnp.bfloat16),
            pltpu.VMEM((groups * slots, hidden), jnp.bfloat16),
            pltpu.VMEM((2, groups * slots, width), jnp.bfloat16),
            pltpu.VMEM((depth, group_rows, width), jnp.bfloat16),
            pltpu.SemaphoreType.DMA((groups, 4)),
            pltpu.SemaphoreType.DMA((2, 2 * tiles + 1)),
            pltpu.SemaphoreType.DMA((groups, 2)),
        ],
        compiler_params=pltpu.CompilerParams(vmem_limit_bytes=56 * 1024 * 1024),
        cost_estimate=pl.CostEstimate(
            flops=12 * groups * slots * width * hidden,
            bytes_accessed=12 * width * hidden + 8 * groups * group_rows * width // 2,
            transcendentals=2 * groups * slots * hidden,
        ),
        name="experts",
    )(pick, place, share, own_gu, far_gu, own_dn, far_dn, *pieces[0], *pieces[1])
    return outs[0::2], outs[1::2]


def per_device(
    hidden_in,
    attn_gain,
    w_query,
    w_keyval,
    q_gain,
    k_gain,
    w_out,
    moe_gain,
    expert_ids,
    gate_fixed,
    w_gateup,
    w_down,
):
    tokens = hidden_in[0].astype(jnp.float32)
    row_count, model_width = tokens.shape
    head_dim = q_gain.shape[0]
    local_heads = w_query.shape[1] // head_dim
    kv_heads = w_keyval.shape[2] // head_dim
    group_size = local_heads * lax.axis_size("rep") // kv_heads
    rep_index = lax.axis_index("rep")
    kv_width = kv_heads * head_dim
    top_count = expert_ids.shape[2]
    expert_count = lax.axis_size(EVERY)

    normed = rms_rows(tokens, attn_gain).astype(jnp.bfloat16)
    pair_rows = swap(normed, "rep", PAIR)
    across_rows = swap(normed, "rep", ACROSS)
    own_keys = jnp.dot(normed, w_keyval[0], preferred_element_type=jnp.float32)
    own_values = jnp.dot(normed, w_keyval[1], preferred_element_type=jnp.float32)
    own_keys = rms_rows(own_keys.reshape(row_count, kv_heads, head_dim), k_gain)
    own_keys = own_keys.reshape(row_count, kv_width).astype(jnp.bfloat16)
    own_kv = jnp.concatenate([own_keys, own_values.astype(jnp.bfloat16)], axis=1)
    line_kv = jnp.concatenate([own_kv] + along_seq(own_kv), axis=0)

    def head_kv(rep):
        index = rep * local_heads // group_size * head_dim
        return jnp.concatenate(
            [
                lax.dynamic_slice_in_dim(line_kv, index, head_dim, 1),
                lax.dynamic_slice_in_dim(line_kv, kv_width + index, head_dim, 1),
            ],
            axis=1,
        )

    far_kv = swap(head_kv(rep_index ^ ACROSS), "rep", ACROSS)
    half_kv = jnp.concatenate([head_kv(rep_index), far_kv], axis=0)
    all_kv = jnp.concatenate([half_kv, swap(half_kv, "rep", PAIR)], axis=0)
    key_rows, value_rows = all_kv[:, :head_dim], all_kv[:, head_dim:]

    corner_rows = swap(across_rows, "rep", PAIR)
    gathered = jnp.concatenate([normed, pair_rows, across_rows, corner_rows], axis=0)
    far_gu = swap(w_gateup[0], "rep", PAIR)
    far_dn = swap(w_down[0], "rep", PAIR)
    projected = jnp.dot(gathered, w_query, preferred_element_type=jnp.float32)
    query_span = projected.shape[0]
    query_part = projected.reshape(query_span, local_heads, head_dim)
    queries = rms_rows(query_part, q_gain).astype(jnp.bfloat16)
    scores = jnp.einsum("qhd,kd->hqk", queries, key_rows, preferred_element_type=jnp.float32)
    scores = scores * head_dim ** (-0.5)
    weights = jnp.exp(scores - jnp.max(scores, axis=2, keepdims=True))
    denom = jnp.sum(weights, axis=2)
    context = jnp.einsum(
        "hqk,kd->qhd", weights.astype(jnp.bfloat16), value_rows, preferred_element_type=jnp.float32
    )
    context = (context / denom.T[:, :, None]).astype(jnp.bfloat16)
    context = context.reshape(query_span, local_heads * head_dim)
    partial = jnp.dot(context, w_out, preferred_element_type=jnp.float32)
    partial = partial.reshape(4, row_count, model_width)
    back = swap(jnp.stack([partial[1], partial[3]]), "rep", PAIR)
    far_sum = (partial[2] + back[1]).astype(jnp.bfloat16)
    mixed = tokens + (partial[0] + back[0]) + swap(far_sum, "rep", ACROSS).astype(jnp.float32)
    moe_in = rms_rows(mixed, moe_gain).astype(jnp.bfloat16)

    routes = spread_routes(jnp.concatenate([expert_ids[0], gate_fixed[0]], axis=1))
    groups, group_rows = routes.shape[:2]
    capacity = max(2, 7 * row_count * top_count // (4 * expert_count))
    slots = -(-capacity * (group_rows // row_count) // 16) * 16
    gates = routes[:, :, top_count:].astype(jnp.float32)
    gate_sum = jnp.sum(gates, axis=2)
    earlier = jnp.tri(group_rows, k=-1, dtype=jnp.bfloat16)
    picks, shares = [], []
    for expert in (lax.axis_index(EVERY), lax.axis_index(EVERY) ^ PAIR):
        named = routes[:, :, :top_count] == expert
        hit = jnp.any(named, axis=2)
        shares.append(jnp.sum(jnp.where(named, gates, 0.0), axis=2) / gate_sum)
        rank = jnp.einsum(
            "ij,gj->gi", earlier, hit.astype(jnp.bfloat16), preferred_element_type=jnp.float32
        )
        rank = jnp.where(hit, rank.astype(jnp.int32), -1)
        picks.append((rank[:, None, :] == jnp.arange(slots)[None, :, None]).astype(jnp.bfloat16))
    pick = jnp.concatenate(picks, axis=1)
    place = jnp.stack([jnp.swapaxes(one, 1, 2) for one in picks])
    share = jnp.stack(shares, axis=2)

    parts = run_experts(
        spread_rows(moe_in), pick, place, share, w_gateup[0], far_gu, w_down[0], far_dn
    )
    routed = collect_rows(parts, row_count)
    return (mixed + routed).astype(jnp.bfloat16)[None]


def solution(mesh):
    placed = (
        P("role", ("seq", "rep"), None),
        P(),
        P(None, "rep"),
        P(),
        P(),
        P(),
        P("rep", None),
        P(),
        P("role", ("seq", "rep"), None),
        P("role", ("seq", "rep"), None),
        P(("role", "seq", "rep"), None, None),
        P(("role", "seq", "rep"), None, None),
    )
    return jax.shard_map(
        per_device,
        mesh=mesh,
        in_specs=placed,
        out_specs=P("role", ("seq", "rep"), None),
        check_vma=False,
    )
```

```python
import jax
import jax.numpy as jnp
from jax import lax
from jax.experimental import pallas as pl
from jax.experimental.pallas import tpu as pltpu
from jax.sharding import PartitionSpec as P

EVERY = ("role", "seq", "rep")
PAIR = 1
ACROSS = 2
TILE = 256


def rms_rows(values_in, gain_vec):
    return (
        values_in
        * lax.rsqrt(jnp.mean(values_in * values_in, axis=-1, keepdims=True) + 1e-06)
        * gain_vec
    )


def swap(block, axis, bits):
    size = lax.axis_size(axis)
    return lax.ppermute(block, axis, [(i, i ^ bits) for i in range(size)])


def seq_bits():
    size = lax.axis_size("seq")
    return [1 << place for place in reversed(range(size.bit_length() - 1))]


def seq_blocks(own):
    blocks = [own]
    for bits in seq_bits():
        blocks = blocks + [swap(block, "seq", bits) for block in blocks]
    return blocks


def spread_routes(own):
    near = jnp.concatenate(seq_blocks(own), axis=0)
    both = jnp.stack([near, swap(near, "rep", ACROSS)])
    return jnp.concatenate([both, swap(both, "role", 1)], axis=0)


def ready(*arrays):
    return lax.optimization_barrier(arrays)


def spread_rows(own, early_work):
    half = own.shape[1] // 2

    def both_ways(part):
        return swap(part, "rep", ACROSS), swap(part, "role", 1)

    def corners(by_rep, by_role):
        return swap(by_rep[:, :half], "role", 1), swap(by_role[:, half:], "rep", ACROSS)

    first_bits, *bits_left = seq_bits()
    blocks = [own, swap(own, "seq", first_bits)]
    for bits in bits_left[:-1]:
        blocks = blocks + [swap(block, "seq", bits) for block in blocks]
    beyond = [swap(block, "seq", bits_left[-1]) for block in blocks[:-1]]
    outer = both_ways(own)
    middle = jnp.concatenate(blocks[1:] + beyond, axis=0)
    middle, by_rep, by_role = ready(middle, *outer)
    outer = by_rep, by_role
    last = swap(blocks[-1], "seq", bits_left[-1])
    rows = own.shape[0] + middle.shape[0] + last.shape[0]
    inner = both_ways(middle)
    outer_corner = corners(*outer)
    last, *outer_corner = ready(last, *outer_corner)
    final = both_ways(last)
    inner_corner = corners(*inner)
    early = early_work([(0, 0, own), (own.shape[0], 0, middle), (rows - last.shape[0], 0, last)])
    by_rep, by_role, *early = ready(*final, *early)
    final_corner = corners(by_rep, by_role)
    groups = [[], [], []]
    start = 0
    for part, beside, corner in (
        (own, outer, outer_corner),
        (middle, inner, inner_corner),
        (last, final, final_corner),
    ):
        groups[0].append((start, 0, beside[0]))
        groups[1].append((start, 0, beside[1]))
        groups[2].append((start, 0, corner[0]))
        groups[2].append((start, half, corner[1]))
        start += part.shape[0]
    return early, groups


def added(first, second):
    return (first.astype(jnp.float32) + second.astype(jnp.float32)).astype(jnp.bfloat16)


def collect_rows(near, by_rep, by_role, corner):
    straight_low = swap(by_role[0], "role", 1)
    straight_high = swap(by_rep[1], "rep", ACROSS)
    straight_low, straight_high, *corner = ready(straight_low, straight_high, *corner)
    corner_low, corner_high = ready(
        swap(corner[0], "role", 1), swap(corner[1], "rep", ACROSS)
    )
    cut = near[0].shape[0] // 2
    low_sum, high_sum = added(by_rep[0], corner_low), added(by_role[1], corner_high)

    def merged(rows, turned_low, turned_high):
        return jnp.concatenate(
            [
                base[rows].astype(jnp.float32)
                + first[rows].astype(jnp.float32)
                + second.astype(jnp.float32)
                for base, first, second in (
                    (near[0], straight_low, turned_low),
                    (near[1], straight_high, turned_high),
                )
            ],
            axis=1,
        )

    def turned(rows):
        return swap(low_sum[rows], "rep", ACROSS), swap(high_sum[rows], "role", 1)

    *far, low_sum, high_sum = ready(*turned(slice(cut, None)), low_sum, high_sum)
    leaving = merged(slice(cut, None), *far).astype(jnp.bfloat16)
    *beside, _ = ready(*turned(slice(0, cut)), leaving)
    total = merged(slice(0, cut), *beside)
    for bits in reversed(seq_bits()):
        total = total + swap(leaving, "seq", bits).astype(jnp.float32)
        if bits != seq_bits()[0]:
            cut = total.shape[0] // 2
            total, leaving = total[:cut], total[cut:].astype(jnp.bfloat16)
    return total


def expert_kernel(spots, *refs):
    pick_ref, place_ref, share_ref, own_gu_ref, far_gu_ref, own_dn_ref, far_dn_ref = refs[:7]
    groups, group_rows, slots = place_ref.shape[1:]
    piece_refs = refs[7 : 7 + len(spots)]
    out_refs = refs[7 + len(spots) : 7 + len(spots) + 2 * groups]
    x_buf, xs_buf, gu_buf, dn_buf, hid_buf, served_buf, y_buf, x_sem, w_sem, y_sem = refs[
        7 + len(spots) + 2 * groups :
    ]
    width = x_buf.shape[2]
    half = width // 2
    hidden = own_dn_ref.shape[0]
    tiles = hidden // TILE

    row_copies = []
    for number, ((group, row, column), piece) in enumerate(zip(spots, piece_refs)):
        rows, columns = piece.shape
        target = x_buf.at[group, pl.ds(row, rows), pl.ds(column, columns)]
        row_copies.append((group, pltpu.make_async_copy(piece, target, x_sem.at[number])))
    weight_copies = []
    for expert, (gu_ref, dn_ref) in enumerate(((own_gu_ref, own_dn_ref), (far_gu_ref, far_dn_ref))):
        mine = []
        for tile in range(tiles):
            for side in range(2):
                mine.append(
                    pltpu.make_async_copy(
                        gu_ref.at[:, pl.ds(side * hidden + tile * TILE, TILE)],
                        gu_buf.at[expert, tile, side],
                        w_sem.at[expert, 2 * tile + side],
                    )
                )
        mine.append(pltpu.make_async_copy(dn_ref, dn_buf.at[expert], w_sem.at[expert, 2 * tiles]))
        weight_copies.append(mine)
    for _, copy in row_copies:
        copy.start()
    for mine in weight_copies:
        for copy in mine:
            copy.start()

    for group in range(groups):
        for where, copy in row_copies:
            if where == group:
                copy.wait()
        chosen = jnp.dot(
            pick_ref[group], x_buf[group], preferred_element_type=jnp.float32
        ).astype(jnp.bfloat16)
        xs_buf[0, pl.ds(group * slots, slots)] = chosen[:slots]
        xs_buf[1, pl.ds(group * slots, slots)] = chosen[slots:]

    for expert in range(2):
        for tile in range(tiles):
            weight_copies[expert][2 * tile].wait()
            weight_copies[expert][2 * tile + 1].wait()
            gate = jnp.dot(
                xs_buf[expert], gu_buf[expert, tile, 0], preferred_element_type=jnp.float32
            )
            up = jnp.dot(
                xs_buf[expert], gu_buf[expert, tile, 1], preferred_element_type=jnp.float32
            )
            value = gate / (1.0 + jnp.exp(-gate)) * up
            hid_buf[:, tile * TILE : (tile + 1) * TILE] = value.astype(jnp.bfloat16)
        weight_copies[expert][2 * tiles].wait()
        for column in range(0, width, 2 * TILE):
            served_buf[expert, :, column : column + 2 * TILE] = jnp.dot(
                hid_buf[...],
                dn_buf[expert, :, column : column + 2 * TILE],
                preferred_element_type=jnp.float32,
            ).astype(jnp.bfloat16)

    out_copies = []
    for group in range(groups):
        for column in range(0, width, 2 * TILE):
            total = None
            for expert in range(2):
                placed = jnp.dot(
                    place_ref[expert, group],
                    served_buf[expert, pl.ds(group * slots, slots), column : column + 2 * TILE],
                    preferred_element_type=jnp.float32,
                )
                term = placed * share_ref[group, :, expert : expert + 1]
                total = term if total is None else total + term
            y_buf[group, :, column : column + 2 * TILE] = total.astype(jnp.bfloat16)
        for side in range(2):
            copy = pltpu.make_async_copy(
                y_buf.at[group, :, pl.ds(side * half, half)],
                out_refs[2 * group + side],
                y_sem.at[group, side],
            )
            copy.start()
            out_copies.append(copy)
    for copy in out_copies:
        copy.wait()


def run_experts(pieces, pick, place, share, weights):
    groups, group_rows, slots = place.shape[1:]
    hidden, width = weights[2].shape
    tiles = hidden // TILE
    spots = [
        (group, row, column) for group, held in enumerate(pieces) for row, column, _ in held
    ]
    arrays = [array for held in pieces for _, _, array in held]
    anywhere = pl.BlockSpec(memory_space=pl.ANY)
    inside = pl.BlockSpec(memory_space=pltpu.VMEM)
    outs = pl.pallas_call(
        lambda *refs: expert_kernel(spots, *refs),
        out_shape=[jax.ShapeDtypeStruct((group_rows, width // 2), jnp.bfloat16)] * (2 * groups),
        in_specs=[inside] * 3 + [anywhere] * (4 + len(arrays)),
        out_specs=[anywhere] * (2 * groups),
        scratch_shapes=[
            pltpu.VMEM((groups, group_rows, width), jnp.bfloat16),
            pltpu.VMEM((2, groups * slots, width), jnp.bfloat16),
            pltpu.VMEM((2, tiles, 2, width, TILE), jnp.bfloat16),
            pltpu.VMEM((2, hidden, width), jnp.bfloat16),
            pltpu.VMEM((groups * slots, hidden), jnp.bfloat16),
            pltpu.VMEM((2, groups * slots, width), jnp.bfloat16),
            pltpu.VMEM((groups, group_rows, width), jnp.bfloat16),
            pltpu.SemaphoreType.DMA((len(arrays),)),
            pltpu.SemaphoreType.DMA((2, 2 * tiles + 1)),
            pltpu.SemaphoreType.DMA((groups, 2)),
        ],
        compiler_params=pltpu.CompilerParams(vmem_limit_bytes=52 * 1024 * 1024),
        cost_estimate=pl.CostEstimate(
            flops=12 * groups * slots * width * hidden,
            bytes_accessed=12 * width * hidden + 4 * groups * group_rows * width,
            transcendentals=2 * groups * slots * hidden,
        ),
        name="experts",
    )(pick, place, share, *weights, *arrays)
    return [(outs[2 * group], outs[2 * group + 1]) for group in range(groups)]


def per_device(
    hidden_in,
    attn_gain,
    w_query,
    w_keyval,
    q_gain,
    k_gain,
    w_out,
    moe_gain,
    expert_ids,
    gate_fixed,
    w_gateup,
    w_down,
):
    tokens = hidden_in[0].astype(jnp.float32)
    row_count, model_width = tokens.shape
    head_dim = q_gain.shape[0]
    local_heads = w_query.shape[1] // head_dim
    kv_heads = w_keyval.shape[2] // head_dim
    group_size = local_heads * lax.axis_size("rep") // kv_heads
    rep_index = lax.axis_index("rep")
    kv_width = kv_heads * head_dim
    top_count = expert_ids.shape[2]
    expert_count = lax.axis_size(EVERY)

    normed = lax.optimization_barrier(rms_rows(tokens, attn_gain).astype(jnp.bfloat16))
    pair_rows = swap(normed, "rep", PAIR)
    across_rows = swap(normed, "rep", ACROSS)
    own_keys = jnp.dot(normed, w_keyval[0], preferred_element_type=jnp.float32)
    own_values = jnp.dot(normed, w_keyval[1], preferred_element_type=jnp.float32)
    own_keys = rms_rows(own_keys.reshape(row_count, kv_heads, head_dim), k_gain)
    own_keys = own_keys.reshape(row_count, kv_width).astype(jnp.bfloat16)
    own_kv = jnp.concatenate([own_keys, own_values.astype(jnp.bfloat16)], axis=1)
    line_kv = jnp.concatenate(seq_blocks(own_kv), axis=0)

    def head_kv(rep):
        index = rep * local_heads // group_size * head_dim
        return jnp.concatenate(
            [
                lax.dynamic_slice_in_dim(line_kv, index, head_dim, 1),
                lax.dynamic_slice_in_dim(line_kv, kv_width + index, head_dim, 1),
            ],
            axis=1,
        )

    far_kv = swap(head_kv(rep_index ^ ACROSS), "rep", ACROSS)
    half_kv = jnp.concatenate([head_kv(rep_index), far_kv], axis=0)
    all_kv = jnp.concatenate([half_kv, swap(half_kv, "rep", PAIR)], axis=0)
    key_rows, value_rows = all_kv[:, :head_dim], all_kv[:, head_dim:]

    routes = spread_routes(jnp.concatenate([expert_ids[0], gate_fixed[0]], axis=1))
    groups, group_rows = routes.shape[:2]
    capacity = max(2, 7 * row_count * top_count // (4 * expert_count))
    slots = -(-capacity * (group_rows // row_count) // 16) * 16
    gates = routes[:, :, top_count:].astype(jnp.float32)
    gate_sum = jnp.sum(gates, axis=2)
    earlier = jnp.tri(group_rows, k=-1, dtype=jnp.bfloat16)
    picks, shares = [], []
    for expert in (lax.axis_index(EVERY), lax.axis_index(EVERY) ^ PAIR):
        named = routes[:, :, :top_count] == expert
        hit = jnp.any(named, axis=2)
        shares.append(jnp.sum(jnp.where(named, gates, 0.0), axis=2) / gate_sum)
        rank = jnp.einsum(
            "ij,gj->gi", earlier, hit.astype(jnp.bfloat16), preferred_element_type=jnp.float32
        )
        rank = jnp.where(hit, rank.astype(jnp.int32), -1)
        picks.append((rank[:, None, :] == jnp.arange(slots)[None, :, None]).astype(jnp.bfloat16))
    pick = jnp.concatenate(picks, axis=1)
    place = jnp.stack([jnp.swapaxes(one, 1, 2) for one in picks])
    share = jnp.stack(shares, axis=2)

    corner_rows = swap(across_rows, "rep", PAIR)
    gathered = jnp.concatenate([normed, pair_rows, across_rows, corner_rows], axis=0)
    far_gu = swap(w_gateup[0], "rep", PAIR)
    far_dn = swap(w_down[0], "rep", PAIR)
    projected = jnp.dot(gathered, w_query, preferred_element_type=jnp.float32)
    query_span = projected.shape[0]
    query_part = projected.reshape(query_span, local_heads, head_dim)
    queries = rms_rows(query_part, q_gain).astype(jnp.bfloat16)
    scores = jnp.einsum("qhd,kd->hqk", queries, key_rows, preferred_element_type=jnp.float32)
    scores = scores * head_dim ** (-0.5)
    weights = jnp.exp(scores - jnp.max(scores, axis=2, keepdims=True))
    denom = jnp.sum(weights, axis=2)
    context = jnp.einsum(
        "hqk,kd->qhd", weights.astype(jnp.bfloat16), value_rows, preferred_element_type=jnp.float32
    )
    context = (context / denom.T[:, :, None]).astype(jnp.bfloat16)
    context = context.reshape(query_span, local_heads * head_dim)
    partial = jnp.dot(context, w_out, preferred_element_type=jnp.float32)
    partial = partial.reshape(4, row_count, model_width)
    back = swap(jnp.stack([partial[1], partial[3]]), "rep", PAIR)
    far_sum = (partial[2] + back[1]).astype(jnp.bfloat16)
    mixed = tokens + (partial[0] + back[0]) + swap(far_sum, "rep", ACROSS).astype(jnp.float32)
    mixed, far_gu, far_dn, pick, place, share = lax.optimization_barrier(
        (mixed, far_gu, far_dn, pick, place, share)
    )
    moe_in = rms_rows(mixed, moe_gain).astype(jnp.bfloat16)

    weights = (w_gateup[0], far_gu, w_down[0], far_dn)

    def serve(pieces, first, last):
        return run_experts(
            pieces, pick[first:last], place[:, first:last], share[first:last], weights
        )

    near, rows = spread_rows(moe_in, lambda pieces: serve([pieces], 0, 1)[0])
    by_rep, by_role = serve(rows[:2], 1, 3)
    rep_low, rep_high, role_low, role_high, *held = ready(
        *by_rep, *by_role, *(array for _, _, array in rows[2])
    )
    by_rep, by_role = (rep_low, rep_high), (role_low, role_high)
    pieces = [(row, column, array) for (row, column, _), array in zip(rows[2], held)]
    corner = serve([pieces], 3, 4)
    routed = collect_rows(near, by_rep, by_role, corner[0])
    routed = collect_rows(near, by_rep, by_role, corner[0])
    return (mixed + routed).astype(jnp.bfloat16)[None]


def solution(mesh):
    placed = (
        P("role", ("seq", "rep"), None),
        P(),
        P(None, "rep"),
        P(),
        P(),
        P(),
        P("rep", None),
        P(),
        P("role", ("seq", "rep"), None),
        P("role", ("seq", "rep"), None),
        P(("role", "seq", "rep"), None, None),
        P(("role", "seq", "rep"), None, None),
    )
    return jax.shard_map(
        per_device,
        mesh=mesh,
        in_specs=placed,
        out_specs=P("role", ("seq", "rep"), None),
        check_vma=False,
    )
```

```python
import jax
import jax.numpy as jnp
from jax import lax
from jax.experimental import pallas as pl
from jax.experimental.pallas import tpu as pltpu
from jax.sharding import PartitionSpec as P

EVERY = ("role", "seq", "rep")
PAIR = 1
ACROSS = 2
TILE = 256
LANES = 128


def rms_rows(values_in, gain_vec):
    return (
        values_in
        * lax.rsqrt(jnp.mean(values_in * values_in, axis=-1, keepdims=True) + 1e-06)
        * gain_vec
    )


def swap(block, axis, bits):
    size = lax.axis_size(axis)
    return lax.ppermute(block, axis, [(i, i ^ bits) for i in range(size)])


def seq_bits():
    size = lax.axis_size("seq")
    return [1 << place for place in reversed(range(size.bit_length() - 1))]


def seq_order():
    order = [0]
    for bits in seq_bits():
        order = order + [place ^ bits for place in order]
    return order


def ready(*arrays):
    return lax.optimization_barrier(arrays)


def spread_rows(own, early_work):
    half = own.shape[1] // 2

    def both_ways(part):
        return swap(part, "rep", ACROSS), swap(part, "role", 1)

    def corners(by_rep, by_role):
        return swap(by_rep[:, :half], "role", 1), swap(by_role[:, half:], "rep", ACROSS)

    first_bits, *bits_left = seq_bits()
    blocks = [own, swap(own, "seq", first_bits)]
    for bits in bits_left[:-1]:
        blocks = blocks + [swap(block, "seq", bits) for block in blocks]
    beyond = [swap(block, "seq", bits_left[-1]) for block in blocks[:-1]]
    outer = both_ways(own)
    middle = jnp.concatenate(blocks[1:] + beyond, axis=0)
    outer_low, outer_high = outer[0][:, :half], outer[1][:, half:]
    middle, outer_low, outer_high = ready(middle, outer_low, outer_high)
    outer_corner = swap(outer_low, "role", 1), swap(outer_high, "rep", ACROSS)
    last = swap(blocks[-1], "seq", bits_left[-1])
    rows = own.shape[0] + middle.shape[0] + last.shape[0]
    inner = both_ways(middle)
    final = both_ways(last)
    inner_corner = corners(*inner)
    early = early_work([(0, 0, own), (own.shape[0], 0, middle), (rows - last.shape[0], 0, last)])
    by_rep, by_role, *early = ready(*final, *early)
    final_corner = corners(by_rep, by_role)
    groups = [[], [], []]
    start = 0
    for part, beside, corner in (
        (own, outer, outer_corner),
        (middle, inner, inner_corner),
        (last, final, final_corner),
    ):
        groups[0].append((start, 0, beside[0]))
        groups[1].append((start, 0, beside[1]))
        groups[2].append((start, 0, corner[0]))
        groups[2].append((start, half, corner[1]))
        start += part.shape[0]
    return early, groups


def added(first, second):
    return (first.astype(jnp.float32) + second.astype(jnp.float32)).astype(jnp.bfloat16)


def collect_rows(near, by_rep, by_role, corner):
    straight_low = swap(by_role[0], "role", 1)
    straight_high = swap(by_rep[1], "rep", ACROSS)
    straight_low, straight_high, *corner = ready(straight_low, straight_high, *corner)
    corner_low, corner_high = ready(
        swap(corner[0], "role", 1), swap(corner[1], "rep", ACROSS)
    )
    cut = near[0].shape[0] // 2
    low_sum, high_sum = added(by_rep[0], corner_low), added(by_role[1], corner_high)

    def merged(rows, turned_low, turned_high):
        return jnp.concatenate(
            [
                base[rows].astype(jnp.float32)
                + first[rows].astype(jnp.float32)
                + second.astype(jnp.float32)
                for base, first, second in (
                    (near[0], straight_low, turned_low),
                    (near[1], straight_high, turned_high),
                )
            ],
            axis=1,
        )

    def turned(rows):
        return swap(low_sum[rows], "rep", ACROSS), swap(high_sum[rows], "role", 1)

    *far, low_sum, high_sum = ready(*turned(slice(cut, None)), low_sum, high_sum)
    leaving = merged(slice(cut, None), *far).astype(jnp.bfloat16)
    *beside, _ = ready(*turned(slice(0, cut)), leaving)
    total = merged(slice(0, cut), *beside)
    for bits in reversed(seq_bits()):
        total = total + swap(leaving, "seq", bits).astype(jnp.float32)
        if bits != seq_bits()[0]:
            cut = total.shape[0] // 2
            total, leaving = total[:cut], total[cut:].astype(jnp.bfloat16)
    return total


def prepare_kernel(tokens_ref, gain_ref, kv_ref, k_gain_ref, ids_ref, gates_ref, normed_ref, out_ref):
    normed = rms_rows(tokens_ref[...].astype(jnp.float32), gain_ref[...]).astype(jnp.bfloat16)
    normed_ref[...] = normed
    kv_width, head_dim = kv_ref.shape[2], k_gain_ref.shape[1]
    keys = jnp.dot(normed, kv_ref[0], preferred_element_type=jnp.float32)
    for start in range(0, kv_width, head_dim):
        head = rms_rows(keys[:, start : start + head_dim], k_gain_ref[...])
        out_ref[:, start : start + head_dim] = head.astype(jnp.bfloat16)
    values = jnp.dot(normed, kv_ref[1], preferred_element_type=jnp.float32)
    out_ref[:, kv_width : 2 * kv_width] = values.astype(jnp.bfloat16)
    ids, gates = ids_ref[...], gates_ref[...]
    rest = jnp.zeros((ids.shape[0], LANES - 3 * ids.shape[1]), jnp.int32)
    coded = jnp.concatenate([ids, gates // 64, gates % 64, rest], axis=1)
    out_ref[:, 2 * kv_width :] = coded.astype(jnp.float32).astype(jnp.bfloat16)


def prepare(tokens, attn_gain, w_keyval, k_gain, ids, gates):
    rows, width = tokens.shape
    return pl.pallas_call(
        prepare_kernel,
        out_shape=[
            jax.ShapeDtypeStruct((rows, width), jnp.bfloat16),
            jax.ShapeDtypeStruct((rows, 2 * w_keyval.shape[2] + LANES), jnp.bfloat16),
        ],
        compiler_params=pltpu.CompilerParams(vmem_limit_bytes=16 * 1024 * 1024),
        cost_estimate=pl.CostEstimate(
            flops=4 * rows * width * w_keyval.shape[2],
            bytes_accessed=4 * width * w_keyval.shape[2] + 4 * rows * width,
            transcendentals=rows,
        ),
        name="prepare",
    )(tokens, attn_gain[None], w_keyval, k_gain[None], ids, gates)


def queries_kernel(first_ref, second_ref, third_ref, fourth_ref, weight_ref, gain_ref, out_ref):
    rows, head_dim = first_ref.shape[0], gain_ref.shape[1]
    refs = (first_ref, second_ref, third_ref, fourth_ref)
    held = jnp.concatenate([ref[...] for ref in refs], axis=0)
    raw = jnp.dot(held, weight_ref[...], preferred_element_type=jnp.float32)
    for start in range(0, weight_ref.shape[1], head_dim):
        head = rms_rows(raw[:, start : start + head_dim], gain_ref[...])
        out_ref[:, start : start + head_dim] = head.astype(jnp.bfloat16)


def make_queries(blocks, w_query, q_gain):
    rows, width = len(blocks) * blocks[0].shape[0], w_query.shape[1]
    return pl.pallas_call(
        queries_kernel,
        out_shape=jax.ShapeDtypeStruct((rows, width), jnp.bfloat16),
        compiler_params=pltpu.CompilerParams(vmem_limit_bytes=16 * 1024 * 1024),
        cost_estimate=pl.CostEstimate(
            flops=2 * rows * width * w_query.shape[0],
            bytes_accessed=2 * width * w_query.shape[0],
            transcendentals=rows,
        ),
        name="queries",
    )(*blocks, w_query, q_gain[None])


def attend_kernel(head_dim, query_ref, near_ref, far_ref, weight_ref, kept_ref, leaving_ref, held_ref):
    keys = [ref[:, :head_dim] for ref in (near_ref, far_ref)]
    values = [ref[:, head_dim:] for ref in (near_ref, far_ref)]
    for start in range(0, query_ref.shape[1], head_dim):
        query = query_ref[:, start : start + head_dim]
        scores = [
            lax.dot_general(
                query, key, (((1,), (1,)), ((), ())), preferred_element_type=jnp.float32
            )
            * head_dim ** (-0.5)
            for key in keys
        ]
        row_max = jnp.maximum(
            jnp.max(scores[0], axis=1, keepdims=True), jnp.max(scores[1], axis=1, keepdims=True)
        )
        denom, total = 0.0, 0.0
        for score, value in zip(scores, values):
            weights = jnp.exp(score - row_max)
            denom = denom + jnp.sum(weights, axis=1, keepdims=True)
            total = total + jnp.dot(
                weights.astype(jnp.bfloat16), value, preferred_element_type=jnp.float32
            )
        held_ref[:, start : start + head_dim] = (total / denom).astype(jnp.bfloat16)
    cut = kept_ref.shape[0]
    for column in range(0, weight_ref.shape[1], 2 * TILE):
        columns = slice(column, column + 2 * TILE)
        partial = jnp.dot(held_ref[...], weight_ref[:, columns], preferred_element_type=jnp.float32)
        kept_ref[:, columns] = partial[:cut]
        leaving_ref[:, columns] = partial[cut:]


def attend(queries, near_kv, far_kv, w_out, head_dim):
    rows, width = queries.shape
    keys = 2 * near_kv.shape[0]
    half = jax.ShapeDtypeStruct((rows // 2, w_out.shape[1]), jnp.float32)
    return pl.pallas_call(
        lambda *refs: attend_kernel(head_dim, *refs),
        out_shape=[half, half],
        scratch_shapes=[pltpu.VMEM((rows, width), jnp.bfloat16)],
        compiler_params=pltpu.CompilerParams(vmem_limit_bytes=40 * 1024 * 1024),
        cost_estimate=pl.CostEstimate(
            flops=4 * rows * width * keys + 2 * rows * width * w_out.shape[1],
            bytes_accessed=2 * width * w_out.shape[1] + 4 * rows * w_out.shape[1],
            transcendentals=rows * keys * width // head_dim,
        ),
        name="attend",
    )(queries, near_kv, far_kv, w_out)


def expert_kernel(spots, *refs):
    pick_ref, place_ref, share_ref, own_gu_ref, far_gu_ref, own_dn_ref, far_dn_ref = refs[:7]
    groups, group_rows, slots = place_ref.shape[1:]
    piece_refs = refs[7 : 7 + len(spots)]
    out_refs = refs[7 + len(spots) : 7 + len(spots) + 2 * groups]
    x_buf, xs_buf, gu_buf, dn_buf, hid_buf, served_buf, y_buf, x_sem, w_sem, y_sem = refs[
        7 + len(spots) + 2 * groups :
    ]
    width = x_buf.shape[2]
    half = width // 2
    hidden = own_dn_ref.shape[0]
    tiles = hidden // TILE

    row_copies = []
    for number, ((group, row, column), piece) in enumerate(zip(spots, piece_refs)):
        rows, columns = piece.shape
        target = x_buf.at[group, pl.ds(row, rows), pl.ds(column, columns)]
        row_copies.append((group, pltpu.make_async_copy(piece, target, x_sem.at[number])))
    weight_copies = []
    for expert, (gu_ref, dn_ref) in enumerate(((own_gu_ref, own_dn_ref), (far_gu_ref, far_dn_ref))):
        mine = []
        for tile in range(tiles):
            for side in range(2):
                mine.append(
                    pltpu.make_async_copy(
                        gu_ref.at[:, pl.ds(side * hidden + tile * TILE, TILE)],
                        gu_buf.at[expert, tile, side],
                        w_sem.at[expert, 2 * tile + side],
                    )
                )
        mine.append(pltpu.make_async_copy(dn_ref, dn_buf.at[expert], w_sem.at[expert, 2 * tiles]))
        weight_copies.append(mine)
    for _, copy in row_copies:
        copy.start()
    for mine in weight_copies:
        for copy in mine:
            copy.start()

    for group in range(groups):
        for where, copy in row_copies:
            if where == group:
                copy.wait()
        chosen = jnp.dot(
            pick_ref[group], x_buf[group], preferred_element_type=jnp.float32
        ).astype(jnp.bfloat16)
        xs_buf[0, pl.ds(group * slots, slots)] = chosen[:slots]
        xs_buf[1, pl.ds(group * slots, slots)] = chosen[slots:]

    for expert in range(2):
        for tile in range(tiles):
            weight_copies[expert][2 * tile].wait()
            weight_copies[expert][2 * tile + 1].wait()
            gate = jnp.dot(
                xs_buf[expert], gu_buf[expert, tile, 0], preferred_element_type=jnp.float32
            )
            up = jnp.dot(
                xs_buf[expert], gu_buf[expert, tile, 1], preferred_element_type=jnp.float32
            )
            value = gate / (1.0 + jnp.exp(-gate)) * up
            hid_buf[:, tile * TILE : (tile + 1) * TILE] = value.astype(jnp.bfloat16)
        weight_copies[expert][2 * tiles].wait()
        for column in range(0, width, 2 * TILE):
            served_buf[expert, :, column : column + 2 * TILE] = jnp.dot(
                hid_buf[...],
                dn_buf[expert, :, column : column + 2 * TILE],
                preferred_element_type=jnp.float32,
            ).astype(jnp.bfloat16)

    out_copies = []
    for group in range(groups):
        for column in range(0, width, 2 * TILE):
            total = None
            for expert in range(2):
                placed = jnp.dot(
                    place_ref[expert, group],
                    served_buf[expert, pl.ds(group * slots, slots), column : column + 2 * TILE],
                    preferred_element_type=jnp.float32,
                )
                term = placed * share_ref[group, :, expert : expert + 1]
                total = term if total is None else total + term
            y_buf[group, :, column : column + 2 * TILE] = total.astype(jnp.bfloat16)
        for side in range(2):
            copy = pltpu.make_async_copy(
                y_buf.at[group, :, pl.ds(side * half, half)],
                out_refs[2 * group + side],
                y_sem.at[group, side],
            )
            copy.start()
            out_copies.append(copy)
    for copy in out_copies:
        copy.wait()


def run_experts(pieces, pick, place, share, weights):
    groups, group_rows, slots = place.shape[1:]
    hidden, width = weights[2].shape
    tiles = hidden // TILE
    spots = [
        (group, row, column) for group, held in enumerate(pieces) for row, column, _ in held
    ]
    arrays = [array for held in pieces for _, _, array in held]
    anywhere = pl.BlockSpec(memory_space=pl.ANY)
    inside = pl.BlockSpec(memory_space=pltpu.VMEM)
    outs = pl.pallas_call(
        lambda *refs: expert_kernel(spots, *refs),
        out_shape=[jax.ShapeDtypeStruct((group_rows, width // 2), jnp.bfloat16)] * (2 * groups),
        in_specs=[inside] * 3 + [anywhere] * (4 + len(arrays)),
        out_specs=[anywhere] * (2 * groups),
        scratch_shapes=[
            pltpu.VMEM((groups, group_rows, width), jnp.bfloat16),
            pltpu.VMEM((2, groups * slots, width), jnp.bfloat16),
            pltpu.VMEM((2, tiles, 2, width, TILE), jnp.bfloat16),
            pltpu.VMEM((2, hidden, width), jnp.bfloat16),
            pltpu.VMEM((groups * slots, hidden), jnp.bfloat16),
            pltpu.VMEM((2, groups * slots, width), jnp.bfloat16),
            pltpu.VMEM((groups, group_rows, width), jnp.bfloat16),
            pltpu.SemaphoreType.DMA((len(arrays),)),
            pltpu.SemaphoreType.DMA((2, 2 * tiles + 1)),
            pltpu.SemaphoreType.DMA((groups, 2)),
        ],
        compiler_params=pltpu.CompilerParams(vmem_limit_bytes=52 * 1024 * 1024),
        cost_estimate=pl.CostEstimate(
            flops=12 * groups * slots * width * hidden,
            bytes_accessed=12 * width * hidden + 4 * groups * group_rows * width,
            transcendentals=2 * groups * slots * hidden,
        ),
        name="experts",
    )(pick, place, share, *weights, *arrays)
    return [(outs[2 * group], outs[2 * group + 1]) for group in range(groups)]


def per_device(
    hidden_in,
    attn_gain,
    w_query,
    w_keyval,
    q_gain,
    k_gain,
    w_out,
    moe_gain,
    expert_ids,
    gate_fixed,
    w_gateup,
    w_down,
):
    tokens = hidden_in[0].astype(jnp.float32)
    row_count, model_width = tokens.shape
    head_dim = q_gain.shape[0]
    local_heads = w_query.shape[1] // head_dim
    kv_heads = w_keyval.shape[2] // head_dim
    group_size = local_heads * lax.axis_size("rep") // kv_heads
    rep_index = lax.axis_index("rep")
    kv_width = kv_heads * head_dim
    top_count = expert_ids.shape[2]
    expert_count = lax.axis_size(EVERY)

    normed, own_payload = prepare(
        hidden_in[0], attn_gain, w_keyval, k_gain, expert_ids[0], gate_fixed[0]
    )
    across_rows = swap(normed, "rep", ACROSS)
    pair_rows = swap(normed, "rep", PAIR)
    line = jnp.concatenate(
        [own_payload] + [swap(own_payload, "seq", bits) for bits in seq_order()[1:]], axis=0
    )
    corner_rows = swap(across_rows, "rep", PAIR)
    line_routes = line[:, 2 * kv_width :]

    def head_kv(rep):
        index = rep * local_heads // group_size * head_dim
        return [
            lax.dynamic_slice_in_dim(line, index, head_dim, 1),
            lax.dynamic_slice_in_dim(line, kv_width + index, head_dim, 1),
        ]

    sent = jnp.concatenate(head_kv(rep_index ^ ACROSS) + [line_routes], axis=1)
    sent, across_rows, pair_rows = ready(sent, across_rows, pair_rows)
    across = swap(sent, "rep", ACROSS)
    half_kv = jnp.concatenate(
        [jnp.concatenate(head_kv(rep_index), axis=1), across[:, : 2 * head_dim]], axis=0
    )
    pair_kv = swap(half_kv, "rep", PAIR)
    both_routes = jnp.stack([line_routes, across[:, 2 * head_dim :]])
    coded = jnp.concatenate([both_routes, swap(both_routes, "role", 1)], axis=0)
    far_gu = swap(w_gateup[0], "rep", PAIR)
    queries = make_queries([normed, across_rows, pair_rows, corner_rows], w_query, q_gain)
    kept, leaving = attend(queries, half_kv, pair_kv, w_out, head_dim)
    leaving, own_dn = ready(swap(leaving, "rep", PAIR), w_down[0])
    halves = kept + leaving
    far_dn = swap(own_dn, "rep", PAIR)
    far_sum = halves[row_count:].astype(jnp.bfloat16)
    attended = halves[:row_count] + swap(far_sum, "rep", ACROSS).astype(jnp.float32)
    mixed = tokens + attended

    coded = coded[:, :, : 3 * top_count].astype(jnp.int32)
    routes = coded[:, :, :top_count]
    gates = coded[:, :, top_count : 2 * top_count] * 64 + coded[:, :, 2 * top_count :]
    gates = gates.astype(jnp.float32)
    groups, group_rows = routes.shape[:2]
    capacity = max(2, 7 * row_count * top_count // (4 * expert_count))
    slots = -(-capacity * (group_rows // row_count) // 16) * 16
    gate_sum = jnp.sum(gates, axis=2)
    earlier = jnp.tri(group_rows, k=-1, dtype=jnp.bfloat16)
    picks, shares = [], []
    for expert in (lax.axis_index(EVERY), lax.axis_index(EVERY) ^ PAIR):
        named = routes == expert
        hit = jnp.any(named, axis=2)
        shares.append(jnp.sum(jnp.where(named, gates, 0.0), axis=2) / gate_sum)
        rank = jnp.einsum(
            "ij,gj->gi", earlier, hit.astype(jnp.bfloat16), preferred_element_type=jnp.float32
        )
        rank = jnp.where(hit, rank.astype(jnp.int32), -1)
        picks.append((rank[:, None, :] == jnp.arange(slots)[None, :, None]).astype(jnp.bfloat16))
    pick = jnp.concatenate(picks, axis=1)
    place = jnp.stack([jnp.swapaxes(one, 1, 2) for one in picks])
    share = jnp.stack(shares, axis=2)
    mixed, far_gu, far_dn, pick, place, share = lax.optimization_barrier(
        (mixed, far_gu, far_dn, pick, place, share)
    )
    moe_in = rms_rows(mixed, moe_gain).astype(jnp.bfloat16)

    weights = (w_gateup[0], far_gu, w_down[0], far_dn)

    def serve(pieces, first, last):
        return run_experts(
            pieces, pick[first:last], place[:, first:last], share[first:last], weights
        )

    near, rows = spread_rows(moe_in, lambda pieces: serve([pieces], 0, 1)[0])
    by_rep, by_role = serve(rows[:2], 1, 3)
    rep_low, rep_high, role_low, role_high, *held = ready(
        *by_rep, *by_role, *(array for _, _, array in rows[2])
    )
    by_rep, by_role = (rep_low, rep_high), (role_low, role_high)
    pieces = [(row, column, array) for (row, column, _), array in zip(rows[2], held)]
    corner = serve([pieces], 3, 4)
    routed = collect_rows(near, by_rep, by_role, corner[0])
    routed = collect_rows(near, by_rep, by_role, corner[0])
    return (mixed + routed).astype(jnp.bfloat16)[None]


def solution(mesh):
    placed = (
        P("role", ("seq", "rep"), None),
        P(),
        P(None, "rep"),
        P(),
        P(),
        P(),
        P("rep", None),
        P(),
        P("role", ("seq", "rep"), None),
        P("role", ("seq", "rep"), None),
        P(("role", "seq", "rep"), None, None),
        P(("role", "seq", "rep"), None, None),
    )
    return jax.shard_map(
        per_device,
        mesh=mesh,
        in_specs=placed,
        out_specs=P("role", ("seq", "rep"), None),
        check_vma=False,
    )
```

```python
import jax
import jax.numpy as jnp
from jax import lax
from jax.experimental import pallas as pl
from jax.experimental.pallas import tpu as pltpu
from jax.sharding import PartitionSpec as P

EVERY = ("role", "seq", "rep")
PAIR = 1
ACROSS = 2
TILE = 256
LANES = 128


def rms_rows(values_in, gain_vec):
    return (
        values_in
        * lax.rsqrt(jnp.mean(values_in * values_in, axis=-1, keepdims=True) + 1e-06)
        * gain_vec
    )


def swap(block, axis, bits):
    size = lax.axis_size(axis)
    return lax.ppermute(block, axis, [(i, i ^ bits) for i in range(size)])


def seq_bits():
    size = lax.axis_size("seq")
    return [1 << place for place in reversed(range(size.bit_length() - 1))]


def seq_order():
    order = [0]
    for bits in seq_bits():
        order = order + [place ^ bits for place in order]
    return order


def ready(*arrays):
    return lax.optimization_barrier(arrays)


def spread_rows(own, early_work):
    half = own.shape[1] // 2

    def both_ways(part):
        return swap(part, "rep", ACROSS), swap(part, "role", 1)

    def corners(by_rep, by_role):
        return swap(by_rep[:, :half], "role", 1), swap(by_role[:, half:], "rep", ACROSS)

    first_bits, *bits_left = seq_bits()
    blocks = [own, swap(own, "seq", first_bits)]
    for bits in bits_left[:-1]:
        blocks = blocks + [swap(block, "seq", bits) for block in blocks]
    beyond = [swap(block, "seq", bits_left[-1]) for block in blocks[:-1]]
    outer = both_ways(own)
    middle = jnp.concatenate(blocks[1:] + beyond, axis=0)
    outer_low, outer_high = outer[0][:, :half], outer[1][:, half:]
    middle, outer_low, outer_high = ready(middle, outer_low, outer_high)
    outer_corner = swap(outer_low, "role", 1), swap(outer_high, "rep", ACROSS)
    last = swap(blocks[-1], "seq", bits_left[-1])
    rows = own.shape[0] + middle.shape[0] + last.shape[0]
    inner = both_ways(middle)
    final = both_ways(last)
    inner_corner = corners(*inner)
    early = early_work([(0, 0, own), (own.shape[0], 0, middle), (rows - last.shape[0], 0, last)])
    by_rep, by_role, *early = ready(*final, *early)
    final_corner = corners(by_rep, by_role)
    groups = [[], [], []]
    start = 0
    for part, beside, corner in (
        (own, outer, outer_corner),
        (middle, inner, inner_corner),
        (last, final, final_corner),
    ):
        groups[0].append((start, 0, beside[0]))
        groups[1].append((start, 0, beside[1]))
        groups[2].append((start, 0, corner[0]))
        groups[2].append((start, half, corner[1]))
        start += part.shape[0]
    return early, groups


def added(first, second):
    return (first.astype(jnp.float32) + second.astype(jnp.float32)).astype(jnp.bfloat16)


def collect_rows(near, by_rep, by_role, corner):
    straight_low = swap(by_role[0], "role", 1)
    straight_high = swap(by_rep[1], "rep", ACROSS)
    straight_low, straight_high, *corner = ready(straight_low, straight_high, *corner)
    corner_low, corner_high = ready(
        swap(corner[0], "role", 1), swap(corner[1], "rep", ACROSS)
    )
    cut = near[0].shape[0] // 2
    low_sum, high_sum = added(by_rep[0], corner_low), added(by_role[1], corner_high)

    def merged(rows, turned_low, turned_high):
        return jnp.concatenate(
            [
                base[rows].astype(jnp.float32)
                + first[rows].astype(jnp.float32)
                + second.astype(jnp.float32)
                for base, first, second in (
                    (near[0], straight_low, turned_low),
                    (near[1], straight_high, turned_high),
                )
            ],
            axis=1,
        )

    def turned(rows):
        return swap(low_sum[rows], "rep", ACROSS), swap(high_sum[rows], "role", 1)

    *far, low_sum, high_sum = ready(*turned(slice(cut, None)), low_sum, high_sum)
    leaving = merged(slice(cut, None), *far).astype(jnp.bfloat16)
    *beside, _ = ready(*turned(slice(0, cut)), leaving)
    total = merged(slice(0, cut), *beside)
    for bits in reversed(seq_bits()):
        total = total + swap(leaving, "seq", bits).astype(jnp.float32)
        if bits != seq_bits()[0]:
            cut = total.shape[0] // 2
            total, leaving = total[:cut], total[cut:].astype(jnp.bfloat16)
    return total


def prepare_kernel(*refs):
    tokens_in, gain_in, kv_in, k_gain_in, ids_in, gates_in, normed_ref, out_ref = refs[:8]
    held, sem = refs[8:14], refs[14]
    sources = (tokens_in, gain_in, kv_in, k_gain_in, ids_in, gates_in)
    copies = [
        pltpu.make_async_copy(src, dst, sem.at[number])
        for number, (src, dst) in enumerate(zip(sources, held))
    ]
    for copy in copies:
        copy.start()
    for copy in copies:
        copy.wait()
    tokens_ref, gain_ref, kv_ref, k_gain_ref, ids_ref, gates_ref = held
    normed = rms_rows(tokens_ref[...].astype(jnp.float32), gain_ref[...]).astype(jnp.bfloat16)
    normed_ref[...] = normed
    kv_width, head_dim = kv_ref.shape[2], k_gain_ref.shape[1]
    keys = jnp.dot(normed, kv_ref[0], preferred_element_type=jnp.float32)
    for start in range(0, kv_width, head_dim):
        head = rms_rows(keys[:, start : start + head_dim], k_gain_ref[...])
        out_ref[:, start : start + head_dim] = head.astype(jnp.bfloat16)
    values = jnp.dot(normed, kv_ref[1], preferred_element_type=jnp.float32)
    out_ref[:, kv_width : 2 * kv_width] = values.astype(jnp.bfloat16)
    coded = jnp.concatenate([ids_ref[...], gates_ref[...] // 64, gates_ref[...] % 64], axis=0)
    count = coded.shape[0]
    spread = lax.broadcasted_iota(jnp.int32, (count, LANES), 0)
    spread = spread == lax.broadcasted_iota(jnp.int32, (count, LANES), 1)
    out_ref[:, 2 * kv_width :] = lax.dot_general(
        coded.astype(jnp.float32).astype(jnp.bfloat16),
        spread.astype(jnp.float32).astype(jnp.bfloat16),
        (((0,), (0,)), ((), ())),
        preferred_element_type=jnp.float32,
    ).astype(jnp.bfloat16)


def prepare(tokens, attn_gain, w_keyval, k_gain, ids, gates):
    rows, width = tokens.shape
    operands = [
        pltpu.with_memory_space_constraint(one, pltpu.HBM)
        for one in (tokens, attn_gain[None], w_keyval, k_gain[None], ids.T, gates.T)
    ]
    return pl.pallas_call(
        prepare_kernel,
        out_shape=[
            jax.ShapeDtypeStruct((rows, width), jnp.bfloat16),
            jax.ShapeDtypeStruct((rows, 2 * w_keyval.shape[2] + LANES), jnp.bfloat16),
        ],
        in_specs=[pl.BlockSpec(memory_space=pltpu.HBM)] * len(operands),
        scratch_shapes=[pltpu.VMEM(one.shape, one.dtype) for one in operands]
        + [pltpu.SemaphoreType.DMA((len(operands),))],
        compiler_params=pltpu.CompilerParams(vmem_limit_bytes=16 * 1024 * 1024),
        cost_estimate=pl.CostEstimate(
            flops=4 * rows * width * w_keyval.shape[2],
            bytes_accessed=4 * width * w_keyval.shape[2] + 4 * rows * width,
            transcendentals=rows,
        ),
        name="prepare",
    )(*operands)


def queries_kernel(first_ref, second_ref, third_ref, fourth_ref, weight_ref, gain_ref, out_ref):
    rows, head_dim = first_ref.shape[0], gain_ref.shape[1]
    refs = (first_ref, second_ref, third_ref, fourth_ref)
    held = jnp.concatenate([ref[...] for ref in refs], axis=0)
    raw = jnp.dot(held, weight_ref[...], preferred_element_type=jnp.float32)
    for start in range(0, weight_ref.shape[1], head_dim):
        head = rms_rows(raw[:, start : start + head_dim], gain_ref[...])
        out_ref[:, start : start + head_dim] = head.astype(jnp.bfloat16)


def make_queries(blocks, w_query, q_gain):
    rows, width = len(blocks) * blocks[0].shape[0], w_query.shape[1]
    return pl.pallas_call(
        queries_kernel,
        out_shape=jax.ShapeDtypeStruct((rows, width), jnp.bfloat16),
        compiler_params=pltpu.CompilerParams(vmem_limit_bytes=16 * 1024 * 1024),
        cost_estimate=pl.CostEstimate(
            flops=2 * rows * width * w_query.shape[0],
            bytes_accessed=2 * width * w_query.shape[0],
            transcendentals=rows,
        ),
        name="queries",
    )(*blocks, w_query, q_gain[None])


def attend_kernel(head_dim, query_ref, near_ref, far_ref, weight_ref, kept_ref, leaving_ref, held_ref):
    keys = [ref[:, :head_dim] for ref in (near_ref, far_ref)]
    values = [ref[:, head_dim:] for ref in (near_ref, far_ref)]
    for start in range(0, query_ref.shape[1], head_dim):
        query = query_ref[:, start : start + head_dim]
        scores = [
            lax.dot_general(
                query, key, (((1,), (1,)), ((), ())), preferred_element_type=jnp.float32
            )
            * head_dim ** (-0.5)
            for key in keys
        ]
        row_max = jnp.maximum(
            jnp.max(scores[0], axis=1, keepdims=True), jnp.max(scores[1], axis=1, keepdims=True)
        )
        denom, total = 0.0, 0.0
        for score, value in zip(scores, values):
            weights = jnp.exp(score - row_max)
            denom = denom + jnp.sum(weights, axis=1, keepdims=True)
            total = total + jnp.dot(
                weights.astype(jnp.bfloat16), value, preferred_element_type=jnp.float32
            )
        held_ref[:, start : start + head_dim] = (total / denom).astype(jnp.bfloat16)
    cut = kept_ref.shape[0]
    for column in range(0, weight_ref.shape[1], 2 * TILE):
        columns = slice(column, column + 2 * TILE)
        partial = jnp.dot(held_ref[...], weight_ref[:, columns], preferred_element_type=jnp.float32)
        kept_ref[:, columns] = partial[:cut]
        leaving_ref[:, columns] = partial[cut:]


def attend(queries, near_kv, far_kv, w_out, head_dim):
    rows, width = queries.shape
    keys = 2 * near_kv.shape[0]
    half = jax.ShapeDtypeStruct((rows // 2, w_out.shape[1]), jnp.float32)
    return pl.pallas_call(
        lambda *refs: attend_kernel(head_dim, *refs),
        out_shape=[half, half],
        scratch_shapes=[pltpu.VMEM((rows, width), jnp.bfloat16)],
        compiler_params=pltpu.CompilerParams(vmem_limit_bytes=40 * 1024 * 1024),
        cost_estimate=pl.CostEstimate(
            flops=4 * rows * width * keys + 2 * rows * width * w_out.shape[1],
            bytes_accessed=2 * width * w_out.shape[1] + 4 * rows * w_out.shape[1],
            transcendentals=rows * keys * width // head_dim,
        ),
        name="attend",
    )(queries, near_kv, far_kv, w_out)


def expert_kernel(spots, *refs):
    pick_ref, place_ref, share_ref, own_gu_ref, far_gu_ref, own_dn_ref, far_dn_ref = refs[:7]
    groups, group_rows, slots = place_ref.shape[1:]
    piece_refs = refs[7 : 7 + len(spots)]
    out_refs = refs[7 + len(spots) : 7 + len(spots) + 2 * groups]
    xs_buf, hid_buf, served_buf = refs[7 + len(spots) + 2 * groups :]
    hidden, width = own_dn_ref.shape
    half = width // 2

    for group in range(groups):
        for column in range(0, width, half):
            held = [
                (row, piece[:, column - start : column - start + half])
                for (where, row, start), piece in zip(spots, piece_refs)
                if where == group and start <= column < start + piece.shape[1]
            ]
            held = jnp.concatenate([block for _, block in sorted(held, key=lambda e: e[0])], axis=0)
            chosen = jnp.dot(pick_ref[group], held, preferred_element_type=jnp.float32)
            chosen = chosen.astype(jnp.bfloat16)
            for expert in range(2):
                xs_buf[expert, pl.ds(group * slots, slots), column : column + half] = chosen[
                    expert * slots : (expert + 1) * slots
                ]

    for expert, (gu_ref, dn_ref) in enumerate(((own_gu_ref, own_dn_ref), (far_gu_ref, far_dn_ref))):
        for column in range(0, hidden, TILE):
            gate, up = (
                jnp.dot(
                    xs_buf[expert],
                    gu_ref[:, start : start + TILE],
                    preferred_element_type=jnp.float32,
                )
                for start in (column, hidden + column)
            )
            value = gate / (1.0 + jnp.exp(-gate)) * up
            hid_buf[:, column : column + TILE] = value.astype(jnp.bfloat16)
        for column in range(0, width, 2 * TILE):
            served_buf[expert, :, column : column + 2 * TILE] = jnp.dot(
                hid_buf[...],
                dn_ref[:, column : column + 2 * TILE],
                preferred_element_type=jnp.float32,
            ).astype(jnp.bfloat16)

    for group in range(groups):
        for column in range(0, width, 2 * TILE):
            total = None
            for expert in range(2):
                placed = jnp.dot(
                    place_ref[expert, group],
                    served_buf[expert, pl.ds(group * slots, slots), column : column + 2 * TILE],
                    preferred_element_type=jnp.float32,
                )
                term = placed * share_ref[group, :, expert : expert + 1]
                total = term if total is None else total + term
            start = column % half
            out_ref = out_refs[2 * group + column // half]
            out_ref[:, start : start + 2 * TILE] = total.astype(jnp.bfloat16)


def run_experts(pieces, pick, place, share, weights):
    groups, group_rows, slots = place.shape[1:]
    hidden, width = weights[2].shape
    spots = [
        (group, row, column) for group, held in enumerate(pieces) for row, column, _ in held
    ]
    arrays = [array for held in pieces for _, _, array in held]
    outs = pl.pallas_call(
        lambda *refs: expert_kernel(spots, *refs),
        out_shape=[jax.ShapeDtypeStruct((group_rows, width // 2), jnp.bfloat16)] * (2 * groups),
        in_specs=[pl.BlockSpec(memory_space=pltpu.VMEM)] * (7 + len(arrays)),
        scratch_shapes=[
            pltpu.VMEM((2, groups * slots, width), jnp.bfloat16),
            pltpu.VMEM((groups * slots, hidden), jnp.bfloat16),
            pltpu.VMEM((2, groups * slots, width), jnp.bfloat16),
        ],
        compiler_params=pltpu.CompilerParams(vmem_limit_bytes=28 * 1024 * 1024),
        cost_estimate=pl.CostEstimate(
            flops=12 * groups * slots * width * hidden,
            bytes_accessed=12 * width * hidden + 4 * groups * group_rows * width,
            transcendentals=2 * groups * slots * hidden,
        ),
        name="experts",
    )(pick, place, share, *weights, *arrays)
    return [(outs[2 * group], outs[2 * group + 1]) for group in range(groups)]


def per_device(
    hidden_in,
    attn_gain,
    w_query,
    w_keyval,
    q_gain,
    k_gain,
    w_out,
    moe_gain,
    expert_ids,
    gate_fixed,
    w_gateup,
    w_down,
):
    tokens = hidden_in[0].astype(jnp.float32)
    row_count, model_width = tokens.shape
    head_dim = q_gain.shape[0]
    local_heads = w_query.shape[1] // head_dim
    kv_heads = w_keyval.shape[2] // head_dim
    group_size = local_heads * lax.axis_size("rep") // kv_heads
    rep_index = lax.axis_index("rep")
    kv_width = kv_heads * head_dim
    top_count = expert_ids.shape[2]
    expert_count = lax.axis_size(EVERY)

    normed, own_payload = prepare(
        hidden_in[0], attn_gain, w_keyval, k_gain, expert_ids[0], gate_fixed[0]
    )
    across_rows = swap(normed, "rep", ACROSS)
    pair_rows = swap(normed, "rep", PAIR)
    line = jnp.concatenate(
        [own_payload] + [swap(own_payload, "seq", bits) for bits in seq_order()[1:]], axis=0
    )
    corner_rows = swap(across_rows, "rep", PAIR)
    line_routes = line[:, 2 * kv_width :]

    def head_kv(rep):
        index = rep * local_heads // group_size * head_dim
        return [
            lax.dynamic_slice_in_dim(line, index, head_dim, 1),
            lax.dynamic_slice_in_dim(line, kv_width + index, head_dim, 1),
        ]

    sent = jnp.concatenate(head_kv(rep_index ^ ACROSS) + [line_routes], axis=1)
    sent, across_rows, pair_rows = ready(sent, across_rows, pair_rows)
    across = swap(sent, "rep", ACROSS)
    half_kv = jnp.concatenate(
        [jnp.concatenate(head_kv(rep_index), axis=1), across[:, : 2 * head_dim]], axis=0
    )
    pair_kv = swap(half_kv, "rep", PAIR)
    both_routes = jnp.stack([line_routes, across[:, 2 * head_dim :]])
    coded = jnp.concatenate([both_routes, swap(both_routes, "role", 1)], axis=0)
    far_gu = swap(w_gateup[0], "rep", PAIR)
    queries = make_queries([normed, across_rows, pair_rows, corner_rows], w_query, q_gain)
    kept, leaving = attend(queries, half_kv, pair_kv, w_out, head_dim)
    kept, leaving, coded = ready(kept, leaving, coded)
    leaving, own_dn = ready(swap(leaving, "rep", PAIR), w_down[0])
    halves = kept + leaving
    far_dn = swap(own_dn, "rep", PAIR)
    far_sum = halves[row_count:].astype(jnp.bfloat16)
    attended = halves[:row_count] + swap(far_sum, "rep", ACROSS).astype(jnp.float32)
    mixed = tokens + attended

    mixed, far_gu, far_dn, coded = ready(mixed, far_gu, far_dn, coded)
    moe_in = rms_rows(mixed, moe_gain).astype(jnp.bfloat16)

    coded = coded[:, :, : 3 * top_count].astype(jnp.int32)
    routes = coded[:, :, :top_count]
    gates = coded[:, :, top_count : 2 * top_count] * 64 + coded[:, :, 2 * top_count :]
    gates = gates.astype(jnp.float32)
    groups, group_rows = routes.shape[:2]
    capacity = max(2, 7 * row_count * top_count // (4 * expert_count))
    slots = -(-capacity * (group_rows // row_count) // 16) * 16
    gate_sum = jnp.sum(gates, axis=2)
    earlier = jnp.tri(group_rows, k=-1, dtype=jnp.bfloat16)
    picks, shares = [], []
    for expert in (lax.axis_index(EVERY), lax.axis_index(EVERY) ^ PAIR):
        named = routes == expert
        hit = jnp.any(named, axis=2)
        shares.append(jnp.sum(jnp.where(named, gates, 0.0), axis=2) / gate_sum)
        rank = jnp.einsum(
            "ij,gj->gi", earlier, hit.astype(jnp.bfloat16), preferred_element_type=jnp.float32
        )
        rank = jnp.where(hit, rank.astype(jnp.int32), -1)
        picks.append((rank[:, None, :] == jnp.arange(slots)[None, :, None]).astype(jnp.bfloat16))
    pick = jnp.concatenate(picks, axis=1)
    place = jnp.stack([jnp.swapaxes(one, 1, 2) for one in picks])
    share = jnp.stack(shares, axis=2)

    weights = [
        pltpu.with_memory_space_constraint(one, pltpu.VMEM)
        for one in (w_gateup[0], far_gu, w_down[0], far_dn)
    ]

    def serve(pieces, first, last):
        return run_experts(
            pieces, pick[first:last], place[:, first:last], share[first:last], weights
        )

    near, rows = spread_rows(moe_in, lambda pieces: serve([pieces], 0, 1)[0])
    by_rep, by_role = serve(rows[:2], 1, 3)
    rep_low, rep_high, role_low, role_high, *held = ready(
        *by_rep, *by_role, *(array for _, _, array in rows[2])
    )
    by_rep, by_role = (rep_low, rep_high), (role_low, role_high)
    pieces = [(row, column, array) for (row, column, _), array in zip(rows[2], held)]
    corner = serve([pieces], 3, 4)
    routed = collect_rows(near, by_rep, by_role, corner[0])
    routed = collect_rows(near, by_rep, by_role, corner[0])
    return (mixed + routed).astype(jnp.bfloat16)[None]


def solution(mesh):
    placed = (
        P("role", ("seq", "rep"), None),
        P(),
        P(None, "rep"),
        P(),
        P(),
        P(),
        P("rep", None),
        P(),
        P("role", ("seq", "rep"), None),
        P("role", ("seq", "rep"), None),
        P(("role", "seq", "rep"), None, None),
        P(("role", "seq", "rep"), None, None),
    )
    return jax.shard_map(
        per_device,
        mesh=mesh,
        in_specs=placed,
        out_specs=P("role", ("seq", "rep"), None),
        check_vma=False,
    )
```

```python
import jax
import jax.numpy as jnp
from jax import lax
from jax.experimental import pallas as pl
from jax.experimental.pallas import tpu as pltpu
from jax.sharding import PartitionSpec as P

EVERY = ("role", "seq", "rep")
PAIR = 1
ACROSS = 2
TILE = 256
LANES = 128


def rms_rows(values_in, gain_vec):
    return (
        values_in
        * lax.rsqrt(jnp.mean(values_in * values_in, axis=-1, keepdims=True) + 1e-06)
        * gain_vec
    )


def swap(block, axis, bits):
    size = lax.axis_size(axis)
    return lax.ppermute(block, axis, [(i, i ^ bits) for i in range(size)])


def seq_bits():
    size = lax.axis_size("seq")
    return [1 << place for place in reversed(range(size.bit_length() - 1))]


def seq_order():
    order = [0]
    for bits in seq_bits():
        order = order + [place ^ bits for place in order]
    return order


def ready(*arrays):
    return lax.optimization_barrier(arrays)


def spread_rows(own, coded):
    half = own.shape[1] // 2

    def both_ways(part):
        return swap(part, "rep", ACROSS), swap(part, "role", 1)

    def corners(by_rep, by_role):
        return swap(by_rep[:, :half], "role", 1), swap(by_role[:, half:], "rep", ACROSS)

    first_bits, *bits_left = seq_bits()
    blocks = [own, swap(own, "seq", first_bits)]
    for bits in bits_left[:-1]:
        blocks = blocks + [swap(block, "seq", bits) for block in blocks]
    beyond = [swap(block, "seq", bits_left[-1]) for block in blocks]
    outer = both_ways(own)
    outer_low, outer_high, first = ready(outer[0][:, :half], outer[1][:, half:], blocks[1])
    middle = jnp.concatenate([first] + blocks[2:] + beyond[:-1], axis=0)
    outer_corner = swap(outer_low, "role", 1), swap(outer_high, "rep", ACROSS)
    last, coded = ready(beyond[-1], coded)
    inner = both_ways(middle)
    final = both_ways(last)
    inner_corner = corners(*inner)
    by_rep, by_role, *outer_corner = ready(*final, *outer_corner)
    final_corner = corners(by_rep, by_role)
    groups = [[], [], [], []]
    start = 0
    for part, beside, corner in (
        (own, outer, outer_corner),
        (middle, inner, inner_corner),
        (last, final, final_corner),
    ):
        groups[0].append((start, 0, part))
        groups[1].append((start, 0, beside[0]))
        groups[2].append((start, 0, beside[1]))
        groups[3].append((start, 0, corner[0]))
        groups[3].append((start, half, corner[1]))
        start += part.shape[0]
    return groups, coded


def added(first, second):
    return (first.astype(jnp.float32) + second.astype(jnp.float32)).astype(jnp.bfloat16)


def collect_rows(make_near, by_rep, by_role, corner):
    straight_low = swap(by_role[0], "role", 1)
    straight_high = swap(by_rep[1], "rep", ACROSS)
    straight_low, straight_high, *corner = ready(straight_low, straight_high, *corner)
    near = make_near(corner[0])
    corner_low, corner_high, *near = ready(
        swap(corner[0], "role", 1), swap(corner[1], "rep", ACROSS), *near
    )
    cut = near[0].shape[0] // 2
    low_sum, high_sum = added(by_rep[0], corner_low), added(by_role[1], corner_high)

    def merged(rows, turned_low, turned_high):
        return jnp.concatenate(
            [
                base[rows].astype(jnp.float32)
                + first[rows].astype(jnp.float32)
                + second.astype(jnp.float32)
                for base, first, second in (
                    (near[0], straight_low, turned_low),
                    (near[1], straight_high, turned_high),
                )
            ],
            axis=1,
        )

    def turned(rows):
        return swap(low_sum[rows], "rep", ACROSS), swap(high_sum[rows], "role", 1)

    *far, low_sum, high_sum = ready(*turned(slice(cut, None)), low_sum, high_sum)
    leaving = merged(slice(cut, None), *far).astype(jnp.bfloat16)
    *beside, _ = ready(*turned(slice(0, cut)), leaving)
    total = merged(slice(0, cut), *beside)
    for bits in reversed(seq_bits()):
        total = total + swap(leaving, "seq", bits).astype(jnp.float32)
        if bits != seq_bits()[0]:
            cut = total.shape[0] // 2
            total, leaving = total[:cut], total[cut:].astype(jnp.bfloat16)
    return total


def prepare_kernel(*refs):
    tokens_in, gain_in, kv_in, k_gain_in, ids_in, gates_in, normed_ref, out_ref = refs[:8]
    held, sem = refs[8:14], refs[14]
    sources = (tokens_in, gain_in, kv_in, k_gain_in, ids_in, gates_in)
    copies = [
        pltpu.make_async_copy(src, dst, sem.at[number])
        for number, (src, dst) in enumerate(zip(sources, held))
    ]
    for copy in copies:
        copy.start()
    for copy in copies:
        copy.wait()
    tokens_ref, gain_ref, kv_ref, k_gain_ref, ids_ref, gates_ref = held
    normed = rms_rows(tokens_ref[...].astype(jnp.float32), gain_ref[...]).astype(jnp.bfloat16)
    normed_ref[...] = normed
    kv_width, head_dim = kv_ref.shape[2], k_gain_ref.shape[1]
    keys = jnp.dot(normed, kv_ref[0], preferred_element_type=jnp.float32)
    for start in range(0, kv_width, head_dim):
        head = rms_rows(keys[:, start : start + head_dim], k_gain_ref[...])
        out_ref[:, start : start + head_dim] = head.astype(jnp.bfloat16)
    values = jnp.dot(normed, kv_ref[1], preferred_element_type=jnp.float32)
    out_ref[:, kv_width : 2 * kv_width] = values.astype(jnp.bfloat16)
    coded = jnp.concatenate([ids_ref[...], gates_ref[...] // 64, gates_ref[...] % 64], axis=0)
    count = coded.shape[0]
    spread = lax.broadcasted_iota(jnp.int32, (count, LANES), 0)
    spread = spread == lax.broadcasted_iota(jnp.int32, (count, LANES), 1)
    out_ref[:, 2 * kv_width :] = lax.dot_general(
        coded.astype(jnp.float32).astype(jnp.bfloat16),
        spread.astype(jnp.float32).astype(jnp.bfloat16),
        (((0,), (0,)), ((), ())),
        preferred_element_type=jnp.float32,
    ).astype(jnp.bfloat16)


def prepare(tokens, attn_gain, w_keyval, k_gain, ids, gates):
    rows, width = tokens.shape
    operands = [
        pltpu.with_memory_space_constraint(one, pltpu.HBM)
        for one in (tokens, attn_gain[None], w_keyval, k_gain[None], ids.T, gates.T)
    ]
    return pl.pallas_call(
        prepare_kernel,
        out_shape=[
            jax.ShapeDtypeStruct((rows, width), jnp.bfloat16),
            jax.ShapeDtypeStruct((rows, 2 * w_keyval.shape[2] + LANES), jnp.bfloat16),
        ],
        in_specs=[pl.BlockSpec(memory_space=pltpu.HBM)] * len(operands),
        scratch_shapes=[pltpu.VMEM(one.shape, one.dtype) for one in operands]
        + [pltpu.SemaphoreType.DMA((len(operands),))],
        compiler_params=pltpu.CompilerParams(vmem_limit_bytes=8 * 1024 * 1024),
        cost_estimate=pl.CostEstimate(
            flops=4 * rows * width * w_keyval.shape[2],
            bytes_accessed=4 * width * w_keyval.shape[2] + 4 * rows * width,
            transcendentals=rows,
        ),
        name="prepare",
    )(*operands)


def queries_kernel(first_ref, second_ref, third_ref, fourth_ref, weight_ref, gain_ref, out_ref):
    rows, head_dim = first_ref.shape[0], gain_ref.shape[1]
    refs = (first_ref, second_ref, third_ref, fourth_ref)
    held = jnp.concatenate([ref[...] for ref in refs], axis=0)
    raw = jnp.dot(held, weight_ref[...], preferred_element_type=jnp.float32)
    for start in range(0, weight_ref.shape[1], head_dim):
        head = rms_rows(raw[:, start : start + head_dim], gain_ref[...])
        out_ref[:, start : start + head_dim] = head.astype(jnp.bfloat16)


def make_queries(blocks, w_query, q_gain):
    rows, width = len(blocks) * blocks[0].shape[0], w_query.shape[1]
    return pl.pallas_call(
        queries_kernel,
        out_shape=jax.ShapeDtypeStruct((rows, width), jnp.bfloat16),
        compiler_params=pltpu.CompilerParams(vmem_limit_bytes=8 * 1024 * 1024),
        cost_estimate=pl.CostEstimate(
            flops=2 * rows * width * w_query.shape[0],
            bytes_accessed=2 * width * w_query.shape[0],
            transcendentals=rows,
        ),
        name="queries",
    )(*blocks, w_query, q_gain[None])


def attend_kernel(head_dim, query_ref, near_ref, far_ref, weight_ref, kept_ref, leaving_ref, held_ref):
    keys = [ref[:, :head_dim] for ref in (near_ref, far_ref)]
    values = [ref[:, head_dim:] for ref in (near_ref, far_ref)]
    for start in range(0, query_ref.shape[1], head_dim):
        query = query_ref[:, start : start + head_dim]
        scores = [
            lax.dot_general(
                query, key, (((1,), (1,)), ((), ())), preferred_element_type=jnp.float32
            )
            * head_dim ** (-0.5)
            for key in keys
        ]
        row_max = jnp.maximum(
            jnp.max(scores[0], axis=1, keepdims=True), jnp.max(scores[1], axis=1, keepdims=True)
        )
        denom, total = 0.0, 0.0
        for score, value in zip(scores, values):
            weights = jnp.exp(score - row_max)
            denom = denom + jnp.sum(weights, axis=1, keepdims=True)
            total = total + jnp.dot(
                weights.astype(jnp.bfloat16), value, preferred_element_type=jnp.float32
            )
        held_ref[:, start : start + head_dim] = (total / denom).astype(jnp.bfloat16)
    cut = kept_ref.shape[0]
    for column in range(0, weight_ref.shape[1], 2 * TILE):
        columns = slice(column, column + 2 * TILE)
        partial = jnp.dot(held_ref[...], weight_ref[:, columns], preferred_element_type=jnp.float32)
        kept_ref[:, columns] = partial[:cut]
        leaving_ref[:, columns] = partial[cut:]


def attend(queries, near_kv, far_kv, w_out, head_dim):
    rows, width = queries.shape
    keys = 2 * near_kv.shape[0]
    half = jax.ShapeDtypeStruct((rows // 2, w_out.shape[1]), jnp.float32)
    return pl.pallas_call(
        lambda *refs: attend_kernel(head_dim, *refs),
        out_shape=[half, half],
        scratch_shapes=[pltpu.VMEM((rows, width), jnp.bfloat16)],
        compiler_params=pltpu.CompilerParams(vmem_limit_bytes=12 * 1024 * 1024),
        cost_estimate=pl.CostEstimate(
            flops=4 * rows * width * keys + 2 * rows * width * w_out.shape[1],
            bytes_accessed=2 * width * w_out.shape[1] + 4 * rows * w_out.shape[1],
            transcendentals=rows * keys * width // head_dim,
        ),
        name="attend",
    )(queries, near_kv, far_kv, w_out)


def expert_kernel(spots, *refs):
    pick_ref, place_ref, share_ref, own_gu_ref, far_gu_ref, own_dn_ref, far_dn_ref = refs[:7]
    groups, group_rows, slots = place_ref.shape[1:]
    piece_refs = refs[7 : 7 + len(spots)]
    out_refs = refs[7 + len(spots) : 7 + len(spots) + 2 * groups]
    x_buf, xs_buf, gu_buf, dn_buf, hid_buf, served_buf, y_buf, x_sem, w_sem, y_sem = refs[
        7 + len(spots) + 2 * groups :
    ]
    width = x_buf.shape[2]
    half = width // 2
    hidden = own_dn_ref.shape[0]
    tiles = hidden // TILE

    row_copies = []
    for number, ((group, row, column), piece) in enumerate(zip(spots, piece_refs)):
        rows, columns = piece.shape
        target = x_buf.at[group, pl.ds(row, rows), pl.ds(column, columns)]
        row_copies.append((group, pltpu.make_async_copy(piece, target, x_sem.at[number])))
    weight_copies = []
    for expert, (gu_ref, dn_ref) in enumerate(((own_gu_ref, own_dn_ref), (far_gu_ref, far_dn_ref))):
        mine = []
        for tile in range(tiles):
            for side in range(2):
                mine.append(
                    pltpu.make_async_copy(
                        gu_ref.at[:, pl.ds(side * hidden + tile * TILE, TILE)],
                        gu_buf.at[expert, tile, side],
                        w_sem.at[expert, 2 * tile + side],
                    )
                )
        mine.append(pltpu.make_async_copy(dn_ref, dn_buf.at[expert], w_sem.at[expert, 2 * tiles]))
        weight_copies.append(mine)
    for _, copy in row_copies:
        copy.start()
    for mine in weight_copies:
        for copy in mine:
            copy.start()

    for group in range(groups):
        for where, copy in row_copies:
            if where == group:
                copy.wait()
        chosen = jnp.dot(
            pick_ref[group], x_buf[group], preferred_element_type=jnp.float32
        ).astype(jnp.bfloat16)
        xs_buf[0, pl.ds(group * slots, slots)] = chosen[:slots]
        xs_buf[1, pl.ds(group * slots, slots)] = chosen[slots:]

    for expert in range(2):
        for tile in range(tiles):
            weight_copies[expert][2 * tile].wait()
            weight_copies[expert][2 * tile + 1].wait()
            gate = jnp.dot(
                xs_buf[expert], gu_buf[expert, tile, 0], preferred_element_type=jnp.float32
            )
            up = jnp.dot(
                xs_buf[expert], gu_buf[expert, tile, 1], preferred_element_type=jnp.float32
            )
            value = gate / (1.0 + jnp.exp(-gate)) * up
            hid_buf[:, tile * TILE : (tile + 1) * TILE] = value.astype(jnp.bfloat16)
        weight_copies[expert][2 * tiles].wait()
        for column in range(0, width, 2 * TILE):
            served_buf[expert, :, column : column + 2 * TILE] = jnp.dot(
                hid_buf[...],
                dn_buf[expert, :, column : column + 2 * TILE],
                preferred_element_type=jnp.float32,
            ).astype(jnp.bfloat16)

    out_copies = []
    for group in range(groups):
        for column in range(0, width, 2 * TILE):
            total = None
            for expert in range(2):
                placed = jnp.dot(
                    place_ref[expert, group],
                    served_buf[expert, pl.ds(group * slots, slots), column : column + 2 * TILE],
                    preferred_element_type=jnp.float32,
                )
                term = placed * share_ref[group, :, expert : expert + 1]
                total = term if total is None else total + term
            y_buf[group, :, column : column + 2 * TILE] = total.astype(jnp.bfloat16)
        for side in range(2):
            copy = pltpu.make_async_copy(
                y_buf.at[group, :, pl.ds(side * half, half)],
                out_refs[2 * group + side],
                y_sem.at[group, side],
            )
            copy.start()
            out_copies.append(copy)
    for copy in out_copies:
        copy.wait()


def run_experts(pieces, pick, place, share, weights):
    groups, group_rows, slots = place.shape[1:]
    hidden, width = weights[2].shape
    tiles = hidden // TILE
    spots = [
        (group, row, column) for group, held in enumerate(pieces) for row, column, _ in held
    ]
    arrays = [array for held in pieces for _, _, array in held]
    anywhere = pl.BlockSpec(memory_space=pl.ANY)
    inside = pl.BlockSpec(memory_space=pltpu.VMEM)
    outs = pl.pallas_call(
        lambda *refs: expert_kernel(spots, *refs),
        out_shape=[jax.ShapeDtypeStruct((group_rows, width // 2), jnp.bfloat16)] * (2 * groups),
        in_specs=[inside] * 3 + [anywhere] * (4 + len(arrays)),
        out_specs=[anywhere] * (2 * groups),
        scratch_shapes=[
            pltpu.VMEM((groups, group_rows, width), jnp.bfloat16),
            pltpu.VMEM((2, groups * slots, width), jnp.bfloat16),
            pltpu.VMEM((2, tiles, 2, width, TILE), jnp.bfloat16),
            pltpu.VMEM((2, hidden, width), jnp.bfloat16),
            pltpu.VMEM((groups * slots, hidden), jnp.bfloat16),
            pltpu.VMEM((2, groups * slots, width), jnp.bfloat16),
            pltpu.VMEM((groups, group_rows, width), jnp.bfloat16),
            pltpu.SemaphoreType.DMA((len(arrays),)),
            pltpu.SemaphoreType.DMA((2, 2 * tiles + 1)),
            pltpu.SemaphoreType.DMA((groups, 2)),
        ],
        compiler_params=pltpu.CompilerParams(vmem_limit_bytes=52 * 1024 * 1024),
        cost_estimate=pl.CostEstimate(
            flops=12 * groups * slots * width * hidden,
            bytes_accessed=12 * width * hidden + 4 * groups * group_rows * width,
            transcendentals=2 * groups * slots * hidden,
        ),
        name="experts",
    )(pick, place, share, *weights, *arrays)
    return [(outs[2 * group], outs[2 * group + 1]) for group in range(groups)]


def per_device(
    hidden_in,
    attn_gain,
    w_query,
    w_keyval,
    q_gain,
    k_gain,
    w_out,
    moe_gain,
    expert_ids,
    gate_fixed,
    w_gateup,
    w_down,
):
    tokens = hidden_in[0].astype(jnp.float32)
    row_count, model_width = tokens.shape
    head_dim = q_gain.shape[0]
    local_heads = w_query.shape[1] // head_dim
    kv_heads = w_keyval.shape[2] // head_dim
    group_size = local_heads * lax.axis_size("rep") // kv_heads
    rep_index = lax.axis_index("rep")
    kv_width = kv_heads * head_dim
    top_count = expert_ids.shape[2]
    expert_count = lax.axis_size(EVERY)

    normed, own_payload = prepare(
        hidden_in[0], attn_gain, w_keyval, k_gain, expert_ids[0], gate_fixed[0]
    )
    across_rows = swap(normed, "rep", ACROSS)
    pair_rows = swap(normed, "rep", PAIR)
    line = jnp.concatenate(
        [own_payload] + [swap(own_payload, "seq", bits) for bits in seq_order()[1:]], axis=0
    )
    corner_rows = swap(across_rows, "rep", PAIR)
    line_routes = line[:, 2 * kv_width :]

    def head_kv(rep):
        index = rep * local_heads // group_size * head_dim
        return [
            lax.dynamic_slice_in_dim(line, index, head_dim, 1),
            lax.dynamic_slice_in_dim(line, kv_width + index, head_dim, 1),
        ]

    sent = jnp.concatenate(head_kv(rep_index ^ ACROSS) + [line_routes], axis=1)
    sent, across_rows, pair_rows = ready(sent, across_rows, pair_rows)
    across = swap(sent, "rep", ACROSS)
    half_kv = jnp.concatenate(
        [jnp.concatenate(head_kv(rep_index), axis=1), across[:, : 2 * head_dim]], axis=0
    )
    pair_kv = swap(half_kv, "rep", PAIR)
    both_routes = jnp.stack([line_routes, across[:, 2 * head_dim :]])
    coded = jnp.concatenate([both_routes, swap(both_routes, "role", 1)], axis=0)
    far_gu = swap(w_gateup[0], "rep", PAIR)
    queries = make_queries([normed, across_rows, pair_rows, corner_rows], w_query, q_gain)
    kept, leaving = attend(queries, half_kv, pair_kv, w_out, head_dim)
    kept, leaving, coded = ready(kept, leaving, coded)
    leaving, own_dn = ready(swap(leaving, "rep", PAIR), w_down[0])
    halves = kept + leaving
    far_dn = swap(own_dn, "rep", PAIR)
    far_sum = halves[row_count:].astype(jnp.bfloat16)
    attended = halves[:row_count] + swap(far_sum, "rep", ACROSS).astype(jnp.float32)
    mixed = tokens + attended

    mixed, far_gu, far_dn, coded = ready(mixed, far_gu, far_dn, coded)
    moe_in = rms_rows(mixed, moe_gain).astype(jnp.bfloat16)

    rows, coded = spread_rows(moe_in, coded)
    coded = coded[:, :, : 3 * top_count].astype(jnp.int32)
    routes = coded[:, :, :top_count]
    gates = coded[:, :, top_count : 2 * top_count] * 64 + coded[:, :, 2 * top_count :]
    gates = gates.astype(jnp.float32)
    groups, group_rows = routes.shape[:2]
    capacity = max(2, 7 * row_count * top_count // (4 * expert_count))
    slots = -(-capacity * (group_rows // row_count) // 16) * 16
    gate_sum = jnp.sum(gates, axis=2)
    earlier = jnp.tri(group_rows, k=-1, dtype=jnp.bfloat16)
    picks, shares = [], []
    for expert in (lax.axis_index(EVERY), lax.axis_index(EVERY) ^ PAIR):
        named = routes == expert
        hit = jnp.any(named, axis=2)
        shares.append(jnp.sum(jnp.where(named, gates, 0.0), axis=2) / gate_sum)
        rank = jnp.einsum(
            "ij,gj->gi", earlier, hit.astype(jnp.bfloat16), preferred_element_type=jnp.float32
        )
        rank = jnp.where(hit, rank.astype(jnp.int32), -1)
        picks.append((rank[:, None, :] == jnp.arange(slots)[None, :, None]).astype(jnp.bfloat16))
    pick = jnp.concatenate(picks, axis=1)
    place = jnp.stack([jnp.swapaxes(one, 1, 2) for one in picks])
    share = jnp.stack(shares, axis=2)

    weights = (w_gateup[0], far_gu, w_down[0], far_dn)

    def serve(pieces, first, last):
        return run_experts(
            pieces, pick[first:last], place[:, first:last], share[first:last], weights
        )

    def with_all(pieces, *others):
        held = ready(*others, *(array for _, _, array in pieces))
        pieces = [
            (row, column, array)
            for (row, column, _), array in zip(pieces, held[len(others) :])
        ]
        return pieces, held[: len(others)]

    by_rep, by_role = serve(rows[1:3], 1, 3)
    pieces, (*by_rep, role_low, role_high) = with_all(rows[3], *by_rep, *by_role)
    (corner,) = serve([pieces], 3, 4)
    routed = collect_rows(
        lambda after: serve([with_all(rows[0], after)[0]], 0, 1)[0],
        by_rep,
        (role_low, role_high),
        corner,
    )
    return (mixed + routed).astype(jnp.bfloat16)[None]


def solution(mesh):
    placed = (
        P("role", ("seq", "rep"), None),
        P(),
        P(None, "rep"),
        P(),
        P(),
        P(),
        P("rep", None),
        P(),
        P("role", ("seq", "rep"), None),
        P("role", ("seq", "rep"), None),
        P(("role", "seq", "rep"), None, None),
        P(("role", "seq", "rep"), None, None),
    )
    return jax.shard_map(
        per_device,
        mesh=mesh,
        in_specs=placed,
        out_specs=P("role", ("seq", "rep"), None),
        check_vma=False,
    )
```

```python
import jax
import jax.numpy as jnp
from jax import lax
from jax.experimental import pallas as pl
from jax.experimental.pallas import tpu as pltpu
from jax.sharding import PartitionSpec as P

EVERY = ("role", "seq", "rep")
PAIR = 1
ACROSS = 2
TILE = 256
LANES = 128


def rms_rows(values_in, gain_vec):
    return (
        values_in
        * lax.rsqrt(jnp.mean(values_in * values_in, axis=-1, keepdims=True) + 1e-06)
        * gain_vec
    )


def swap(block, axis, bits):
    size = lax.axis_size(axis)
    return lax.ppermute(block, axis, [(i, i ^ bits) for i in range(size)])


def seq_bits():
    size = lax.axis_size("seq")
    return [1 << place for place in reversed(range(size.bit_length() - 1))]


def seq_order():
    order = [0]
    for bits in seq_bits():
        order = order + [place ^ bits for place in order]
    return order


def ready(*arrays):
    return lax.optimization_barrier(arrays)


def spread_rows(own, coded):
    half = own.shape[1] // 2

    def both_ways(part):
        return swap(part, "rep", ACROSS), swap(part, "role", 1)

    def corners(by_rep, by_role):
        return swap(by_rep[:, :half], "role", 1), swap(by_role[:, half:], "rep", ACROSS)

    first_bits, *bits_left = seq_bits()
    blocks = [own, swap(own, "seq", first_bits)]
    for bits in bits_left[:-1]:
        blocks = blocks + [swap(block, "seq", bits) for block in blocks]
    beyond = [swap(block, "seq", bits_left[-1]) for block in blocks]
    outer = both_ways(own)
    middle = jnp.concatenate(blocks[1:] + beyond[:-1], axis=0)
    middle, *outer_corner = ready(middle, *corners(*outer))
    last, coded = ready(beyond[-1], coded)
    inner = both_ways(middle)
    final = both_ways(last)
    inner_corner = corners(*inner)
    final_corner = corners(*final)
    groups = [[], [], [], []]
    start = 0
    for part, beside, corner in (
        (own, outer, outer_corner),
        (middle, inner, inner_corner),
        (last, final, final_corner),
    ):
        groups[0].append((start, 0, beside[0]))
        groups[1].append((start, 0, beside[1]))
        groups[2].append((start, 0, corner[0]))
        groups[2].append((start, half, corner[1]))
        groups[3].append((start, 0, part))
        start += part.shape[0]
    return groups, coded


def added(first, second):
    return (first.astype(jnp.float32) + second.astype(jnp.float32)).astype(jnp.bfloat16)


def collect_rows(near, by_rep, by_role, corner):
    straight_low = swap(by_role[0], "role", 1)
    straight_high = swap(by_rep[1], "rep", ACROSS)
    straight_low, straight_high, near_low, near_high, *corner = ready(
        straight_low, straight_high, *near, *corner[0], *corner[1]
    )
    cut = near_low.shape[0] // 2
    halves = slice(0, cut), slice(cut, None)

    def merged(rows, turned_low, turned_high):
        return jnp.concatenate(
            [
                base[rows].astype(jnp.float32)
                + first[rows].astype(jnp.float32)
                + second.astype(jnp.float32)
                for base, first, second in (
                    (near_low, straight_low, turned_low),
                    (near_high, straight_high, turned_high),
                )
            ],
            axis=1,
        )

    def corners(number):
        low, high = corner[2 * number : 2 * number + 2]
        return swap(low, "role", 1), swap(high, "rep", ACROSS)

    def turned(number, corner_low, corner_high):
        rows = halves[number]
        return (
            swap(added(by_rep[0][rows], corner_low), "rep", ACROSS),
            swap(added(by_role[1][rows], corner_high), "role", 1),
        )

    far_corner, beside_corner = corners(1), corners(0)
    far = turned(1, *far_corner)
    *far, corner_low, corner_high = ready(*far, *beside_corner)
    leaving = merged(halves[1], *far).astype(jnp.bfloat16)
    *beside, _ = ready(*turned(0, corner_low, corner_high), leaving)
    total = merged(halves[0], *beside)
    for bits in reversed(seq_bits()):
        total = total + swap(leaving, "seq", bits).astype(jnp.float32)
        if bits != seq_bits()[0]:
            cut = total.shape[0] // 2
            total, leaving = total[:cut], total[cut:].astype(jnp.bfloat16)
    return total


def prepare_kernel(*refs):
    tokens_in, gain_in, kv_in, k_gain_in, ids_in, gates_in, normed_ref, out_ref = refs[:8]
    held, sem = refs[8:14], refs[14]
    sources = (tokens_in, gain_in, kv_in, k_gain_in, ids_in, gates_in)
    copies = [
        pltpu.make_async_copy(src, dst, sem.at[number])
        for number, (src, dst) in enumerate(zip(sources, held))
    ]
    for copy in copies:
        copy.start()
    for copy in copies:
        copy.wait()
    tokens_ref, gain_ref, kv_ref, k_gain_ref, ids_ref, gates_ref = held
    normed = rms_rows(tokens_ref[...].astype(jnp.float32), gain_ref[...]).astype(jnp.bfloat16)
    normed_ref[...] = normed
    kv_width, head_dim = kv_ref.shape[2], k_gain_ref.shape[1]
    keys = jnp.dot(normed, kv_ref[0], preferred_element_type=jnp.float32)
    for start in range(0, kv_width, head_dim):
        head = rms_rows(keys[:, start : start + head_dim], k_gain_ref[...])
        out_ref[:, start : start + head_dim] = head.astype(jnp.bfloat16)
    values = jnp.dot(normed, kv_ref[1], preferred_element_type=jnp.float32)
    out_ref[:, kv_width : 2 * kv_width] = values.astype(jnp.bfloat16)
    coded = jnp.concatenate([ids_ref[...], gates_ref[...] // 64, gates_ref[...] % 64], axis=0)
    count = coded.shape[0]
    spread = lax.broadcasted_iota(jnp.int32, (count, LANES), 0)
    spread = spread == lax.broadcasted_iota(jnp.int32, (count, LANES), 1)
    out_ref[:, 2 * kv_width :] = lax.dot_general(
        coded.astype(jnp.float32).astype(jnp.bfloat16),
        spread.astype(jnp.float32).astype(jnp.bfloat16),
        (((0,), (0,)), ((), ())),
        preferred_element_type=jnp.float32,
    ).astype(jnp.bfloat16)


def prepare(tokens, attn_gain, w_keyval, k_gain, ids, gates):
    rows, width = tokens.shape
    operands = [
        pltpu.with_memory_space_constraint(one, pltpu.HBM)
        for one in (tokens, attn_gain[None], w_keyval, k_gain[None], ids.T, gates.T)
    ]
    return pl.pallas_call(
        prepare_kernel,
        out_shape=[
            jax.ShapeDtypeStruct((rows, width), jnp.bfloat16),
            jax.ShapeDtypeStruct((rows, 2 * w_keyval.shape[2] + LANES), jnp.bfloat16),
        ],
        in_specs=[pl.BlockSpec(memory_space=pltpu.HBM)] * len(operands),
        scratch_shapes=[pltpu.VMEM(one.shape, one.dtype) for one in operands]
        + [pltpu.SemaphoreType.DMA((len(operands),))],
        compiler_params=pltpu.CompilerParams(vmem_limit_bytes=8 * 1024 * 1024),
        cost_estimate=pl.CostEstimate(
            flops=4 * rows * width * w_keyval.shape[2],
            bytes_accessed=4 * width * w_keyval.shape[2] + 4 * rows * width,
            transcendentals=rows,
        ),
        name="prepare",
    )(*operands)


def queries_kernel(first_ref, second_ref, third_ref, fourth_ref, weight_ref, gain_ref, out_ref):
    rows, head_dim = first_ref.shape[0], gain_ref.shape[1]
    refs = (first_ref, second_ref, third_ref, fourth_ref)
    held = jnp.concatenate([ref[...] for ref in refs], axis=0)
    raw = jnp.dot(held, weight_ref[...], preferred_element_type=jnp.float32)
    for start in range(0, weight_ref.shape[1], head_dim):
        head = rms_rows(raw[:, start : start + head_dim], gain_ref[...])
        out_ref[:, start : start + head_dim] = head.astype(jnp.bfloat16)


def make_queries(blocks, w_query, q_gain):
    rows, width = len(blocks) * blocks[0].shape[0], w_query.shape[1]
    return pl.pallas_call(
        queries_kernel,
        out_shape=jax.ShapeDtypeStruct((rows, width), jnp.bfloat16),
        compiler_params=pltpu.CompilerParams(vmem_limit_bytes=8 * 1024 * 1024),
        cost_estimate=pl.CostEstimate(
            flops=2 * rows * width * w_query.shape[0],
            bytes_accessed=2 * width * w_query.shape[0],
            transcendentals=rows,
        ),
        name="queries",
    )(*blocks, w_query, q_gain[None])


def attend_kernel(head_dim, query_ref, near_ref, far_ref, weight_ref, kept_ref, leaving_ref, held_ref):
    keys = [ref[:, :head_dim] for ref in (near_ref, far_ref)]
    values = [ref[:, head_dim:] for ref in (near_ref, far_ref)]
    for start in range(0, query_ref.shape[1], head_dim):
        query = query_ref[:, start : start + head_dim]
        scores = [
            lax.dot_general(
                query, key, (((1,), (1,)), ((), ())), preferred_element_type=jnp.float32
            )
            * head_dim ** (-0.5)
            for key in keys
        ]
        row_max = jnp.maximum(
            jnp.max(scores[0], axis=1, keepdims=True), jnp.max(scores[1], axis=1, keepdims=True)
        )
        denom, total = 0.0, 0.0
        for score, value in zip(scores, values):
            weights = jnp.exp(score - row_max)
            denom = denom + jnp.sum(weights, axis=1, keepdims=True)
            total = total + jnp.dot(
                weights.astype(jnp.bfloat16), value, preferred_element_type=jnp.float32
            )
        held_ref[:, start : start + head_dim] = (total / denom).astype(jnp.bfloat16)
    cut = kept_ref.shape[0]
    for column in range(0, weight_ref.shape[1], 2 * TILE):
        columns = slice(column, column + 2 * TILE)
        partial = jnp.dot(held_ref[...], weight_ref[:, columns], preferred_element_type=jnp.float32)
        kept_ref[:, columns] = partial[:cut]
        leaving_ref[:, columns] = partial[cut:]


def attend(queries, near_kv, far_kv, w_out, head_dim):
    rows, width = queries.shape
    keys = 2 * near_kv.shape[0]
    half = jax.ShapeDtypeStruct((rows // 2, w_out.shape[1]), jnp.float32)
    return pl.pallas_call(
        lambda *refs: attend_kernel(head_dim, *refs),
        out_shape=[half, half],
        scratch_shapes=[pltpu.VMEM((rows, width), jnp.bfloat16)],
        compiler_params=pltpu.CompilerParams(vmem_limit_bytes=12 * 1024 * 1024),
        cost_estimate=pl.CostEstimate(
            flops=4 * rows * width * keys + 2 * rows * width * w_out.shape[1],
            bytes_accessed=2 * width * w_out.shape[1] + 4 * rows * w_out.shape[1],
            transcendentals=rows * keys * width // head_dim,
        ),
        name="attend",
    )(queries, near_kv, far_kv, w_out)


def expert_kernel(first, spots, cuts, *refs):
    pick_ref, place_ref, share_ref, own_gu_ref, far_gu_ref, own_dn_ref, far_dn_ref = refs[:7]
    group_rows, slots = place_ref.shape[2:]
    groups = len(cuts)
    piece_refs = refs[7 : 7 + len(spots)]
    out_refs = refs[7 + len(spots) : 7 + len(spots) + 2 * sum(cuts)]
    x_buf, xs_buf, gu_buf, dn_buf, hid_buf, served_buf, y_buf, x_sem, w_sem, y_sem = refs[
        7 + len(spots) + len(out_refs) :
    ]
    width = x_buf.shape[2]
    half = width // 2
    hidden = own_dn_ref.shape[0]
    tiles = hidden // TILE

    row_copies = []
    for number, ((group, row, column), piece) in enumerate(zip(spots, piece_refs)):
        rows, columns = piece.shape
        target = x_buf.at[group, pl.ds(row, rows), pl.ds(column, columns)]
        row_copies.append((group, pltpu.make_async_copy(piece, target, x_sem.at[number])))
    weight_copies = []
    for expert, (gu_ref, dn_ref) in enumerate(((own_gu_ref, own_dn_ref), (far_gu_ref, far_dn_ref))):
        mine = []
        for tile in range(tiles):
            for side in range(2):
                mine.append(
                    pltpu.make_async_copy(
                        gu_ref.at[:, pl.ds(side * hidden + tile * TILE, TILE)],
                        gu_buf.at[expert, tile, side],
                        w_sem.at[expert, 2 * tile + side],
                    )
                )
        mine.append(pltpu.make_async_copy(dn_ref, dn_buf.at[expert], w_sem.at[expert, 2 * tiles]))
        weight_copies.append(mine)
    for _, copy in row_copies:
        copy.start()
    for mine in weight_copies:
        for copy in mine:
            copy.start()

    for group in range(groups):
        for where, copy in row_copies:
            if where == group:
                copy.wait()
        chosen = jnp.dot(
            pick_ref[first + group], x_buf[group], preferred_element_type=jnp.float32
        ).astype(jnp.bfloat16)
        xs_buf[0, pl.ds(group * slots, slots)] = chosen[:slots]
        xs_buf[1, pl.ds(group * slots, slots)] = chosen[slots:]

    for expert in range(2):
        for tile in range(tiles):
            weight_copies[expert][2 * tile].wait()
            weight_copies[expert][2 * tile + 1].wait()
            gate = jnp.dot(
                xs_buf[expert], gu_buf[expert, tile, 0], preferred_element_type=jnp.float32
            )
            up = jnp.dot(
                xs_buf[expert], gu_buf[expert, tile, 1], preferred_element_type=jnp.float32
            )
            value = gate / (1.0 + jnp.exp(-gate)) * up
            hid_buf[:, tile * TILE : (tile + 1) * TILE] = value.astype(jnp.bfloat16)
        weight_copies[expert][2 * tiles].wait()
        for column in range(0, width, 2 * TILE):
            served_buf[expert, :, column : column + 2 * TILE] = jnp.dot(
                hid_buf[...],
                dn_buf[expert, :, column : column + 2 * TILE],
                preferred_element_type=jnp.float32,
            ).astype(jnp.bfloat16)

    out_copies = []
    for group in range(groups):
        for column in range(0, width, 2 * TILE):
            total = None
            for expert in range(2):
                placed = jnp.dot(
                    place_ref[expert, first + group],
                    served_buf[expert, pl.ds(group * slots, slots), column : column + 2 * TILE],
                    preferred_element_type=jnp.float32,
                )
                term = placed * share_ref[first + group, :, expert : expert + 1]
                total = term if total is None else total + term
            y_buf[group, :, column : column + 2 * TILE] = total.astype(jnp.bfloat16)
        cut = group_rows // cuts[group]
        for number in range(2 * cuts[group]):
            row, side = divmod(number, 2)
            done = len(out_copies)
            copy = pltpu.make_async_copy(
                y_buf.at[group, pl.ds(row * cut, cut), pl.ds(side * half, half)],
                out_refs[done],
                y_sem.at[done],
            )
            copy.start()
            out_copies.append(copy)
    for copy in out_copies:
        copy.wait()


def run_experts(first, pieces, cuts, pick, place, share, weights):
    group_rows, slots = place.shape[2:]
    groups = len(pieces)
    hidden, width = weights[2].shape
    tiles = hidden // TILE
    spots = [
        (group, row, column) for group, held in enumerate(pieces) for row, column, _ in held
    ]
    arrays = [array for held in pieces for _, _, array in held]
    anywhere = pl.BlockSpec(memory_space=pl.ANY)
    inside = pl.BlockSpec(memory_space=pltpu.VMEM)
    outs = pl.pallas_call(
        lambda *refs: expert_kernel(first, spots, cuts, *refs),
        out_shape=[
            jax.ShapeDtypeStruct((group_rows // cut, width // 2), jnp.bfloat16)
            for cut in cuts
            for _ in range(2 * cut)
        ],
        in_specs=[inside] * 3 + [anywhere] * (4 + len(arrays)),
        out_specs=[anywhere] * (2 * sum(cuts)),
        scratch_shapes=[
            pltpu.VMEM((groups, group_rows, width), jnp.bfloat16),
            pltpu.VMEM((2, groups * slots, width), jnp.bfloat16),
            pltpu.VMEM((2, tiles, 2, width, TILE), jnp.bfloat16),
            pltpu.VMEM((2, hidden, width), jnp.bfloat16),
            pltpu.VMEM((groups * slots, hidden), jnp.bfloat16),
            pltpu.VMEM((2, groups * slots, width), jnp.bfloat16),
            pltpu.VMEM((groups, group_rows, width), jnp.bfloat16),
            pltpu.SemaphoreType.DMA((len(arrays),)),
            pltpu.SemaphoreType.DMA((2, 2 * tiles + 1)),
            pltpu.SemaphoreType.DMA((2 * sum(cuts),)),
        ],
        compiler_params=pltpu.CompilerParams(vmem_limit_bytes=(28 + 6 * group_rows // 256) * 1024 * 1024),
        cost_estimate=pl.CostEstimate(
            flops=12 * groups * slots * width * hidden,
            bytes_accessed=12 * width * hidden + 4 * groups * group_rows * width,
            transcendentals=2 * groups * slots * hidden,
        ),
        name="experts",
    )(pick, place, share, *weights, *arrays)
    return list(zip(outs[0::2], outs[1::2]))


def per_device(
    hidden_in,
    attn_gain,
    w_query,
    w_keyval,
    q_gain,
    k_gain,
    w_out,
    moe_gain,
    expert_ids,
    gate_fixed,
    w_gateup,
    w_down,
):
    tokens = hidden_in[0].astype(jnp.float32)
    row_count, model_width = tokens.shape
    head_dim = q_gain.shape[0]
    local_heads = w_query.shape[1] // head_dim
    kv_heads = w_keyval.shape[2] // head_dim
    group_size = local_heads * lax.axis_size("rep") // kv_heads
    rep_index = lax.axis_index("rep")
    kv_width = kv_heads * head_dim
    top_count = expert_ids.shape[2]
    expert_count = lax.axis_size(EVERY)

    normed, own_payload = prepare(
        hidden_in[0], attn_gain, w_keyval, k_gain, expert_ids[0], gate_fixed[0]
    )
    across_rows = swap(normed, "rep", ACROSS)
    pair_rows = swap(normed, "rep", PAIR)
    line = jnp.concatenate(
        [own_payload] + [swap(own_payload, "seq", bits) for bits in seq_order()[1:]], axis=0
    )
    corner_rows = swap(across_rows, "rep", PAIR)
    line_routes = line[:, 2 * kv_width :]

    def head_kv(rep):
        index = rep * local_heads // group_size * head_dim
        return [
            lax.dynamic_slice_in_dim(line, index, head_dim, 1),
            lax.dynamic_slice_in_dim(line, kv_width + index, head_dim, 1),
        ]

    sent = jnp.concatenate(head_kv(rep_index ^ ACROSS) + [line_routes], axis=1)
    sent, across_rows, pair_rows = ready(sent, across_rows, pair_rows)
    across = swap(sent, "rep", ACROSS)
    half_kv = jnp.concatenate(
        [jnp.concatenate(head_kv(rep_index), axis=1), across[:, : 2 * head_dim]], axis=0
    )
    pair_kv = swap(half_kv, "rep", PAIR)
    both_routes = jnp.stack([line_routes, across[:, 2 * head_dim :]])
    far_routes = swap(both_routes, "role", 1)
    coded = jnp.concatenate([both_routes[1:], far_routes[:1], far_routes[1:], both_routes[:1]])
    far_gu = swap(w_gateup[0], "rep", PAIR)
    queries = make_queries([normed, across_rows, pair_rows, corner_rows], w_query, q_gain)
    kept, leaving = attend(queries, half_kv, pair_kv, w_out, head_dim)
    leaving, own_dn = ready(swap(leaving, "rep", PAIR), w_down[0])
    halves = kept + leaving
    far_dn = swap(own_dn, "rep", PAIR)
    far_sum = halves[row_count:].astype(jnp.bfloat16)
    across_sum, coded = ready(swap(far_sum, "rep", ACROSS), coded)
    attended = halves[:row_count] + across_sum.astype(jnp.float32)
    mixed = tokens + attended

    mixed, far_gu, far_dn, coded = ready(mixed, far_gu, far_dn, coded)
    moe_in = rms_rows(mixed, moe_gain).astype(jnp.bfloat16)

    rows, coded = spread_rows(moe_in, coded)
    coded = coded[:, :, : 3 * top_count].astype(jnp.int32)
    routes = coded[:, :, :top_count]
    gates = coded[:, :, top_count : 2 * top_count] * 64 + coded[:, :, 2 * top_count :]
    gates = gates.astype(jnp.float32)
    groups, group_rows = routes.shape[:2]
    capacity = max(2, 7 * row_count * top_count // (4 * expert_count))
    slots = -(-capacity * (group_rows // row_count) // 16) * 16
    gate_sum = jnp.sum(gates, axis=2)
    earlier = jnp.tri(group_rows, k=-1, dtype=jnp.bfloat16)
    picks, shares = [], []
    for expert in (lax.axis_index(EVERY), lax.axis_index(EVERY) ^ PAIR):
        named = routes == expert
        hit = jnp.any(named, axis=2)
        shares.append(jnp.sum(jnp.where(named, gates, 0.0), axis=2) / gate_sum)
        rank = jnp.einsum(
            "ij,gj->gi", earlier, hit.astype(jnp.bfloat16), preferred_element_type=jnp.float32
        )
        rank = jnp.where(hit, rank.astype(jnp.int32), -1)
        picks.append((rank[:, None, :] == jnp.arange(slots)[None, :, None]).astype(jnp.bfloat16))
    pick = jnp.concatenate(picks, axis=1)
    place = jnp.stack([jnp.swapaxes(one, 1, 2) for one in picks])
    share = jnp.stack(shares, axis=2)

    weights = (w_gateup[0], far_gu, w_down[0], far_dn)

    tables = (pick, place, share, weights)
    by_rep, by_role = run_experts(0, rows[:2], (1, 1), *tables)
    rep_low, rep_high, role_low, role_high, *held = ready(
        *by_rep, *by_role, *(array for _, _, array in rows[2])
    )
    by_rep, by_role = (rep_low, rep_high), (role_low, role_high)
    pieces = [(row, column, array) for (row, column, _), array in zip(rows[2], held)]
    *corner, near = run_experts(2, [pieces, rows[3]], (2, 1), *tables)
    routed = collect_rows(near, by_rep, by_role, corner)
    return (mixed + routed).astype(jnp.bfloat16)[None]


def solution(mesh):
    placed = (
        P("role", ("seq", "rep"), None),
        P(),
        P(None, "rep"),
        P(),
        P(),
        P(),
        P("rep", None),
        P(),
        P("role", ("seq", "rep"), None),
        P("role", ("seq", "rep"), None),
        P(("role", "seq", "rep"), None, None),
        P(("role", "seq", "rep"), None, None),
    )
    return jax.shard_map(
        per_device,
        mesh=mesh,
        in_specs=placed,
        out_specs=P("role", ("seq", "rep"), None),
        check_vma=False,
    )
```

```python
import jax
import jax.numpy as jnp
from jax import lax
from jax.experimental import pallas as pl
from jax.experimental.pallas import tpu as pltpu
from jax.sharding import PartitionSpec as P

EVERY = ("role", "seq", "rep")
PAIR = 1
ACROSS = 2
TILE = 256
LANES = 128


def rms_rows(values_in, gain_vec):
    return (
        values_in
        * lax.rsqrt(jnp.mean(values_in * values_in, axis=-1, keepdims=True) + 1e-06)
        * gain_vec
    )


def swap(block, axis, bits):
    size = lax.axis_size(axis)
    return lax.ppermute(block, axis, [(i, i ^ bits) for i in range(size)])


def seq_bits():
    size = lax.axis_size("seq")
    return [1 << place for place in reversed(range(size.bit_length() - 1))]


def seq_order():
    order = [0]
    for bits in seq_bits():
        order = order + [place ^ bits for place in order]
    return order


def ready(*arrays):
    return lax.optimization_barrier(arrays)


def spread_rows(own, coded):
    half = own.shape[1] // 2

    def both_ways(part):
        return swap(part, "rep", ACROSS), swap(part, "role", 1)

    def corners(by_rep, by_role):
        return swap(by_rep[:, :half], "role", 1), swap(by_role[:, half:], "rep", ACROSS)

    first_bits, *bits_left = seq_bits()
    blocks = [own, swap(own, "seq", first_bits)]
    for bits in bits_left[:-1]:
        blocks = blocks + [swap(block, "seq", bits) for block in blocks]
    beyond = [swap(block, "seq", bits_left[-1]) for block in blocks]
    outer = both_ways(own)
    middle = jnp.concatenate(blocks[1:] + beyond[:-1], axis=0)
    middle, *outer_corner = ready(middle, *corners(*outer))
    last, coded = ready(beyond[-1], coded)
    inner = both_ways(middle)
    final = both_ways(last)
    inner_corner = corners(*inner)
    final_corner = corners(*final)
    groups = [[], [], [], []]
    start = 0
    for part, beside, corner in (
        (own, outer, outer_corner),
        (middle, inner, inner_corner),
        (last, final, final_corner),
    ):
        groups[0].append((start, 0, beside[0]))
        groups[1].append((start, 0, beside[1]))
        groups[2].append((start, 0, corner[0]))
        groups[2].append((start, half, corner[1]))
        groups[3].append((start, 0, part))
        start += part.shape[0]
    return groups, coded


def added(first, second):
    return (first.astype(jnp.float32) + second.astype(jnp.float32)).astype(jnp.bfloat16)


def collect_rows(near, by_rep, by_role, corner):
    straight_low = swap(by_role[0], "role", 1)
    straight_high = swap(by_rep[1], "rep", ACROSS)
    straight_low, straight_high, near_low, near_high, *corner = ready(
        straight_low, straight_high, *near, *corner[0], *corner[1]
    )
    cut = near_low.shape[0] // 2
    halves = slice(0, cut), slice(cut, None)

    def merged(rows, turned_low, turned_high):
        return jnp.concatenate(
            [
                base[rows].astype(jnp.float32)
                + first[rows].astype(jnp.float32)
                + second.astype(jnp.float32)
                for base, first, second in (
                    (near_low, straight_low, turned_low),
                    (near_high, straight_high, turned_high),
                )
            ],
            axis=1,
        )

    def corners(number):
        low, high = corner[2 * number : 2 * number + 2]
        return swap(low, "role", 1), swap(high, "rep", ACROSS)

    def turned(number, corner_low, corner_high):
        rows = halves[number]
        return (
            swap(added(by_rep[0][rows], corner_low), "rep", ACROSS),
            swap(added(by_role[1][rows], corner_high), "role", 1),
        )

    far_corner, beside_corner = corners(1), corners(0)
    far = turned(1, *far_corner)
    *far, corner_low, corner_high = ready(*far, *beside_corner)
    leaving = merged(halves[1], *far).astype(jnp.bfloat16)
    *beside, _ = ready(*turned(0, corner_low, corner_high), leaving)
    total = merged(halves[0], *beside)
    for bits in reversed(seq_bits()):
        total = total + swap(leaving, "seq", bits).astype(jnp.float32)
        if bits != seq_bits()[0]:
            cut = total.shape[0] // 2
            total, leaving = total[:cut], total[cut:].astype(jnp.bfloat16)
    return total


def prepare_kernel(*refs):
    tokens_in, gain_in, kv_in, k_gain_in, ids_in, gates_in, normed_ref, out_ref = refs[:8]
    held, sem = refs[8:14], refs[14]
    sources = (tokens_in, gain_in, kv_in, k_gain_in, ids_in, gates_in)
    copies = [
        pltpu.make_async_copy(src, dst, sem.at[number])
        for number, (src, dst) in enumerate(zip(sources, held))
    ]
    for copy in copies:
        copy.start()
    for copy in copies:
        copy.wait()
    tokens_ref, gain_ref, kv_ref, k_gain_ref, ids_ref, gates_ref = held
    normed = rms_rows(tokens_ref[...].astype(jnp.float32), gain_ref[...]).astype(jnp.bfloat16)
    normed_ref[...] = normed
    kv_width, head_dim = kv_ref.shape[2], k_gain_ref.shape[1]
    keys = jnp.dot(normed, kv_ref[0], preferred_element_type=jnp.float32)
    for start in range(0, kv_width, head_dim):
        head = rms_rows(keys[:, start : start + head_dim], k_gain_ref[...])
        out_ref[:, start : start + head_dim] = head.astype(jnp.bfloat16)
    values = jnp.dot(normed, kv_ref[1], preferred_element_type=jnp.float32)
    out_ref[:, kv_width : 2 * kv_width] = values.astype(jnp.bfloat16)
    coded = jnp.concatenate([ids_ref[...], gates_ref[...] // 64, gates_ref[...] % 64], axis=0)
    count = coded.shape[0]
    spread = lax.broadcasted_iota(jnp.int32, (count, LANES), 0)
    spread = spread == lax.broadcasted_iota(jnp.int32, (count, LANES), 1)
    out_ref[:, 2 * kv_width :] = lax.dot_general(
        coded.astype(jnp.float32).astype(jnp.bfloat16),
        spread.astype(jnp.float32).astype(jnp.bfloat16),
        (((0,), (0,)), ((), ())),
        preferred_element_type=jnp.float32,
    ).astype(jnp.bfloat16)


def prepare(tokens, attn_gain, w_keyval, k_gain, ids, gates):
    rows, width = tokens.shape
    operands = [
        pltpu.with_memory_space_constraint(one, pltpu.HBM)
        for one in (tokens, attn_gain[None], w_keyval, k_gain[None], ids.T, gates.T)
    ]
    return pl.pallas_call(
        prepare_kernel,
        out_shape=[
            jax.ShapeDtypeStruct((rows, width), jnp.bfloat16),
            jax.ShapeDtypeStruct((rows, 2 * w_keyval.shape[2] + LANES), jnp.bfloat16),
        ],
        in_specs=[pl.BlockSpec(memory_space=pltpu.HBM)] * len(operands),
        scratch_shapes=[pltpu.VMEM(one.shape, one.dtype) for one in operands]
        + [pltpu.SemaphoreType.DMA((len(operands),))],
        compiler_params=pltpu.CompilerParams(vmem_limit_bytes=8 * 1024 * 1024),
        cost_estimate=pl.CostEstimate(
            flops=4 * rows * width * w_keyval.shape[2],
            bytes_accessed=4 * width * w_keyval.shape[2] + 4 * rows * width,
            transcendentals=rows,
        ),
        name="prepare",
    )(*operands)


def queries_kernel(first_ref, second_ref, third_ref, fourth_ref, weight_ref, gain_ref, out_ref):
    rows, head_dim = first_ref.shape[0], gain_ref.shape[1]
    refs = (first_ref, second_ref, third_ref, fourth_ref)
    held = jnp.concatenate([ref[...] for ref in refs], axis=0)
    raw = jnp.dot(held, weight_ref[...], preferred_element_type=jnp.float32)
    for start in range(0, weight_ref.shape[1], head_dim):
        head = rms_rows(raw[:, start : start + head_dim], gain_ref[...])
        out_ref[:, start : start + head_dim] = head.astype(jnp.bfloat16)


def make_queries(blocks, w_query, q_gain):
    rows, width = len(blocks) * blocks[0].shape[0], w_query.shape[1]
    return pl.pallas_call(
        queries_kernel,
        out_shape=jax.ShapeDtypeStruct((rows, width), jnp.bfloat16),
        compiler_params=pltpu.CompilerParams(vmem_limit_bytes=8 * 1024 * 1024),
        cost_estimate=pl.CostEstimate(
            flops=2 * rows * width * w_query.shape[0],
            bytes_accessed=2 * width * w_query.shape[0],
            transcendentals=rows,
        ),
        name="queries",
    )(*blocks, w_query, q_gain[None])


def attend_kernel(head_dim, query_ref, near_ref, far_ref, weight_ref, kept_ref, leaving_ref, held_ref):
    keys = [ref[:, :head_dim] for ref in (near_ref, far_ref)]
    values = [ref[:, head_dim:] for ref in (near_ref, far_ref)]
    for start in range(0, query_ref.shape[1], head_dim):
        query = query_ref[:, start : start + head_dim]
        scores = [
            lax.dot_general(
                query, key, (((1,), (1,)), ((), ())), preferred_element_type=jnp.float32
            )
            * head_dim ** (-0.5)
            for key in keys
        ]
        row_max = jnp.maximum(
            jnp.max(scores[0], axis=1, keepdims=True), jnp.max(scores[1], axis=1, keepdims=True)
        )
        denom, total = 0.0, 0.0
        for score, value in zip(scores, values):
            weights = jnp.exp(score - row_max)
            denom = denom + jnp.sum(weights, axis=1, keepdims=True)
            total = total + jnp.dot(
                weights.astype(jnp.bfloat16), value, preferred_element_type=jnp.float32
            )
        held_ref[:, start : start + head_dim] = (total / denom).astype(jnp.bfloat16)
    cut = kept_ref.shape[0]
    for column in range(0, weight_ref.shape[1], 2 * TILE):
        columns = slice(column, column + 2 * TILE)
        partial = jnp.dot(held_ref[...], weight_ref[:, columns], preferred_element_type=jnp.float32)
        kept_ref[:, columns] = partial[:cut]
        leaving_ref[:, columns] = partial[cut:]


def attend(queries, near_kv, far_kv, w_out, head_dim):
    rows, width = queries.shape
    keys = 2 * near_kv.shape[0]
    half = jax.ShapeDtypeStruct((rows // 2, w_out.shape[1]), jnp.float32)
    return pl.pallas_call(
        lambda *refs: attend_kernel(head_dim, *refs),
        out_shape=[half, half],
        scratch_shapes=[pltpu.VMEM((rows, width), jnp.bfloat16)],
        compiler_params=pltpu.CompilerParams(vmem_limit_bytes=12 * 1024 * 1024),
        cost_estimate=pl.CostEstimate(
            flops=4 * rows * width * keys + 2 * rows * width * w_out.shape[1],
            bytes_accessed=2 * width * w_out.shape[1] + 4 * rows * w_out.shape[1],
            transcendentals=rows * keys * width // head_dim,
        ),
        name="attend",
    )(queries, near_kv, far_kv, w_out)


def tables_kernel(top_count, expert_ref, coded_ref, pick_ref, place_ref, share_ref):
    groups, rows, lanes = coded_ref.shape
    slots = place_ref.shape[3]
    lane = lax.broadcasted_iota(jnp.int32, (rows, lanes), 1)
    source = lax.broadcasted_iota(jnp.int32, (lanes, lanes), 0)
    target = lax.broadcasted_iota(jnp.int32, (lanes, lanes), 1)
    joined = jnp.where(source == target + top_count, 64.0, 0.0)
    joined = joined + jnp.where(source == target + 2 * top_count, 1.0, 0.0)
    joined = jnp.where(target < top_count, joined, 0.0).astype(jnp.bfloat16)
    first = lax.broadcasted_iota(jnp.int32, (rows, rows), 0)
    second = lax.broadcasted_iota(jnp.int32, (rows, rows), 1)
    later = jnp.where(first < second, 1.0, 0.0).astype(jnp.bfloat16)
    earlier = jnp.where(second < first, 1.0, 0.0).astype(jnp.bfloat16)
    ones = jnp.ones((8, lanes), jnp.bfloat16)
    slot_row = lax.broadcasted_iota(jnp.int32, (slots, rows), 0).astype(jnp.float32)
    slot_lane = lax.broadcasted_iota(jnp.int32, (rows, slots), 1).astype(jnp.float32)
    for group in range(groups):
        coded = coded_ref[group]
        gates = jnp.dot(coded, joined, preferred_element_type=jnp.float32)
        gate_sum = jnp.sum(gates, axis=1, keepdims=True)
        named = coded.astype(jnp.float32).astype(jnp.int32)
        for number in range(2):
            expert = expert_ref[0] ^ (number * PAIR)
            hits = jnp.where((named == expert) & (lane < top_count), 1.0, 0.0)
            share_ref[group, :, number : number + 1] = (
                jnp.sum(hits * gates, axis=1, keepdims=True) / gate_sum
            )
            hit = jnp.sum(hits, axis=1, keepdims=True)
            held = jnp.broadcast_to(hit, (rows, lanes)).astype(jnp.bfloat16)
            rank = jnp.dot(earlier, held, preferred_element_type=jnp.float32)[:, :1]
            rank = jnp.where(hit > 0.0, rank, -1.0)
            place_ref[number, group] = jnp.where(rank == slot_lane, 1.0, 0.0).astype(jnp.bfloat16)
            hit_row = lax.dot_general(
                ones,
                hits.astype(jnp.bfloat16),
                (((1,), (1,)), ((), ())),
                preferred_element_type=jnp.float32,
            )
            rank_row = jnp.dot(
                hit_row.astype(jnp.bfloat16), later, preferred_element_type=jnp.float32
            )
            rank_row = jnp.where(hit_row > 0.0, rank_row, -1.0)[:1]
            pick_ref[group, number * slots : (number + 1) * slots] = jnp.where(
                rank_row == slot_row, 1.0, 0.0
            ).astype(jnp.bfloat16)


def make_tables(coded, expert, slots, top_count):
    groups, rows, lanes = coded.shape
    return pl.pallas_call(
        lambda *refs: tables_kernel(top_count, *refs),
        out_shape=[
            jax.ShapeDtypeStruct((groups, 2 * slots, rows), jnp.bfloat16),
            jax.ShapeDtypeStruct((2, groups, rows, slots), jnp.bfloat16),
            jax.ShapeDtypeStruct((groups, rows, 2), jnp.float32),
        ],
        in_specs=[
            pl.BlockSpec(memory_space=pltpu.SMEM),
            pl.BlockSpec(memory_space=pltpu.VMEM),
        ],
        compiler_params=pltpu.CompilerParams(vmem_limit_bytes=24 * 1024 * 1024),
        cost_estimate=pl.CostEstimate(
            flops=4 * groups * rows * rows * lanes,
            bytes_accessed=8 * groups * rows * slots,
            transcendentals=0,
        ),
        name="tables",
    )(expert.astype(jnp.int32)[None], coded)


def expert_kernel(first, spots, cuts, *refs):
    pick_ref, place_ref, share_ref, own_gu_ref, far_gu_ref, own_dn_ref, far_dn_ref = refs[:7]
    group_rows, slots = place_ref.shape[2:]
    groups = len(cuts)
    piece_refs = refs[7 : 7 + len(spots)]
    out_refs = refs[7 + len(spots) : 7 + len(spots) + 2 * sum(cuts)]
    x_buf, xs_buf, gu_buf, dn_buf, hid_buf, served_buf, y_buf, x_sem, w_sem, y_sem = refs[
        7 + len(spots) + len(out_refs) :
    ]
    width = x_buf.shape[2]
    half = width // 2
    hidden = own_dn_ref.shape[0]
    tiles = hidden // TILE

    row_copies = []
    for number, ((group, row, column), piece) in enumerate(zip(spots, piece_refs)):
        rows, columns = piece.shape
        target = x_buf.at[group, pl.ds(row, rows), pl.ds(column, columns)]
        row_copies.append((group, pltpu.make_async_copy(piece, target, x_sem.at[number])))
    weight_copies = []
    for expert, (gu_ref, dn_ref) in enumerate(((own_gu_ref, own_dn_ref), (far_gu_ref, far_dn_ref))):
        mine = []
        for tile in range(tiles):
            for side in range(2):
                mine.append(
                    pltpu.make_async_copy(
                        gu_ref.at[:, pl.ds(side * hidden + tile * TILE, TILE)],
                        gu_buf.at[expert, tile, side],
                        w_sem.at[expert, 2 * tile + side],
                    )
                )
        mine.append(pltpu.make_async_copy(dn_ref, dn_buf.at[expert], w_sem.at[expert, 2 * tiles]))
        weight_copies.append(mine)
    for _, copy in row_copies:
        copy.start()
    for mine in weight_copies:
        for copy in mine:
            copy.start()

    for group in range(groups):
        for where, copy in row_copies:
            if where == group:
                copy.wait()
        chosen = jnp.dot(
            pick_ref[first + group], x_buf[group], preferred_element_type=jnp.float32
        ).astype(jnp.bfloat16)
        xs_buf[0, pl.ds(group * slots, slots)] = chosen[:slots]
        xs_buf[1, pl.ds(group * slots, slots)] = chosen[slots:]

    for expert in range(2):
        for tile in range(tiles):
            weight_copies[expert][2 * tile].wait()
            weight_copies[expert][2 * tile + 1].wait()
            gate = jnp.dot(
                xs_buf[expert], gu_buf[expert, tile, 0], preferred_element_type=jnp.float32
            )
            up = jnp.dot(
                xs_buf[expert], gu_buf[expert, tile, 1], preferred_element_type=jnp.float32
            )
            value = gate / (1.0 + jnp.exp(-gate)) * up
            hid_buf[:, tile * TILE : (tile + 1) * TILE] = value.astype(jnp.bfloat16)
        weight_copies[expert][2 * tiles].wait()
        for column in range(0, width, 2 * TILE):
            served_buf[expert, :, column : column + 2 * TILE] = jnp.dot(
                hid_buf[...],
                dn_buf[expert, :, column : column + 2 * TILE],
                preferred_element_type=jnp.float32,
            ).astype(jnp.bfloat16)

    out_copies = []
    for group in range(groups):
        for column in range(0, width, 2 * TILE):
            total = None
            for expert in range(2):
                placed = jnp.dot(
                    place_ref[expert, first + group],
                    served_buf[expert, pl.ds(group * slots, slots), column : column + 2 * TILE],
                    preferred_element_type=jnp.float32,
                )
                term = placed * share_ref[first + group, :, expert : expert + 1]
                total = term if total is None else total + term
            y_buf[group, :, column : column + 2 * TILE] = total.astype(jnp.bfloat16)
        cut = group_rows // cuts[group]
        for number in range(2 * cuts[group]):
            row, side = divmod(number, 2)
            done = len(out_copies)
            copy = pltpu.make_async_copy(
                y_buf.at[group, pl.ds(row * cut, cut), pl.ds(side * half, half)],
                out_refs[done],
                y_sem.at[done],
            )
            copy.start()
            out_copies.append(copy)
    for copy in out_copies:
        copy.wait()


def run_experts(first, pieces, cuts, pick, place, share, weights):
    group_rows, slots = place.shape[2:]
    groups = len(pieces)
    hidden, width = weights[2].shape
    tiles = hidden // TILE
    spots = [
        (group, row, column) for group, held in enumerate(pieces) for row, column, _ in held
    ]
    arrays = [array for held in pieces for _, _, array in held]
    anywhere = pl.BlockSpec(memory_space=pl.ANY)
    stored = pl.BlockSpec(memory_space=pltpu.HBM)
    inside = pl.BlockSpec(memory_space=pltpu.VMEM)
    outs = pl.pallas_call(
        lambda *refs: expert_kernel(first, spots, cuts, *refs),
        out_shape=[
            jax.ShapeDtypeStruct((group_rows // cut, width // 2), jnp.bfloat16)
            for cut in cuts
            for _ in range(2 * cut)
        ],
        in_specs=[inside] * 3 + [stored] * 4 + [anywhere] * len(arrays),
        out_specs=[anywhere] * (2 * sum(cuts)),
        scratch_shapes=[
            pltpu.VMEM((groups, group_rows, width), jnp.bfloat16),
            pltpu.VMEM((2, groups * slots, width), jnp.bfloat16),
            pltpu.VMEM((2, tiles, 2, width, TILE), jnp.bfloat16),
            pltpu.VMEM((2, hidden, width), jnp.bfloat16),
            pltpu.VMEM((groups * slots, hidden), jnp.bfloat16),
            pltpu.VMEM((2, groups * slots, width), jnp.bfloat16),
            pltpu.VMEM((groups, group_rows, width), jnp.bfloat16),
            pltpu.SemaphoreType.DMA((len(arrays),)),
            pltpu.SemaphoreType.DMA((2, 2 * tiles + 1)),
            pltpu.SemaphoreType.DMA((2 * sum(cuts),)),
        ],
        compiler_params=pltpu.CompilerParams(vmem_limit_bytes=(28 + 6 * group_rows // 256) * 1024 * 1024),
        cost_estimate=pl.CostEstimate(
            flops=12 * groups * slots * width * hidden,
            bytes_accessed=12 * width * hidden + 4 * groups * group_rows * width,
            transcendentals=2 * groups * slots * hidden,
        ),
        name="experts",
    )(pick, place, share, *weights, *arrays)
    return list(zip(outs[0::2], outs[1::2]))


def per_device(
    hidden_in,
    attn_gain,
    w_query,
    w_keyval,
    q_gain,
    k_gain,
    w_out,
    moe_gain,
    expert_ids,
    gate_fixed,
    w_gateup,
    w_down,
):
    tokens = hidden_in[0].astype(jnp.float32)
    row_count, model_width = tokens.shape
    head_dim = q_gain.shape[0]
    local_heads = w_query.shape[1] // head_dim
    kv_heads = w_keyval.shape[2] // head_dim
    group_size = local_heads * lax.axis_size("rep") // kv_heads
    rep_index = lax.axis_index("rep")
    kv_width = kv_heads * head_dim
    top_count = expert_ids.shape[2]
    expert_count = lax.axis_size(EVERY)

    normed, own_payload = prepare(
        hidden_in[0], attn_gain, w_keyval, k_gain, expert_ids[0], gate_fixed[0]
    )
    across_rows = swap(normed, "rep", ACROSS)
    pair_rows = swap(normed, "rep", PAIR)
    line = jnp.concatenate(
        [own_payload] + [swap(own_payload, "seq", bits) for bits in seq_order()[1:]], axis=0
    )
    corner_rows = swap(across_rows, "rep", PAIR)
    line_routes = line[:, 2 * kv_width :]

    def head_kv(rep):
        index = rep * local_heads // group_size * head_dim
        return [
            lax.dynamic_slice_in_dim(line, index, head_dim, 1),
            lax.dynamic_slice_in_dim(line, kv_width + index, head_dim, 1),
        ]

    sent = jnp.concatenate(head_kv(rep_index ^ ACROSS) + [line_routes], axis=1)
    sent, across_rows, pair_rows = ready(sent, across_rows, pair_rows)
    across = swap(sent, "rep", ACROSS)
    half_kv = jnp.concatenate(
        [jnp.concatenate(head_kv(rep_index), axis=1), across[:, : 2 * head_dim]], axis=0
    )
    pair_kv = swap(half_kv, "rep", PAIR)
    both_routes = jnp.stack([line_routes, across[:, 2 * head_dim :]])
    far_routes = swap(both_routes, "role", 1)
    coded = jnp.concatenate([both_routes[1:], far_routes[:1], far_routes[1:], both_routes[:1]])
    far_gu = swap(w_gateup[0], "rep", PAIR)
    queries = make_queries([normed, across_rows, pair_rows, corner_rows], w_query, q_gain)
    kept, leaving = attend(queries, half_kv, pair_kv, w_out, head_dim)
    leaving, own_dn = ready(swap(leaving, "rep", PAIR), w_down[0])
    halves = kept + leaving
    far_dn = swap(own_dn, "rep", PAIR)
    far_sum = halves[row_count:].astype(jnp.bfloat16)
    across_sum, coded = ready(swap(far_sum, "rep", ACROSS), coded)
    attended = halves[:row_count] + across_sum.astype(jnp.float32)
    mixed = tokens + attended

    mixed, far_gu, far_dn, coded = ready(mixed, far_gu, far_dn, coded)
    moe_in = rms_rows(mixed, moe_gain).astype(jnp.bfloat16)

    rows, coded = spread_rows(moe_in, coded)
    capacity = max(2, 7 * row_count * top_count // (4 * expert_count))
    slots = -(-capacity * (coded.shape[1] // row_count) // 16) * 16
    pick, place, share = make_tables(coded, lax.axis_index(EVERY), slots, top_count)
    weights = [
        pltpu.with_memory_space_constraint(one, pltpu.HBM)
        for one in (w_gateup[0], far_gu, w_down[0], far_dn)
    ]

    tables = (pick, place, share, weights)
    by_rep, by_role = run_experts(0, rows[:2], (1, 1), *tables)
    rep_low, rep_high, role_low, role_high, *held = ready(
        *by_rep, *by_role, *(array for _, _, array in rows[2])
    )
    by_rep, by_role = (rep_low, rep_high), (role_low, role_high)
    pieces = [(row, column, array) for (row, column, _), array in zip(rows[2], held)]
    *corner, near = run_experts(2, [pieces, rows[3]], (2, 1), *tables)
    routed = collect_rows(near, by_rep, by_role, corner)
    return (mixed + routed).astype(jnp.bfloat16)[None]


def solution(mesh):
    placed = (
        P("role", ("seq", "rep"), None),
        P(),
        P(None, "rep"),
        P(),
        P(),
        P(),
        P("rep", None),
        P(),
        P("role", ("seq", "rep"), None),
        P("role", ("seq", "rep"), None),
        P(("role", "seq", "rep"), None, None),
        P(("role", "seq", "rep"), None, None),
    )
    return jax.shard_map(
        per_device,
        mesh=mesh,
        in_specs=placed,
        out_specs=P("role", ("seq", "rep"), None),
        check_vma=False,
    )
```

```python
import jax
import jax.numpy as jnp
from jax import lax
from jax.experimental import pallas as pl
from jax.experimental.pallas import tpu as pltpu
from jax.sharding import PartitionSpec as P

EVERY = ("role", "seq", "rep")
PAIR = 1
ACROSS = 2
TILE = 256
LANES = 128


def rms_rows(values_in, gain_vec):
    return (
        values_in
        * lax.rsqrt(jnp.mean(values_in * values_in, axis=-1, keepdims=True) + 1e-06)
        * gain_vec
    )


def swap(block, axis, bits):
    size = lax.axis_size(axis)
    return lax.ppermute(block, axis, [(i, i ^ bits) for i in range(size)])


def seq_bits():
    size = lax.axis_size("seq")
    return [1 << place for place in reversed(range(size.bit_length() - 1))]


def seq_order():
    order = [0]
    for bits in seq_bits():
        order = order + [place ^ bits for place in order]
    return order


def ready(*arrays):
    return lax.optimization_barrier(arrays)


def spread_rows(own, coded, weight):
    half = own.shape[1] // 2

    def both_ways(part):
        return swap(part, "rep", ACROSS), swap(part, "role", 1)

    def corners(by_rep, by_role):
        return swap(by_rep[:, :half], "role", 1), swap(by_role[:, half:], "rep", ACROSS)

    first_bits, *bits_left = seq_bits()
    blocks = [own, swap(own, "seq", first_bits)]
    for bits in bits_left[:-1]:
        blocks = blocks + [swap(block, "seq", bits) for block in blocks]
    beyond = [swap(block, "seq", bits_left[-1]) for block in blocks]
    middle = jnp.concatenate(blocks[1:] + beyond[:-1], axis=0)
    middle, weight, *outer = ready(middle, weight, *both_ways(own))
    outer_corner = corners(*outer)
    last, coded = ready(beyond[-1], coded)
    inner = both_ways(middle)
    final = both_ways(last)
    by_rep, by_role, *outer_corner = ready(*inner, *outer_corner)
    inner_corner = corners(by_rep, by_role)
    final_corner = corners(*final)
    groups = [[], [], [], []]
    start = 0
    for part, beside, corner in (
        (own, outer, outer_corner),
        (middle, inner, inner_corner),
        (last, final, final_corner),
    ):
        groups[0].append((start, 0, beside[0]))
        groups[1].append((start, 0, beside[1]))
        groups[2].append((start, 0, corner[0]))
        groups[2].append((start, half, corner[1]))
        groups[3].append((start, 0, part))
        start += part.shape[0]
    return groups, coded, weight


def added(first, second):
    return (first.astype(jnp.float32) + second.astype(jnp.float32)).astype(jnp.bfloat16)


def collect_rows(near, by_rep, by_role, corner):
    straight_low = swap(by_role[0], "role", 1)
    straight_high = swap(by_rep[1], "rep", ACROSS)
    straight_low, straight_high, near_low, near_high, *corner = ready(
        straight_low, straight_high, *near, *corner[0], *corner[1]
    )
    cut = near_low.shape[0] // 2
    halves = slice(0, cut), slice(cut, None)

    def merged(rows, turned_low, turned_high):
        return jnp.concatenate(
            [
                base[rows].astype(jnp.float32)
                + first[rows].astype(jnp.float32)
                + second.astype(jnp.float32)
                for base, first, second in (
                    (near_low, straight_low, turned_low),
                    (near_high, straight_high, turned_high),
                )
            ],
            axis=1,
        )

    def corners(number):
        low, high = corner[2 * number : 2 * number + 2]
        return swap(low, "role", 1), swap(high, "rep", ACROSS)

    def sums(number, corner_low, corner_high):
        rows = halves[number]
        return added(by_rep[0][rows], corner_low), added(by_role[1][rows], corner_high)

    def turned(low, high):
        return swap(low, "rep", ACROSS), swap(high, "role", 1)

    far_corner, beside_corner = corners(1), corners(0)
    *far, corner_low, corner_high = ready(*turned(*sums(1, *far_corner)), *beside_corner)
    leaving = merged(halves[1], *far).astype(jnp.bfloat16)
    *near_sums, leaving = ready(*sums(0, corner_low, corner_high), leaving)
    beside = turned(*near_sums)
    total = merged(halves[0], *beside)
    *later_bits, last_bits = reversed(seq_bits())
    for bits in later_bits:
        cut = total.shape[0] // 2
        far, near = ready(swap(leaving[cut:], "seq", bits), leaving[:cut])
        leaving = (total[cut:] + far.astype(jnp.float32)).astype(jnp.bfloat16)
        total = total[:cut] + swap(near, "seq", bits).astype(jnp.float32)
    return total + swap(leaving, "seq", last_bits).astype(jnp.float32)


def prepare_kernel(*refs):
    tokens_in, gain_in, kv_in, k_gain_in, ids_in, gates_in, normed_ref, out_ref = refs[:8]
    held, sem = refs[8:14], refs[14]
    sources = (tokens_in, gain_in, kv_in, k_gain_in, ids_in, gates_in)
    copies = [
        pltpu.make_async_copy(src, dst, sem.at[number])
        for number, (src, dst) in enumerate(zip(sources, held))
    ]
    for copy in copies:
        copy.start()
    for copy in copies:
        copy.wait()
    tokens_ref, gain_ref, kv_ref, k_gain_ref, ids_ref, gates_ref = held
    normed = rms_rows(tokens_ref[...].astype(jnp.float32), gain_ref[...]).astype(jnp.bfloat16)
    normed_ref[...] = normed
    kv_width, head_dim = kv_ref.shape[2], k_gain_ref.shape[1]
    keys = jnp.dot(normed, kv_ref[0], preferred_element_type=jnp.float32)
    for start in range(0, kv_width, head_dim):
        head = rms_rows(keys[:, start : start + head_dim], k_gain_ref[...])
        out_ref[:, start : start + head_dim] = head.astype(jnp.bfloat16)
    values = jnp.dot(normed, kv_ref[1], preferred_element_type=jnp.float32)
    out_ref[:, kv_width : 2 * kv_width] = values.astype(jnp.bfloat16)
    coded = jnp.concatenate([ids_ref[...], gates_ref[...] // 64, gates_ref[...] % 64], axis=0)
    count = coded.shape[0]
    spread = lax.broadcasted_iota(jnp.int32, (count, LANES), 0)
    spread = spread == lax.broadcasted_iota(jnp.int32, (count, LANES), 1)
    out_ref[:, 2 * kv_width :] = lax.dot_general(
        coded.astype(jnp.float32).astype(jnp.bfloat16),
        spread.astype(jnp.float32).astype(jnp.bfloat16),
        (((0,), (0,)), ((), ())),
        preferred_element_type=jnp.float32,
    ).astype(jnp.bfloat16)


def prepare(tokens, attn_gain, w_keyval, k_gain, ids, gates):
    rows, width = tokens.shape
    operands = [
        pltpu.with_memory_space_constraint(one, pltpu.HBM)
        for one in (tokens, attn_gain[None], w_keyval, k_gain[None], ids.T, gates.T)
    ]
    return pl.pallas_call(
        prepare_kernel,
        out_shape=[
            jax.ShapeDtypeStruct((rows, width), jnp.bfloat16),
            jax.ShapeDtypeStruct((rows, 2 * w_keyval.shape[2] + LANES), jnp.bfloat16),
        ],
        in_specs=[pl.BlockSpec(memory_space=pltpu.HBM)] * len(operands),
        scratch_shapes=[pltpu.VMEM(one.shape, one.dtype) for one in operands]
        + [pltpu.SemaphoreType.DMA((len(operands),))],
        compiler_params=pltpu.CompilerParams(vmem_limit_bytes=8 * 1024 * 1024),
        cost_estimate=pl.CostEstimate(
            flops=4 * rows * width * w_keyval.shape[2],
            bytes_accessed=4 * width * w_keyval.shape[2] + 4 * rows * width,
            transcendentals=rows,
        ),
        name="prepare",
    )(*operands)


def queries_kernel(first_ref, second_ref, third_ref, fourth_ref, weight_ref, gain_ref, out_ref):
    rows, head_dim = first_ref.shape[0], gain_ref.shape[1]
    refs = (first_ref, second_ref, third_ref, fourth_ref)
    held = jnp.concatenate([ref[...] for ref in refs], axis=0)
    raw = jnp.dot(held, weight_ref[...], preferred_element_type=jnp.float32)
    for start in range(0, weight_ref.shape[1], head_dim):
        head = rms_rows(raw[:, start : start + head_dim], gain_ref[...])
        out_ref[:, start : start + head_dim] = head.astype(jnp.bfloat16)


def make_queries(blocks, w_query, q_gain):
    rows, width = len(blocks) * blocks[0].shape[0], w_query.shape[1]
    return pl.pallas_call(
        queries_kernel,
        out_shape=jax.ShapeDtypeStruct((rows, width), jnp.bfloat16),
        compiler_params=pltpu.CompilerParams(vmem_limit_bytes=8 * 1024 * 1024),
        cost_estimate=pl.CostEstimate(
            flops=2 * rows * width * w_query.shape[0],
            bytes_accessed=2 * width * w_query.shape[0],
            transcendentals=rows,
        ),
        name="queries",
    )(*blocks, w_query, q_gain[None])


def attend_kernel(head_dim, query_ref, near_ref, far_ref, weight_ref, kept_ref, leaving_ref, held_ref):
    keys = [ref[:, :head_dim] for ref in (near_ref, far_ref)]
    values = [ref[:, head_dim:] for ref in (near_ref, far_ref)]
    for start in range(0, query_ref.shape[1], head_dim):
        query = query_ref[:, start : start + head_dim]
        scores = [
            lax.dot_general(
                query, key, (((1,), (1,)), ((), ())), preferred_element_type=jnp.float32
            )
            * head_dim ** (-0.5)
            for key in keys
        ]
        row_max = jnp.maximum(
            jnp.max(scores[0], axis=1, keepdims=True), jnp.max(scores[1], axis=1, keepdims=True)
        )
        denom, total = 0.0, 0.0
        for score, value in zip(scores, values):
            weights = jnp.exp(score - row_max)
            denom = denom + jnp.sum(weights, axis=1, keepdims=True)
            total = total + jnp.dot(
                weights.astype(jnp.bfloat16), value, preferred_element_type=jnp.float32
            )
        held_ref[:, start : start + head_dim] = (total / denom).astype(jnp.bfloat16)
    cut = kept_ref.shape[0]
    for column in range(0, weight_ref.shape[1], 2 * TILE):
        columns = slice(column, column + 2 * TILE)
        partial = jnp.dot(held_ref[...], weight_ref[:, columns], preferred_element_type=jnp.float32)
        kept_ref[:, columns] = partial[:cut]
        leaving_ref[:, columns] = partial[cut:]


def attend(queries, near_kv, far_kv, w_out, head_dim):
    rows, width = queries.shape
    keys = 2 * near_kv.shape[0]
    half = jax.ShapeDtypeStruct((rows // 2, w_out.shape[1]), jnp.float32)
    return pl.pallas_call(
        lambda *refs: attend_kernel(head_dim, *refs),
        out_shape=[half, half],
        scratch_shapes=[pltpu.VMEM((rows, width), jnp.bfloat16)],
        compiler_params=pltpu.CompilerParams(vmem_limit_bytes=12 * 1024 * 1024),
        cost_estimate=pl.CostEstimate(
            flops=4 * rows * width * keys + 2 * rows * width * w_out.shape[1],
            bytes_accessed=2 * width * w_out.shape[1] + 4 * rows * w_out.shape[1],
            transcendentals=rows * keys * width // head_dim,
        ),
        name="attend",
    )(queries, near_kv, far_kv, w_out)


def tables_kernel(top_count, expert_ref, coded_ref, pick_ref, place_ref, share_ref):
    groups, rows, lanes = coded_ref.shape
    slots = place_ref.shape[3]
    lane = lax.broadcasted_iota(jnp.int32, (rows, lanes), 1)
    source = lax.broadcasted_iota(jnp.int32, (lanes, lanes), 0)
    target = lax.broadcasted_iota(jnp.int32, (lanes, lanes), 1)
    joined = jnp.where(source == target + top_count, 64.0, 0.0)
    joined = joined + jnp.where(source == target + 2 * top_count, 1.0, 0.0)
    joined = jnp.where(target < top_count, joined, 0.0).astype(jnp.bfloat16)
    first = lax.broadcasted_iota(jnp.int32, (rows, rows), 0)
    second = lax.broadcasted_iota(jnp.int32, (rows, rows), 1)
    later = jnp.where(first < second, 1.0, 0.0).astype(jnp.bfloat16)
    earlier = jnp.where(second < first, 1.0, 0.0).astype(jnp.bfloat16)
    ones = jnp.ones((8, lanes), jnp.bfloat16)
    slot_row = lax.broadcasted_iota(jnp.int32, (slots, rows), 0).astype(jnp.float32)
    slot_lane = lax.broadcasted_iota(jnp.int32, (rows, slots), 1).astype(jnp.float32)
    for group in range(groups):
        coded = coded_ref[group]
        gates = jnp.dot(coded, joined, preferred_element_type=jnp.float32)
        gate_sum = jnp.sum(gates, axis=1, keepdims=True)
        named = coded.astype(jnp.float32).astype(jnp.int32)
        for number in range(2):
            expert = expert_ref[0] ^ (number * PAIR)
            hits = jnp.where((named == expert) & (lane < top_count), 1.0, 0.0)
            share_ref[group, :, number : number + 1] = (
                jnp.sum(hits * gates, axis=1, keepdims=True) / gate_sum
            )
            hit = jnp.sum(hits, axis=1, keepdims=True)
            held = jnp.broadcast_to(hit, (rows, lanes)).astype(jnp.bfloat16)
            rank = jnp.dot(earlier, held, preferred_element_type=jnp.float32)[:, :1]
            rank = jnp.where(hit > 0.0, rank, -1.0)
            place_ref[number, group] = jnp.where(rank == slot_lane, 1.0, 0.0).astype(jnp.bfloat16)
            hit_row = lax.dot_general(
                ones,
                hits.astype(jnp.bfloat16),
                (((1,), (1,)), ((), ())),
                preferred_element_type=jnp.float32,
            )
            rank_row = jnp.dot(
                hit_row.astype(jnp.bfloat16), later, preferred_element_type=jnp.float32
            )
            rank_row = jnp.where(hit_row > 0.0, rank_row, -1.0)[:1]
            pick_ref[group, number * slots : (number + 1) * slots] = jnp.where(
                rank_row == slot_row, 1.0, 0.0
            ).astype(jnp.bfloat16)


def make_tables(coded, expert, slots, top_count):
    groups, rows, lanes = coded.shape
    return pl.pallas_call(
        lambda *refs: tables_kernel(top_count, *refs),
        out_shape=[
            jax.ShapeDtypeStruct((groups, 2 * slots, rows), jnp.bfloat16),
            jax.ShapeDtypeStruct((2, groups, rows, slots), jnp.bfloat16),
            jax.ShapeDtypeStruct((groups, rows, 2), jnp.float32),
        ],
        in_specs=[
            pl.BlockSpec(memory_space=pltpu.SMEM),
            pl.BlockSpec(memory_space=pltpu.VMEM),
        ],
        compiler_params=pltpu.CompilerParams(vmem_limit_bytes=24 * 1024 * 1024),
        cost_estimate=pl.CostEstimate(
            flops=4 * groups * rows * rows * lanes,
            bytes_accessed=8 * groups * rows * slots,
            transcendentals=0,
        ),
        name="tables",
    )(expert.astype(jnp.int32)[None], coded)


def expert_kernel(first, spots, cuts, *refs):
    pick_ref, place_ref, share_ref, own_gu_ref, far_gu_ref, own_dn_ref, far_dn_ref = refs[:7]
    group_rows, slots = place_ref.shape[2:]
    groups = len(cuts)
    piece_refs = refs[7 : 7 + len(spots)]
    out_refs = refs[7 + len(spots) : 7 + len(spots) + 2 * sum(cuts)]
    x_buf, xs_buf, gu_buf, dn_buf, hid_buf, served_buf, y_buf, x_sem, w_sem, y_sem = refs[
        7 + len(spots) + len(out_refs) :
    ]
    width = x_buf.shape[2]
    half = width // 2
    hidden = own_dn_ref.shape[0]
    tiles = hidden // TILE

    row_copies = []
    for number, ((group, row, column), piece) in enumerate(zip(spots, piece_refs)):
        rows, columns = piece.shape
        target = x_buf.at[group, pl.ds(row, rows), pl.ds(column, columns)]
        row_copies.append((group, pltpu.make_async_copy(piece, target, x_sem.at[number])))
    weight_copies = []
    for expert, (gu_ref, dn_ref) in enumerate(((own_gu_ref, own_dn_ref), (far_gu_ref, far_dn_ref))):
        mine = []
        for tile in range(tiles):
            for side in range(2):
                mine.append(
                    pltpu.make_async_copy(
                        gu_ref.at[:, pl.ds(side * hidden + tile * TILE, TILE)],
                        gu_buf.at[expert, tile, side],
                        w_sem.at[expert, 2 * tile + side],
                    )
                )
        mine.append(pltpu.make_async_copy(dn_ref, dn_buf.at[expert], w_sem.at[expert, 2 * tiles]))
        weight_copies.append(mine)
    for _, copy in row_copies:
        copy.start()
    for mine in weight_copies:
        for copy in mine:
            copy.start()

    for group in range(groups):
        for where, copy in row_copies:
            if where == group:
                copy.wait()
        chosen = jnp.dot(
            pick_ref[first + group], x_buf[group], preferred_element_type=jnp.float32
        ).astype(jnp.bfloat16)
        xs_buf[0, pl.ds(group * slots, slots)] = chosen[:slots]
        xs_buf[1, pl.ds(group * slots, slots)] = chosen[slots:]

    for expert in range(2):
        for tile in range(tiles):
            weight_copies[expert][2 * tile].wait()
            weight_copies[expert][2 * tile + 1].wait()
            gate = jnp.dot(
                xs_buf[expert], gu_buf[expert, tile, 0], preferred_element_type=jnp.float32
            )
            up = jnp.dot(
                xs_buf[expert], gu_buf[expert, tile, 1], preferred_element_type=jnp.float32
            )
            value = gate / (1.0 + jnp.exp(-gate)) * up
            hid_buf[:, tile * TILE : (tile + 1) * TILE] = value.astype(jnp.bfloat16)
        weight_copies[expert][2 * tiles].wait()
        for column in range(0, width, 2 * TILE):
            served_buf[expert, :, column : column + 2 * TILE] = jnp.dot(
                hid_buf[...],
                dn_buf[expert, :, column : column + 2 * TILE],
                preferred_element_type=jnp.float32,
            ).astype(jnp.bfloat16)

    out_copies = []
    for group in range(groups):
        for column in range(0, width, 2 * TILE):
            total = None
            for expert in range(2):
                placed = jnp.dot(
                    place_ref[expert, first + group],
                    served_buf[expert, pl.ds(group * slots, slots), column : column + 2 * TILE],
                    preferred_element_type=jnp.float32,
                )
                term = placed * share_ref[first + group, :, expert : expert + 1]
                total = term if total is None else total + term
            y_buf[group, :, column : column + 2 * TILE] = total.astype(jnp.bfloat16)
        cut = group_rows // cuts[group]
        for number in range(2 * cuts[group]):
            row, side = divmod(number, 2)
            done = len(out_copies)
            copy = pltpu.make_async_copy(
                y_buf.at[group, pl.ds(row * cut, cut), pl.ds(side * half, half)],
                out_refs[done],
                y_sem.at[done],
            )
            copy.start()
            out_copies.append(copy)
    for copy in out_copies:
        copy.wait()


def run_experts(first, pieces, cuts, pick, place, share, weights):
    group_rows, slots = place.shape[2:]
    groups = len(pieces)
    hidden, width = weights[2].shape
    tiles = hidden // TILE
    spots = [
        (group, row, column) for group, held in enumerate(pieces) for row, column, _ in held
    ]
    arrays = [array for held in pieces for _, _, array in held]
    anywhere = pl.BlockSpec(memory_space=pl.ANY)
    stored = pl.BlockSpec(memory_space=pltpu.HBM)
    inside = pl.BlockSpec(memory_space=pltpu.VMEM)
    outs = pl.pallas_call(
        lambda *refs: expert_kernel(first, spots, cuts, *refs),
        out_shape=[
            jax.ShapeDtypeStruct((group_rows // cut, width // 2), jnp.bfloat16)
            for cut in cuts
            for _ in range(2 * cut)
        ],
        in_specs=[inside] * 3 + [stored] * 4 + [anywhere] * len(arrays),
        out_specs=[anywhere] * (2 * sum(cuts)),
        scratch_shapes=[
            pltpu.VMEM((groups, group_rows, width), jnp.bfloat16),
            pltpu.VMEM((2, groups * slots, width), jnp.bfloat16),
            pltpu.VMEM((2, tiles, 2, width, TILE), jnp.bfloat16),
            pltpu.VMEM((2, hidden, width), jnp.bfloat16),
            pltpu.VMEM((groups * slots, hidden), jnp.bfloat16),
            pltpu.VMEM((2, groups * slots, width), jnp.bfloat16),
            pltpu.VMEM((groups, group_rows, width), jnp.bfloat16),
            pltpu.SemaphoreType.DMA((len(arrays),)),
            pltpu.SemaphoreType.DMA((2, 2 * tiles + 1)),
            pltpu.SemaphoreType.DMA((2 * sum(cuts),)),
        ],
        compiler_params=pltpu.CompilerParams(vmem_limit_bytes=(28 + 6 * group_rows // 256) * 1024 * 1024),
        cost_estimate=pl.CostEstimate(
            flops=12 * groups * slots * width * hidden,
            bytes_accessed=12 * width * hidden + 4 * groups * group_rows * width,
            transcendentals=2 * groups * slots * hidden,
        ),
        name="experts",
    )(pick, place, share, *weights, *arrays)
    return list(zip(outs[0::2], outs[1::2]))


def per_device(
    hidden_in,
    attn_gain,
    w_query,
    w_keyval,
    q_gain,
    k_gain,
    w_out,
    moe_gain,
    expert_ids,
    gate_fixed,
    w_gateup,
    w_down,
):
    tokens = hidden_in[0].astype(jnp.float32)
    row_count, model_width = tokens.shape
    head_dim = q_gain.shape[0]
    local_heads = w_query.shape[1] // head_dim
    kv_heads = w_keyval.shape[2] // head_dim
    group_size = local_heads * lax.axis_size("rep") // kv_heads
    rep_index = lax.axis_index("rep")
    kv_width = kv_heads * head_dim
    top_count = expert_ids.shape[2]
    expert_count = lax.axis_size(EVERY)

    normed, own_payload = prepare(
        hidden_in[0], attn_gain, w_keyval, k_gain, expert_ids[0], gate_fixed[0]
    )
    across_rows = swap(normed, "rep", ACROSS)
    pair_rows = swap(normed, "rep", PAIR)
    line = jnp.concatenate(
        [own_payload] + [swap(own_payload, "seq", bits) for bits in seq_order()[1:]], axis=0
    )
    corner_rows = swap(across_rows, "rep", PAIR)
    line_routes = line[:, 2 * kv_width :]

    def head_kv(rep):
        index = rep * local_heads // group_size * head_dim
        return [
            lax.dynamic_slice_in_dim(line, index, head_dim, 1),
            lax.dynamic_slice_in_dim(line, kv_width + index, head_dim, 1),
        ]

    sent = jnp.concatenate(head_kv(rep_index ^ ACROSS) + [line_routes], axis=1)
    sent, across_rows, pair_rows = ready(sent, across_rows, pair_rows)
    across = swap(sent, "rep", ACROSS)
    half_kv = jnp.concatenate(
        [jnp.concatenate(head_kv(rep_index), axis=1), across[:, : 2 * head_dim]], axis=0
    )
    pair_kv = swap(half_kv, "rep", PAIR)
    both_routes = jnp.stack([line_routes, across[:, 2 * head_dim :]])
    far_routes = swap(both_routes, "role", 1)
    coded = jnp.concatenate([both_routes[1:], far_routes[:1], far_routes[1:], both_routes[:1]])
    queries = make_queries([normed, across_rows, pair_rows, corner_rows], w_query, q_gain)
    kept, leaving = attend(queries, half_kv, pair_kv, w_out, head_dim)
    leaving, own_dn, own_gu = ready(swap(leaving, "rep", PAIR), w_down[0], w_gateup[0])
    halves = kept + leaving
    far_dn, far_gu = swap(own_dn, "rep", PAIR), swap(own_gu, "rep", PAIR)
    far_sum = halves[row_count:].astype(jnp.bfloat16)
    across_sum, coded = ready(swap(far_sum, "rep", ACROSS), coded)
    attended = halves[:row_count] + across_sum.astype(jnp.float32)
    mixed = tokens + attended

    mixed, far_dn, coded = ready(mixed, far_dn, coded)
    moe_in = rms_rows(mixed, moe_gain).astype(jnp.bfloat16)

    rows, coded, far_gu = spread_rows(moe_in, coded, far_gu)
    capacity = max(2, 7 * row_count * top_count // (4 * expert_count))
    slots = -(-capacity * (coded.shape[1] // row_count) // 16) * 16
    pick, place, share = make_tables(coded, lax.axis_index(EVERY), slots, top_count)
    weights = [
        pltpu.with_memory_space_constraint(one, pltpu.HBM)
        for one in (w_gateup[0], far_gu, w_down[0], far_dn)
    ]

    tables = (pick, place, share, weights)
    by_rep, by_role = run_experts(0, rows[:2], (1, 1), *tables)
    rep_low, rep_high, role_low, role_high, *held = ready(
        *by_rep, *by_role, *(array for _, _, array in rows[2])
    )
    by_rep, by_role = (rep_low, rep_high), (role_low, role_high)
    pieces = [(row, column, array) for (row, column, _), array in zip(rows[2], held)]
    *corner, near = run_experts(2, [pieces, rows[3]], (2, 1), *tables)
    routed = collect_rows(near, by_rep, by_role, corner)
    return (mixed + routed).astype(jnp.bfloat16)[None]


def solution(mesh):
    placed = (
        P("role", ("seq", "rep"), None),
        P(),
        P(None, "rep"),
        P(),
        P(),
        P(),
        P("rep", None),
        P(),
        P("role", ("seq", "rep"), None),
        P("role", ("seq", "rep"), None),
        P(("role", "seq", "rep"), None, None),
        P(("role", "seq", "rep"), None, None),
    )
    return jax.shard_map(
        per_device,
        mesh=mesh,
        in_specs=placed,
        out_specs=P("role", ("seq", "rep"), None),
        check_vma=False,
    )
```

```python
import jax
import jax.numpy as jnp
from jax import lax
from jax.experimental import pallas as pl
from jax.experimental.pallas import tpu as pltpu
from jax.sharding import PartitionSpec as P

EVERY = ("role", "seq", "rep")
PAIR = 1
ACROSS = 2
TILE = 256
LANES = 128


def rms_rows(values_in, gain_vec):
    return (
        values_in
        * lax.rsqrt(jnp.mean(values_in * values_in, axis=-1, keepdims=True) + 1e-06)
        * gain_vec
    )


def swap(block, axis, bits):
    size = lax.axis_size(axis)
    return lax.ppermute(block, axis, [(i, i ^ bits) for i in range(size)])


def seq_bits():
    size = lax.axis_size("seq")
    return [1 << place for place in reversed(range(size.bit_length() - 1))]


def seq_order():
    order = [0]
    for bits in seq_bits():
        order = order + [place ^ bits for place in order]
    return order


def ready(*arrays):
    return lax.optimization_barrier(arrays)


def pack_kernel(*refs):
    low_ref, high_ref = refs[-2:]
    count = len(refs) // 2 - 1
    half = low_ref.shape[1]
    start = 0
    for rep_ref, role_ref in zip(refs[:count], refs[count:-2]):
        rows = pl.ds(start, rep_ref.shape[0])
        low_ref[rows] = rep_ref[:, :half]
        high_ref[rows] = role_ref[:, half:]
        start += rep_ref.shape[0]


def pack_corners(by_rep, by_role):
    rows, width = sum(part.shape[0] for part in by_rep), by_rep[0].shape[1]
    half = jax.ShapeDtypeStruct((rows, width // 2), jnp.bfloat16)
    return pl.pallas_call(
        pack_kernel,
        out_shape=[half, half],
        compiler_params=pltpu.CompilerParams(vmem_limit_bytes=(4 + rows // 64) * 1024 * 1024),
        cost_estimate=pl.CostEstimate(
            flops=0, bytes_accessed=4 * rows * width, transcendentals=0
        ),
        name="pack_corners",
    )(*by_rep, *by_role)


def spread_rows(own, weight, coded, tables_of):
    rows, half = own.shape[0], own.shape[1] // 2

    def both_ways(part):
        return swap(part, "rep", ACROSS), swap(part, "role", 1)

    first_bits, *bits_left = seq_bits()
    blocks = [own, swap(own, "seq", first_bits)]
    for bits in bits_left[:-1]:
        blocks = blocks + [swap(block, "seq", bits) for block in blocks]
    beyond = [swap(block, "seq", bits_left[-1]) for block in blocks]
    middle = jnp.concatenate(blocks[1:] + beyond[:-1], axis=0)
    middle, weight, coded, *outer = ready(middle, weight, coded, *both_ways(own))
    last, *tables = ready(beyond[-1], *tables_of(coded))
    by_rep, by_role = zip(outer, both_ways(middle), both_ways(last))
    low, high = pack_corners(by_rep, by_role)
    corner_low, corner_high = swap(low, "role", 1), swap(high, "rep", ACROSS)
    starts = (0, rows, rows + middle.shape[0])
    groups = [
        [(start, 0, part) for start, part in zip(starts, parts)]
        for parts in (by_rep, by_role, (own, middle, last))
    ]
    groups.insert(2, [(0, 0, corner_low), (0, half, corner_high)])
    return groups, weight, tables


def added(first, second):
    return (first.astype(jnp.float32) + second.astype(jnp.float32)).astype(jnp.bfloat16)


def collect_rows(near, by_rep, by_role, corner):
    straight_low = swap(by_role[0], "role", 1)
    straight_high = swap(by_rep[1], "rep", ACROSS)
    straight_low, straight_high, near_low, near_high, *corner = ready(
        straight_low, straight_high, *near, *corner[0], *corner[1]
    )
    cut = near_low.shape[0] // 2
    halves = slice(0, cut), slice(cut, None)

    def merged(rows, turned_low, turned_high):
        return jnp.concatenate(
            [
                base[rows].astype(jnp.float32)
                + first[rows].astype(jnp.float32)
                + second.astype(jnp.float32)
                for base, first, second in (
                    (near_low, straight_low, turned_low),
                    (near_high, straight_high, turned_high),
                )
            ],
            axis=1,
        )

    def corners(number):
        low, high = corner[2 * number : 2 * number + 2]
        return swap(low, "role", 1), swap(high, "rep", ACROSS)

    def sums(number, corner_low, corner_high):
        rows = halves[number]
        return added(by_rep[0][rows], corner_low), added(by_role[1][rows], corner_high)

    def turned(low, high):
        return swap(low, "rep", ACROSS), swap(high, "role", 1)

    far_corner, beside_corner = corners(1), corners(0)
    *far, corner_low, corner_high = ready(*turned(*sums(1, *far_corner)), *beside_corner)
    leaving = merged(halves[1], *far).astype(jnp.bfloat16)
    *near_sums, leaving = ready(*sums(0, corner_low, corner_high), leaving)
    beside = turned(*near_sums)
    total = merged(halves[0], *beside)
    *later_bits, last_bits = reversed(seq_bits())
    for bits in later_bits:
        cut = total.shape[0] // 2
        far, near = ready(swap(leaving[cut:], "seq", bits), leaving[:cut])
        leaving = (total[cut:] + far.astype(jnp.float32)).astype(jnp.bfloat16)
        total = total[:cut] + swap(near, "seq", bits).astype(jnp.float32)
    return total + swap(leaving, "seq", last_bits).astype(jnp.float32)


def prepare_kernel(*refs):
    tokens_in, gain_in, kv_in, k_gain_in, ids_in, gates_in, normed_ref, out_ref = refs[:8]
    held, sem = refs[8:14], refs[14]
    sources = (tokens_in, gain_in, kv_in, k_gain_in, ids_in, gates_in)
    copies = [
        pltpu.make_async_copy(src, dst, sem.at[number])
        for number, (src, dst) in enumerate(zip(sources, held))
    ]
    for copy in copies:
        copy.start()
    for copy in copies:
        copy.wait()
    tokens_ref, gain_ref, kv_ref, k_gain_ref, ids_ref, gates_ref = held
    normed = rms_rows(tokens_ref[...].astype(jnp.float32), gain_ref[...]).astype(jnp.bfloat16)
    normed_ref[...] = normed
    kv_width, head_dim = kv_ref.shape[2], k_gain_ref.shape[1]
    keys = jnp.dot(normed, kv_ref[0], preferred_element_type=jnp.float32)
    for start in range(0, kv_width, head_dim):
        head = rms_rows(keys[:, start : start + head_dim], k_gain_ref[...])
        out_ref[:, start : start + head_dim] = head.astype(jnp.bfloat16)
    values = jnp.dot(normed, kv_ref[1], preferred_element_type=jnp.float32)
    out_ref[:, kv_width : 2 * kv_width] = values.astype(jnp.bfloat16)
    coded = jnp.concatenate([ids_ref[...], gates_ref[...] // 64, gates_ref[...] % 64], axis=0)
    count = coded.shape[0]
    spread = lax.broadcasted_iota(jnp.int32, (count, LANES), 0)
    spread = spread == lax.broadcasted_iota(jnp.int32, (count, LANES), 1)
    out_ref[:, 2 * kv_width :] = lax.dot_general(
        coded.astype(jnp.float32).astype(jnp.bfloat16),
        spread.astype(jnp.float32).astype(jnp.bfloat16),
        (((0,), (0,)), ((), ())),
        preferred_element_type=jnp.float32,
    ).astype(jnp.bfloat16)


def prepare(tokens, attn_gain, w_keyval, k_gain, ids, gates):
    rows, width = tokens.shape
    operands = [
        pltpu.with_memory_space_constraint(one, pltpu.HBM)
        for one in (tokens, attn_gain[None], w_keyval, k_gain[None], ids.T, gates.T)
    ]
    return pl.pallas_call(
        prepare_kernel,
        out_shape=[
            jax.ShapeDtypeStruct((rows, width), jnp.bfloat16),
            jax.ShapeDtypeStruct((rows, 2 * w_keyval.shape[2] + LANES), jnp.bfloat16),
        ],
        in_specs=[pl.BlockSpec(memory_space=pltpu.HBM)] * len(operands),
        scratch_shapes=[pltpu.VMEM(one.shape, one.dtype) for one in operands]
        + [pltpu.SemaphoreType.DMA((len(operands),))],
        compiler_params=pltpu.CompilerParams(vmem_limit_bytes=8 * 1024 * 1024),
        cost_estimate=pl.CostEstimate(
            flops=4 * rows * width * w_keyval.shape[2],
            bytes_accessed=4 * width * w_keyval.shape[2] + 4 * rows * width,
            transcendentals=rows,
        ),
        name="prepare",
    )(*operands)


def queries_kernel(first_ref, second_ref, third_ref, fourth_ref, weight_ref, gain_ref, out_ref):
    rows, head_dim = first_ref.shape[0], gain_ref.shape[1]
    refs = (first_ref, second_ref, third_ref, fourth_ref)
    held = jnp.concatenate([ref[...] for ref in refs], axis=0)
    raw = jnp.dot(held, weight_ref[...], preferred_element_type=jnp.float32)
    for start in range(0, weight_ref.shape[1], head_dim):
        head = rms_rows(raw[:, start : start + head_dim], gain_ref[...])
        out_ref[:, start : start + head_dim] = head.astype(jnp.bfloat16)


def make_queries(blocks, w_query, q_gain):
    rows, width = len(blocks) * blocks[0].shape[0], w_query.shape[1]
    return pl.pallas_call(
        queries_kernel,
        out_shape=jax.ShapeDtypeStruct((rows, width), jnp.bfloat16),
        compiler_params=pltpu.CompilerParams(vmem_limit_bytes=8 * 1024 * 1024),
        cost_estimate=pl.CostEstimate(
            flops=2 * rows * width * w_query.shape[0],
            bytes_accessed=2 * width * w_query.shape[0],
            transcendentals=rows,
        ),
        name="queries",
    )(*blocks, w_query, q_gain[None])


def attend_kernel(head_dim, query_ref, near_ref, far_ref, weight_ref, kept_ref, leaving_ref, held_ref):
    keys = [ref[:, :head_dim] for ref in (near_ref, far_ref)]
    values = [ref[:, head_dim:] for ref in (near_ref, far_ref)]
    for start in range(0, query_ref.shape[1], head_dim):
        query = query_ref[:, start : start + head_dim]
        scores = [
            lax.dot_general(
                query, key, (((1,), (1,)), ((), ())), preferred_element_type=jnp.float32
            )
            * head_dim ** (-0.5)
            for key in keys
        ]
        row_max = jnp.maximum(
            jnp.max(scores[0], axis=1, keepdims=True), jnp.max(scores[1], axis=1, keepdims=True)
        )
        denom, total = 0.0, 0.0
        for score, value in zip(scores, values):
            weights = jnp.exp(score - row_max)
            denom = denom + jnp.sum(weights, axis=1, keepdims=True)
            total = total + jnp.dot(
                weights.astype(jnp.bfloat16), value, preferred_element_type=jnp.float32
            )
        held_ref[:, start : start + head_dim] = (total / denom).astype(jnp.bfloat16)
    cut = kept_ref.shape[0]
    for column in range(0, weight_ref.shape[1], 2 * TILE):
        columns = slice(column, column + 2 * TILE)
        partial = jnp.dot(held_ref[...], weight_ref[:, columns], preferred_element_type=jnp.float32)
        kept_ref[:, columns] = partial[:cut]
        leaving_ref[:, columns] = partial[cut:]


def attend(queries, near_kv, far_kv, w_out, head_dim):
    rows, width = queries.shape
    keys = 2 * near_kv.shape[0]
    half = jax.ShapeDtypeStruct((rows // 2, w_out.shape[1]), jnp.float32)
    return pl.pallas_call(
        lambda *refs: attend_kernel(head_dim, *refs),
        out_shape=[half, half],
        scratch_shapes=[pltpu.VMEM((rows, width), jnp.bfloat16)],
        compiler_params=pltpu.CompilerParams(vmem_limit_bytes=12 * 1024 * 1024),
        cost_estimate=pl.CostEstimate(
            flops=4 * rows * width * keys + 2 * rows * width * w_out.shape[1],
            bytes_accessed=2 * width * w_out.shape[1] + 4 * rows * w_out.shape[1],
            transcendentals=rows * keys * width // head_dim,
        ),
        name="attend",
    )(queries, near_kv, far_kv, w_out)


def tables_kernel(top_count, expert_ref, coded_ref, pick_ref, place_ref, share_ref):
    groups, rows, lanes = coded_ref.shape
    slots = place_ref.shape[3]
    lane = lax.broadcasted_iota(jnp.int32, (rows, lanes), 1)
    source = lax.broadcasted_iota(jnp.int32, (lanes, lanes), 0)
    target = lax.broadcasted_iota(jnp.int32, (lanes, lanes), 1)
    joined = jnp.where(source == target + top_count, 64.0, 0.0)
    joined = joined + jnp.where(source == target + 2 * top_count, 1.0, 0.0)
    joined = jnp.where(target < top_count, joined, 0.0).astype(jnp.bfloat16)
    first = lax.broadcasted_iota(jnp.int32, (rows, rows), 0)
    second = lax.broadcasted_iota(jnp.int32, (rows, rows), 1)
    later = jnp.where(first < second, 1.0, 0.0).astype(jnp.bfloat16)
    earlier = jnp.where(second < first, 1.0, 0.0).astype(jnp.bfloat16)
    ones = jnp.ones((8, lanes), jnp.bfloat16)
    slot_row = lax.broadcasted_iota(jnp.int32, (slots, rows), 0).astype(jnp.float32)
    slot_lane = lax.broadcasted_iota(jnp.int32, (rows, slots), 1).astype(jnp.float32)
    for group in range(groups):
        coded = coded_ref[group]
        gates = jnp.dot(coded, joined, preferred_element_type=jnp.float32)
        gate_sum = jnp.sum(gates, axis=1, keepdims=True)
        named = coded.astype(jnp.float32).astype(jnp.int32)
        for number in range(2):
            expert = expert_ref[0] ^ (number * PAIR)
            hits = jnp.where((named == expert) & (lane < top_count), 1.0, 0.0)
            share_ref[group, :, number : number + 1] = (
                jnp.sum(hits * gates, axis=1, keepdims=True) / gate_sum
            )
            hit = jnp.sum(hits, axis=1, keepdims=True)
            held = jnp.broadcast_to(hit, (rows, lanes)).astype(jnp.bfloat16)
            rank = jnp.dot(earlier, held, preferred_element_type=jnp.float32)[:, :1]
            rank = jnp.where(hit > 0.0, rank, -1.0)
            place_ref[number, group] = jnp.where(rank == slot_lane, 1.0, 0.0).astype(jnp.bfloat16)
            hit_row = lax.dot_general(
                ones,
                hits.astype(jnp.bfloat16),
                (((1,), (1,)), ((), ())),
                preferred_element_type=jnp.float32,
            )
            rank_row = jnp.dot(
                hit_row.astype(jnp.bfloat16), later, preferred_element_type=jnp.float32
            )
            rank_row = jnp.where(hit_row > 0.0, rank_row, -1.0)[:1]
            pick_ref[group, number * slots : (number + 1) * slots] = jnp.where(
                rank_row == slot_row, 1.0, 0.0
            ).astype(jnp.bfloat16)


def make_tables(coded, expert, slots, top_count):
    groups, rows, lanes = coded.shape
    return pl.pallas_call(
        lambda *refs: tables_kernel(top_count, *refs),
        out_shape=[
            jax.ShapeDtypeStruct((groups, 2 * slots, rows), jnp.bfloat16),
            jax.ShapeDtypeStruct((2, groups, rows, slots), jnp.bfloat16),
            jax.ShapeDtypeStruct((groups, rows, 2), jnp.float32),
        ],
        in_specs=[
            pl.BlockSpec(memory_space=pltpu.SMEM),
            pl.BlockSpec(memory_space=pltpu.VMEM),
        ],
        compiler_params=pltpu.CompilerParams(vmem_limit_bytes=24 * 1024 * 1024),
        cost_estimate=pl.CostEstimate(
            flops=4 * groups * rows * rows * lanes,
            bytes_accessed=8 * groups * rows * slots,
            transcendentals=0,
        ),
        name="tables",
    )(expert.astype(jnp.int32)[None], coded)


def expert_kernel(first, spots, cuts, *refs):
    pick_ref, place_ref, share_ref, own_gu_ref, far_gu_ref, own_dn_ref, far_dn_ref = refs[:7]
    group_rows, slots = place_ref.shape[2:]
    groups = len(cuts)
    piece_refs = refs[7 : 7 + len(spots)]
    out_refs = refs[7 + len(spots) : 7 + len(spots) + 2 * sum(cuts)]
    x_buf, xs_buf, gu_buf, dn_buf, hid_buf, served_buf, y_buf, x_sem, w_sem, y_sem = refs[
        7 + len(spots) + len(out_refs) :
    ]
    width = x_buf.shape[2]
    half = width // 2
    hidden = own_dn_ref.shape[0]
    tiles = hidden // TILE

    row_copies = []
    for number, ((group, row, column), piece) in enumerate(zip(spots, piece_refs)):
        rows, columns = piece.shape
        target = x_buf.at[group, pl.ds(row, rows), pl.ds(column, columns)]
        row_copies.append((group, pltpu.make_async_copy(piece, target, x_sem.at[number])))
    weight_copies = []
    for expert, (gu_ref, dn_ref) in enumerate(((own_gu_ref, own_dn_ref), (far_gu_ref, far_dn_ref))):
        mine = []
        for tile in range(tiles):
            for side in range(2):
                mine.append(
                    pltpu.make_async_copy(
                        gu_ref.at[:, pl.ds(side * hidden + tile * TILE, TILE)],
                        gu_buf.at[expert, tile, side],
                        w_sem.at[expert, 2 * tile + side],
                    )
                )
        mine.append(pltpu.make_async_copy(dn_ref, dn_buf.at[expert], w_sem.at[expert, 2 * tiles]))
        weight_copies.append(mine)
    for _, copy in row_copies:
        copy.start()
    for mine in weight_copies:
        for copy in mine:
            copy.start()

    for group in range(groups):
        for where, copy in row_copies:
            if where == group:
                copy.wait()
        chosen = jnp.dot(
            pick_ref[first + group], x_buf[group], preferred_element_type=jnp.float32
        ).astype(jnp.bfloat16)
        xs_buf[0, pl.ds(group * slots, slots)] = chosen[:slots]
        xs_buf[1, pl.ds(group * slots, slots)] = chosen[slots:]

    for expert in range(2):
        for tile in range(tiles):
            weight_copies[expert][2 * tile].wait()
            weight_copies[expert][2 * tile + 1].wait()
            gate = jnp.dot(
                xs_buf[expert], gu_buf[expert, tile, 0], preferred_element_type=jnp.float32
            )
            up = jnp.dot(
                xs_buf[expert], gu_buf[expert, tile, 1], preferred_element_type=jnp.float32
            )
            value = gate / (1.0 + jnp.exp(-gate)) * up
            hid_buf[:, tile * TILE : (tile + 1) * TILE] = value.astype(jnp.bfloat16)
        weight_copies[expert][2 * tiles].wait()
        for column in range(0, width, 2 * TILE):
            served_buf[expert, :, column : column + 2 * TILE] = jnp.dot(
                hid_buf[...],
                dn_buf[expert, :, column : column + 2 * TILE],
                preferred_element_type=jnp.float32,
            ).astype(jnp.bfloat16)

    out_copies = []
    for group in range(groups):
        for column in range(0, width, 2 * TILE):
            total = None
            for expert in range(2):
                placed = jnp.dot(
                    place_ref[expert, first + group],
                    served_buf[expert, pl.ds(group * slots, slots), column : column + 2 * TILE],
                    preferred_element_type=jnp.float32,
                )
                term = placed * share_ref[first + group, :, expert : expert + 1]
                total = term if total is None else total + term
            y_buf[group, :, column : column + 2 * TILE] = total.astype(jnp.bfloat16)
        cut = group_rows // cuts[group]
        for number in range(2 * cuts[group]):
            row, side = divmod(number, 2)
            done = len(out_copies)
            copy = pltpu.make_async_copy(
                y_buf.at[group, pl.ds(row * cut, cut), pl.ds(side * half, half)],
                out_refs[done],
                y_sem.at[done],
            )
            copy.start()
            out_copies.append(copy)
    for copy in out_copies:
        copy.wait()


def run_experts(first, pieces, cuts, pick, place, share, weights):
    group_rows, slots = place.shape[2:]
    groups = len(pieces)
    hidden, width = weights[2].shape
    tiles = hidden // TILE
    spots = [
        (group, row, column) for group, held in enumerate(pieces) for row, column, _ in held
    ]
    arrays = [array for held in pieces for _, _, array in held]
    anywhere = pl.BlockSpec(memory_space=pl.ANY)
    stored = pl.BlockSpec(memory_space=pltpu.HBM)
    inside = pl.BlockSpec(memory_space=pltpu.VMEM)
    outs = pl.pallas_call(
        lambda *refs: expert_kernel(first, spots, cuts, *refs),
        out_shape=[
            jax.ShapeDtypeStruct((group_rows // cut, width // 2), jnp.bfloat16)
            for cut in cuts
            for _ in range(2 * cut)
        ],
        in_specs=[inside] * 3 + [stored] * 4 + [anywhere] * len(arrays),
        out_specs=[anywhere] * (2 * sum(cuts)),
        scratch_shapes=[
            pltpu.VMEM((groups, group_rows, width), jnp.bfloat16),
            pltpu.VMEM((2, groups * slots, width), jnp.bfloat16),
            pltpu.VMEM((2, tiles, 2, width, TILE), jnp.bfloat16),
            pltpu.VMEM((2, hidden, width), jnp.bfloat16),
            pltpu.VMEM((groups * slots, hidden), jnp.bfloat16),
            pltpu.VMEM((2, groups * slots, width), jnp.bfloat16),
            pltpu.VMEM((groups, group_rows, width), jnp.bfloat16),
            pltpu.SemaphoreType.DMA((len(arrays),)),
            pltpu.SemaphoreType.DMA((2, 2 * tiles + 1)),
            pltpu.SemaphoreType.DMA((2 * sum(cuts),)),
        ],
        compiler_params=pltpu.CompilerParams(vmem_limit_bytes=(28 + 6 * group_rows // 256) * 1024 * 1024),
        cost_estimate=pl.CostEstimate(
            flops=12 * groups * slots * width * hidden,
            bytes_accessed=12 * width * hidden + 4 * groups * group_rows * width,
            transcendentals=2 * groups * slots * hidden,
        ),
        name="experts",
    )(pick, place, share, *weights, *arrays)
    return list(zip(outs[0::2], outs[1::2]))


def per_device(
    hidden_in,
    attn_gain,
    w_query,
    w_keyval,
    q_gain,
    k_gain,
    w_out,
    moe_gain,
    expert_ids,
    gate_fixed,
    w_gateup,
    w_down,
):
    tokens = hidden_in[0].astype(jnp.float32)
    row_count, model_width = tokens.shape
    head_dim = q_gain.shape[0]
    local_heads = w_query.shape[1] // head_dim
    kv_heads = w_keyval.shape[2] // head_dim
    group_size = local_heads * lax.axis_size("rep") // kv_heads
    rep_index = lax.axis_index("rep")
    kv_width = kv_heads * head_dim
    top_count = expert_ids.shape[2]
    expert_count = lax.axis_size(EVERY)

    normed, own_payload = prepare(
        hidden_in[0], attn_gain, w_keyval, k_gain, expert_ids[0], gate_fixed[0]
    )
    across_rows = swap(normed, "rep", ACROSS)
    pair_rows = swap(normed, "rep", PAIR)
    line = jnp.concatenate(
        [own_payload] + [swap(own_payload, "seq", bits) for bits in seq_order()[1:]], axis=0
    )
    corner_rows = swap(across_rows, "rep", PAIR)
    line_routes = line[:, 2 * kv_width :]

    def head_kv(rep):
        index = rep * local_heads // group_size * head_dim
        return [
            lax.dynamic_slice_in_dim(line, index, head_dim, 1),
            lax.dynamic_slice_in_dim(line, kv_width + index, head_dim, 1),
        ]

    sent = jnp.concatenate(head_kv(rep_index ^ ACROSS) + [line_routes], axis=1)
    sent, across_rows, pair_rows = ready(sent, across_rows, pair_rows)
    across = swap(sent, "rep", ACROSS)
    half_kv = jnp.concatenate(
        [jnp.concatenate(head_kv(rep_index), axis=1), across[:, : 2 * head_dim]], axis=0
    )
    pair_kv = swap(half_kv, "rep", PAIR)
    both_routes = jnp.stack([line_routes, across[:, 2 * head_dim :]])
    far_routes = swap(both_routes, "role", 1)
    coded = jnp.concatenate([both_routes[1:], far_routes[:1], far_routes[1:], both_routes[:1]])
    queries = make_queries([normed, across_rows, pair_rows, corner_rows], w_query, q_gain)
    kept, leaving = attend(queries, half_kv, pair_kv, w_out, head_dim)
    leaving, own_dn = ready(swap(leaving, "rep", PAIR), w_down[0])
    halves = kept + leaving
    far_dn = swap(own_dn, "rep", PAIR)
    far_sum = halves[row_count:].astype(jnp.bfloat16)
    across_sum, coded, far_dn, own_gu = ready(
        swap(far_sum, "rep", ACROSS), coded, far_dn, w_gateup[0]
    )
    far_gu = swap(own_gu, "rep", PAIR)
    attended = halves[:row_count] + across_sum.astype(jnp.float32)
    mixed = tokens + attended

    moe_in = rms_rows(mixed, moe_gain).astype(jnp.bfloat16)

    capacity = max(2, 7 * row_count * top_count // (4 * expert_count))
    slots = -(-capacity * (coded.shape[1] // row_count) // 16) * 16
    rows, far_gu, tables = spread_rows(
        moe_in,
        far_gu,
        coded,
        lambda codes: make_tables(codes, lax.axis_index(EVERY), slots, top_count),
    )
    weights = [
        pltpu.with_memory_space_constraint(one, pltpu.HBM)
        for one in (w_gateup[0], far_gu, w_down[0], far_dn)
    ]

    tables = (*tables, weights)
    by_rep, by_role = run_experts(0, rows[:2], (1, 1), *tables)
    rep_low, rep_high, role_low, role_high, *held = ready(
        *by_rep, *by_role, *(array for _, _, array in rows[2])
    )
    by_rep, by_role = (rep_low, rep_high), (role_low, role_high)
    pieces = [(row, column, array) for (row, column, _), array in zip(rows[2], held)]
    *corner, near = run_experts(2, [pieces, rows[3]], (2, 1), *tables)
    routed = collect_rows(near, by_rep, by_role, corner)
    return (mixed + routed).astype(jnp.bfloat16)[None]


def solution(mesh):
    placed = (
        P("role", ("seq", "rep"), None),
        P(),
        P(None, "rep"),
        P(),
        P(),
        P(),
        P("rep", None),
        P(),
        P("role", ("seq", "rep"), None),
        P("role", ("seq", "rep"), None),
        P(("role", "seq", "rep"), None, None),
        P(("role", "seq", "rep"), None, None),
    )
    return jax.shard_map(
        per_device,
        mesh=mesh,
        in_specs=placed,
        out_specs=P("role", ("seq", "rep"), None),
        check_vma=False,
    )
```

```python
import jax
import jax.numpy as jnp
from jax import lax
from jax.experimental import pallas as pl
from jax.experimental.pallas import tpu as pltpu
from jax.sharding import PartitionSpec as P

EVERY = ("role", "seq", "rep")
PAIR = 1
ACROSS = 2
TILE = 256
LANES = 128


def rms_rows(values_in, gain_vec):
    return (
        values_in
        * lax.rsqrt(jnp.mean(values_in * values_in, axis=-1, keepdims=True) + 1e-06)
        * gain_vec
    )


def swap(block, axis, bits):
    size = lax.axis_size(axis)
    return lax.ppermute(block, axis, [(i, i ^ bits) for i in range(size)])


def seq_bits():
    size = lax.axis_size("seq")
    return [1 << place for place in reversed(range(size.bit_length() - 1))]


def seq_order():
    order = [0]
    for bits in seq_bits():
        order = order + [place ^ bits for place in order]
    return order


def ready(*arrays):
    return lax.optimization_barrier(arrays)


def pack_kernel(*refs):
    low_ref, high_ref = refs[-2:]
    count = len(refs) // 2 - 1
    half = low_ref.shape[1]
    start = 0
    for rep_ref, role_ref in zip(refs[:count], refs[count:-2]):
        rows = pl.ds(start, rep_ref.shape[0])
        low_ref[rows] = rep_ref[:, :half]
        high_ref[rows] = role_ref[:, half:]
        start += rep_ref.shape[0]


def pack_corners(by_rep, by_role):
    rows, width = sum(part.shape[0] for part in by_rep), by_rep[0].shape[1]
    half = jax.ShapeDtypeStruct((rows, width // 2), jnp.bfloat16)
    return pl.pallas_call(
        pack_kernel,
        out_shape=[half, half],
        compiler_params=pltpu.CompilerParams(vmem_limit_bytes=(4 + rows // 64) * 1024 * 1024),
        cost_estimate=pl.CostEstimate(
            flops=0, bytes_accessed=4 * rows * width, transcendentals=0
        ),
        name="pack_corners",
    )(*by_rep, *by_role)


def spread_rows(own, coded, tables_of):
    rows, half = own.shape[0], own.shape[1] // 2

    def both_ways(part):
        return swap(part, "rep", ACROSS), swap(part, "role", 1)

    first_bits, *bits_left = seq_bits()
    blocks = [own, swap(own, "seq", first_bits)]
    for bits in bits_left[:-1]:
        blocks = blocks + [swap(block, "seq", bits) for block in blocks]
    beyond = [swap(block, "seq", bits_left[-1]) for block in blocks]
    middle = jnp.concatenate(blocks[1:] + beyond[:-1], axis=0)
    middle, coded, *outer = ready(middle, coded, *both_ways(own))
    last, *tables = ready(beyond[-1], *tables_of(coded))
    by_rep, by_role = zip(outer, both_ways(middle), both_ways(last))
    low, high = pack_corners(by_rep, by_role)
    corner_low, corner_high = swap(low, "role", 1), swap(high, "rep", ACROSS)
    starts = (0, rows, rows + middle.shape[0])
    groups = [
        [(start, 0, part) for start, part in zip(starts, parts)]
        for parts in (by_rep, by_role, (own, middle, last))
    ]
    groups.insert(2, [(0, 0, corner_low), (0, half, corner_high)])
    return groups, tables


def added(first, second):
    return (first.astype(jnp.float32) + second.astype(jnp.float32)).astype(jnp.bfloat16)


def collect_rows(near, by_rep, by_role, corner):
    straight_low = swap(by_role[0], "role", 1)
    straight_high = swap(by_rep[1], "rep", ACROSS)
    straight_low, straight_high, near_low, near_high, *corner = ready(
        straight_low, straight_high, *near, *corner[0], *corner[1]
    )
    cut = near_low.shape[0] // 2
    halves = slice(0, cut), slice(cut, None)

    def merged(rows, turned_low, turned_high):
        return jnp.concatenate(
            [
                base[rows].astype(jnp.float32)
                + first[rows].astype(jnp.float32)
                + second.astype(jnp.float32)
                for base, first, second in (
                    (near_low, straight_low, turned_low),
                    (near_high, straight_high, turned_high),
                )
            ],
            axis=1,
        )

    def corners(number):
        low, high = corner[2 * number : 2 * number + 2]
        return swap(low, "role", 1), swap(high, "rep", ACROSS)

    def sums(number, corner_low, corner_high):
        rows = halves[number]
        return added(by_rep[0][rows], corner_low), added(by_role[1][rows], corner_high)

    def turned(low, high):
        return swap(low, "rep", ACROSS), swap(high, "role", 1)

    far_corner, beside_corner = corners(1), corners(0)
    *far, corner_low, corner_high = ready(*turned(*sums(1, *far_corner)), *beside_corner)
    leaving = merged(halves[1], *far).astype(jnp.bfloat16)
    *near_sums, leaving = ready(*sums(0, corner_low, corner_high), leaving)
    beside = turned(*near_sums)
    total = merged(halves[0], *beside)
    *later_bits, last_bits = reversed(seq_bits())
    for bits in later_bits:
        cut = total.shape[0] // 2
        far, near = ready(swap(leaving[cut:], "seq", bits), leaving[:cut])
        leaving = (total[cut:] + far.astype(jnp.float32)).astype(jnp.bfloat16)
        total = total[:cut] + swap(near, "seq", bits).astype(jnp.float32)
    return total + swap(leaving, "seq", last_bits).astype(jnp.float32)


def prepare_kernel(*refs):
    tokens_in, gain_in, kv_in, k_gain_in, ids_in, gates_in, normed_ref, out_ref = refs[:8]
    held, sem = refs[8:14], refs[14]
    sources = (tokens_in, gain_in, kv_in, k_gain_in, ids_in, gates_in)
    copies = [
        pltpu.make_async_copy(src, dst, sem.at[number])
        for number, (src, dst) in enumerate(zip(sources, held))
    ]
    for copy in copies:
        copy.start()
    for copy in copies:
        copy.wait()
    tokens_ref, gain_ref, kv_ref, k_gain_ref, ids_ref, gates_ref = held
    normed = rms_rows(tokens_ref[...].astype(jnp.float32), gain_ref[...]).astype(jnp.bfloat16)
    normed_ref[...] = normed
    kv_width, head_dim = kv_ref.shape[2], k_gain_ref.shape[1]
    keys = jnp.dot(normed, kv_ref[0], preferred_element_type=jnp.float32)
    for start in range(0, kv_width, head_dim):
        head = rms_rows(keys[:, start : start + head_dim], k_gain_ref[...])
        out_ref[:, start : start + head_dim] = head.astype(jnp.bfloat16)
    values = jnp.dot(normed, kv_ref[1], preferred_element_type=jnp.float32)
    out_ref[:, kv_width : 2 * kv_width] = values.astype(jnp.bfloat16)
    coded = jnp.concatenate([ids_ref[...], gates_ref[...] // 64, gates_ref[...] % 64], axis=0)
    count = coded.shape[0]
    spread = lax.broadcasted_iota(jnp.int32, (count, LANES), 0)
    spread = spread == lax.broadcasted_iota(jnp.int32, (count, LANES), 1)
    out_ref[:, 2 * kv_width :] = lax.dot_general(
        coded.astype(jnp.float32).astype(jnp.bfloat16),
        spread.astype(jnp.float32).astype(jnp.bfloat16),
        (((0,), (0,)), ((), ())),
        preferred_element_type=jnp.float32,
    ).astype(jnp.bfloat16)


def prepare(tokens, attn_gain, w_keyval, k_gain, ids, gates):
    rows, width = tokens.shape
    operands = [
        pltpu.with_memory_space_constraint(one, pltpu.HBM)
        for one in (tokens, attn_gain[None], w_keyval, k_gain[None], ids.T, gates.T)
    ]
    return pl.pallas_call(
        prepare_kernel,
        out_shape=[
            jax.ShapeDtypeStruct((rows, width), jnp.bfloat16),
            jax.ShapeDtypeStruct((rows, 2 * w_keyval.shape[2] + LANES), jnp.bfloat16),
        ],
        in_specs=[pl.BlockSpec(memory_space=pltpu.HBM)] * len(operands),
        scratch_shapes=[pltpu.VMEM(one.shape, one.dtype) for one in operands]
        + [pltpu.SemaphoreType.DMA((len(operands),))],
        compiler_params=pltpu.CompilerParams(vmem_limit_bytes=8 * 1024 * 1024),
        cost_estimate=pl.CostEstimate(
            flops=4 * rows * width * w_keyval.shape[2],
            bytes_accessed=4 * width * w_keyval.shape[2] + 4 * rows * width,
            transcendentals=rows,
        ),
        name="prepare",
    )(*operands)


def queries_kernel(first_ref, second_ref, third_ref, fourth_ref, weight_ref, gain_ref, out_ref):
    rows, head_dim = first_ref.shape[0], gain_ref.shape[1]
    refs = (first_ref, second_ref, third_ref, fourth_ref)
    held = jnp.concatenate([ref[...] for ref in refs], axis=0)
    raw = jnp.dot(held, weight_ref[...], preferred_element_type=jnp.float32)
    for start in range(0, weight_ref.shape[1], head_dim):
        head = rms_rows(raw[:, start : start + head_dim], gain_ref[...])
        out_ref[:, start : start + head_dim] = head.astype(jnp.bfloat16)


def make_queries(blocks, w_query, q_gain):
    rows, width = len(blocks) * blocks[0].shape[0], w_query.shape[1]
    return pl.pallas_call(
        queries_kernel,
        out_shape=jax.ShapeDtypeStruct((rows, width), jnp.bfloat16),
        compiler_params=pltpu.CompilerParams(vmem_limit_bytes=8 * 1024 * 1024),
        cost_estimate=pl.CostEstimate(
            flops=2 * rows * width * w_query.shape[0],
            bytes_accessed=2 * width * w_query.shape[0],
            transcendentals=rows,
        ),
        name="queries",
    )(*blocks, w_query, q_gain[None])


def attend_kernel(head_dim, query_ref, near_ref, far_ref, weight_ref, kept_ref, leaving_ref, held_ref):
    keys = [ref[:, :head_dim] for ref in (near_ref, far_ref)]
    values = [ref[:, head_dim:] for ref in (near_ref, far_ref)]
    for start in range(0, query_ref.shape[1], head_dim):
        query = query_ref[:, start : start + head_dim]
        scores = [
            lax.dot_general(
                query, key, (((1,), (1,)), ((), ())), preferred_element_type=jnp.float32
            )
            * head_dim ** (-0.5)
            for key in keys
        ]
        row_max = jnp.maximum(
            jnp.max(scores[0], axis=1, keepdims=True), jnp.max(scores[1], axis=1, keepdims=True)
        )
        denom, total = 0.0, 0.0
        for score, value in zip(scores, values):
            weights = jnp.exp(score - row_max)
            denom = denom + jnp.sum(weights, axis=1, keepdims=True)
            total = total + jnp.dot(
                weights.astype(jnp.bfloat16), value, preferred_element_type=jnp.float32
            )
        held_ref[:, start : start + head_dim] = (total / denom).astype(jnp.bfloat16)
    cut = kept_ref.shape[0]
    for column in range(0, weight_ref.shape[1], 2 * TILE):
        columns = slice(column, column + 2 * TILE)
        partial = jnp.dot(held_ref[...], weight_ref[:, columns], preferred_element_type=jnp.float32)
        kept_ref[:, columns] = partial[:cut]
        leaving_ref[:, columns] = partial[cut:]


def attend(queries, near_kv, far_kv, w_out, head_dim):
    rows, width = queries.shape
    keys = 2 * near_kv.shape[0]
    half = jax.ShapeDtypeStruct((rows // 2, w_out.shape[1]), jnp.float32)
    return pl.pallas_call(
        lambda *refs: attend_kernel(head_dim, *refs),
        out_shape=[half, half],
        scratch_shapes=[pltpu.VMEM((rows, width), jnp.bfloat16)],
        compiler_params=pltpu.CompilerParams(vmem_limit_bytes=12 * 1024 * 1024),
        cost_estimate=pl.CostEstimate(
            flops=4 * rows * width * keys + 2 * rows * width * w_out.shape[1],
            bytes_accessed=2 * width * w_out.shape[1] + 4 * rows * w_out.shape[1],
            transcendentals=rows * keys * width // head_dim,
        ),
        name="attend",
    )(queries, near_kv, far_kv, w_out)


def tables_kernel(top_count, expert_ref, coded_ref, pick_ref, place_ref, share_ref):
    groups, rows, lanes = coded_ref.shape
    slots = place_ref.shape[3]
    lane = lax.broadcasted_iota(jnp.int32, (rows, lanes), 1)
    source = lax.broadcasted_iota(jnp.int32, (lanes, lanes), 0)
    target = lax.broadcasted_iota(jnp.int32, (lanes, lanes), 1)
    joined = jnp.where(source == target + top_count, 64.0, 0.0)
    joined = joined + jnp.where(source == target + 2 * top_count, 1.0, 0.0)
    joined = jnp.where(target < top_count, joined, 0.0).astype(jnp.bfloat16)
    first = lax.broadcasted_iota(jnp.int32, (rows, rows), 0)
    second = lax.broadcasted_iota(jnp.int32, (rows, rows), 1)
    later = jnp.where(first < second, 1.0, 0.0).astype(jnp.bfloat16)
    earlier = jnp.where(second < first, 1.0, 0.0).astype(jnp.bfloat16)
    ones = jnp.ones((8, lanes), jnp.bfloat16)
    slot_row = lax.broadcasted_iota(jnp.int32, (slots, rows), 0).astype(jnp.float32)
    slot_lane = lax.broadcasted_iota(jnp.int32, (rows, slots), 1).astype(jnp.float32)
    for group in range(groups):
        coded = coded_ref[group]
        gates = jnp.dot(coded, joined, preferred_element_type=jnp.float32)
        gate_sum = jnp.sum(gates, axis=1, keepdims=True)
        named = coded.astype(jnp.float32).astype(jnp.int32)
        for number in range(2):
            expert = expert_ref[0] ^ (number * PAIR)
            hits = jnp.where((named == expert) & (lane < top_count), 1.0, 0.0)
            share_ref[group, :, number : number + 1] = (
                jnp.sum(hits * gates, axis=1, keepdims=True) / gate_sum
            )
            hit = jnp.sum(hits, axis=1, keepdims=True)
            held = jnp.broadcast_to(hit, (rows, lanes)).astype(jnp.bfloat16)
            rank = jnp.dot(earlier, held, preferred_element_type=jnp.float32)[:, :1]
            rank = jnp.where(hit > 0.0, rank, -1.0)
            place_ref[number, group] = jnp.where(rank == slot_lane, 1.0, 0.0).astype(jnp.bfloat16)
            hit_row = lax.dot_general(
                ones,
                hits.astype(jnp.bfloat16),
                (((1,), (1,)), ((), ())),
                preferred_element_type=jnp.float32,
            )
            rank_row = jnp.dot(
                hit_row.astype(jnp.bfloat16), later, preferred_element_type=jnp.float32
            )
            rank_row = jnp.where(hit_row > 0.0, rank_row, -1.0)[:1]
            pick_ref[group, number * slots : (number + 1) * slots] = jnp.where(
                rank_row == slot_row, 1.0, 0.0
            ).astype(jnp.bfloat16)


def make_tables(coded, expert, slots, top_count):
    groups, rows, lanes = coded.shape
    return pl.pallas_call(
        lambda *refs: tables_kernel(top_count, *refs),
        out_shape=[
            jax.ShapeDtypeStruct((groups, 2 * slots, rows), jnp.bfloat16),
            jax.ShapeDtypeStruct((2, groups, rows, slots), jnp.bfloat16),
            jax.ShapeDtypeStruct((groups, rows, 2), jnp.float32),
        ],
        in_specs=[
            pl.BlockSpec(memory_space=pltpu.SMEM),
            pl.BlockSpec(memory_space=pltpu.VMEM),
        ],
        compiler_params=pltpu.CompilerParams(vmem_limit_bytes=24 * 1024 * 1024),
        cost_estimate=pl.CostEstimate(
            flops=4 * groups * rows * rows * lanes,
            bytes_accessed=8 * groups * rows * slots,
            transcendentals=0,
        ),
        name="tables",
    )(expert.astype(jnp.int32)[None], coded)


def expert_kernel(first, spots, cuts, *refs):
    pick_ref, place_ref, share_ref, own_gu_ref, far_gu_ref, own_dn_ref, far_dn_ref = refs[:7]
    group_rows, slots = place_ref.shape[2:]
    groups = len(cuts)
    piece_refs = refs[7 : 7 + len(spots)]
    out_refs = refs[7 + len(spots) : 7 + len(spots) + 2 * sum(cuts)]
    x_buf, xs_buf, gu_buf, dn_buf, hid_buf, served_buf, y_buf, x_sem, w_sem, y_sem = refs[
        7 + len(spots) + len(out_refs) :
    ]
    width = x_buf.shape[2]
    half = width // 2
    hidden = own_dn_ref.shape[0]
    tiles = hidden // TILE

    row_copies = []
    for number, ((group, row, column), piece) in enumerate(zip(spots, piece_refs)):
        rows, columns = piece.shape
        target = x_buf.at[group, pl.ds(row, rows), pl.ds(column, columns)]
        row_copies.append((group, pltpu.make_async_copy(piece, target, x_sem.at[number])))
    weight_copies = []
    for expert, (gu_ref, dn_ref) in enumerate(((own_gu_ref, own_dn_ref), (far_gu_ref, far_dn_ref))):
        mine = []
        for tile in range(tiles):
            for side in range(2):
                mine.append(
                    pltpu.make_async_copy(
                        gu_ref.at[:, pl.ds(side * hidden + tile * TILE, TILE)],
                        gu_buf.at[expert, tile, side],
                        w_sem.at[expert, 2 * tile + side],
                    )
                )
        mine.append(pltpu.make_async_copy(dn_ref, dn_buf.at[expert], w_sem.at[expert, 2 * tiles]))
        weight_copies.append(mine)
    for _, copy in row_copies:
        copy.start()
    for mine in weight_copies:
        for copy in mine:
            copy.start()

    for group in range(groups):
        for where, copy in row_copies:
            if where == group:
                copy.wait()
        chosen = jnp.dot(
            pick_ref[first + group], x_buf[group], preferred_element_type=jnp.float32
        ).astype(jnp.bfloat16)
        xs_buf[0, pl.ds(group * slots, slots)] = chosen[:slots]
        xs_buf[1, pl.ds(group * slots, slots)] = chosen[slots:]

    for expert in range(2):
        for tile in range(tiles):
            weight_copies[expert][2 * tile].wait()
            weight_copies[expert][2 * tile + 1].wait()
            gate = jnp.dot(
                xs_buf[expert], gu_buf[expert, tile, 0], preferred_element_type=jnp.float32
            )
            up = jnp.dot(
                xs_buf[expert], gu_buf[expert, tile, 1], preferred_element_type=jnp.float32
            )
            value = gate / (1.0 + jnp.exp(-gate)) * up
            hid_buf[:, tile * TILE : (tile + 1) * TILE] = value.astype(jnp.bfloat16)
        weight_copies[expert][2 * tiles].wait()
        for column in range(0, width, 2 * TILE):
            served_buf[expert, :, column : column + 2 * TILE] = jnp.dot(
                hid_buf[...],
                dn_buf[expert, :, column : column + 2 * TILE],
                preferred_element_type=jnp.float32,
            ).astype(jnp.bfloat16)

    out_copies = []
    for group in range(groups):
        for column in range(0, width, 2 * TILE):
            total = None
            for expert in range(2):
                placed = jnp.dot(
                    place_ref[expert, first + group],
                    served_buf[expert, pl.ds(group * slots, slots), column : column + 2 * TILE],
                    preferred_element_type=jnp.float32,
                )
                term = placed * share_ref[first + group, :, expert : expert + 1]
                total = term if total is None else total + term
            y_buf[group, :, column : column + 2 * TILE] = total.astype(jnp.bfloat16)
        cut = group_rows // cuts[group]
        for number in range(2 * cuts[group]):
            row, side = divmod(number, 2)
            done = len(out_copies)
            copy = pltpu.make_async_copy(
                y_buf.at[group, pl.ds(row * cut, cut), pl.ds(side * half, half)],
                out_refs[done],
                y_sem.at[done],
            )
            copy.start()
            out_copies.append(copy)
    for copy in out_copies:
        copy.wait()


def run_experts(first, pieces, cuts, pick, place, share, weights):
    group_rows, slots = place.shape[2:]
    groups = len(pieces)
    hidden, width = weights[2].shape
    tiles = hidden // TILE
    spots = [
        (group, row, column) for group, held in enumerate(pieces) for row, column, _ in held
    ]
    arrays = [array for held in pieces for _, _, array in held]
    anywhere = pl.BlockSpec(memory_space=pl.ANY)
    stored = pl.BlockSpec(memory_space=pltpu.HBM)
    inside = pl.BlockSpec(memory_space=pltpu.VMEM)
    outs = pl.pallas_call(
        lambda *refs: expert_kernel(first, spots, cuts, *refs),
        out_shape=[
            jax.ShapeDtypeStruct((group_rows // cut, width // 2), jnp.bfloat16)
            for cut in cuts
            for _ in range(2 * cut)
        ],
        in_specs=[inside] * 3 + [stored] * 4 + [anywhere] * len(arrays),
        out_specs=[anywhere] * (2 * sum(cuts)),
        scratch_shapes=[
            pltpu.VMEM((groups, group_rows, width), jnp.bfloat16),
            pltpu.VMEM((2, groups * slots, width), jnp.bfloat16),
            pltpu.VMEM((2, tiles, 2, width, TILE), jnp.bfloat16),
            pltpu.VMEM((2, hidden, width), jnp.bfloat16),
            pltpu.VMEM((groups * slots, hidden), jnp.bfloat16),
            pltpu.VMEM((2, groups * slots, width), jnp.bfloat16),
            pltpu.VMEM((groups, group_rows, width), jnp.bfloat16),
            pltpu.SemaphoreType.DMA((len(arrays),)),
            pltpu.SemaphoreType.DMA((2, 2 * tiles + 1)),
            pltpu.SemaphoreType.DMA((2 * sum(cuts),)),
        ],
        compiler_params=pltpu.CompilerParams(vmem_limit_bytes=(28 + 6 * group_rows // 256) * 1024 * 1024),
        cost_estimate=pl.CostEstimate(
            flops=12 * groups * slots * width * hidden,
            bytes_accessed=12 * width * hidden + 4 * groups * group_rows * width,
            transcendentals=2 * groups * slots * hidden,
        ),
        name="experts",
    )(pick, place, share, *weights, *arrays)
    return list(zip(outs[0::2], outs[1::2]))


def per_device(
    hidden_in,
    attn_gain,
    w_query,
    w_keyval,
    q_gain,
    k_gain,
    w_out,
    moe_gain,
    expert_ids,
    gate_fixed,
    w_gateup,
    w_down,
):
    tokens = hidden_in[0].astype(jnp.float32)
    row_count, model_width = tokens.shape
    head_dim = q_gain.shape[0]
    local_heads = w_query.shape[1] // head_dim
    kv_heads = w_keyval.shape[2] // head_dim
    group_size = local_heads * lax.axis_size("rep") // kv_heads
    rep_index = lax.axis_index("rep")
    kv_width = kv_heads * head_dim
    top_count = expert_ids.shape[2]
    expert_count = lax.axis_size(EVERY)

    normed, own_payload = prepare(
        hidden_in[0], attn_gain, w_keyval, k_gain, expert_ids[0], gate_fixed[0]
    )
    across_rows = swap(normed, "rep", ACROSS)
    line = jnp.concatenate(
        [own_payload] + [swap(own_payload, "seq", bits) for bits in seq_order()[1:]], axis=0
    )
    pair_rows = swap(ready(normed, line)[0], "rep", PAIR)
    corner_rows = swap(across_rows, "rep", PAIR)
    line_routes = line[:, 2 * kv_width :]

    def head_kv(rep):
        index = rep * local_heads // group_size * head_dim
        return [
            lax.dynamic_slice_in_dim(line, index, head_dim, 1),
            lax.dynamic_slice_in_dim(line, kv_width + index, head_dim, 1),
        ]

    sent = jnp.concatenate(head_kv(rep_index ^ ACROSS) + [line_routes], axis=1)
    sent, across_rows = ready(sent, across_rows)
    across = swap(sent, "rep", ACROSS)
    half_kv = jnp.concatenate(
        [jnp.concatenate(head_kv(rep_index), axis=1), across[:, : 2 * head_dim]], axis=0
    )
    pair_kv = swap(half_kv, "rep", PAIR)
    both_routes = jnp.stack([line_routes, across[:, 2 * head_dim :]])
    far_routes = swap(both_routes, "role", 1)
    coded = jnp.concatenate([both_routes[1:], far_routes[:1], far_routes[1:], both_routes[:1]])
    queries = make_queries([normed, across_rows, pair_rows, corner_rows], w_query, q_gain)
    kept, leaving = attend(queries, half_kv, pair_kv, w_out, head_dim)
    leaving, own_dn = ready(swap(leaving, "rep", PAIR), w_down[0])
    halves = kept + leaving
    far_dn, far_gu = swap(own_dn, "rep", PAIR), swap(w_gateup[0], "rep", PAIR)
    far_sum = halves[row_count:].astype(jnp.bfloat16)
    across_sum, coded, far_dn, far_gu = ready(
        swap(far_sum, "rep", ACROSS), coded, far_dn, far_gu
    )
    attended = halves[:row_count] + across_sum.astype(jnp.float32)
    mixed = tokens + attended

    moe_in = rms_rows(mixed, moe_gain).astype(jnp.bfloat16)

    capacity = max(2, 7 * row_count * top_count // (4 * expert_count))
    slots = -(-capacity * (coded.shape[1] // row_count) // 16) * 16
    rows, tables = spread_rows(
        moe_in,
        coded,
        lambda codes: make_tables(codes, lax.axis_index(EVERY), slots, top_count),
    )
    weights = [
        pltpu.with_memory_space_constraint(one, pltpu.HBM)
        for one in (w_gateup[0], far_gu, w_down[0], far_dn)
    ]

    tables = (*tables, weights)
    by_rep, by_role = run_experts(0, rows[:2], (1, 1), *tables)
    rep_low, rep_high, role_low, role_high, *held = ready(
        *by_rep, *by_role, *(array for _, _, array in rows[2])
    )
    by_rep, by_role = (rep_low, rep_high), (role_low, role_high)
    pieces = [(row, column, array) for (row, column, _), array in zip(rows[2], held)]
    *corner, near = run_experts(2, [pieces, rows[3]], (2, 1), *tables)
    routed = collect_rows(near, by_rep, by_role, corner)
    return (mixed + routed).astype(jnp.bfloat16)[None]


def solution(mesh):
    placed = (
        P("role", ("seq", "rep"), None),
        P(),
        P(None, "rep"),
        P(),
        P(),
        P(),
        P("rep", None),
        P(),
        P("role", ("seq", "rep"), None),
        P("role", ("seq", "rep"), None),
        P(("role", "seq", "rep"), None, None),
        P(("role", "seq", "rep"), None, None),
    )
    return jax.shard_map(
        per_device,
        mesh=mesh,
        in_specs=placed,
        out_specs=P("role", ("seq", "rep"), None),
        check_vma=False,
    )
```

```python
import jax
import jax.numpy as jnp
from jax import lax
from jax.experimental import pallas as pl
from jax.experimental.pallas import tpu as pltpu
from jax.sharding import PartitionSpec as P

EVERY = ("role", "seq", "rep")
PAIR = 1
ACROSS = 2
TILE = 256
LANES = 128


def rms_rows(values_in, gain_vec):
    return (
        values_in
        * lax.rsqrt(jnp.mean(values_in * values_in, axis=-1, keepdims=True) + 1e-06)
        * gain_vec
    )


def swap(block, axis, bits):
    size = lax.axis_size(axis)
    return lax.ppermute(block, axis, [(i, i ^ bits) for i in range(size)])


def seq_bits():
    size = lax.axis_size("seq")
    return [1 << place for place in reversed(range(size.bit_length() - 1))]


def ready(*arrays):
    return lax.optimization_barrier(arrays)


def pack_kernel(*refs):
    low_ref, high_ref = refs[-2:]
    count = len(refs) // 2 - 1
    half = low_ref.shape[1]
    start = 0
    for rep_ref, role_ref in zip(refs[:count], refs[count:-2]):
        rows = pl.ds(start, rep_ref.shape[0])
        low_ref[rows] = rep_ref[:, :half]
        high_ref[rows] = role_ref[:, half:]
        start += rep_ref.shape[0]


def pack_corners(by_rep, by_role):
    rows, width = sum(part.shape[0] for part in by_rep), by_rep[0].shape[1]
    half = jax.ShapeDtypeStruct((rows, width // 2), jnp.bfloat16)
    return pl.pallas_call(
        pack_kernel,
        out_shape=[half, half],
        compiler_params=pltpu.CompilerParams(vmem_limit_bytes=(4 + rows // 64) * 1024 * 1024),
        cost_estimate=pl.CostEstimate(
            flops=0, bytes_accessed=4 * rows * width, transcendentals=0
        ),
        name="pack_corners",
    )(*by_rep, *by_role)


def spread_rows(own, coded, tables_of):
    rows, half = own.shape[0], own.shape[1] // 2

    def both_ways(part):
        return swap(part, "rep", ACROSS), swap(part, "role", 1)

    blocks = {0: own}
    for bits in seq_bits():
        blocks |= {place ^ bits: swap(block, "seq", bits) for place, block in blocks.items()}
    middle = jnp.concatenate([blocks[place] for place in range(1, len(blocks) - 1)], axis=0)
    middle, coded, *outer = ready(middle, coded, *both_ways(own))
    last, *tables = ready(blocks[len(blocks) - 1], *tables_of(coded))
    by_rep, by_role = zip(outer, both_ways(middle), both_ways(last))
    low, high = pack_corners(by_rep, by_role)
    corner_low, corner_high = swap(low, "role", 1), swap(high, "rep", ACROSS)
    starts = (0, rows, rows + middle.shape[0])
    groups = [
        [(start, 0, part) for start, part in zip(starts, parts)]
        for parts in (by_rep, by_role, (own, middle, last))
    ]
    groups.insert(2, [(0, 0, corner_low), (0, half, corner_high)])
    return groups, tables


def added(first, second):
    return (first.astype(jnp.float32) + second.astype(jnp.float32)).astype(jnp.bfloat16)


def collect_rows(row_count, near, by_rep, by_role, corner):
    straight_low = swap(by_role[0], "role", 1)
    straight_high = swap(by_rep[1], "rep", ACROSS)
    straight_low, straight_high, near_low, near_high, *corner = ready(
        straight_low, straight_high, *near, *corner[0], *corner[1]
    )
    cut = near_low.shape[0] // 2
    halves = slice(0, cut), slice(cut, None)

    def merged(rows, turned_low, turned_high):
        return jnp.concatenate(
            [
                base[rows].astype(jnp.float32)
                + first[rows].astype(jnp.float32)
                + second.astype(jnp.float32)
                for base, first, second in (
                    (near_low, straight_low, turned_low),
                    (near_high, straight_high, turned_high),
                )
            ],
            axis=1,
        )

    def corners(number):
        low, high = corner[2 * number : 2 * number + 2]
        return swap(low, "role", 1), swap(high, "rep", ACROSS)

    def sums(number, corner_low, corner_high):
        rows = halves[number]
        return added(by_rep[0][rows], corner_low), added(by_role[1][rows], corner_high)

    def turned(low, high):
        return swap(low, "rep", ACROSS), swap(high, "role", 1)

    far_corner, beside_corner = corners(1), corners(0)
    *far, corner_low, corner_high = ready(*turned(*sums(1, *far_corner)), *beside_corner)
    upper = merged(halves[1], *far)
    *near_sums, upper = ready(*sums(0, corner_low, corner_high), upper)
    lower = merged(halves[0], *turned(*near_sums))
    top_bits, *low_bits = seq_bits()

    def folded(rows):
        for bits in reversed(low_bits):
            pairs = rows.reshape(-1, 2, row_count, rows.shape[1])
            leaving = pairs[:, 1].astype(jnp.bfloat16).reshape(-1, rows.shape[1])
            kept = pairs[:, 0].reshape(-1, rows.shape[1]).astype(jnp.float32)
            rows = kept + swap(leaving, "seq", bits).astype(jnp.float32)
        return rows

    upper = folded(upper).astype(jnp.bfloat16)
    return folded(lower) + swap(upper, "seq", top_bits).astype(jnp.float32)


def prepare_kernel(*refs):
    tokens_in, gain_in, kv_in, k_gain_in, ids_in, gates_in, normed_ref, out_ref = refs[:8]
    held, sem = refs[8:14], refs[14]
    sources = (tokens_in, gain_in, kv_in, k_gain_in, ids_in, gates_in)
    copies = [
        pltpu.make_async_copy(src, dst, sem.at[number])
        for number, (src, dst) in enumerate(zip(sources, held))
    ]
    for copy in copies:
        copy.start()
    for copy in copies:
        copy.wait()
    tokens_ref, gain_ref, kv_ref, k_gain_ref, ids_ref, gates_ref = held
    normed = rms_rows(tokens_ref[...].astype(jnp.float32), gain_ref[...]).astype(jnp.bfloat16)
    normed_ref[...] = normed
    kv_width, head_dim = kv_ref.shape[2], k_gain_ref.shape[1]
    keys = jnp.dot(normed, kv_ref[0], preferred_element_type=jnp.float32)
    for start in range(0, kv_width, head_dim):
        head = rms_rows(keys[:, start : start + head_dim], k_gain_ref[...])
        out_ref[:, start : start + head_dim] = head.astype(jnp.bfloat16)
    values = jnp.dot(normed, kv_ref[1], preferred_element_type=jnp.float32)
    out_ref[:, kv_width : 2 * kv_width] = values.astype(jnp.bfloat16)
    coded = jnp.concatenate([ids_ref[...], gates_ref[...] // 64, gates_ref[...] % 64], axis=0)
    count = coded.shape[0]
    spread = lax.broadcasted_iota(jnp.int32, (count, LANES), 0)
    spread = spread == lax.broadcasted_iota(jnp.int32, (count, LANES), 1)
    out_ref[:, 2 * kv_width :] = lax.dot_general(
        coded.astype(jnp.float32).astype(jnp.bfloat16),
        spread.astype(jnp.float32).astype(jnp.bfloat16),
        (((0,), (0,)), ((), ())),
        preferred_element_type=jnp.float32,
    ).astype(jnp.bfloat16)


def prepare(tokens, attn_gain, w_keyval, k_gain, ids, gates):
    rows, width = tokens.shape
    operands = [
        pltpu.with_memory_space_constraint(one, pltpu.HBM)
        for one in (tokens, attn_gain[None], w_keyval, k_gain[None], ids.T, gates.T)
    ]
    return pl.pallas_call(
        prepare_kernel,
        out_shape=[
            jax.ShapeDtypeStruct((rows, width), jnp.bfloat16),
            jax.ShapeDtypeStruct((rows, 2 * w_keyval.shape[2] + LANES), jnp.bfloat16),
        ],
        in_specs=[pl.BlockSpec(memory_space=pltpu.HBM)] * len(operands),
        scratch_shapes=[pltpu.VMEM(one.shape, one.dtype) for one in operands]
        + [pltpu.SemaphoreType.DMA((len(operands),))],
        compiler_params=pltpu.CompilerParams(vmem_limit_bytes=8 * 1024 * 1024),
        cost_estimate=pl.CostEstimate(
            flops=4 * rows * width * w_keyval.shape[2],
            bytes_accessed=4 * width * w_keyval.shape[2] + 4 * rows * width,
            transcendentals=rows,
        ),
        name="prepare",
    )(*operands)


def queries_kernel(first_ref, second_ref, third_ref, fourth_ref, weight_ref, gain_ref, out_ref):
    rows, head_dim = first_ref.shape[0], gain_ref.shape[1]
    refs = (first_ref, second_ref, third_ref, fourth_ref)
    held = jnp.concatenate([ref[...] for ref in refs], axis=0)
    raw = jnp.dot(held, weight_ref[...], preferred_element_type=jnp.float32)
    for start in range(0, weight_ref.shape[1], head_dim):
        head = rms_rows(raw[:, start : start + head_dim], gain_ref[...])
        out_ref[:, start : start + head_dim] = head.astype(jnp.bfloat16)


def make_queries(blocks, w_query, q_gain):
    rows, width = len(blocks) * blocks[0].shape[0], w_query.shape[1]
    return pl.pallas_call(
        queries_kernel,
        out_shape=jax.ShapeDtypeStruct((rows, width), jnp.bfloat16),
        compiler_params=pltpu.CompilerParams(vmem_limit_bytes=8 * 1024 * 1024),
        cost_estimate=pl.CostEstimate(
            flops=2 * rows * width * w_query.shape[0],
            bytes_accessed=2 * width * w_query.shape[0],
            transcendentals=rows,
        ),
        name="queries",
    )(*blocks, w_query, q_gain[None])


def attend_kernel(head_dim, query_ref, near_ref, far_ref, weight_ref, kept_ref, leaving_ref, held_ref):
    keys = [ref[:, :head_dim] for ref in (near_ref, far_ref)]
    values = [ref[:, head_dim:] for ref in (near_ref, far_ref)]
    for start in range(0, query_ref.shape[1], head_dim):
        query = query_ref[:, start : start + head_dim]
        scores = [
            lax.dot_general(
                query, key, (((1,), (1,)), ((), ())), preferred_element_type=jnp.float32
            )
            * head_dim ** (-0.5)
            for key in keys
        ]
        row_max = jnp.maximum(
            jnp.max(scores[0], axis=1, keepdims=True), jnp.max(scores[1], axis=1, keepdims=True)
        )
        denom, total = 0.0, 0.0
        for score, value in zip(scores, values):
            weights = jnp.exp(score - row_max)
            denom = denom + jnp.sum(weights, axis=1, keepdims=True)
            total = total + jnp.dot(
                weights.astype(jnp.bfloat16), value, preferred_element_type=jnp.float32
            )
        held_ref[:, start : start + head_dim] = (total / denom).astype(jnp.bfloat16)
    cut = kept_ref.shape[0]
    for column in range(0, weight_ref.shape[1], 2 * TILE):
        columns = slice(column, column + 2 * TILE)
        partial = jnp.dot(held_ref[...], weight_ref[:, columns], preferred_element_type=jnp.float32)
        kept_ref[:, columns] = partial[:cut]
        leaving_ref[:, columns] = partial[cut:]


def attend(queries, near_kv, far_kv, w_out, head_dim):
    rows, width = queries.shape
    keys = 2 * near_kv.shape[0]
    half = jax.ShapeDtypeStruct((rows // 2, w_out.shape[1]), jnp.float32)
    return pl.pallas_call(
        lambda *refs: attend_kernel(head_dim, *refs),
        out_shape=[half, half],
        scratch_shapes=[pltpu.VMEM((rows, width), jnp.bfloat16)],
        compiler_params=pltpu.CompilerParams(vmem_limit_bytes=12 * 1024 * 1024),
        cost_estimate=pl.CostEstimate(
            flops=4 * rows * width * keys + 2 * rows * width * w_out.shape[1],
            bytes_accessed=2 * width * w_out.shape[1] + 4 * rows * w_out.shape[1],
            transcendentals=rows * keys * width // head_dim,
        ),
        name="attend",
    )(queries, near_kv, far_kv, w_out)


def tables_kernel(top_count, expert_ref, coded_ref, pick_ref, place_ref, share_ref):
    groups, rows, lanes = coded_ref.shape
    slots = place_ref.shape[3]
    lane = lax.broadcasted_iota(jnp.int32, (rows, lanes), 1)
    source = lax.broadcasted_iota(jnp.int32, (lanes, lanes), 0)
    target = lax.broadcasted_iota(jnp.int32, (lanes, lanes), 1)
    joined = jnp.where(source == target + top_count, 64.0, 0.0)
    joined = joined + jnp.where(source == target + 2 * top_count, 1.0, 0.0)
    joined = jnp.where(target < top_count, joined, 0.0).astype(jnp.bfloat16)
    first = lax.broadcasted_iota(jnp.int32, (rows, rows), 0)
    second = lax.broadcasted_iota(jnp.int32, (rows, rows), 1)
    later = jnp.where(first < second, 1.0, 0.0).astype(jnp.bfloat16)
    earlier = jnp.where(second < first, 1.0, 0.0).astype(jnp.bfloat16)
    ones = jnp.ones((8, lanes), jnp.bfloat16)
    slot_row = lax.broadcasted_iota(jnp.int32, (slots, rows), 0).astype(jnp.float32)
    slot_lane = lax.broadcasted_iota(jnp.int32, (rows, slots), 1).astype(jnp.float32)
    for group in range(groups):
        coded = coded_ref[group]
        gates = jnp.dot(coded, joined, preferred_element_type=jnp.float32)
        gate_sum = jnp.sum(gates, axis=1, keepdims=True)
        named = coded.astype(jnp.float32).astype(jnp.int32)
        for number in range(2):
            expert = expert_ref[0] ^ (number * PAIR)
            hits = jnp.where((named == expert) & (lane < top_count), 1.0, 0.0)
            share_ref[group, :, number : number + 1] = (
                jnp.sum(hits * gates, axis=1, keepdims=True) / gate_sum
            )
            hit = jnp.sum(hits, axis=1, keepdims=True)
            held = jnp.broadcast_to(hit, (rows, lanes)).astype(jnp.bfloat16)
            rank = jnp.dot(earlier, held, preferred_element_type=jnp.float32)[:, :1]
            rank = jnp.where(hit > 0.0, rank, -1.0)
            place_ref[number, group] = jnp.where(rank == slot_lane, 1.0, 0.0).astype(jnp.bfloat16)
            hit_row = lax.dot_general(
                ones,
                hits.astype(jnp.bfloat16),
                (((1,), (1,)), ((), ())),
                preferred_element_type=jnp.float32,
            )
            rank_row = jnp.dot(
                hit_row.astype(jnp.bfloat16), later, preferred_element_type=jnp.float32
            )
            rank_row = jnp.where(hit_row > 0.0, rank_row, -1.0)[:1]
            pick_ref[group, number * slots : (number + 1) * slots] = jnp.where(
                rank_row == slot_row, 1.0, 0.0
            ).astype(jnp.bfloat16)


def make_tables(coded, expert, slots, top_count):
    groups, rows, lanes = coded.shape
    return pl.pallas_call(
        lambda *refs: tables_kernel(top_count, *refs),
        out_shape=[
            jax.ShapeDtypeStruct((groups, 2 * slots, rows), jnp.bfloat16),
            jax.ShapeDtypeStruct((2, groups, rows, slots), jnp.bfloat16),
            jax.ShapeDtypeStruct((groups, rows, 2), jnp.float32),
        ],
        in_specs=[
            pl.BlockSpec(memory_space=pltpu.SMEM),
            pl.BlockSpec(memory_space=pltpu.VMEM),
        ],
        compiler_params=pltpu.CompilerParams(vmem_limit_bytes=24 * 1024 * 1024),
        cost_estimate=pl.CostEstimate(
            flops=4 * groups * rows * rows * lanes,
            bytes_accessed=8 * groups * rows * slots,
            transcendentals=0,
        ),
        name="tables",
    )(expert.astype(jnp.int32)[None], coded)


def expert_kernel(first, spots, cuts, *refs):
    pick_ref, place_ref, share_ref, own_gu_ref, far_gu_ref, own_dn_ref, far_dn_ref = refs[:7]
    group_rows, slots = place_ref.shape[2:]
    groups = len(cuts)
    piece_refs = refs[7 : 7 + len(spots)]
    out_refs = refs[7 + len(spots) : 7 + len(spots) + 2 * sum(cuts)]
    x_buf, xs_buf, gu_buf, dn_buf, hid_buf, served_buf, y_buf, x_sem, w_sem, y_sem = refs[
        7 + len(spots) + len(out_refs) :
    ]
    width = x_buf.shape[2]
    half = width // 2
    hidden = own_dn_ref.shape[0]
    tiles = hidden // TILE

    row_copies = []
    for number, ((group, row, column), piece) in enumerate(zip(spots, piece_refs)):
        rows, columns = piece.shape
        target = x_buf.at[group, pl.ds(row, rows), pl.ds(column, columns)]
        row_copies.append((group, pltpu.make_async_copy(piece, target, x_sem.at[number])))
    weight_copies = []
    for expert, (gu_ref, dn_ref) in enumerate(((own_gu_ref, own_dn_ref), (far_gu_ref, far_dn_ref))):
        mine = []
        for tile in range(tiles):
            for side in range(2):
                mine.append(
                    pltpu.make_async_copy(
                        gu_ref.at[:, pl.ds(side * hidden + tile * TILE, TILE)],
                        gu_buf.at[expert, tile, side],
                        w_sem.at[expert, 2 * tile + side],
                    )
                )
        mine.append(pltpu.make_async_copy(dn_ref, dn_buf.at[expert], w_sem.at[expert, 2 * tiles]))
        weight_copies.append(mine)
    for _, copy in row_copies:
        copy.start()
    for mine in weight_copies:
        for copy in mine:
            copy.start()

    for group in range(groups):
        for where, copy in row_copies:
            if where == group:
                copy.wait()
        chosen = jnp.dot(
            pick_ref[first + group], x_buf[group], preferred_element_type=jnp.float32
        ).astype(jnp.bfloat16)
        xs_buf[0, pl.ds(group * slots, slots)] = chosen[:slots]
        xs_buf[1, pl.ds(group * slots, slots)] = chosen[slots:]

    for expert in range(2):
        for tile in range(tiles):
            weight_copies[expert][2 * tile].wait()
            weight_copies[expert][2 * tile + 1].wait()
            gate = jnp.dot(
                xs_buf[expert], gu_buf[expert, tile, 0], preferred_element_type=jnp.float32
            )
            up = jnp.dot(
                xs_buf[expert], gu_buf[expert, tile, 1], preferred_element_type=jnp.float32
            )
            value = gate / (1.0 + jnp.exp(-gate)) * up
            hid_buf[:, tile * TILE : (tile + 1) * TILE] = value.astype(jnp.bfloat16)
        weight_copies[expert][2 * tiles].wait()
        for column in range(0, width, 2 * TILE):
            served_buf[expert, :, column : column + 2 * TILE] = jnp.dot(
                hid_buf[...],
                dn_buf[expert, :, column : column + 2 * TILE],
                preferred_element_type=jnp.float32,
            ).astype(jnp.bfloat16)

    out_copies = []
    for group in range(groups):
        for column in range(0, width, 2 * TILE):
            total = None
            for expert in range(2):
                placed = jnp.dot(
                    place_ref[expert, first + group],
                    served_buf[expert, pl.ds(group * slots, slots), column : column + 2 * TILE],
                    preferred_element_type=jnp.float32,
                )
                term = placed * share_ref[first + group, :, expert : expert + 1]
                total = term if total is None else total + term
            y_buf[group, :, column : column + 2 * TILE] = total.astype(jnp.bfloat16)
        cut = group_rows // cuts[group]
        for number in range(2 * cuts[group]):
            row, side = divmod(number, 2)
            done = len(out_copies)
            copy = pltpu.make_async_copy(
                y_buf.at[group, pl.ds(row * cut, cut), pl.ds(side * half, half)],
                out_refs[done],
                y_sem.at[done],
            )
            copy.start()
            out_copies.append(copy)
    for copy in out_copies:
        copy.wait()


def run_experts(first, pieces, cuts, pick, place, share, weights):
    group_rows, slots = place.shape[2:]
    groups = len(pieces)
    hidden, width = weights[2].shape
    tiles = hidden // TILE
    spots = [
        (group, row, column) for group, held in enumerate(pieces) for row, column, _ in held
    ]
    arrays = [array for held in pieces for _, _, array in held]
    anywhere = pl.BlockSpec(memory_space=pl.ANY)
    stored = pl.BlockSpec(memory_space=pltpu.HBM)
    inside = pl.BlockSpec(memory_space=pltpu.VMEM)
    outs = pl.pallas_call(
        lambda *refs: expert_kernel(first, spots, cuts, *refs),
        out_shape=[
            jax.ShapeDtypeStruct((group_rows // cut, width // 2), jnp.bfloat16)
            for cut in cuts
            for _ in range(2 * cut)
        ],
        in_specs=[inside] * 3 + [stored] * 4 + [anywhere] * len(arrays),
        out_specs=[anywhere] * (2 * sum(cuts)),
        scratch_shapes=[
            pltpu.VMEM((groups, group_rows, width), jnp.bfloat16),
            pltpu.VMEM((2, groups * slots, width), jnp.bfloat16),
            pltpu.VMEM((2, tiles, 2, width, TILE), jnp.bfloat16),
            pltpu.VMEM((2, hidden, width), jnp.bfloat16),
            pltpu.VMEM((groups * slots, hidden), jnp.bfloat16),
            pltpu.VMEM((2, groups * slots, width), jnp.bfloat16),
            pltpu.VMEM((groups, group_rows, width), jnp.bfloat16),
            pltpu.SemaphoreType.DMA((len(arrays),)),
            pltpu.SemaphoreType.DMA((2, 2 * tiles + 1)),
            pltpu.SemaphoreType.DMA((2 * sum(cuts),)),
        ],
        compiler_params=pltpu.CompilerParams(vmem_limit_bytes=(28 + 6 * group_rows // 256) * 1024 * 1024),
        cost_estimate=pl.CostEstimate(
            flops=12 * groups * slots * width * hidden,
            bytes_accessed=12 * width * hidden + 4 * groups * group_rows * width,
            transcendentals=2 * groups * slots * hidden,
        ),
        name="experts",
    )(pick, place, share, *weights, *arrays)
    return list(zip(outs[0::2], outs[1::2]))


def per_device(
    hidden_in,
    attn_gain,
    w_query,
    w_keyval,
    q_gain,
    k_gain,
    w_out,
    moe_gain,
    expert_ids,
    gate_fixed,
    w_gateup,
    w_down,
):
    tokens = hidden_in[0].astype(jnp.float32)
    row_count, model_width = tokens.shape
    head_dim = q_gain.shape[0]
    local_heads = w_query.shape[1] // head_dim
    kv_heads = w_keyval.shape[2] // head_dim
    group_size = local_heads * lax.axis_size("rep") // kv_heads
    rep_index = lax.axis_index("rep")
    kv_width = kv_heads * head_dim
    top_count = expert_ids.shape[2]
    expert_count = lax.axis_size(EVERY)

    normed, own_payload = prepare(
        hidden_in[0], attn_gain, w_keyval, k_gain, expert_ids[0], gate_fixed[0]
    )
    across_rows = swap(normed, "rep", ACROSS)
    line = jnp.concatenate(
        [own_payload] + [swap(own_payload, "seq", bits) for bits in range(1, lax.axis_size("seq"))], axis=0
    )
    pair_rows = swap(ready(normed, line)[0], "rep", PAIR)
    corner_rows = swap(across_rows, "rep", PAIR)
    line_routes = line[:, 2 * kv_width :]

    def head_kv(rep):
        index = rep * local_heads // group_size * head_dim
        return [
            lax.dynamic_slice_in_dim(line, index, head_dim, 1),
            lax.dynamic_slice_in_dim(line, kv_width + index, head_dim, 1),
        ]

    sent = jnp.concatenate(head_kv(rep_index ^ ACROSS) + [line_routes], axis=1)
    sent, across_rows = ready(sent, across_rows)
    across = swap(sent, "rep", ACROSS)
    half_kv = jnp.concatenate(
        [jnp.concatenate(head_kv(rep_index), axis=1), across[:, : 2 * head_dim]], axis=0
    )
    pair_kv = swap(half_kv, "rep", PAIR)
    both_routes = jnp.stack([line_routes, across[:, 2 * head_dim :]])
    far_routes = swap(both_routes, "role", 1)
    coded = jnp.concatenate([both_routes[1:], far_routes[:1], far_routes[1:], both_routes[:1]])
    queries = make_queries([normed, across_rows, pair_rows, corner_rows], w_query, q_gain)
    kept, leaving = attend(queries, half_kv, pair_kv, w_out, head_dim)
    leaving, own_dn = ready(swap(leaving, "rep", PAIR), w_down[0])
    halves = kept + leaving
    far_dn, far_gu = swap(own_dn, "rep", PAIR), swap(w_gateup[0], "rep", PAIR)
    far_sum = halves[row_count:].astype(jnp.bfloat16)
    across_sum, coded, far_dn, far_gu = ready(
        swap(far_sum, "rep", ACROSS), coded, far_dn, far_gu
    )
    attended = halves[:row_count] + across_sum.astype(jnp.float32)
    mixed = tokens + attended

    moe_in = rms_rows(mixed, moe_gain).astype(jnp.bfloat16)

    capacity = max(2, 7 * row_count * top_count // (4 * expert_count))
    slots = -(-capacity * (coded.shape[1] // row_count) // 16) * 16
    rows, tables = spread_rows(
        moe_in,
        coded,
        lambda codes: make_tables(codes, lax.axis_index(EVERY), slots, top_count),
    )
    weights = [
        pltpu.with_memory_space_constraint(one, pltpu.HBM)
        for one in (w_gateup[0], far_gu, w_down[0], far_dn)
    ]

    tables = (*tables, weights)
    by_rep, by_role = run_experts(0, rows[:2], (1, 1), *tables)
    rep_low, rep_high, role_low, role_high, *held = ready(
        *by_rep, *by_role, *(array for _, _, array in rows[2])
    )
    by_rep, by_role = (rep_low, rep_high), (role_low, role_high)
    pieces = [(row, column, array) for (row, column, _), array in zip(rows[2], held)]
    *corner, near = run_experts(2, [pieces, rows[3]], (2, 1), *tables)
    routed = collect_rows(row_count, near, by_rep, by_role, corner)
    return (mixed + routed).astype(jnp.bfloat16)[None]


def solution(mesh):
    placed = (
        P("role", ("seq", "rep"), None),
        P(),
        P(None, "rep"),
        P(),
        P(),
        P(),
        P("rep", None),
        P(),
        P("role", ("seq", "rep"), None),
        P("role", ("seq", "rep"), None),
        P(("role", "seq", "rep"), None, None),
        P(("role", "seq", "rep"), None, None),
    )
    return jax.shard_map(
        per_device,
        mesh=mesh,
        in_specs=placed,
        out_specs=P("role", ("seq", "rep"), None),
        check_vma=False,
    )
```

```python
import jax
import jax.numpy as jnp
from jax import lax
from jax.experimental import pallas as pl
from jax.experimental.pallas import tpu as pltpu
from jax.sharding import PartitionSpec as P

EVERY = ("role", "seq", "rep")
PAIR = 1
ACROSS = 2
TILE = 256
LANES = 128


def rms_rows(values_in, gain_vec):
    return (
        values_in
        * lax.rsqrt(jnp.mean(values_in * values_in, axis=-1, keepdims=True) + 1e-06)
        * gain_vec
    )


def swap(block, axis, bits):
    size = lax.axis_size(axis)
    return lax.ppermute(block, axis, [(i, i ^ bits) for i in range(size)])


def seq_bits():
    size = lax.axis_size("seq")
    return [1 << place for place in reversed(range(size.bit_length() - 1))]


def ready(*arrays):
    return lax.optimization_barrier(arrays)


def pack_kernel(*refs):
    low_ref, high_ref = refs[-2:]
    count = len(refs) // 2 - 1
    half = low_ref.shape[1]
    start = 0
    for rep_ref, role_ref in zip(refs[:count], refs[count:-2]):
        rows = pl.ds(start, rep_ref.shape[0])
        low_ref[rows] = rep_ref[:, :half]
        high_ref[rows] = role_ref[:, half:]
        start += rep_ref.shape[0]


def pack_corners(by_rep, by_role):
    rows, width = sum(part.shape[0] for part in by_rep), by_rep[0].shape[1]
    half = jax.ShapeDtypeStruct((rows, width // 2), jnp.bfloat16)
    return pl.pallas_call(
        pack_kernel,
        out_shape=[half, half],
        compiler_params=pltpu.CompilerParams(vmem_limit_bytes=(4 + rows // 64) * 1024 * 1024),
        cost_estimate=pl.CostEstimate(
            flops=0, bytes_accessed=4 * rows * width, transcendentals=0
        ),
        name="pack_corners",
    )(*by_rep, *by_role)


def spread_rows(own, coded, tables_of):
    rows, half = own.shape[0], own.shape[1] // 2

    def both_ways(part):
        return swap(part, "rep", ACROSS), swap(part, "role", 1)

    blocks = {0: own}
    for bits in seq_bits():
        blocks |= {place ^ bits: swap(block, "seq", bits) for place, block in blocks.items()}
    middle = [blocks[place] for place in range(2, len(blocks) - 1)]
    middle = jnp.concatenate(middle, axis=0) if len(middle) > 1 else middle[0]
    parts = [own, blocks[1], middle, blocks[len(blocks) - 1]]
    parts[2], coded, *early = ready(parts[2], coded, *both_ways(own), *both_ways(parts[1]))
    parts[3], *tables = ready(parts[3], *tables_of(coded))
    by_rep, by_role = zip(early[:2], early[2:], both_ways(parts[2]), both_ways(parts[3]))
    low, high = pack_corners(by_rep, by_role)
    corner_low, corner_high = swap(low, "role", 1), swap(high, "rep", ACROSS)
    starts = (0, rows, 2 * rows, 2 * rows + middle.shape[0])
    groups = [
        [(start, 0, part) for start, part in zip(starts, held)]
        for held in (by_rep, by_role, parts)
    ]
    groups.insert(2, [(0, 0, corner_low), (0, half, corner_high)])
    return groups, tables


def added(first, second):
    return (first.astype(jnp.float32) + second.astype(jnp.float32)).astype(jnp.bfloat16)


def collect_rows(row_count, near, by_rep, by_role, corner):
    straight_low = swap(by_role[0], "role", 1)
    straight_high = swap(by_rep[1], "rep", ACROSS)
    straight_low, straight_high, near_low, near_high, *corner = ready(
        straight_low, straight_high, *near, *corner[0], *corner[1]
    )
    cut = near_low.shape[0] // 2
    halves = slice(0, cut), slice(cut, None)

    def merged(rows, turned_low, turned_high):
        return jnp.concatenate(
            [
                base[rows].astype(jnp.float32)
                + first[rows].astype(jnp.float32)
                + second.astype(jnp.float32)
                for base, first, second in (
                    (near_low, straight_low, turned_low),
                    (near_high, straight_high, turned_high),
                )
            ],
            axis=1,
        )

    def corners(number):
        low, high = corner[2 * number : 2 * number + 2]
        return swap(low, "role", 1), swap(high, "rep", ACROSS)

    def sums(number, corner_low, corner_high):
        rows = halves[number]
        return added(by_rep[0][rows], corner_low), added(by_role[1][rows], corner_high)

    def turned(low, high):
        return swap(low, "rep", ACROSS), swap(high, "role", 1)

    far_corner, beside_corner = corners(1), corners(0)
    *far, corner_low, corner_high = ready(*turned(*sums(1, *far_corner)), *beside_corner)
    upper = merged(halves[1], *far)
    *near_sums, upper = ready(*sums(0, corner_low, corner_high), upper)
    lower = merged(halves[0], *turned(*near_sums))
    top_bits, *low_bits = seq_bits()

    def folded(rows):
        for bits in reversed(low_bits):
            pairs = rows.reshape(-1, 2, row_count, rows.shape[1])
            leaving = pairs[:, 1].astype(jnp.bfloat16).reshape(-1, rows.shape[1])
            kept = pairs[:, 0].reshape(-1, rows.shape[1]).astype(jnp.float32)
            rows = kept + swap(leaving, "seq", bits).astype(jnp.float32)
        return rows

    upper = folded(upper).astype(jnp.bfloat16)
    return folded(lower) + swap(upper, "seq", top_bits).astype(jnp.float32)


def prepare_kernel(*refs):
    tokens_in, gain_in, kv_in, k_gain_in, ids_in, gates_in, normed_ref, out_ref = refs[:8]
    held, sem = refs[8:14], refs[14]
    sources = (tokens_in, gain_in, kv_in, k_gain_in, ids_in, gates_in)
    copies = [
        pltpu.make_async_copy(src, dst, sem.at[number])
        for number, (src, dst) in enumerate(zip(sources, held))
    ]
    for copy in copies:
        copy.start()
    for copy in copies:
        copy.wait()
    tokens_ref, gain_ref, kv_ref, k_gain_ref, ids_ref, gates_ref = held
    normed = rms_rows(tokens_ref[...].astype(jnp.float32), gain_ref[...]).astype(jnp.bfloat16)
    normed_ref[...] = normed
    kv_width, head_dim = kv_ref.shape[2], k_gain_ref.shape[1]
    keys = jnp.dot(normed, kv_ref[0], preferred_element_type=jnp.float32)
    for start in range(0, kv_width, head_dim):
        head = rms_rows(keys[:, start : start + head_dim], k_gain_ref[...])
        out_ref[:, start : start + head_dim] = head.astype(jnp.bfloat16)
    values = jnp.dot(normed, kv_ref[1], preferred_element_type=jnp.float32)
    out_ref[:, kv_width : 2 * kv_width] = values.astype(jnp.bfloat16)
    coded = jnp.concatenate([ids_ref[...], gates_ref[...] // 64, gates_ref[...] % 64], axis=0)
    count = coded.shape[0]
    spread = lax.broadcasted_iota(jnp.int32, (count, LANES), 0)
    spread = spread == lax.broadcasted_iota(jnp.int32, (count, LANES), 1)
    out_ref[:, 2 * kv_width :] = lax.dot_general(
        coded.astype(jnp.float32).astype(jnp.bfloat16),
        spread.astype(jnp.float32).astype(jnp.bfloat16),
        (((0,), (0,)), ((), ())),
        preferred_element_type=jnp.float32,
    ).astype(jnp.bfloat16)


def prepare(tokens, attn_gain, w_keyval, k_gain, ids, gates):
    rows, width = tokens.shape
    operands = [
        pltpu.with_memory_space_constraint(one, pltpu.HBM)
        for one in (tokens, attn_gain[None], w_keyval, k_gain[None], ids.T, gates.T)
    ]
    return pl.pallas_call(
        prepare_kernel,
        out_shape=[
            jax.ShapeDtypeStruct((rows, width), jnp.bfloat16),
            jax.ShapeDtypeStruct((rows, 2 * w_keyval.shape[2] + LANES), jnp.bfloat16),
        ],
        in_specs=[pl.BlockSpec(memory_space=pltpu.HBM)] * len(operands),
        scratch_shapes=[pltpu.VMEM(one.shape, one.dtype) for one in operands]
        + [pltpu.SemaphoreType.DMA((len(operands),))],
        compiler_params=pltpu.CompilerParams(vmem_limit_bytes=8 * 1024 * 1024),
        cost_estimate=pl.CostEstimate(
            flops=4 * rows * width * w_keyval.shape[2],
            bytes_accessed=4 * width * w_keyval.shape[2] + 4 * rows * width,
            transcendentals=rows,
        ),
        name="prepare",
    )(*operands)


def queries_kernel(first_ref, second_ref, third_ref, fourth_ref, weight_ref, gain_ref, out_ref):
    rows, head_dim = first_ref.shape[0], gain_ref.shape[1]
    refs = (first_ref, second_ref, third_ref, fourth_ref)
    held = jnp.concatenate([ref[...] for ref in refs], axis=0)
    raw = jnp.dot(held, weight_ref[...], preferred_element_type=jnp.float32)
    for start in range(0, weight_ref.shape[1], head_dim):
        head = rms_rows(raw[:, start : start + head_dim], gain_ref[...])
        out_ref[:, start : start + head_dim] = head.astype(jnp.bfloat16)


def make_queries(blocks, w_query, q_gain):
    rows, width = len(blocks) * blocks[0].shape[0], w_query.shape[1]
    return pl.pallas_call(
        queries_kernel,
        out_shape=jax.ShapeDtypeStruct((rows, width), jnp.bfloat16),
        compiler_params=pltpu.CompilerParams(vmem_limit_bytes=8 * 1024 * 1024),
        cost_estimate=pl.CostEstimate(
            flops=2 * rows * width * w_query.shape[0],
            bytes_accessed=2 * width * w_query.shape[0],
            transcendentals=rows,
        ),
        name="queries",
    )(*blocks, w_query, q_gain[None])


def attend_kernel(head_dim, query_ref, near_ref, far_ref, weight_ref, kept_ref, leaving_ref, held_ref):
    keys = [ref[:, :head_dim] for ref in (near_ref, far_ref)]
    values = [ref[:, head_dim:] for ref in (near_ref, far_ref)]
    for start in range(0, query_ref.shape[1], head_dim):
        query = query_ref[:, start : start + head_dim]
        scores = [
            lax.dot_general(
                query, key, (((1,), (1,)), ((), ())), preferred_element_type=jnp.float32
            )
            * head_dim ** (-0.5)
            for key in keys
        ]
        row_max = jnp.maximum(
            jnp.max(scores[0], axis=1, keepdims=True), jnp.max(scores[1], axis=1, keepdims=True)
        )
        denom, total = 0.0, 0.0
        for score, value in zip(scores, values):
            weights = jnp.exp(score - row_max)
            denom = denom + jnp.sum(weights, axis=1, keepdims=True)
            total = total + jnp.dot(
                weights.astype(jnp.bfloat16), value, preferred_element_type=jnp.float32
            )
        held_ref[:, start : start + head_dim] = (total / denom).astype(jnp.bfloat16)
    cut = kept_ref.shape[0]
    for column in range(0, weight_ref.shape[1], 2 * TILE):
        columns = slice(column, column + 2 * TILE)
        partial = jnp.dot(held_ref[...], weight_ref[:, columns], preferred_element_type=jnp.float32)
        kept_ref[:, columns] = partial[:cut]
        leaving_ref[:, columns] = partial[cut:]


def attend(queries, near_kv, far_kv, w_out, head_dim):
    rows, width = queries.shape
    keys = 2 * near_kv.shape[0]
    half = jax.ShapeDtypeStruct((rows // 2, w_out.shape[1]), jnp.float32)
    return pl.pallas_call(
        lambda *refs: attend_kernel(head_dim, *refs),
        out_shape=[half, half],
        scratch_shapes=[pltpu.VMEM((rows, width), jnp.bfloat16)],
        compiler_params=pltpu.CompilerParams(vmem_limit_bytes=12 * 1024 * 1024),
        cost_estimate=pl.CostEstimate(
            flops=4 * rows * width * keys + 2 * rows * width * w_out.shape[1],
            bytes_accessed=2 * width * w_out.shape[1] + 4 * rows * w_out.shape[1],
            transcendentals=rows * keys * width // head_dim,
        ),
        name="attend",
    )(queries, near_kv, far_kv, w_out)


def tables_kernel(top_count, expert_ref, coded_ref, pick_ref, place_ref, share_ref):
    groups, rows, lanes = coded_ref.shape
    slots = place_ref.shape[3]
    lane = lax.broadcasted_iota(jnp.int32, (rows, lanes), 1)
    source = lax.broadcasted_iota(jnp.int32, (lanes, lanes), 0)
    target = lax.broadcasted_iota(jnp.int32, (lanes, lanes), 1)
    joined = jnp.where(source == target + top_count, 64.0, 0.0)
    joined = joined + jnp.where(source == target + 2 * top_count, 1.0, 0.0)
    joined = jnp.where(target < top_count, joined, 0.0).astype(jnp.bfloat16)
    first = lax.broadcasted_iota(jnp.int32, (rows, rows), 0)
    second = lax.broadcasted_iota(jnp.int32, (rows, rows), 1)
    later = jnp.where(first < second, 1.0, 0.0).astype(jnp.bfloat16)
    earlier = jnp.where(second < first, 1.0, 0.0).astype(jnp.bfloat16)
    ones = jnp.ones((8, lanes), jnp.bfloat16)
    slot_row = lax.broadcasted_iota(jnp.int32, (slots, rows), 0).astype(jnp.float32)
    slot_lane = lax.broadcasted_iota(jnp.int32, (rows, slots), 1).astype(jnp.float32)
    for group in range(groups):
        coded = coded_ref[group]
        gates = jnp.dot(coded, joined, preferred_element_type=jnp.float32)
        gate_sum = jnp.sum(gates, axis=1, keepdims=True)
        named = coded.astype(jnp.float32).astype(jnp.int32)
        for number in range(2):
            expert = expert_ref[0] ^ (number * PAIR)
            hits = jnp.where((named == expert) & (lane < top_count), 1.0, 0.0)
            share_ref[group, :, number : number + 1] = (
                jnp.sum(hits * gates, axis=1, keepdims=True) / gate_sum
            )
            hit = jnp.sum(hits, axis=1, keepdims=True)
            held = jnp.broadcast_to(hit, (rows, lanes)).astype(jnp.bfloat16)
            rank = jnp.dot(earlier, held, preferred_element_type=jnp.float32)[:, :1]
            rank = jnp.where(hit > 0.0, rank, -1.0)
            place_ref[number, group] = jnp.where(rank == slot_lane, 1.0, 0.0).astype(jnp.bfloat16)
            hit_row = lax.dot_general(
                ones,
                hits.astype(jnp.bfloat16),
                (((1,), (1,)), ((), ())),
                preferred_element_type=jnp.float32,
            )
            rank_row = jnp.dot(
                hit_row.astype(jnp.bfloat16), later, preferred_element_type=jnp.float32
            )
            rank_row = jnp.where(hit_row > 0.0, rank_row, -1.0)[:1]
            pick_ref[group, number * slots : (number + 1) * slots] = jnp.where(
                rank_row == slot_row, 1.0, 0.0
            ).astype(jnp.bfloat16)


def make_tables(coded, expert, slots, top_count):
    groups, rows, lanes = coded.shape
    return pl.pallas_call(
        lambda *refs: tables_kernel(top_count, *refs),
        out_shape=[
            jax.ShapeDtypeStruct((groups, 2 * slots, rows), jnp.bfloat16),
            jax.ShapeDtypeStruct((2, groups, rows, slots), jnp.bfloat16),
            jax.ShapeDtypeStruct((groups, rows, 2), jnp.float32),
        ],
        in_specs=[
            pl.BlockSpec(memory_space=pltpu.SMEM),
            pl.BlockSpec(memory_space=pltpu.VMEM),
        ],
        compiler_params=pltpu.CompilerParams(vmem_limit_bytes=24 * 1024 * 1024),
        cost_estimate=pl.CostEstimate(
            flops=4 * groups * rows * rows * lanes,
            bytes_accessed=8 * groups * rows * slots,
            transcendentals=0,
        ),
        name="tables",
    )(expert.astype(jnp.int32)[None], coded)


def expert_kernel(first, spots, cuts, *refs):
    pick_ref, place_ref, share_ref, own_gu_ref, far_gu_ref, own_dn_ref, far_dn_ref = refs[:7]
    group_rows, slots = place_ref.shape[2:]
    groups = len(cuts)
    piece_refs = refs[7 : 7 + len(spots)]
    out_refs = refs[7 + len(spots) : 7 + len(spots) + 2 * sum(cuts)]
    x_buf, xs_buf, gu_buf, dn_buf, hid_buf, served_buf, y_buf, x_sem, w_sem, y_sem = refs[
        7 + len(spots) + len(out_refs) :
    ]
    width = x_buf.shape[2]
    half = width // 2
    hidden = own_dn_ref.shape[0]
    tiles = hidden // TILE

    row_copies = []
    for number, ((group, row, column), piece) in enumerate(zip(spots, piece_refs)):
        rows, columns = piece.shape
        target = x_buf.at[group, pl.ds(row, rows), pl.ds(column, columns)]
        row_copies.append((group, pltpu.make_async_copy(piece, target, x_sem.at[number])))
    weight_copies = []
    for expert, (gu_ref, dn_ref) in enumerate(((own_gu_ref, own_dn_ref), (far_gu_ref, far_dn_ref))):
        mine = []
        for tile in range(tiles):
            for side in range(2):
                mine.append(
                    pltpu.make_async_copy(
                        gu_ref.at[:, pl.ds(side * hidden + tile * TILE, TILE)],
                        gu_buf.at[expert, tile, side],
                        w_sem.at[expert, 2 * tile + side],
                    )
                )
        mine.append(pltpu.make_async_copy(dn_ref, dn_buf.at[expert], w_sem.at[expert, 2 * tiles]))
        weight_copies.append(mine)
    for _, copy in row_copies:
        copy.start()
    for mine in weight_copies:
        for copy in mine:
            copy.start()

    for group in range(groups):
        for where, copy in row_copies:
            if where == group:
                copy.wait()
        chosen = jnp.dot(
            pick_ref[first + group], x_buf[group], preferred_element_type=jnp.float32
        ).astype(jnp.bfloat16)
        xs_buf[0, pl.ds(group * slots, slots)] = chosen[:slots]
        xs_buf[1, pl.ds(group * slots, slots)] = chosen[slots:]

    for expert in range(2):
        for tile in range(tiles):
            weight_copies[expert][2 * tile].wait()
            weight_copies[expert][2 * tile + 1].wait()
            gate = jnp.dot(
                xs_buf[expert], gu_buf[expert, tile, 0], preferred_element_type=jnp.float32
            )
            up = jnp.dot(
                xs_buf[expert], gu_buf[expert, tile, 1], preferred_element_type=jnp.float32
            )
            value = gate / (1.0 + jnp.exp(-gate)) * up
            hid_buf[:, tile * TILE : (tile + 1) * TILE] = value.astype(jnp.bfloat16)
        weight_copies[expert][2 * tiles].wait()
        for column in range(0, width, 2 * TILE):
            served_buf[expert, :, column : column + 2 * TILE] = jnp.dot(
                hid_buf[...],
                dn_buf[expert, :, column : column + 2 * TILE],
                preferred_element_type=jnp.float32,
            ).astype(jnp.bfloat16)

    out_copies = []
    for group in range(groups):
        for column in range(0, width, 2 * TILE):
            total = None
            for expert in range(2):
                placed = jnp.dot(
                    place_ref[expert, first + group],
                    served_buf[expert, pl.ds(group * slots, slots), column : column + 2 * TILE],
                    preferred_element_type=jnp.float32,
                )
                term = placed * share_ref[first + group, :, expert : expert + 1]
                total = term if total is None else total + term
            y_buf[group, :, column : column + 2 * TILE] = total.astype(jnp.bfloat16)
        cut = group_rows // cuts[group]
        for number in range(2 * cuts[group]):
            row, side = divmod(number, 2)
            done = len(out_copies)
            copy = pltpu.make_async_copy(
                y_buf.at[group, pl.ds(row * cut, cut), pl.ds(side * half, half)],
                out_refs[done],
                y_sem.at[done],
            )
            copy.start()
            out_copies.append(copy)
    for copy in out_copies:
        copy.wait()


def run_experts(first, pieces, cuts, pick, place, share, weights):
    group_rows, slots = place.shape[2:]
    groups = len(pieces)
    hidden, width = weights[2].shape
    tiles = hidden // TILE
    spots = [
        (group, row, column) for group, held in enumerate(pieces) for row, column, _ in held
    ]
    arrays = [array for held in pieces for _, _, array in held]
    anywhere = pl.BlockSpec(memory_space=pl.ANY)
    stored = pl.BlockSpec(memory_space=pltpu.HBM)
    inside = pl.BlockSpec(memory_space=pltpu.VMEM)
    outs = pl.pallas_call(
        lambda *refs: expert_kernel(first, spots, cuts, *refs),
        out_shape=[
            jax.ShapeDtypeStruct((group_rows // cut, width // 2), jnp.bfloat16)
            for cut in cuts
            for _ in range(2 * cut)
        ],
        in_specs=[inside] * 3 + [stored] * 4 + [anywhere] * len(arrays),
        out_specs=[anywhere] * (2 * sum(cuts)),
        scratch_shapes=[
            pltpu.VMEM((groups, group_rows, width), jnp.bfloat16),
            pltpu.VMEM((2, groups * slots, width), jnp.bfloat16),
            pltpu.VMEM((2, tiles, 2, width, TILE), jnp.bfloat16),
            pltpu.VMEM((2, hidden, width), jnp.bfloat16),
            pltpu.VMEM((groups * slots, hidden), jnp.bfloat16),
            pltpu.VMEM((2, groups * slots, width), jnp.bfloat16),
            pltpu.VMEM((groups, group_rows, width), jnp.bfloat16),
            pltpu.SemaphoreType.DMA((len(arrays),)),
            pltpu.SemaphoreType.DMA((2, 2 * tiles + 1)),
            pltpu.SemaphoreType.DMA((2 * sum(cuts),)),
        ],
        compiler_params=pltpu.CompilerParams(vmem_limit_bytes=(28 + 6 * group_rows // 256) * 1024 * 1024),
        cost_estimate=pl.CostEstimate(
            flops=12 * groups * slots * width * hidden,
            bytes_accessed=12 * width * hidden + 4 * groups * group_rows * width,
            transcendentals=2 * groups * slots * hidden,
        ),
        name="experts",
    )(pick, place, share, *weights, *arrays)
    return list(zip(outs[0::2], outs[1::2]))


def per_device(
    hidden_in,
    attn_gain,
    w_query,
    w_keyval,
    q_gain,
    k_gain,
    w_out,
    moe_gain,
    expert_ids,
    gate_fixed,
    w_gateup,
    w_down,
):
    tokens = hidden_in[0].astype(jnp.float32)
    row_count, model_width = tokens.shape
    head_dim = q_gain.shape[0]
    local_heads = w_query.shape[1] // head_dim
    kv_heads = w_keyval.shape[2] // head_dim
    group_size = local_heads * lax.axis_size("rep") // kv_heads
    rep_index = lax.axis_index("rep")
    kv_width = kv_heads * head_dim
    top_count = expert_ids.shape[2]
    expert_count = lax.axis_size(EVERY)

    normed, own_payload = prepare(
        hidden_in[0], attn_gain, w_keyval, k_gain, expert_ids[0], gate_fixed[0]
    )
    across_rows = swap(normed, "rep", ACROSS)
    line = jnp.concatenate(
        [own_payload] + [swap(own_payload, "seq", bits) for bits in range(1, lax.axis_size("seq"))], axis=0
    )
    pair_rows = swap(ready(normed, line)[0], "rep", PAIR)
    corner_rows = swap(across_rows, "rep", PAIR)
    line_routes = line[:, 2 * kv_width :]

    def head_kv(rep):
        index = rep * local_heads // group_size * head_dim
        return [
            lax.dynamic_slice_in_dim(line, index, head_dim, 1),
            lax.dynamic_slice_in_dim(line, kv_width + index, head_dim, 1),
        ]

    sent = jnp.concatenate(head_kv(rep_index ^ ACROSS) + [line_routes], axis=1)
    sent, across_rows = ready(sent, across_rows)
    across = swap(sent, "rep", ACROSS)
    half_kv = jnp.concatenate(
        [jnp.concatenate(head_kv(rep_index), axis=1), across[:, : 2 * head_dim]], axis=0
    )
    pair_kv = swap(half_kv, "rep", PAIR)
    both_routes = jnp.stack([line_routes, across[:, 2 * head_dim :]])
    far_routes = swap(both_routes, "role", 1)
    coded = jnp.concatenate([both_routes[1:], far_routes[:1], far_routes[1:], both_routes[:1]])
    queries = make_queries([normed, across_rows, pair_rows, corner_rows], w_query, q_gain)
    kept, leaving = attend(queries, half_kv, pair_kv, w_out, head_dim)
    leaving, own_dn = ready(swap(leaving, "rep", PAIR), w_down[0])
    halves = kept + leaving
    far_dn, far_gu = swap(own_dn, "rep", PAIR), swap(w_gateup[0], "rep", PAIR)
    far_sum = halves[row_count:].astype(jnp.bfloat16)
    across_sum, coded, far_dn, far_gu = ready(
        swap(far_sum, "rep", ACROSS), coded, far_dn, far_gu
    )
    attended = halves[:row_count] + across_sum.astype(jnp.float32)
    mixed = tokens + attended

    moe_in = rms_rows(mixed, moe_gain).astype(jnp.bfloat16)

    capacity = max(2, 7 * row_count * top_count // (4 * expert_count))
    slots = -(-capacity * (coded.shape[1] // row_count) // 16) * 16
    rows, tables = spread_rows(
        moe_in,
        coded,
        lambda codes: make_tables(codes, lax.axis_index(EVERY), slots, top_count),
    )
    weights = [
        pltpu.with_memory_space_constraint(one, pltpu.HBM)
        for one in (w_gateup[0], far_gu, w_down[0], far_dn)
    ]

    tables = (*tables, weights)
    by_rep, by_role = run_experts(0, rows[:2], (1, 1), *tables)
    rep_low, rep_high, role_low, role_high, *held = ready(
        *by_rep, *by_role, *(array for _, _, array in rows[2])
    )
    by_rep, by_role = (rep_low, rep_high), (role_low, role_high)
    pieces = [(row, column, array) for (row, column, _), array in zip(rows[2], held)]
    *corner, near = run_experts(2, [pieces, rows[3]], (2, 1), *tables)
    routed = collect_rows(row_count, near, by_rep, by_role, corner)
    return (mixed + routed).astype(jnp.bfloat16)[None]


def solution(mesh):
    placed = (
        P("role", ("seq", "rep"), None),
        P(),
        P(None, "rep"),
        P(),
        P(),
        P(),
        P("rep", None),
        P(),
        P("role", ("seq", "rep"), None),
        P("role", ("seq", "rep"), None),
        P(("role", "seq", "rep"), None, None),
        P(("role", "seq", "rep"), None, None),
    )
    return jax.shard_map(
        per_device,
        mesh=mesh,
        in_specs=placed,
        out_specs=P("role", ("seq", "rep"), None),
        check_vma=False,
    )
```

```python
import jax
import jax.numpy as jnp
from jax import lax
from jax.experimental import pallas as pl
from jax.experimental.pallas import tpu as pltpu
from jax.sharding import PartitionSpec as P

EVERY = ("role", "seq", "rep")
PAIR = 1
ACROSS = 2
TILE = 256
LANES = 128
WINDOW = 6


def rms_rows(values_in, gain_vec):
    return (
        values_in
        * lax.rsqrt(jnp.mean(values_in * values_in, axis=-1, keepdims=True) + 1e-06)
        * gain_vec
    )


def swap(block, axis, bits):
    size = lax.axis_size(axis)
    return lax.ppermute(block, axis, [(i, i ^ bits) for i in range(size)])


def seq_bits():
    size = lax.axis_size("seq")
    return [1 << place for place in reversed(range(size.bit_length() - 1))]


def ready(*arrays):
    return lax.optimization_barrier(arrays)


def pack_kernel(*refs):
    low_ref, high_ref = refs[-2:]
    count = len(refs) // 2 - 1
    half = low_ref.shape[1]
    start = 0
    for rep_ref, role_ref in zip(refs[:count], refs[count:-2]):
        rows = pl.ds(start, rep_ref.shape[0])
        low_ref[rows] = rep_ref[:, :half]
        high_ref[rows] = role_ref[:, half:]
        start += rep_ref.shape[0]


def pack_corners(by_rep, by_role):
    rows, width = sum(part.shape[0] for part in by_rep), by_rep[0].shape[1]
    half = jax.ShapeDtypeStruct((rows, width // 2), jnp.bfloat16)
    return pl.pallas_call(
        pack_kernel,
        out_shape=[half, half],
        compiler_params=pltpu.CompilerParams(vmem_limit_bytes=(4 + rows // 64) * 1024 * 1024),
        cost_estimate=pl.CostEstimate(
            flops=0, bytes_accessed=4 * rows * width, transcendentals=0
        ),
        name="pack_corners",
    )(*by_rep, *by_role)


def spread_rows(own, coded, tables_of):
    rows, half = own.shape[0], own.shape[1] // 2

    def both_ways(part):
        return swap(part, "rep", ACROSS), swap(part, "role", 1)

    blocks = {0: own}
    for bits in seq_bits():
        blocks |= {place ^ bits: swap(block, "seq", bits) for place, block in blocks.items()}
    middle = [blocks[place] for place in range(2, len(blocks) - 1)]
    middle = jnp.concatenate(middle, axis=0) if len(middle) > 1 else middle[0]
    parts = [own, blocks[1], middle, blocks[len(blocks) - 1]]
    parts[2], coded, *early = ready(parts[2], coded, *both_ways(own), *both_ways(parts[1]))
    parts[3], *tables = ready(parts[3], *tables_of(coded))
    by_rep, by_role = zip(early[:2], early[2:], both_ways(parts[2]), both_ways(parts[3]))
    low, high = pack_corners(by_rep, by_role)
    corner_low, corner_high = swap(low, "role", 1), swap(high, "rep", ACROSS)
    starts = (0, rows, 2 * rows, 2 * rows + middle.shape[0])
    groups = [
        [(start, 0, part) for start, part in zip(starts, held)]
        for held in (by_rep, by_role, parts)
    ]
    groups.insert(2, [(0, 0, corner_low), (0, half, corner_high)])
    return groups, tables


def added(first, second):
    return (first.astype(jnp.float32) + second.astype(jnp.float32)).astype(jnp.bfloat16)


def collect_rows(row_count, near, by_rep, by_role, corner):
    straight_low = swap(by_role[0], "role", 1)
    straight_high = swap(by_rep[1], "rep", ACROSS)
    straight_low, straight_high, near_low, near_high, *corner = ready(
        straight_low, straight_high, *near, *corner[0], *corner[1]
    )
    cut = near_low.shape[0] // 2
    halves = slice(0, cut), slice(cut, None)

    def merged(rows, turned_low, turned_high):
        return jnp.concatenate(
            [
                base[rows].astype(jnp.float32)
                + first[rows].astype(jnp.float32)
                + second.astype(jnp.float32)
                for base, first, second in (
                    (near_low, straight_low, turned_low),
                    (near_high, straight_high, turned_high),
                )
            ],
            axis=1,
        )

    def corners(number):
        low, high = corner[2 * number : 2 * number + 2]
        return swap(low, "role", 1), swap(high, "rep", ACROSS)

    def sums(number, corner_low, corner_high):
        rows = halves[number]
        return added(by_rep[0][rows], corner_low), added(by_role[1][rows], corner_high)

    def turned(low, high):
        return swap(low, "rep", ACROSS), swap(high, "role", 1)

    far_corner, beside_corner = corners(1), corners(0)
    *far, corner_low, corner_high = ready(*turned(*sums(1, *far_corner)), *beside_corner)
    upper = merged(halves[1], *far)
    *near_sums, upper = ready(*sums(0, corner_low, corner_high), upper)
    lower = merged(halves[0], *turned(*near_sums))
    top_bits, *low_bits = seq_bits()

    def folded(rows):
        for bits in reversed(low_bits):
            pairs = rows.reshape(-1, 2, row_count, rows.shape[1])
            leaving = pairs[:, 1].astype(jnp.bfloat16).reshape(-1, rows.shape[1])
            kept = pairs[:, 0].reshape(-1, rows.shape[1]).astype(jnp.float32)
            rows = kept + swap(leaving, "seq", bits).astype(jnp.float32)
        return rows

    upper = folded(upper).astype(jnp.bfloat16)
    return folded(lower) + swap(upper, "seq", top_bits).astype(jnp.float32)


def prepare_kernel(*refs):
    tokens_in, gain_in, kv_in, k_gain_in, ids_in, gates_in, normed_ref, out_ref = refs[:8]
    held, sem = refs[8:14], refs[14]
    sources = (tokens_in, gain_in, kv_in, k_gain_in, ids_in, gates_in)
    copies = [
        pltpu.make_async_copy(src, dst, sem.at[number])
        for number, (src, dst) in enumerate(zip(sources, held))
    ]
    for copy in copies:
        copy.start()
    for copy in copies:
        copy.wait()
    tokens_ref, gain_ref, kv_ref, k_gain_ref, ids_ref, gates_ref = held
    normed = rms_rows(tokens_ref[...].astype(jnp.float32), gain_ref[...]).astype(jnp.bfloat16)
    normed_ref[...] = normed
    kv_width, head_dim = kv_ref.shape[2], k_gain_ref.shape[1]
    keys = jnp.dot(normed, kv_ref[0], preferred_element_type=jnp.float32)
    for start in range(0, kv_width, head_dim):
        head = rms_rows(keys[:, start : start + head_dim], k_gain_ref[...])
        out_ref[:, start : start + head_dim] = head.astype(jnp.bfloat16)
    values = jnp.dot(normed, kv_ref[1], preferred_element_type=jnp.float32)
    out_ref[:, kv_width : 2 * kv_width] = values.astype(jnp.bfloat16)
    coded = jnp.concatenate([ids_ref[...], gates_ref[...] // 64, gates_ref[...] % 64], axis=0)
    count = coded.shape[0]
    spread = lax.broadcasted_iota(jnp.int32, (count, LANES), 0)
    spread = spread == lax.broadcasted_iota(jnp.int32, (count, LANES), 1)
    out_ref[:, 2 * kv_width :] = lax.dot_general(
        coded.astype(jnp.float32).astype(jnp.bfloat16),
        spread.astype(jnp.float32).astype(jnp.bfloat16),
        (((0,), (0,)), ((), ())),
        preferred_element_type=jnp.float32,
    ).astype(jnp.bfloat16)


def prepare(tokens, attn_gain, w_keyval, k_gain, ids, gates):
    rows, width = tokens.shape
    operands = [
        pltpu.with_memory_space_constraint(one, pltpu.HBM)
        for one in (tokens, attn_gain[None], w_keyval, k_gain[None], ids.T, gates.T)
    ]
    return pl.pallas_call(
        prepare_kernel,
        out_shape=[
            jax.ShapeDtypeStruct((rows, width), jnp.bfloat16),
            jax.ShapeDtypeStruct((rows, 2 * w_keyval.shape[2] + LANES), jnp.bfloat16),
        ],
        in_specs=[pl.BlockSpec(memory_space=pltpu.HBM)] * len(operands),
        scratch_shapes=[pltpu.VMEM(one.shape, one.dtype) for one in operands]
        + [pltpu.SemaphoreType.DMA((len(operands),))],
        compiler_params=pltpu.CompilerParams(vmem_limit_bytes=8 * 1024 * 1024),
        cost_estimate=pl.CostEstimate(
            flops=4 * rows * width * w_keyval.shape[2],
            bytes_accessed=4 * width * w_keyval.shape[2] + 4 * rows * width,
            transcendentals=rows,
        ),
        name="prepare",
    )(*operands)


def queries_kernel(first_ref, second_ref, third_ref, fourth_ref, weight_ref, gain_ref, out_ref):
    rows, head_dim = first_ref.shape[0], gain_ref.shape[1]
    refs = (first_ref, second_ref, third_ref, fourth_ref)
    held = jnp.concatenate([ref[...] for ref in refs], axis=0)
    raw = jnp.dot(held, weight_ref[...], preferred_element_type=jnp.float32)
    for start in range(0, weight_ref.shape[1], head_dim):
        head = rms_rows(raw[:, start : start + head_dim], gain_ref[...])
        out_ref[:, start : start + head_dim] = head.astype(jnp.bfloat16)


def make_queries(blocks, w_query, q_gain):
    rows, width = len(blocks) * blocks[0].shape[0], w_query.shape[1]
    return pl.pallas_call(
        queries_kernel,
        out_shape=jax.ShapeDtypeStruct((rows, width), jnp.bfloat16),
        compiler_params=pltpu.CompilerParams(vmem_limit_bytes=8 * 1024 * 1024),
        cost_estimate=pl.CostEstimate(
            flops=2 * rows * width * w_query.shape[0],
            bytes_accessed=2 * width * w_query.shape[0],
            transcendentals=rows,
        ),
        name="queries",
    )(*blocks, w_query, q_gain[None])


def attend_kernel(head_dim, query_ref, near_ref, far_ref, weight_ref, kept_ref, leaving_ref, held_ref):
    keys = [ref[:, :head_dim] for ref in (near_ref, far_ref)]
    values = [ref[:, head_dim:] for ref in (near_ref, far_ref)]
    for start in range(0, query_ref.shape[1], head_dim):
        query = query_ref[:, start : start + head_dim]
        scores = [
            lax.dot_general(
                query, key, (((1,), (1,)), ((), ())), preferred_element_type=jnp.float32
            )
            * head_dim ** (-0.5)
            for key in keys
        ]
        row_max = jnp.maximum(
            jnp.max(scores[0], axis=1, keepdims=True), jnp.max(scores[1], axis=1, keepdims=True)
        )
        denom, total = 0.0, 0.0
        for score, value in zip(scores, values):
            weights = jnp.exp(score - row_max)
            denom = denom + jnp.sum(weights, axis=1, keepdims=True)
            total = total + jnp.dot(
                weights.astype(jnp.bfloat16), value, preferred_element_type=jnp.float32
            )
        held_ref[:, start : start + head_dim] = (total / denom).astype(jnp.bfloat16)
    cut = kept_ref.shape[0]
    for column in range(0, weight_ref.shape[1], 2 * TILE):
        columns = slice(column, column + 2 * TILE)
        partial = jnp.dot(held_ref[...], weight_ref[:, columns], preferred_element_type=jnp.float32)
        kept_ref[:, columns] = partial[:cut]
        leaving_ref[:, columns] = partial[cut:]


def attend(queries, near_kv, far_kv, w_out, head_dim):
    rows, width = queries.shape
    keys = 2 * near_kv.shape[0]
    half = jax.ShapeDtypeStruct((rows // 2, w_out.shape[1]), jnp.float32)
    return pl.pallas_call(
        lambda *refs: attend_kernel(head_dim, *refs),
        out_shape=[half, half],
        scratch_shapes=[pltpu.VMEM((rows, width), jnp.bfloat16)],
        compiler_params=pltpu.CompilerParams(vmem_limit_bytes=12 * 1024 * 1024),
        cost_estimate=pl.CostEstimate(
            flops=4 * rows * width * keys + 2 * rows * width * w_out.shape[1],
            bytes_accessed=2 * width * w_out.shape[1] + 4 * rows * w_out.shape[1],
            transcendentals=rows * keys * width // head_dim,
        ),
        name="attend",
    )(queries, near_kv, far_kv, w_out)


def tables_kernel(top_count, expert_ref, coded_ref, pick_ref, place_ref, share_ref):
    groups, rows, lanes = coded_ref.shape
    slots = place_ref.shape[3]
    lane = lax.broadcasted_iota(jnp.int32, (rows, lanes), 1)
    source = lax.broadcasted_iota(jnp.int32, (lanes, lanes), 0)
    target = lax.broadcasted_iota(jnp.int32, (lanes, lanes), 1)
    joined = jnp.where(source == target + top_count, 64.0, 0.0)
    joined = joined + jnp.where(source == target + 2 * top_count, 1.0, 0.0)
    joined = jnp.where(target < top_count, joined, 0.0).astype(jnp.bfloat16)
    first = lax.broadcasted_iota(jnp.int32, (rows, rows), 0)
    second = lax.broadcasted_iota(jnp.int32, (rows, rows), 1)
    later = jnp.where(first < second, 1.0, 0.0).astype(jnp.bfloat16)
    earlier = jnp.where(second < first, 1.0, 0.0).astype(jnp.bfloat16)
    ones = jnp.ones((8, lanes), jnp.bfloat16)
    slot_row = lax.broadcasted_iota(jnp.int32, (slots, rows), 0).astype(jnp.float32)
    slot_lane = lax.broadcasted_iota(jnp.int32, (rows, slots), 1).astype(jnp.float32)
    for group in range(groups):
        coded = coded_ref[group]
        gates = jnp.dot(coded, joined, preferred_element_type=jnp.float32)
        gate_sum = jnp.sum(gates, axis=1, keepdims=True)
        named = coded.astype(jnp.float32).astype(jnp.int32)
        for number in range(2):
            expert = expert_ref[0] ^ (number * PAIR)
            hits = jnp.where((named == expert) & (lane < top_count), 1.0, 0.0)
            share_ref[group, :, number : number + 1] = (
                jnp.sum(hits * gates, axis=1, keepdims=True) / gate_sum
            )
            hit = jnp.sum(hits, axis=1, keepdims=True)
            held = jnp.broadcast_to(hit, (rows, lanes)).astype(jnp.bfloat16)
            rank = jnp.dot(earlier, held, preferred_element_type=jnp.float32)[:, :1]
            rank = jnp.where(hit > 0.0, rank, -1.0)
            place_ref[number, group] = jnp.where(rank == slot_lane, 1.0, 0.0).astype(jnp.bfloat16)
            hit_row = lax.dot_general(
                ones,
                hits.astype(jnp.bfloat16),
                (((1,), (1,)), ((), ())),
                preferred_element_type=jnp.float32,
            )
            rank_row = jnp.dot(
                hit_row.astype(jnp.bfloat16), later, preferred_element_type=jnp.float32
            )
            rank_row = jnp.where(hit_row > 0.0, rank_row, -1.0)[:1]
            pick_ref[group, number * slots : (number + 1) * slots] = jnp.where(
                rank_row == slot_row, 1.0, 0.0
            ).astype(jnp.bfloat16)


def make_tables(coded, expert, slots, top_count):
    groups, rows, lanes = coded.shape
    return pl.pallas_call(
        lambda *refs: tables_kernel(top_count, *refs),
        out_shape=[
            jax.ShapeDtypeStruct((groups, 2 * slots, rows), jnp.bfloat16),
            jax.ShapeDtypeStruct((2, groups, rows, slots), jnp.bfloat16),
            jax.ShapeDtypeStruct((groups, rows, 2), jnp.float32),
        ],
        in_specs=[
            pl.BlockSpec(memory_space=pltpu.SMEM),
            pl.BlockSpec(memory_space=pltpu.VMEM),
        ],
        compiler_params=pltpu.CompilerParams(vmem_limit_bytes=24 * 1024 * 1024),
        cost_estimate=pl.CostEstimate(
            flops=4 * groups * rows * rows * lanes,
            bytes_accessed=8 * groups * rows * slots,
            transcendentals=0,
        ),
        name="tables",
    )(expert.astype(jnp.int32)[None], coded)


def expert_kernel(first, spots, cuts, *refs):
    pick_ref, place_ref, share_ref, own_gu_ref, far_gu_ref, own_dn_ref, far_dn_ref = refs[:7]
    group_rows, slots = place_ref.shape[2:]
    groups = len(cuts)
    piece_refs = refs[7 : 7 + len(spots)]
    out_refs = refs[7 + len(spots) : 7 + len(spots) + 2 * sum(cuts)]
    x_buf, xs_buf, gu_buf, dn_buf, hid_buf, served_buf, y_buf, x_sem, w_sem, y_sem = refs[
        7 + len(spots) + len(out_refs) :
    ]
    width = x_buf.shape[2]
    half = width // 2
    hidden = own_dn_ref.shape[0]
    tiles = hidden // TILE

    row_copies = []
    for number, ((group, row, column), piece) in enumerate(zip(spots, piece_refs)):
        rows, columns = piece.shape
        target = x_buf.at[group, pl.ds(row, rows), pl.ds(column, columns)]
        row_copies.append((group, pltpu.make_async_copy(piece, target, x_sem.at[number])))
    weight_copies = []
    for expert, (gu_ref, dn_ref) in enumerate(((own_gu_ref, own_dn_ref), (far_gu_ref, far_dn_ref))):
        mine = []
        for tile in range(tiles):
            for side in range(2):
                mine.append(
                    pltpu.make_async_copy(
                        gu_ref.at[:, pl.ds(side * hidden + tile * TILE, TILE)],
                        gu_buf.at[expert, tile, side],
                        w_sem.at[expert, 2 * tile + side],
                    )
                )
        mine.append(pltpu.make_async_copy(dn_ref, dn_buf.at[expert], w_sem.at[expert, 2 * tiles]))
        weight_copies.append(mine)
    waiting = [copy for mine in weight_copies for copy in mine]

    def arrived(copy):
        copy.wait()
        if waiting:
            waiting.pop(0).start()

    for _, copy in row_copies:
        copy.start()
    for _ in range(WINDOW):
        waiting.pop(0).start()

    for group in range(groups):
        for where, copy in row_copies:
            if where == group:
                copy.wait()
        chosen = jnp.dot(
            pick_ref[first + group], x_buf[group], preferred_element_type=jnp.float32
        ).astype(jnp.bfloat16)
        xs_buf[0, pl.ds(group * slots, slots)] = chosen[:slots]
        xs_buf[1, pl.ds(group * slots, slots)] = chosen[slots:]

    for expert in range(2):
        for tile in range(tiles):
            arrived(weight_copies[expert][2 * tile])
            arrived(weight_copies[expert][2 * tile + 1])
            gate = jnp.dot(
                xs_buf[expert], gu_buf[expert, tile, 0], preferred_element_type=jnp.float32
            )
            up = jnp.dot(
                xs_buf[expert], gu_buf[expert, tile, 1], preferred_element_type=jnp.float32
            )
            value = gate / (1.0 + jnp.exp(-gate)) * up
            hid_buf[:, tile * TILE : (tile + 1) * TILE] = value.astype(jnp.bfloat16)
        arrived(weight_copies[expert][2 * tiles])
        for column in range(0, width, 2 * TILE):
            served_buf[expert, :, column : column + 2 * TILE] = jnp.dot(
                hid_buf[...],
                dn_buf[expert, :, column : column + 2 * TILE],
                preferred_element_type=jnp.float32,
            ).astype(jnp.bfloat16)

    out_copies = []
    for group in range(groups):
        for column in range(0, width, 2 * TILE):
            total = None
            for expert in range(2):
                placed = jnp.dot(
                    place_ref[expert, first + group],
                    served_buf[expert, pl.ds(group * slots, slots), column : column + 2 * TILE],
                    preferred_element_type=jnp.float32,
                )
                term = placed * share_ref[first + group, :, expert : expert + 1]
                total = term if total is None else total + term
            y_buf[group, :, column : column + 2 * TILE] = total.astype(jnp.bfloat16)
        cut = group_rows // cuts[group]
        for number in range(2 * cuts[group]):
            row, side = divmod(number, 2)
            done = len(out_copies)
            copy = pltpu.make_async_copy(
                y_buf.at[group, pl.ds(row * cut, cut), pl.ds(side * half, half)],
                out_refs[done],
                y_sem.at[done],
            )
            copy.start()
            out_copies.append(copy)
    for copy in out_copies:
        copy.wait()


def run_experts(first, pieces, cuts, pick, place, share, weights):
    group_rows, slots = place.shape[2:]
    groups = len(pieces)
    hidden, width = weights[2].shape
    tiles = hidden // TILE
    spots = [
        (group, row, column) for group, held in enumerate(pieces) for row, column, _ in held
    ]
    arrays = [array for held in pieces for _, _, array in held]
    anywhere = pl.BlockSpec(memory_space=pl.ANY)
    stored = pl.BlockSpec(memory_space=pltpu.HBM)
    inside = pl.BlockSpec(memory_space=pltpu.VMEM)
    outs = pl.pallas_call(
        lambda *refs: expert_kernel(first, spots, cuts, *refs),
        out_shape=[
            jax.ShapeDtypeStruct((group_rows // cut, width // 2), jnp.bfloat16)
            for cut in cuts
            for _ in range(2 * cut)
        ],
        in_specs=[inside] * 3 + [stored] * 4 + [anywhere] * len(arrays),
        out_specs=[anywhere] * (2 * sum(cuts)),
        scratch_shapes=[
            pltpu.VMEM((groups, group_rows, width), jnp.bfloat16),
            pltpu.VMEM((2, groups * slots, width), jnp.bfloat16),
            pltpu.VMEM((2, tiles, 2, width, TILE), jnp.bfloat16),
            pltpu.VMEM((2, hidden, width), jnp.bfloat16),
            pltpu.VMEM((groups * slots, hidden), jnp.bfloat16),
            pltpu.VMEM((2, groups * slots, width), jnp.bfloat16),
            pltpu.VMEM((groups, group_rows, width), jnp.bfloat16),
            pltpu.SemaphoreType.DMA((len(arrays),)),
            pltpu.SemaphoreType.DMA((2, 2 * tiles + 1)),
            pltpu.SemaphoreType.DMA((2 * sum(cuts),)),
        ],
        compiler_params=pltpu.CompilerParams(vmem_limit_bytes=(28 + 6 * group_rows // 256) * 1024 * 1024),
        cost_estimate=pl.CostEstimate(
            flops=12 * groups * slots * width * hidden,
            bytes_accessed=12 * width * hidden + 4 * groups * group_rows * width,
            transcendentals=2 * groups * slots * hidden,
        ),
        name="experts",
    )(pick, place, share, *weights, *arrays)
    return list(zip(outs[0::2], outs[1::2]))


def per_device(
    hidden_in,
    attn_gain,
    w_query,
    w_keyval,
    q_gain,
    k_gain,
    w_out,
    moe_gain,
    expert_ids,
    gate_fixed,
    w_gateup,
    w_down,
):
    tokens = hidden_in[0].astype(jnp.float32)
    row_count, model_width = tokens.shape
    head_dim = q_gain.shape[0]
    local_heads = w_query.shape[1] // head_dim
    kv_heads = w_keyval.shape[2] // head_dim
    group_size = local_heads * lax.axis_size("rep") // kv_heads
    rep_index = lax.axis_index("rep")
    kv_width = kv_heads * head_dim
    top_count = expert_ids.shape[2]
    expert_count = lax.axis_size(EVERY)

    normed, own_payload = prepare(
        hidden_in[0], attn_gain, w_keyval, k_gain, expert_ids[0], gate_fixed[0]
    )
    across_rows = swap(normed, "rep", ACROSS)
    line = jnp.concatenate(
        [own_payload] + [swap(own_payload, "seq", bits) for bits in range(1, lax.axis_size("seq"))], axis=0
    )
    pair_rows = swap(ready(normed, line)[0], "rep", PAIR)
    corner_rows = swap(across_rows, "rep", PAIR)
    line_routes = line[:, 2 * kv_width :]

    def head_kv(rep):
        index = rep * local_heads // group_size * head_dim
        return [
            lax.dynamic_slice_in_dim(line, index, head_dim, 1),
            lax.dynamic_slice_in_dim(line, kv_width + index, head_dim, 1),
        ]

    sent = jnp.concatenate(head_kv(rep_index ^ ACROSS) + [line_routes], axis=1)
    sent, across_rows = ready(sent, across_rows)
    across = swap(sent, "rep", ACROSS)
    half_kv = jnp.concatenate(
        [jnp.concatenate(head_kv(rep_index), axis=1), across[:, : 2 * head_dim]], axis=0
    )
    pair_kv = swap(half_kv, "rep", PAIR)
    both_routes = jnp.stack([line_routes, across[:, 2 * head_dim :]])
    far_routes = swap(both_routes, "role", 1)
    coded = jnp.concatenate([both_routes[1:], far_routes[:1], far_routes[1:], both_routes[:1]])
    queries = make_queries([normed, across_rows, pair_rows, corner_rows], w_query, q_gain)
    kept, leaving = attend(queries, half_kv, pair_kv, w_out, head_dim)
    leaving, own_dn = ready(swap(leaving, "rep", PAIR), w_down[0])
    halves = kept + leaving
    far_dn, far_gu = swap(own_dn, "rep", PAIR), swap(w_gateup[0], "rep", PAIR)
    far_sum = halves[row_count:].astype(jnp.bfloat16)
    across_sum, coded, far_dn, far_gu = ready(
        swap(far_sum, "rep", ACROSS), coded, far_dn, far_gu
    )
    attended = halves[:row_count] + across_sum.astype(jnp.float32)
    mixed = tokens + attended

    moe_in = rms_rows(mixed, moe_gain).astype(jnp.bfloat16)

    capacity = max(2, 7 * row_count * top_count // (4 * expert_count))
    slots = -(-capacity * (coded.shape[1] // row_count) // 16) * 16
    rows, tables = spread_rows(
        moe_in,
        coded,
        lambda codes: make_tables(codes, lax.axis_index(EVERY), slots, top_count),
    )
    weights = [
        pltpu.with_memory_space_constraint(one, pltpu.HBM)
        for one in (w_gateup[0], far_gu, w_down[0], far_dn)
    ]

    tables = (*tables, weights)
    by_rep, by_role = run_experts(0, rows[:2], (1, 1), *tables)
    rep_low, rep_high, role_low, role_high, *held = ready(
        *by_rep, *by_role, *(array for _, _, array in rows[2])
    )
    by_rep, by_role = (rep_low, rep_high), (role_low, role_high)
    pieces = [(row, column, array) for (row, column, _), array in zip(rows[2], held)]
    *corner, near = run_experts(2, [pieces, rows[3]], (2, 1), *tables)
    routed = collect_rows(row_count, near, by_rep, by_role, corner)
    return (mixed + routed).astype(jnp.bfloat16)[None]


def solution(mesh):
    placed = (
        P("role", ("seq", "rep"), None),
        P(),
        P(None, "rep"),
        P(),
        P(),
        P(),
        P("rep", None),
        P(),
        P("role", ("seq", "rep"), None),
        P("role", ("seq", "rep"), None),
        P(("role", "seq", "rep"), None, None),
        P(("role", "seq", "rep"), None, None),
    )
    return jax.shard_map(
        per_device,
        mesh=mesh,
        in_specs=placed,
        out_specs=P("role", ("seq", "rep"), None),
        check_vma=False,
    )
```

```python
import jax
import jax.numpy as jnp
from jax import lax
from jax.experimental import pallas as pl
from jax.experimental.pallas import tpu as pltpu
from jax.sharding import PartitionSpec as P

EVERY = ("role", "seq", "rep")
PAIR = 1
ACROSS = 2
TILE = 256
LANES = 128


def rms_rows(values_in, gain_vec):
    return (
        values_in
        * lax.rsqrt(jnp.mean(values_in * values_in, axis=-1, keepdims=True) + 1e-06)
        * gain_vec
    )


def swap(block, axis, bits):
    size = lax.axis_size(axis)
    return lax.ppermute(block, axis, [(i, i ^ bits) for i in range(size)])


def seq_bits():
    size = lax.axis_size("seq")
    return [1 << place for place in reversed(range(size.bit_length() - 1))]


def ready(*arrays):
    return lax.optimization_barrier(arrays)


def pack_kernel(*refs):
    low_ref, high_ref = refs[-2:]
    count = len(refs) // 2 - 1
    half = low_ref.shape[1]
    start = 0
    for rep_ref, role_ref in zip(refs[:count], refs[count:-2]):
        rows = pl.ds(start, rep_ref.shape[0])
        low_ref[rows] = rep_ref[:, :half]
        high_ref[rows] = role_ref[:, half:]
        start += rep_ref.shape[0]


def pack_corners(by_rep, by_role):
    rows, width = sum(part.shape[0] for part in by_rep), by_rep[0].shape[1]
    half = jax.ShapeDtypeStruct((rows, width // 2), jnp.bfloat16)
    return pl.pallas_call(
        pack_kernel,
        out_shape=[half, half],
        compiler_params=pltpu.CompilerParams(vmem_limit_bytes=(4 + rows // 64) * 1024 * 1024),
        cost_estimate=pl.CostEstimate(
            flops=0, bytes_accessed=4 * rows * width, transcendentals=0
        ),
        name="pack_corners",
    )(*by_rep, *by_role)


def spread_rows(own, coded, tables_of):
    rows, half = own.shape[0], own.shape[1] // 2

    def both_ways(part):
        return swap(part, "rep", ACROSS), swap(part, "role", 1)

    blocks = {0: own}
    for bits in seq_bits():
        blocks |= {place ^ bits: swap(block, "seq", bits) for place, block in blocks.items()}
    middle = [blocks[place] for place in range(2, len(blocks) - 1)]
    middle = jnp.concatenate(middle, axis=0) if len(middle) > 1 else middle[0]
    parts = [own, blocks[1], middle, blocks[len(blocks) - 1]]
    parts[2], coded, *outer = ready(parts[2], coded, *both_ways(own))
    parts[3], *early = ready(parts[3], *both_ways(parts[1]), *tables_of(coded))
    by_rep, by_role = zip(outer, early[:2], both_ways(parts[2]), both_ways(parts[3]))
    tables = early[2:]
    low, high = pack_corners(by_rep, by_role)
    corner_low, corner_high = swap(low, "role", 1), swap(high, "rep", ACROSS)
    starts = (0, rows, 2 * rows, 2 * rows + middle.shape[0])
    groups = [
        [(start, 0, part) for start, part in zip(starts, held)]
        for held in (by_rep, by_role, parts)
    ]
    groups.insert(2, [(0, 0, corner_low), (0, half, corner_high)])
    return groups, tables


def added(first, second):
    return (first.astype(jnp.float32) + second.astype(jnp.float32)).astype(jnp.bfloat16)


def collect_rows(row_count, near, by_rep, by_role, corner):
    straight_low = swap(by_role[0], "role", 1)
    straight_high = swap(by_rep[1], "rep", ACROSS)
    straight_low, straight_high, near_low, near_high, *corner = ready(
        straight_low, straight_high, *near, *corner[0], *corner[1]
    )
    cut = near_low.shape[0] // 2
    halves = slice(0, cut), slice(cut, None)

    def merged(rows, turned_low, turned_high):
        return jnp.concatenate(
            [
                base[rows].astype(jnp.float32)
                + first[rows].astype(jnp.float32)
                + second.astype(jnp.float32)
                for base, first, second in (
                    (near_low, straight_low, turned_low),
                    (near_high, straight_high, turned_high),
                )
            ],
            axis=1,
        )

    def corners(number):
        low, high = corner[2 * number : 2 * number + 2]
        return swap(low, "role", 1), swap(high, "rep", ACROSS)

    def sums(number, corner_low, corner_high):
        rows = halves[number]
        return added(by_rep[0][rows], corner_low), added(by_role[1][rows], corner_high)

    def turned(low, high):
        return swap(low, "rep", ACROSS), swap(high, "role", 1)

    far_corner, beside_corner = corners(1), corners(0)
    *far, corner_low, corner_high = ready(*turned(*sums(1, *far_corner)), *beside_corner)
    upper = merged(halves[1], *far)
    *near_sums, upper = ready(*sums(0, corner_low, corner_high), upper)
    lower = merged(halves[0], *turned(*near_sums))
    top_bits, *low_bits = seq_bits()

    def folded(rows):
        for bits in reversed(low_bits):
            pairs = rows.reshape(-1, 2, row_count, rows.shape[1])
            leaving = pairs[:, 1].astype(jnp.bfloat16).reshape(-1, rows.shape[1])
            kept = pairs[:, 0].reshape(-1, rows.shape[1]).astype(jnp.float32)
            rows = kept + swap(leaving, "seq", bits).astype(jnp.float32)
        return rows

    upper = folded(upper).astype(jnp.bfloat16)
    return folded(lower) + swap(upper, "seq", top_bits).astype(jnp.float32)


def prepare_kernel(*refs):
    tokens_in, gain_in, kv_in, k_gain_in, ids_in, gates_in, normed_ref, out_ref = refs[:8]
    held, sem = refs[8:14], refs[14]
    sources = (tokens_in, gain_in, kv_in, k_gain_in, ids_in, gates_in)
    copies = [
        pltpu.make_async_copy(src, dst, sem.at[number])
        for number, (src, dst) in enumerate(zip(sources, held))
    ]
    for copy in copies:
        copy.start()
    for copy in copies:
        copy.wait()
    tokens_ref, gain_ref, kv_ref, k_gain_ref, ids_ref, gates_ref = held
    normed = rms_rows(tokens_ref[...].astype(jnp.float32), gain_ref[...]).astype(jnp.bfloat16)
    normed_ref[...] = normed
    kv_width, head_dim = kv_ref.shape[2], k_gain_ref.shape[1]
    keys = jnp.dot(normed, kv_ref[0], preferred_element_type=jnp.float32)
    for start in range(0, kv_width, head_dim):
        head = rms_rows(keys[:, start : start + head_dim], k_gain_ref[...])
        out_ref[:, start : start + head_dim] = head.astype(jnp.bfloat16)
    values = jnp.dot(normed, kv_ref[1], preferred_element_type=jnp.float32)
    out_ref[:, kv_width : 2 * kv_width] = values.astype(jnp.bfloat16)
    coded = jnp.concatenate([ids_ref[...], gates_ref[...] // 64, gates_ref[...] % 64], axis=0)
    count = coded.shape[0]
    spread = lax.broadcasted_iota(jnp.int32, (count, LANES), 0)
    spread = spread == lax.broadcasted_iota(jnp.int32, (count, LANES), 1)
    out_ref[:, 2 * kv_width :] = lax.dot_general(
        coded.astype(jnp.float32).astype(jnp.bfloat16),
        spread.astype(jnp.float32).astype(jnp.bfloat16),
        (((0,), (0,)), ((), ())),
        preferred_element_type=jnp.float32,
    ).astype(jnp.bfloat16)


def prepare(tokens, attn_gain, w_keyval, k_gain, ids, gates):
    rows, width = tokens.shape
    operands = [
        pltpu.with_memory_space_constraint(one, pltpu.HBM)
        for one in (tokens, attn_gain[None], w_keyval, k_gain[None], ids.T, gates.T)
    ]
    return pl.pallas_call(
        prepare_kernel,
        out_shape=[
            jax.ShapeDtypeStruct((rows, width), jnp.bfloat16),
            jax.ShapeDtypeStruct((rows, 2 * w_keyval.shape[2] + LANES), jnp.bfloat16),
        ],
        in_specs=[pl.BlockSpec(memory_space=pltpu.HBM)] * len(operands),
        scratch_shapes=[pltpu.VMEM(one.shape, one.dtype) for one in operands]
        + [pltpu.SemaphoreType.DMA((len(operands),))],
        compiler_params=pltpu.CompilerParams(vmem_limit_bytes=8 * 1024 * 1024),
        cost_estimate=pl.CostEstimate(
            flops=4 * rows * width * w_keyval.shape[2],
            bytes_accessed=4 * width * w_keyval.shape[2] + 4 * rows * width,
            transcendentals=rows,
        ),
        name="prepare",
    )(*operands)


def queries_kernel(first_ref, second_ref, third_ref, fourth_ref, weight_ref, gain_ref, out_ref):
    rows, head_dim = first_ref.shape[0], gain_ref.shape[1]
    refs = (first_ref, second_ref, third_ref, fourth_ref)
    held = jnp.concatenate([ref[...] for ref in refs], axis=0)
    raw = jnp.dot(held, weight_ref[...], preferred_element_type=jnp.float32)
    for start in range(0, weight_ref.shape[1], head_dim):
        head = rms_rows(raw[:, start : start + head_dim], gain_ref[...])
        out_ref[:, start : start + head_dim] = head.astype(jnp.bfloat16)


def make_queries(blocks, w_query, q_gain):
    rows, width = len(blocks) * blocks[0].shape[0], w_query.shape[1]
    return pl.pallas_call(
        queries_kernel,
        out_shape=jax.ShapeDtypeStruct((rows, width), jnp.bfloat16),
        compiler_params=pltpu.CompilerParams(vmem_limit_bytes=8 * 1024 * 1024),
        cost_estimate=pl.CostEstimate(
            flops=2 * rows * width * w_query.shape[0],
            bytes_accessed=2 * width * w_query.shape[0],
            transcendentals=rows,
        ),
        name="queries",
    )(*blocks, w_query, q_gain[None])


def attend_kernel(head_dim, query_ref, near_ref, far_ref, weight_ref, kept_ref, leaving_ref, held_ref):
    keys = [ref[:, :head_dim] for ref in (near_ref, far_ref)]
    values = [ref[:, head_dim:] for ref in (near_ref, far_ref)]
    for start in range(0, query_ref.shape[1], head_dim):
        query = query_ref[:, start : start + head_dim]
        scores = [
            lax.dot_general(
                query, key, (((1,), (1,)), ((), ())), preferred_element_type=jnp.float32
            )
            * head_dim ** (-0.5)
            for key in keys
        ]
        row_max = jnp.maximum(
            jnp.max(scores[0], axis=1, keepdims=True), jnp.max(scores[1], axis=1, keepdims=True)
        )
        denom, total = 0.0, 0.0
        for score, value in zip(scores, values):
            weights = jnp.exp(score - row_max)
            denom = denom + jnp.sum(weights, axis=1, keepdims=True)
            total = total + jnp.dot(
                weights.astype(jnp.bfloat16), value, preferred_element_type=jnp.float32
            )
        held_ref[:, start : start + head_dim] = (total / denom).astype(jnp.bfloat16)
    cut = kept_ref.shape[0]
    for column in range(0, weight_ref.shape[1], 2 * TILE):
        columns = slice(column, column + 2 * TILE)
        partial = jnp.dot(held_ref[...], weight_ref[:, columns], preferred_element_type=jnp.float32)
        kept_ref[:, columns] = partial[:cut]
        leaving_ref[:, columns] = partial[cut:].astype(jnp.bfloat16)


def attend(queries, near_kv, far_kv, w_out, head_dim):
    rows, width = queries.shape
    keys = 2 * near_kv.shape[0]
    half = (rows // 2, w_out.shape[1])
    return pl.pallas_call(
        lambda *refs: attend_kernel(head_dim, *refs),
        out_shape=[
            jax.ShapeDtypeStruct(half, jnp.float32),
            jax.ShapeDtypeStruct(half, jnp.bfloat16),
        ],
        scratch_shapes=[pltpu.VMEM((rows, width), jnp.bfloat16)],
        compiler_params=pltpu.CompilerParams(vmem_limit_bytes=12 * 1024 * 1024),
        cost_estimate=pl.CostEstimate(
            flops=4 * rows * width * keys + 2 * rows * width * w_out.shape[1],
            bytes_accessed=2 * width * w_out.shape[1] + 4 * rows * w_out.shape[1],
            transcendentals=rows * keys * width // head_dim,
        ),
        name="attend",
    )(queries, near_kv, far_kv, w_out)


def tables_kernel(top_count, expert_ref, coded_ref, pick_ref, place_ref, share_ref):
    groups, rows, lanes = coded_ref.shape
    slots = place_ref.shape[3]
    lane = lax.broadcasted_iota(jnp.int32, (rows, lanes), 1)
    source = lax.broadcasted_iota(jnp.int32, (lanes, lanes), 0)
    target = lax.broadcasted_iota(jnp.int32, (lanes, lanes), 1)
    joined = jnp.where(source == target + top_count, 64.0, 0.0)
    joined = joined + jnp.where(source == target + 2 * top_count, 1.0, 0.0)
    joined = jnp.where(target < top_count, joined, 0.0).astype(jnp.bfloat16)
    first = lax.broadcasted_iota(jnp.int32, (rows, rows), 0)
    second = lax.broadcasted_iota(jnp.int32, (rows, rows), 1)
    later = jnp.where(first < second, 1.0, 0.0).astype(jnp.bfloat16)
    earlier = jnp.where(second < first, 1.0, 0.0).astype(jnp.bfloat16)
    ones = jnp.ones((8, lanes), jnp.bfloat16)
    slot_row = lax.broadcasted_iota(jnp.int32, (slots, rows), 0).astype(jnp.float32)
    slot_lane = lax.broadcasted_iota(jnp.int32, (rows, slots), 1).astype(jnp.float32)
    for group in range(groups):
        coded = coded_ref[group]
        gates = jnp.dot(coded, joined, preferred_element_type=jnp.float32)
        gate_sum = jnp.sum(gates, axis=1, keepdims=True)
        named = coded.astype(jnp.float32).astype(jnp.int32)
        for number in range(2):
            expert = expert_ref[0] ^ (number * PAIR)
            hits = jnp.where((named == expert) & (lane < top_count), 1.0, 0.0)
            share_ref[group, :, number : number + 1] = (
                jnp.sum(hits * gates, axis=1, keepdims=True) / gate_sum
            )
            hit = jnp.sum(hits, axis=1, keepdims=True)
            held = jnp.broadcast_to(hit, (rows, lanes)).astype(jnp.bfloat16)
            rank = jnp.dot(earlier, held, preferred_element_type=jnp.float32)[:, :1]
            rank = jnp.where(hit > 0.0, rank, -1.0)
            place_ref[number, group] = jnp.where(rank == slot_lane, 1.0, 0.0).astype(jnp.bfloat16)
            hit_row = lax.dot_general(
                ones,
                hits.astype(jnp.bfloat16),
                (((1,), (1,)), ((), ())),
                preferred_element_type=jnp.float32,
            )
            rank_row = jnp.dot(
                hit_row.astype(jnp.bfloat16), later, preferred_element_type=jnp.float32
            )
            rank_row = jnp.where(hit_row > 0.0, rank_row, -1.0)[:1]
            pick_ref[group, number * slots : (number + 1) * slots] = jnp.where(
                rank_row == slot_row, 1.0, 0.0
            ).astype(jnp.bfloat16)


def make_tables(coded, expert, slots, top_count):
    groups, rows, lanes = coded.shape
    return pl.pallas_call(
        lambda *refs: tables_kernel(top_count, *refs),
        out_shape=[
            jax.ShapeDtypeStruct((groups, 2 * slots, rows), jnp.bfloat16),
            jax.ShapeDtypeStruct((2, groups, rows, slots), jnp.bfloat16),
            jax.ShapeDtypeStruct((groups, rows, 2), jnp.float32),
        ],
        in_specs=[
            pl.BlockSpec(memory_space=pltpu.SMEM),
            pl.BlockSpec(memory_space=pltpu.VMEM),
        ],
        compiler_params=pltpu.CompilerParams(vmem_limit_bytes=24 * 1024 * 1024),
        cost_estimate=pl.CostEstimate(
            flops=4 * groups * rows * rows * lanes,
            bytes_accessed=8 * groups * rows * slots,
            transcendentals=0,
        ),
        name="tables",
    )(expert.astype(jnp.int32)[None], coded)


def expert_kernel(first, spots, cuts, *refs):
    pick_ref, place_ref, share_ref, own_gu_ref, far_gu_ref, own_dn_ref, far_dn_ref = refs[:7]
    group_rows, slots = place_ref.shape[2:]
    groups = len(cuts)
    piece_refs = refs[7 : 7 + len(spots)]
    out_refs = refs[7 + len(spots) : 7 + len(spots) + 2 * sum(cuts)]
    x_buf, xs_buf, gu_buf, dn_buf, hid_buf, served_buf, y_buf, x_sem, w_sem, y_sem = refs[
        7 + len(spots) + len(out_refs) :
    ]
    width = x_buf.shape[2]
    half = width // 2
    hidden = own_dn_ref.shape[0]
    tiles = hidden // TILE

    row_copies = []
    for number, ((group, row, column), piece) in enumerate(zip(spots, piece_refs)):
        rows, columns = piece.shape
        target = x_buf.at[group, pl.ds(row, rows), pl.ds(column, columns)]
        row_copies.append((group, pltpu.make_async_copy(piece, target, x_sem.at[number])))
    weight_copies = []
    for expert, (gu_ref, dn_ref) in enumerate(((own_gu_ref, own_dn_ref), (far_gu_ref, far_dn_ref))):
        mine = []
        for tile in range(tiles):
            for side in range(2):
                mine.append(
                    pltpu.make_async_copy(
                        gu_ref.at[:, pl.ds(side * hidden + tile * TILE, TILE)],
                        gu_buf.at[expert, tile, side],
                        w_sem.at[expert, 2 * tile + side],
                    )
                )
        mine.append(pltpu.make_async_copy(dn_ref, dn_buf.at[expert], w_sem.at[expert, 2 * tiles]))
        weight_copies.append(mine)
    for _, copy in row_copies:
        copy.start()
    for mine in weight_copies:
        for copy in mine:
            copy.start()

    for group in range(groups):
        for where, copy in row_copies:
            if where == group:
                copy.wait()
        chosen = jnp.dot(
            pick_ref[first + group], x_buf[group], preferred_element_type=jnp.float32
        ).astype(jnp.bfloat16)
        xs_buf[0, pl.ds(group * slots, slots)] = chosen[:slots]
        xs_buf[1, pl.ds(group * slots, slots)] = chosen[slots:]

    for expert in range(2):
        for tile in range(tiles):
            weight_copies[expert][2 * tile].wait()
            weight_copies[expert][2 * tile + 1].wait()
            gate = jnp.dot(
                xs_buf[expert], gu_buf[expert, tile, 0], preferred_element_type=jnp.float32
            )
            up = jnp.dot(
                xs_buf[expert], gu_buf[expert, tile, 1], preferred_element_type=jnp.float32
            )
            value = gate / (1.0 + jnp.exp(-gate)) * up
            hid_buf[:, tile * TILE : (tile + 1) * TILE] = value.astype(jnp.bfloat16)
        weight_copies[expert][2 * tiles].wait()
        for column in range(0, width, 2 * TILE):
            served_buf[expert, :, column : column + 2 * TILE] = jnp.dot(
                hid_buf[...],
                dn_buf[expert, :, column : column + 2 * TILE],
                preferred_element_type=jnp.float32,
            ).astype(jnp.bfloat16)

    out_copies = []
    for group in range(groups):
        for column in range(0, width, 2 * TILE):
            total = None
            for expert in range(2):
                placed = jnp.dot(
                    place_ref[expert, first + group],
                    served_buf[expert, pl.ds(group * slots, slots), column : column + 2 * TILE],
                    preferred_element_type=jnp.float32,
                )
                term = placed * share_ref[first + group, :, expert : expert + 1]
                total = term if total is None else total + term
            y_buf[group, :, column : column + 2 * TILE] = total.astype(jnp.bfloat16)
        cut = group_rows // cuts[group]
        for number in range(2 * cuts[group]):
            row, side = divmod(number, 2)
            done = len(out_copies)
            copy = pltpu.make_async_copy(
                y_buf.at[group, pl.ds(row * cut, cut), pl.ds(side * half, half)],
                out_refs[done],
                y_sem.at[done],
            )
            copy.start()
            out_copies.append(copy)
    for copy in out_copies:
        copy.wait()


def run_experts(first, pieces, cuts, pick, place, share, weights):
    group_rows, slots = place.shape[2:]
    groups = len(pieces)
    hidden, width = weights[2].shape
    tiles = hidden // TILE
    spots = [
        (group, row, column) for group, held in enumerate(pieces) for row, column, _ in held
    ]
    arrays = [array for held in pieces for _, _, array in held]
    anywhere = pl.BlockSpec(memory_space=pl.ANY)
    stored = pl.BlockSpec(memory_space=pltpu.HBM)
    inside = pl.BlockSpec(memory_space=pltpu.VMEM)
    outs = pl.pallas_call(
        lambda *refs: expert_kernel(first, spots, cuts, *refs),
        out_shape=[
            jax.ShapeDtypeStruct((group_rows // cut, width // 2), jnp.bfloat16)
            for cut in cuts
            for _ in range(2 * cut)
        ],
        in_specs=[inside] * 3 + [stored] * 4 + [anywhere] * len(arrays),
        out_specs=[anywhere] * (2 * sum(cuts)),
        scratch_shapes=[
            pltpu.VMEM((groups, group_rows, width), jnp.bfloat16),
            pltpu.VMEM((2, groups * slots, width), jnp.bfloat16),
            pltpu.VMEM((2, tiles, 2, width, TILE), jnp.bfloat16),
            pltpu.VMEM((2, hidden, width), jnp.bfloat16),
            pltpu.VMEM((groups * slots, hidden), jnp.bfloat16),
            pltpu.VMEM((2, groups * slots, width), jnp.bfloat16),
            pltpu.VMEM((groups, group_rows, width), jnp.bfloat16),
            pltpu.SemaphoreType.DMA((len(arrays),)),
            pltpu.SemaphoreType.DMA((2, 2 * tiles + 1)),
            pltpu.SemaphoreType.DMA((2 * sum(cuts),)),
        ],
        compiler_params=pltpu.CompilerParams(vmem_limit_bytes=(28 + 6 * group_rows // 256) * 1024 * 1024),
        cost_estimate=pl.CostEstimate(
            flops=12 * groups * slots * width * hidden,
            bytes_accessed=12 * width * hidden + 4 * groups * group_rows * width,
            transcendentals=2 * groups * slots * hidden,
        ),
        name="experts",
    )(pick, place, share, *weights, *arrays)
    return list(zip(outs[0::2], outs[1::2]))


def per_device(
    hidden_in,
    attn_gain,
    w_query,
    w_keyval,
    q_gain,
    k_gain,
    w_out,
    moe_gain,
    expert_ids,
    gate_fixed,
    w_gateup,
    w_down,
):
    tokens = hidden_in[0].astype(jnp.float32)
    row_count, model_width = tokens.shape
    head_dim = q_gain.shape[0]
    local_heads = w_query.shape[1] // head_dim
    kv_heads = w_keyval.shape[2] // head_dim
    group_size = local_heads * lax.axis_size("rep") // kv_heads
    rep_index = lax.axis_index("rep")
    kv_width = kv_heads * head_dim
    top_count = expert_ids.shape[2]
    expert_count = lax.axis_size(EVERY)

    normed, own_payload = prepare(
        hidden_in[0], attn_gain, w_keyval, k_gain, expert_ids[0], gate_fixed[0]
    )
    across_rows = swap(normed, "rep", ACROSS)
    line = jnp.concatenate(
        [own_payload] + [swap(own_payload, "seq", bits) for bits in range(1, lax.axis_size("seq"))], axis=0
    )
    pair_rows = swap(ready(normed, line)[0], "rep", PAIR)
    corner_rows = swap(across_rows, "rep", PAIR)
    line_routes = line[:, 2 * kv_width :]

    def head_kv(rep):
        index = rep * local_heads // group_size * head_dim
        return [
            lax.dynamic_slice_in_dim(line, index, head_dim, 1),
            lax.dynamic_slice_in_dim(line, kv_width + index, head_dim, 1),
        ]

    sent = jnp.concatenate(head_kv(rep_index ^ ACROSS) + [line_routes], axis=1)
    sent, across_rows = ready(sent, across_rows)
    across = swap(sent, "rep", ACROSS)
    half_kv = jnp.concatenate(
        [jnp.concatenate(head_kv(rep_index), axis=1), across[:, : 2 * head_dim]], axis=0
    )
    pair_kv = swap(half_kv, "rep", PAIR)
    both_routes = jnp.stack([line_routes, across[:, 2 * head_dim :]])
    far_routes = swap(both_routes, "role", 1)
    coded = jnp.concatenate([both_routes[1:], far_routes[:1], far_routes[1:], both_routes[:1]])
    queries = make_queries([normed, across_rows, pair_rows, corner_rows], w_query, q_gain)
    kept, leaving = attend(queries, half_kv, pair_kv, w_out, head_dim)
    leaving, own_dn = ready(swap(leaving, "rep", PAIR), w_down[0])
    halves = kept + leaving.astype(jnp.float32)
    far_dn, far_gu = swap(own_dn, "rep", PAIR), swap(w_gateup[0], "rep", PAIR)
    far_sum = halves[row_count:].astype(jnp.bfloat16)
    across_sum, coded, far_dn, far_gu = ready(
        swap(far_sum, "rep", ACROSS), coded, far_dn, far_gu
    )
    attended = halves[:row_count] + across_sum.astype(jnp.float32)
    mixed = tokens + attended

    moe_in = rms_rows(mixed, moe_gain).astype(jnp.bfloat16)

    capacity = max(2, 7 * row_count * top_count // (4 * expert_count))
    slots = -(-capacity * (coded.shape[1] // row_count) // 16) * 16
    rows, tables = spread_rows(
        moe_in,
        coded,
        lambda codes: make_tables(codes, lax.axis_index(EVERY), slots, top_count),
    )
    weights = [
        pltpu.with_memory_space_constraint(one, pltpu.HBM)
        for one in (w_gateup[0], far_gu, w_down[0], far_dn)
    ]

    tables = (*tables, weights)
    by_rep, by_role = run_experts(0, rows[:2], (1, 1), *tables)
    rep_low, rep_high, role_low, role_high, *held = ready(
        *by_rep, *by_role, *(array for _, _, array in rows[2])
    )
    by_rep, by_role = (rep_low, rep_high), (role_low, role_high)
    pieces = [(row, column, array) for (row, column, _), array in zip(rows[2], held)]
    *corner, near = run_experts(2, [pieces, rows[3]], (2, 1), *tables)
    routed = collect_rows(row_count, near, by_rep, by_role, corner)
    return (mixed + routed).astype(jnp.bfloat16)[None]


def solution(mesh):
    placed = (
        P("role", ("seq", "rep"), None),
        P(),
        P(None, "rep"),
        P(),
        P(),
        P(),
        P("rep", None),
        P(),
        P("role", ("seq", "rep"), None),
        P("role", ("seq", "rep"), None),
        P(("role", "seq", "rep"), None, None),
        P(("role", "seq", "rep"), None, None),
    )
    return jax.shard_map(
        per_device,
        mesh=mesh,
        in_specs=placed,
        out_specs=P("role", ("seq", "rep"), None),
        check_vma=False,
    )
```

```python
import jax
import jax.numpy as jnp
from jax import lax
from jax.experimental import pallas as pl
from jax.experimental.pallas import tpu as pltpu
from jax.sharding import PartitionSpec as P

EVERY = ("role", "seq", "rep")
PAIR = 1
ACROSS = 2
TILE = 256
LANES = 128


def rms_rows(values_in, gain_vec):
    return (
        values_in
        * lax.rsqrt(jnp.mean(values_in * values_in, axis=-1, keepdims=True) + 1e-06)
        * gain_vec
    )


def swap(block, axis, bits):
    size = lax.axis_size(axis)
    return lax.ppermute(block, axis, [(i, i ^ bits) for i in range(size)])


def seq_bits():
    size = lax.axis_size("seq")
    return [1 << place for place in reversed(range(size.bit_length() - 1))]


def ready(*arrays):
    return lax.optimization_barrier(arrays)


def pack_kernel(*refs):
    low_ref, high_ref = refs[-2:]
    count = len(refs) // 2 - 1
    half = low_ref.shape[1]
    start = 0
    for rep_ref, role_ref in zip(refs[:count], refs[count:-2]):
        rows = pl.ds(start, rep_ref.shape[0])
        low_ref[rows] = rep_ref[:, :half]
        high_ref[rows] = role_ref[:, half:]
        start += rep_ref.shape[0]


def pack_corners(by_rep, by_role):
    rows, width = sum(part.shape[0] for part in by_rep), by_rep[0].shape[1]
    half = jax.ShapeDtypeStruct((rows, width // 2), jnp.bfloat16)
    return pl.pallas_call(
        pack_kernel,
        out_shape=[half, half],
        compiler_params=pltpu.CompilerParams(vmem_limit_bytes=(4 + rows // 64) * 1024 * 1024),
        cost_estimate=pl.CostEstimate(
            flops=0, bytes_accessed=4 * rows * width, transcendentals=0
        ),
        name="pack_corners",
    )(*by_rep, *by_role)


def spread_rows(own, coded, tables_of):
    rows, half = own.shape[0], own.shape[1] // 2

    def both_ways(part):
        return swap(part, "rep", ACROSS), swap(part, "role", 1)

    blocks = {0: own}
    for bits in seq_bits():
        blocks |= {place ^ bits: swap(block, "seq", bits) for place, block in blocks.items()}
    middle = [blocks[place] for place in range(2, len(blocks) - 1)]
    middle = jnp.concatenate(middle, axis=0) if len(middle) > 1 else middle[0]
    parts = [own, blocks[1], middle, blocks[len(blocks) - 1]]
    parts[2], coded, *outer = ready(parts[2], coded, *both_ways(own))
    parts[3], *early = ready(parts[3], *both_ways(parts[1]), *tables_of(coded))
    by_rep, by_role = zip(outer, early[:2], both_ways(parts[2]), both_ways(parts[3]))
    tables = early[2:]
    low, high = pack_corners(by_rep, by_role)
    corner_low, corner_high = swap(low, "role", 1), swap(high, "rep", ACROSS)
    starts = (0, rows, 2 * rows, 2 * rows + middle.shape[0])
    groups = [
        [(start, 0, part) for start, part in zip(starts, held)]
        for held in (by_rep, by_role, parts)
    ]
    groups.insert(2, [(0, 0, corner_low), (0, half, corner_high)])
    return groups, tables


def added(first, second):
    return (first.astype(jnp.float32) + second.astype(jnp.float32)).astype(jnp.bfloat16)


def collect_rows(row_count, near, by_rep, by_role, corner):
    straight_low = swap(by_role[0], "role", 1)
    straight_high = swap(by_rep[1], "rep", ACROSS)
    straight_low, straight_high, near_low, near_high, *corner = ready(
        straight_low, straight_high, *near, *corner[0], *corner[1]
    )
    cut = near_low.shape[0] // 2
    halves = slice(0, cut), slice(cut, None)

    def merged(rows, turned_low, turned_high):
        return jnp.concatenate(
            [
                base[rows].astype(jnp.float32)
                + first[rows].astype(jnp.float32)
                + second.astype(jnp.float32)
                for base, first, second in (
                    (near_low, straight_low, turned_low),
                    (near_high, straight_high, turned_high),
                )
            ],
            axis=1,
        )

    def corners(number):
        low, high = corner[2 * number : 2 * number + 2]
        return swap(low, "role", 1), swap(high, "rep", ACROSS)

    def sums(number, corner_low, corner_high):
        rows = halves[number]
        return added(by_rep[0][rows], corner_low), added(by_role[1][rows], corner_high)

    def turned(low, high):
        return swap(low, "rep", ACROSS), swap(high, "role", 1)

    far_sums = sums(1, *corners(1))
    corner[:2] = ready(*corner[:2], *far_sums)[:2]
    far, beside = turned(*far_sums), turned(*sums(0, *corners(0)))
    upper = merged(halves[1], *far)
    lower = merged(halves[0], *ready(*beside, upper)[:2])
    top_bits, *low_bits = seq_bits()

    def folded(rows):
        for bits in reversed(low_bits):
            pairs = rows.reshape(-1, 2, row_count, rows.shape[1])
            leaving = pairs[:, 1].astype(jnp.bfloat16).reshape(-1, rows.shape[1])
            kept = pairs[:, 0].reshape(-1, rows.shape[1]).astype(jnp.float32)
            rows = kept + swap(leaving, "seq", bits).astype(jnp.float32)
        return rows

    upper = folded(upper).astype(jnp.bfloat16)
    return folded(lower) + swap(upper, "seq", top_bits).astype(jnp.float32)


def prepare_kernel(*refs):
    tokens_in, gain_in, kv_in, k_gain_in, ids_in, gates_in, normed_ref, out_ref = refs[:8]
    held, sem = refs[8:14], refs[14]
    sources = (tokens_in, gain_in, kv_in, k_gain_in, ids_in, gates_in)
    copies = [
        pltpu.make_async_copy(src, dst, sem.at[number])
        for number, (src, dst) in enumerate(zip(sources, held))
    ]
    for copy in copies:
        copy.start()
    for copy in copies:
        copy.wait()
    tokens_ref, gain_ref, kv_ref, k_gain_ref, ids_ref, gates_ref = held
    normed = rms_rows(tokens_ref[...].astype(jnp.float32), gain_ref[...]).astype(jnp.bfloat16)
    normed_ref[...] = normed
    kv_width, head_dim = kv_ref.shape[2], k_gain_ref.shape[1]
    keys = jnp.dot(normed, kv_ref[0], preferred_element_type=jnp.float32)
    for start in range(0, kv_width, head_dim):
        head = rms_rows(keys[:, start : start + head_dim], k_gain_ref[...])
        out_ref[:, start : start + head_dim] = head.astype(jnp.bfloat16)
    values = jnp.dot(normed, kv_ref[1], preferred_element_type=jnp.float32)
    out_ref[:, kv_width : 2 * kv_width] = values.astype(jnp.bfloat16)
    coded = jnp.concatenate([ids_ref[...], gates_ref[...] // 64, gates_ref[...] % 64], axis=0)
    count = coded.shape[0]
    spread = lax.broadcasted_iota(jnp.int32, (count, LANES), 0)
    spread = spread == lax.broadcasted_iota(jnp.int32, (count, LANES), 1)
    out_ref[:, 2 * kv_width :] = lax.dot_general(
        coded.astype(jnp.float32).astype(jnp.bfloat16),
        spread.astype(jnp.float32).astype(jnp.bfloat16),
        (((0,), (0,)), ((), ())),
        preferred_element_type=jnp.float32,
    ).astype(jnp.bfloat16)


def prepare(tokens, attn_gain, w_keyval, k_gain, ids, gates):
    rows, width = tokens.shape
    operands = [
        pltpu.with_memory_space_constraint(one, pltpu.HBM)
        for one in (tokens, attn_gain[None], w_keyval, k_gain[None], ids.T, gates.T)
    ]
    return pl.pallas_call(
        prepare_kernel,
        out_shape=[
            jax.ShapeDtypeStruct((rows, width), jnp.bfloat16),
            jax.ShapeDtypeStruct((rows, 2 * w_keyval.shape[2] + LANES), jnp.bfloat16),
        ],
        in_specs=[pl.BlockSpec(memory_space=pltpu.HBM)] * len(operands),
        scratch_shapes=[pltpu.VMEM(one.shape, one.dtype) for one in operands]
        + [pltpu.SemaphoreType.DMA((len(operands),))],
        compiler_params=pltpu.CompilerParams(vmem_limit_bytes=8 * 1024 * 1024),
        cost_estimate=pl.CostEstimate(
            flops=4 * rows * width * w_keyval.shape[2],
            bytes_accessed=4 * width * w_keyval.shape[2] + 4 * rows * width,
            transcendentals=rows,
        ),
        name="prepare",
    )(*operands)


def queries_kernel(first_ref, second_ref, third_ref, fourth_ref, weight_ref, gain_ref, out_ref):
    rows, head_dim = first_ref.shape[0], gain_ref.shape[1]
    refs = (first_ref, second_ref, third_ref, fourth_ref)
    held = jnp.concatenate([ref[...] for ref in refs], axis=0)
    raw = jnp.dot(held, weight_ref[...], preferred_element_type=jnp.float32)
    for start in range(0, weight_ref.shape[1], head_dim):
        head = rms_rows(raw[:, start : start + head_dim], gain_ref[...])
        out_ref[:, start : start + head_dim] = head.astype(jnp.bfloat16)


def make_queries(blocks, w_query, q_gain):
    rows, width = len(blocks) * blocks[0].shape[0], w_query.shape[1]
    return pl.pallas_call(
        queries_kernel,
        out_shape=jax.ShapeDtypeStruct((rows, width), jnp.bfloat16),
        compiler_params=pltpu.CompilerParams(vmem_limit_bytes=8 * 1024 * 1024),
        cost_estimate=pl.CostEstimate(
            flops=2 * rows * width * w_query.shape[0],
            bytes_accessed=2 * width * w_query.shape[0],
            transcendentals=rows,
        ),
        name="queries",
    )(*blocks, w_query, q_gain[None])


def attend_kernel(head_dim, query_ref, near_ref, far_ref, weight_ref, kept_ref, leaving_ref, held_ref):
    keys = [ref[:, :head_dim] for ref in (near_ref, far_ref)]
    values = [ref[:, head_dim:] for ref in (near_ref, far_ref)]
    for start in range(0, query_ref.shape[1], head_dim):
        query = query_ref[:, start : start + head_dim]
        scores = [
            lax.dot_general(
                query, key, (((1,), (1,)), ((), ())), preferred_element_type=jnp.float32
            )
            * head_dim ** (-0.5)
            for key in keys
        ]
        row_max = jnp.maximum(
            jnp.max(scores[0], axis=1, keepdims=True), jnp.max(scores[1], axis=1, keepdims=True)
        )
        denom, total = 0.0, 0.0
        for score, value in zip(scores, values):
            weights = jnp.exp(score - row_max)
            denom = denom + jnp.sum(weights, axis=1, keepdims=True)
            total = total + jnp.dot(
                weights.astype(jnp.bfloat16), value, preferred_element_type=jnp.float32
            )
        held_ref[:, start : start + head_dim] = (total / denom).astype(jnp.bfloat16)
    cut = kept_ref.shape[0]
    for column in range(0, weight_ref.shape[1], 2 * TILE):
        columns = slice(column, column + 2 * TILE)
        partial = jnp.dot(held_ref[...], weight_ref[:, columns], preferred_element_type=jnp.float32)
        kept_ref[:, columns] = partial[:cut]
        leaving_ref[:, columns] = partial[cut:].astype(jnp.bfloat16)


def attend(queries, near_kv, far_kv, w_out, head_dim):
    rows, width = queries.shape
    keys = 2 * near_kv.shape[0]
    half = (rows // 2, w_out.shape[1])
    return pl.pallas_call(
        lambda *refs: attend_kernel(head_dim, *refs),
        out_shape=[
            jax.ShapeDtypeStruct(half, jnp.float32),
            jax.ShapeDtypeStruct(half, jnp.bfloat16),
        ],
        scratch_shapes=[pltpu.VMEM((rows, width), jnp.bfloat16)],
        compiler_params=pltpu.CompilerParams(vmem_limit_bytes=12 * 1024 * 1024),
        cost_estimate=pl.CostEstimate(
            flops=4 * rows * width * keys + 2 * rows * width * w_out.shape[1],
            bytes_accessed=2 * width * w_out.shape[1] + 4 * rows * w_out.shape[1],
            transcendentals=rows * keys * width // head_dim,
        ),
        name="attend",
    )(queries, near_kv, far_kv, w_out)


def tables_kernel(top_count, expert_ref, coded_ref, pick_ref, place_ref, share_ref):
    groups, rows, lanes = coded_ref.shape
    slots = place_ref.shape[3]
    lane = lax.broadcasted_iota(jnp.int32, (rows, lanes), 1)
    source = lax.broadcasted_iota(jnp.int32, (lanes, lanes), 0)
    target = lax.broadcasted_iota(jnp.int32, (lanes, lanes), 1)
    joined = jnp.where(source == target + top_count, 64.0, 0.0)
    joined = joined + jnp.where(source == target + 2 * top_count, 1.0, 0.0)
    joined = jnp.where(target < top_count, joined, 0.0).astype(jnp.bfloat16)
    first = lax.broadcasted_iota(jnp.int32, (rows, rows), 0)
    second = lax.broadcasted_iota(jnp.int32, (rows, rows), 1)
    later = jnp.where(first < second, 1.0, 0.0).astype(jnp.bfloat16)
    earlier = jnp.where(second < first, 1.0, 0.0).astype(jnp.bfloat16)
    ones = jnp.ones((8, lanes), jnp.bfloat16)
    slot_row = lax.broadcasted_iota(jnp.int32, (slots, rows), 0).astype(jnp.float32)
    slot_lane = lax.broadcasted_iota(jnp.int32, (rows, slots), 1).astype(jnp.float32)
    for group in range(groups):
        coded = coded_ref[group]
        gates = jnp.dot(coded, joined, preferred_element_type=jnp.float32)
        gate_sum = jnp.sum(gates, axis=1, keepdims=True)
        named = coded.astype(jnp.float32).astype(jnp.int32)
        for number in range(2):
            expert = expert_ref[0] ^ (number * PAIR)
            hits = jnp.where((named == expert) & (lane < top_count), 1.0, 0.0)
            share_ref[group, :, number : number + 1] = (
                jnp.sum(hits * gates, axis=1, keepdims=True) / gate_sum
            )
            hit = jnp.sum(hits, axis=1, keepdims=True)
            held = jnp.broadcast_to(hit, (rows, lanes)).astype(jnp.bfloat16)
            rank = jnp.dot(earlier, held, preferred_element_type=jnp.float32)[:, :1]
            rank = jnp.where(hit > 0.0, rank, -1.0)
            place_ref[number, group] = jnp.where(rank == slot_lane, 1.0, 0.0).astype(jnp.bfloat16)
            hit_row = lax.dot_general(
                ones,
                hits.astype(jnp.bfloat16),
                (((1,), (1,)), ((), ())),
                preferred_element_type=jnp.float32,
            )
            rank_row = jnp.dot(
                hit_row.astype(jnp.bfloat16), later, preferred_element_type=jnp.float32
            )
            rank_row = jnp.where(hit_row > 0.0, rank_row, -1.0)[:1]
            pick_ref[group, number * slots : (number + 1) * slots] = jnp.where(
                rank_row == slot_row, 1.0, 0.0
            ).astype(jnp.bfloat16)


def make_tables(coded, expert, slots, top_count):
    groups, rows, lanes = coded.shape
    return pl.pallas_call(
        lambda *refs: tables_kernel(top_count, *refs),
        out_shape=[
            jax.ShapeDtypeStruct((groups, 2 * slots, rows), jnp.bfloat16),
            jax.ShapeDtypeStruct((2, groups, rows, slots), jnp.bfloat16),
            jax.ShapeDtypeStruct((groups, rows, 2), jnp.float32),
        ],
        in_specs=[
            pl.BlockSpec(memory_space=pltpu.SMEM),
            pl.BlockSpec(memory_space=pltpu.VMEM),
        ],
        compiler_params=pltpu.CompilerParams(vmem_limit_bytes=24 * 1024 * 1024),
        cost_estimate=pl.CostEstimate(
            flops=4 * groups * rows * rows * lanes,
            bytes_accessed=8 * groups * rows * slots,
            transcendentals=0,
        ),
        name="tables",
    )(expert.astype(jnp.int32)[None], coded)


def expert_kernel(first, spots, cuts, *refs):
    pick_ref, place_ref, share_ref, own_gu_ref, far_gu_ref, own_dn_ref, far_dn_ref = refs[:7]
    group_rows, slots = place_ref.shape[2:]
    groups = len(cuts)
    piece_refs = refs[7 : 7 + len(spots)]
    out_refs = refs[7 + len(spots) : 7 + len(spots) + 2 * sum(cuts)]
    x_buf, xs_buf, gu_buf, dn_buf, hid_buf, served_buf, y_buf, x_sem, w_sem, y_sem = refs[
        7 + len(spots) + len(out_refs) :
    ]
    width = x_buf.shape[2]
    half = width // 2
    hidden = own_dn_ref.shape[0]
    tiles = hidden // TILE

    row_copies = []
    for number, ((group, row, column), piece) in enumerate(zip(spots, piece_refs)):
        rows, columns = piece.shape
        target = x_buf.at[group, pl.ds(row, rows), pl.ds(column, columns)]
        row_copies.append((group, pltpu.make_async_copy(piece, target, x_sem.at[number])))
    weight_copies = []
    for expert, (gu_ref, dn_ref) in enumerate(((own_gu_ref, own_dn_ref), (far_gu_ref, far_dn_ref))):
        mine = []
        for tile in range(tiles):
            for side in range(2):
                mine.append(
                    pltpu.make_async_copy(
                        gu_ref.at[:, pl.ds(side * hidden + tile * TILE, TILE)],
                        gu_buf.at[expert, tile, side],
                        w_sem.at[expert, 2 * tile + side],
                    )
                )
        mine.append(pltpu.make_async_copy(dn_ref, dn_buf.at[expert], w_sem.at[expert, 2 * tiles]))
        weight_copies.append(mine)
    for _, copy in row_copies:
        copy.start()
    for mine in weight_copies:
        for copy in mine:
            copy.start()

    for group in range(groups):
        for where, copy in row_copies:
            if where == group:
                copy.wait()
        chosen = jnp.dot(
            pick_ref[first + group], x_buf[group], preferred_element_type=jnp.float32
        ).astype(jnp.bfloat16)
        xs_buf[0, pl.ds(group * slots, slots)] = chosen[:slots]
        xs_buf[1, pl.ds(group * slots, slots)] = chosen[slots:]

    for expert in range(2):
        for tile in range(tiles):
            weight_copies[expert][2 * tile].wait()
            weight_copies[expert][2 * tile + 1].wait()
            gate = jnp.dot(
                xs_buf[expert], gu_buf[expert, tile, 0], preferred_element_type=jnp.float32
            )
            up = jnp.dot(
                xs_buf[expert], gu_buf[expert, tile, 1], preferred_element_type=jnp.float32
            )
            value = gate / (1.0 + jnp.exp(-gate)) * up
            hid_buf[:, tile * TILE : (tile + 1) * TILE] = value.astype(jnp.bfloat16)
        weight_copies[expert][2 * tiles].wait()
        for column in range(0, width, 2 * TILE):
            served_buf[expert, :, column : column + 2 * TILE] = jnp.dot(
                hid_buf[...],
                dn_buf[expert, :, column : column + 2 * TILE],
                preferred_element_type=jnp.float32,
            ).astype(jnp.bfloat16)

    out_copies = []
    for group in range(groups):
        for column in range(0, width, 2 * TILE):
            total = None
            for expert in range(2):
                placed = jnp.dot(
                    place_ref[expert, first + group],
                    served_buf[expert, pl.ds(group * slots, slots), column : column + 2 * TILE],
                    preferred_element_type=jnp.float32,
                )
                term = placed * share_ref[first + group, :, expert : expert + 1]
                total = term if total is None else total + term
            y_buf[group, :, column : column + 2 * TILE] = total.astype(jnp.bfloat16)
        cut = group_rows // cuts[group]
        for number in range(2 * cuts[group]):
            row, side = divmod(number, 2)
            done = len(out_copies)
            copy = pltpu.make_async_copy(
                y_buf.at[group, pl.ds(row * cut, cut), pl.ds(side * half, half)],
                out_refs[done],
                y_sem.at[done],
            )
            copy.start()
            out_copies.append(copy)
    for copy in out_copies:
        copy.wait()


def run_experts(first, pieces, cuts, pick, place, share, weights):
    group_rows, slots = place.shape[2:]
    groups = len(pieces)
    hidden, width = weights[2].shape
    tiles = hidden // TILE
    spots = [
        (group, row, column) for group, held in enumerate(pieces) for row, column, _ in held
    ]
    arrays = [array for held in pieces for _, _, array in held]
    anywhere = pl.BlockSpec(memory_space=pl.ANY)
    stored = pl.BlockSpec(memory_space=pltpu.HBM)
    inside = pl.BlockSpec(memory_space=pltpu.VMEM)
    outs = pl.pallas_call(
        lambda *refs: expert_kernel(first, spots, cuts, *refs),
        out_shape=[
            jax.ShapeDtypeStruct((group_rows // cut, width // 2), jnp.bfloat16)
            for cut in cuts
            for _ in range(2 * cut)
        ],
        in_specs=[inside] * 3 + [stored] * 4 + [anywhere] * len(arrays),
        out_specs=[anywhere] * (2 * sum(cuts)),
        scratch_shapes=[
            pltpu.VMEM((groups, group_rows, width), jnp.bfloat16),
            pltpu.VMEM((2, groups * slots, width), jnp.bfloat16),
            pltpu.VMEM((2, tiles, 2, width, TILE), jnp.bfloat16),
            pltpu.VMEM((2, hidden, width), jnp.bfloat16),
            pltpu.VMEM((groups * slots, hidden), jnp.bfloat16),
            pltpu.VMEM((2, groups * slots, width), jnp.bfloat16),
            pltpu.VMEM((groups, group_rows, width), jnp.bfloat16),
            pltpu.SemaphoreType.DMA((len(arrays),)),
            pltpu.SemaphoreType.DMA((2, 2 * tiles + 1)),
            pltpu.SemaphoreType.DMA((2 * sum(cuts),)),
        ],
        compiler_params=pltpu.CompilerParams(vmem_limit_bytes=(28 + 6 * group_rows // 256) * 1024 * 1024),
        cost_estimate=pl.CostEstimate(
            flops=12 * groups * slots * width * hidden,
            bytes_accessed=12 * width * hidden + 4 * groups * group_rows * width,
            transcendentals=2 * groups * slots * hidden,
        ),
        name="experts",
    )(pick, place, share, *weights, *arrays)
    return list(zip(outs[0::2], outs[1::2]))


def per_device(
    hidden_in,
    attn_gain,
    w_query,
    w_keyval,
    q_gain,
    k_gain,
    w_out,
    moe_gain,
    expert_ids,
    gate_fixed,
    w_gateup,
    w_down,
):
    tokens = hidden_in[0].astype(jnp.float32)
    row_count, model_width = tokens.shape
    head_dim = q_gain.shape[0]
    local_heads = w_query.shape[1] // head_dim
    kv_heads = w_keyval.shape[2] // head_dim
    group_size = local_heads * lax.axis_size("rep") // kv_heads
    rep_index = lax.axis_index("rep")
    kv_width = kv_heads * head_dim
    top_count = expert_ids.shape[2]
    expert_count = lax.axis_size(EVERY)

    normed, own_payload = prepare(
        hidden_in[0], attn_gain, w_keyval, k_gain, expert_ids[0], gate_fixed[0]
    )
    across_rows = swap(normed, "rep", ACROSS)
    line = jnp.concatenate(
        [own_payload] + [swap(own_payload, "seq", bits) for bits in range(1, lax.axis_size("seq"))], axis=0
    )
    pair_rows = swap(ready(normed, line)[0], "rep", PAIR)
    corner_rows = swap(across_rows, "rep", PAIR)
    line_routes = line[:, 2 * kv_width :]

    def head_kv(rep):
        index = rep * local_heads // group_size * head_dim
        return [
            lax.dynamic_slice_in_dim(line, index, head_dim, 1),
            lax.dynamic_slice_in_dim(line, kv_width + index, head_dim, 1),
        ]

    sent = jnp.concatenate(head_kv(rep_index ^ ACROSS) + [line_routes], axis=1)
    sent, across_rows = ready(sent, across_rows)
    across = swap(sent, "rep", ACROSS)
    half_kv = jnp.concatenate(
        [jnp.concatenate(head_kv(rep_index), axis=1), across[:, : 2 * head_dim]], axis=0
    )
    pair_kv = swap(half_kv, "rep", PAIR)
    both_routes = jnp.stack([line_routes, across[:, 2 * head_dim :]])
    far_routes = swap(both_routes, "role", 1)
    coded = jnp.concatenate([both_routes[1:], far_routes[:1], far_routes[1:], both_routes[:1]])
    queries = make_queries([normed, across_rows, pair_rows, corner_rows], w_query, q_gain)
    kept, leaving = attend(queries, half_kv, pair_kv, w_out, head_dim)
    leaving, own_dn = ready(swap(leaving, "rep", PAIR), w_down[0])
    halves = kept + leaving.astype(jnp.float32)
    far_dn, far_gu = swap(own_dn, "rep", PAIR), swap(w_gateup[0], "rep", PAIR)
    far_sum = halves[row_count:].astype(jnp.bfloat16)
    across_sum, coded, far_dn, far_gu = ready(
        swap(far_sum, "rep", ACROSS), coded, far_dn, far_gu
    )
    attended = halves[:row_count] + across_sum.astype(jnp.float32)
    mixed = tokens + attended

    moe_in = rms_rows(mixed, moe_gain).astype(jnp.bfloat16)

    capacity = max(2, 7 * row_count * top_count // (4 * expert_count))
    slots = -(-capacity * (coded.shape[1] // row_count) // 16) * 16
    rows, tables = spread_rows(
        moe_in,
        coded,
        lambda codes: make_tables(codes, lax.axis_index(EVERY), slots, top_count),
    )
    weights = [
        pltpu.with_memory_space_constraint(one, pltpu.HBM)
        for one in (w_gateup[0], far_gu, w_down[0], far_dn)
    ]

    tables = (*tables, weights)
    by_rep, by_role = run_experts(0, rows[:2], (1, 1), *tables)
    rep_low, rep_high, role_low, role_high, *held = ready(
        *by_rep, *by_role, *(array for _, _, array in rows[2])
    )
    by_rep, by_role = (rep_low, rep_high), (role_low, role_high)
    pieces = [(row, column, array) for (row, column, _), array in zip(rows[2], held)]
    *corner, near = run_experts(2, [pieces, rows[3]], (2, 1), *tables)
    routed = collect_rows(row_count, near, by_rep, by_role, corner)
    return (mixed + routed).astype(jnp.bfloat16)[None]


def solution(mesh):
    placed = (
        P("role", ("seq", "rep"), None),
        P(),
        P(None, "rep"),
        P(),
        P(),
        P(),
        P("rep", None),
        P(),
        P("role", ("seq", "rep"), None),
        P("role", ("seq", "rep"), None),
        P(("role", "seq", "rep"), None, None),
        P(("role", "seq", "rep"), None, None),
    )
    return jax.shard_map(
        per_device,
        mesh=mesh,
        in_specs=placed,
        out_specs=P("role", ("seq", "rep"), None),
        check_vma=False,
    )
```

```python
import jax
import jax.numpy as jnp
from jax import lax
from jax.experimental import pallas as pl
from jax.experimental.pallas import tpu as pltpu
from jax.sharding import PartitionSpec as P

EVERY = ("role", "seq", "rep")
PAIR = 1
ACROSS = 2
TILE = 256
LANES = 128


def rms_rows(values_in, gain_vec):
    return (
        values_in
        * lax.rsqrt(jnp.mean(values_in * values_in, axis=-1, keepdims=True) + 1e-06)
        * gain_vec
    )


def swap(block, axis, bits):
    size = lax.axis_size(axis)
    return lax.ppermute(block, axis, [(i, i ^ bits) for i in range(size)])


def seq_bits():
    size = lax.axis_size("seq")
    return [1 << place for place in reversed(range(size.bit_length() - 1))]


def ready(*arrays):
    return lax.optimization_barrier(arrays)


def pack_kernel(*refs):
    low_ref, high_ref = refs[-2:]
    count = len(refs) // 2 - 1
    half = low_ref.shape[1]
    start = 0
    for rep_ref, role_ref in zip(refs[:count], refs[count:-2]):
        rows = pl.ds(start, rep_ref.shape[0])
        low_ref[rows] = rep_ref[:, :half]
        high_ref[rows] = role_ref[:, half:]
        start += rep_ref.shape[0]


def pack_corners(by_rep, by_role):
    rows, width = sum(part.shape[0] for part in by_rep), by_rep[0].shape[1]
    half = jax.ShapeDtypeStruct((rows, width // 2), jnp.bfloat16)
    return pl.pallas_call(
        pack_kernel,
        out_shape=[half, half],
        compiler_params=pltpu.CompilerParams(vmem_limit_bytes=(4 + rows // 64) * 1024 * 1024),
        cost_estimate=pl.CostEstimate(
            flops=0, bytes_accessed=4 * rows * width, transcendentals=0
        ),
        name="pack_corners",
    )(*by_rep, *by_role)


def spread_rows(own, coded, tables_of):
    rows, half = own.shape[0], own.shape[1] // 2

    def both_ways(part):
        return swap(part, "rep", ACROSS), swap(part, "role", 1)

    blocks = {0: own}
    for bits in seq_bits():
        blocks |= {place ^ bits: swap(block, "seq", bits) for place, block in blocks.items()}
    middle = [blocks[place] for place in range(2, len(blocks) - 1)]
    middle = jnp.concatenate(middle, axis=0) if len(middle) > 1 else middle[0]
    parts = [own, blocks[1], middle, blocks[len(blocks) - 1]]
    parts[2], coded, *outer = ready(parts[2], coded, *both_ways(own))
    parts[3], *early = ready(parts[3], *both_ways(parts[1]), *tables_of(coded))
    by_rep, by_role = zip(outer, early[:2], both_ways(parts[2]), both_ways(parts[3]))
    tables = early[2:]
    low, high = pack_corners(by_rep, by_role)
    corner_low, corner_high = swap(low, "role", 1), swap(high, "rep", ACROSS)
    starts = (0, rows, 2 * rows, 2 * rows + middle.shape[0])
    groups = [
        [(start, 0, part) for start, part in zip(starts, held)]
        for held in (by_rep, by_role, parts)
    ]
    groups.insert(2, [(0, 0, corner_low), (0, half, corner_high)])
    return groups, tables


def added(first, second):
    return (first.astype(jnp.float32) + second.astype(jnp.float32)).astype(jnp.bfloat16)


def collect_rows(row_count, near, by_rep, by_role, corner):
    straight_low = swap(by_role[0], "role", 1)
    straight_high = swap(by_rep[1], "rep", ACROSS)
    straight_low, straight_high, near_low, near_high, *corner = ready(
        straight_low, straight_high, *near, *corner[0], *corner[1]
    )
    cut = near_low.shape[0] // 2
    halves = slice(0, cut), slice(cut, None)

    def merged(rows, turned_low, turned_high):
        return jnp.concatenate(
            [
                base[rows].astype(jnp.float32)
                + first[rows].astype(jnp.float32)
                + second.astype(jnp.float32)
                for base, first, second in (
                    (near_low, straight_low, turned_low),
                    (near_high, straight_high, turned_high),
                )
            ],
            axis=1,
        )

    def corners(number):
        low, high = corner[2 * number : 2 * number + 2]
        return swap(low, "role", 1), swap(high, "rep", ACROSS)

    def sums(number, corner_low, corner_high):
        rows = halves[number]
        return added(by_rep[0][rows], corner_low), added(by_role[1][rows], corner_high)

    def turned(low, high):
        return swap(low, "rep", ACROSS), swap(high, "role", 1)

    far_sums = sums(1, *corners(1))
    corner[:2] = ready(*corner[:2], *far_sums)[:2]
    far, beside = turned(*far_sums), turned(*sums(0, *corners(0)))
    upper = merged(halves[1], *far)
    lower = merged(halves[0], *ready(*beside, upper)[:2])
    top_bits, *low_bits = seq_bits()

    def folded(rows):
        for bits in reversed(low_bits):
            pairs = rows.reshape(-1, 2, row_count, rows.shape[1])
            leaving = pairs[:, 1].astype(jnp.bfloat16).reshape(-1, rows.shape[1])
            kept = pairs[:, 0].reshape(-1, rows.shape[1]).astype(jnp.float32)
            rows = kept + swap(leaving, "seq", bits).astype(jnp.float32)
        return rows

    upper, lower = ready(folded(upper).astype(jnp.bfloat16), folded(lower))
    return lower + swap(upper, "seq", top_bits).astype(jnp.float32)


def prepare_kernel(*refs):
    tokens_in, gain_in, kv_in, k_gain_in, ids_in, gates_in, normed_ref, out_ref = refs[:8]
    held, sem = refs[8:14], refs[14]
    sources = (tokens_in, gain_in, kv_in, k_gain_in, ids_in, gates_in)
    copies = [
        pltpu.make_async_copy(src, dst, sem.at[number])
        for number, (src, dst) in enumerate(zip(sources, held))
    ]
    for copy in copies:
        copy.start()
    for copy in copies:
        copy.wait()
    tokens_ref, gain_ref, kv_ref, k_gain_ref, ids_ref, gates_ref = held
    normed = rms_rows(tokens_ref[...].astype(jnp.float32), gain_ref[...]).astype(jnp.bfloat16)
    normed_ref[...] = normed
    kv_width, head_dim = kv_ref.shape[2], k_gain_ref.shape[1]
    keys = jnp.dot(normed, kv_ref[0], preferred_element_type=jnp.float32)
    for start in range(0, kv_width, head_dim):
        head = rms_rows(keys[:, start : start + head_dim], k_gain_ref[...])
        out_ref[:, start : start + head_dim] = head.astype(jnp.bfloat16)
    values = jnp.dot(normed, kv_ref[1], preferred_element_type=jnp.float32)
    out_ref[:, kv_width : 2 * kv_width] = values.astype(jnp.bfloat16)
    coded = jnp.concatenate([ids_ref[...], gates_ref[...] // 64, gates_ref[...] % 64], axis=0)
    count = coded.shape[0]
    spread = lax.broadcasted_iota(jnp.int32, (count, LANES), 0)
    spread = spread == lax.broadcasted_iota(jnp.int32, (count, LANES), 1)
    out_ref[:, 2 * kv_width :] = lax.dot_general(
        coded.astype(jnp.float32).astype(jnp.bfloat16),
        spread.astype(jnp.float32).astype(jnp.bfloat16),
        (((0,), (0,)), ((), ())),
        preferred_element_type=jnp.float32,
    ).astype(jnp.bfloat16)


def prepare(tokens, attn_gain, w_keyval, k_gain, ids, gates):
    rows, width = tokens.shape
    operands = [
        pltpu.with_memory_space_constraint(one, pltpu.HBM)
        for one in (tokens, attn_gain[None], w_keyval, k_gain[None], ids.T, gates.T)
    ]
    return pl.pallas_call(
        prepare_kernel,
        out_shape=[
            jax.ShapeDtypeStruct((rows, width), jnp.bfloat16),
            jax.ShapeDtypeStruct((rows, 2 * w_keyval.shape[2] + LANES), jnp.bfloat16),
        ],
        in_specs=[pl.BlockSpec(memory_space=pltpu.HBM)] * len(operands),
        scratch_shapes=[pltpu.VMEM(one.shape, one.dtype) for one in operands]
        + [pltpu.SemaphoreType.DMA((len(operands),))],
        compiler_params=pltpu.CompilerParams(vmem_limit_bytes=8 * 1024 * 1024),
        cost_estimate=pl.CostEstimate(
            flops=4 * rows * width * w_keyval.shape[2],
            bytes_accessed=4 * width * w_keyval.shape[2] + 4 * rows * width,
            transcendentals=rows,
        ),
        name="prepare",
    )(*operands)


def queries_kernel(first_ref, second_ref, third_ref, fourth_ref, weight_ref, gain_ref, out_ref):
    rows, head_dim = first_ref.shape[0], gain_ref.shape[1]
    refs = (first_ref, second_ref, third_ref, fourth_ref)
    held = jnp.concatenate([ref[...] for ref in refs], axis=0)
    raw = jnp.dot(held, weight_ref[...], preferred_element_type=jnp.float32)
    for start in range(0, weight_ref.shape[1], head_dim):
        head = rms_rows(raw[:, start : start + head_dim], gain_ref[...])
        out_ref[:, start : start + head_dim] = head.astype(jnp.bfloat16)


def make_queries(blocks, w_query, q_gain):
    rows, width = len(blocks) * blocks[0].shape[0], w_query.shape[1]
    return pl.pallas_call(
        queries_kernel,
        out_shape=jax.ShapeDtypeStruct((rows, width), jnp.bfloat16),
        compiler_params=pltpu.CompilerParams(vmem_limit_bytes=8 * 1024 * 1024),
        cost_estimate=pl.CostEstimate(
            flops=2 * rows * width * w_query.shape[0],
            bytes_accessed=2 * width * w_query.shape[0],
            transcendentals=rows,
        ),
        name="queries",
    )(*blocks, w_query, q_gain[None])


def attend_kernel(head_dim, query_ref, near_ref, far_ref, weight_ref, kept_ref, leaving_ref, held_ref):
    keys = [ref[:, :head_dim] for ref in (near_ref, far_ref)]
    values = [ref[:, head_dim:] for ref in (near_ref, far_ref)]
    for start in range(0, query_ref.shape[1], head_dim):
        query = query_ref[:, start : start + head_dim]
        scores = [
            lax.dot_general(
                query, key, (((1,), (1,)), ((), ())), preferred_element_type=jnp.float32
            )
            * head_dim ** (-0.5)
            for key in keys
        ]
        row_max = jnp.maximum(
            jnp.max(scores[0], axis=1, keepdims=True), jnp.max(scores[1], axis=1, keepdims=True)
        )
        denom, total = 0.0, 0.0
        for score, value in zip(scores, values):
            weights = jnp.exp(score - row_max)
            denom = denom + jnp.sum(weights, axis=1, keepdims=True)
            total = total + jnp.dot(
                weights.astype(jnp.bfloat16), value, preferred_element_type=jnp.float32
            )
        held_ref[:, start : start + head_dim] = (total / denom).astype(jnp.bfloat16)
    cut = kept_ref.shape[0]
    for column in range(0, weight_ref.shape[1], 2 * TILE):
        columns = slice(column, column + 2 * TILE)
        partial = jnp.dot(held_ref[...], weight_ref[:, columns], preferred_element_type=jnp.float32)
        kept_ref[:, columns] = partial[:cut]
        leaving_ref[:, columns] = partial[cut:].astype(jnp.bfloat16)


def attend(queries, near_kv, far_kv, w_out, head_dim):
    rows, width = queries.shape
    keys = 2 * near_kv.shape[0]
    half = (rows // 2, w_out.shape[1])
    return pl.pallas_call(
        lambda *refs: attend_kernel(head_dim, *refs),
        out_shape=[
            jax.ShapeDtypeStruct(half, jnp.float32),
            jax.ShapeDtypeStruct(half, jnp.bfloat16),
        ],
        scratch_shapes=[pltpu.VMEM((rows, width), jnp.bfloat16)],
        compiler_params=pltpu.CompilerParams(vmem_limit_bytes=12 * 1024 * 1024),
        cost_estimate=pl.CostEstimate(
            flops=4 * rows * width * keys + 2 * rows * width * w_out.shape[1],
            bytes_accessed=2 * width * w_out.shape[1] + 4 * rows * w_out.shape[1],
            transcendentals=rows * keys * width // head_dim,
        ),
        name="attend",
    )(queries, near_kv, far_kv, w_out)


def tables_kernel(top_count, expert_ref, coded_ref, pick_ref, place_ref, share_ref):
    groups, rows, lanes = coded_ref.shape
    slots = place_ref.shape[3]
    lane = lax.broadcasted_iota(jnp.int32, (rows, lanes), 1)
    source = lax.broadcasted_iota(jnp.int32, (lanes, lanes), 0)
    target = lax.broadcasted_iota(jnp.int32, (lanes, lanes), 1)
    joined = jnp.where(source == target + top_count, 64.0, 0.0)
    joined = joined + jnp.where(source == target + 2 * top_count, 1.0, 0.0)
    joined = jnp.where(target < top_count, joined, 0.0).astype(jnp.bfloat16)
    first = lax.broadcasted_iota(jnp.int32, (rows, rows), 0)
    second = lax.broadcasted_iota(jnp.int32, (rows, rows), 1)
    later = jnp.where(first < second, 1.0, 0.0).astype(jnp.bfloat16)
    earlier = jnp.where(second < first, 1.0, 0.0).astype(jnp.bfloat16)
    ones = jnp.ones((8, lanes), jnp.bfloat16)
    slot_row = lax.broadcasted_iota(jnp.int32, (slots, rows), 0).astype(jnp.float32)
    slot_lane = lax.broadcasted_iota(jnp.int32, (rows, slots), 1).astype(jnp.float32)
    for group in range(groups):
        coded = coded_ref[group]
        gates = jnp.dot(coded, joined, preferred_element_type=jnp.float32)
        gate_sum = jnp.sum(gates, axis=1, keepdims=True)
        named = coded.astype(jnp.float32).astype(jnp.int32)
        for number in range(2):
            expert = expert_ref[0] ^ (number * PAIR)
            hits = jnp.where((named == expert) & (lane < top_count), 1.0, 0.0)
            share_ref[group, :, number : number + 1] = (
                jnp.sum(hits * gates, axis=1, keepdims=True) / gate_sum
            )
            hit = jnp.sum(hits, axis=1, keepdims=True)
            held = jnp.broadcast_to(hit, (rows, lanes)).astype(jnp.bfloat16)
            rank = jnp.dot(earlier, held, preferred_element_type=jnp.float32)[:, :1]
            rank = jnp.where(hit > 0.0, rank, -1.0)
            place_ref[number, group] = jnp.where(rank == slot_lane, 1.0, 0.0).astype(jnp.bfloat16)
            hit_row = lax.dot_general(
                ones,
                hits.astype(jnp.bfloat16),
                (((1,), (1,)), ((), ())),
                preferred_element_type=jnp.float32,
            )
            rank_row = jnp.dot(
                hit_row.astype(jnp.bfloat16), later, preferred_element_type=jnp.float32
            )
            rank_row = jnp.where(hit_row > 0.0, rank_row, -1.0)[:1]
            pick_ref[group, number * slots : (number + 1) * slots] = jnp.where(
                rank_row == slot_row, 1.0, 0.0
            ).astype(jnp.bfloat16)


def make_tables(coded, expert, slots, top_count):
    groups, rows, lanes = coded.shape
    return pl.pallas_call(
        lambda *refs: tables_kernel(top_count, *refs),
        out_shape=[
            jax.ShapeDtypeStruct((groups, 2 * slots, rows), jnp.bfloat16),
            jax.ShapeDtypeStruct((2, groups, rows, slots), jnp.bfloat16),
            jax.ShapeDtypeStruct((groups, rows, 2), jnp.float32),
        ],
        in_specs=[
            pl.BlockSpec(memory_space=pltpu.SMEM),
            pl.BlockSpec(memory_space=pltpu.VMEM),
        ],
        compiler_params=pltpu.CompilerParams(vmem_limit_bytes=24 * 1024 * 1024),
        cost_estimate=pl.CostEstimate(
            flops=4 * groups * rows * rows * lanes,
            bytes_accessed=8 * groups * rows * slots,
            transcendentals=0,
        ),
        name="tables",
    )(expert.astype(jnp.int32)[None], coded)


def expert_kernel(first, spots, cuts, *refs):
    pick_ref, place_ref, share_ref, own_gu_ref, far_gu_ref, own_dn_ref, far_dn_ref = refs[:7]
    group_rows, slots = place_ref.shape[2:]
    groups = len(cuts)
    piece_refs = refs[7 : 7 + len(spots)]
    out_refs = refs[7 + len(spots) : 7 + len(spots) + 2 * sum(cuts)]
    x_buf, xs_buf, gu_buf, dn_buf, hid_buf, served_buf, y_buf, x_sem, w_sem, y_sem = refs[
        7 + len(spots) + len(out_refs) :
    ]
    width = x_buf.shape[2]
    half = width // 2
    hidden = own_dn_ref.shape[0]
    tiles = hidden // TILE

    row_copies = []
    for number, ((group, row, column), piece) in enumerate(zip(spots, piece_refs)):
        rows, columns = piece.shape
        target = x_buf.at[group, pl.ds(row, rows), pl.ds(column, columns)]
        row_copies.append((group, pltpu.make_async_copy(piece, target, x_sem.at[number])))
    weight_copies = []
    for expert, (gu_ref, dn_ref) in enumerate(((own_gu_ref, own_dn_ref), (far_gu_ref, far_dn_ref))):
        mine = []
        for tile in range(tiles):
            for side in range(2):
                mine.append(
                    pltpu.make_async_copy(
                        gu_ref.at[:, pl.ds(side * hidden + tile * TILE, TILE)],
                        gu_buf.at[expert, tile, side],
                        w_sem.at[expert, 2 * tile + side],
                    )
                )
        mine.append(pltpu.make_async_copy(dn_ref, dn_buf.at[expert], w_sem.at[expert, 2 * tiles]))
        weight_copies.append(mine)
    for _, copy in row_copies:
        copy.start()
    for mine in weight_copies:
        for copy in mine:
            copy.start()

    for group in range(groups):
        for where, copy in row_copies:
            if where == group:
                copy.wait()
        chosen = jnp.dot(
            pick_ref[first + group], x_buf[group], preferred_element_type=jnp.float32
        ).astype(jnp.bfloat16)
        xs_buf[0, pl.ds(group * slots, slots)] = chosen[:slots]
        xs_buf[1, pl.ds(group * slots, slots)] = chosen[slots:]

    for expert in range(2):
        for tile in range(tiles):
            weight_copies[expert][2 * tile].wait()
            weight_copies[expert][2 * tile + 1].wait()
            gate = jnp.dot(
                xs_buf[expert], gu_buf[expert, tile, 0], preferred_element_type=jnp.float32
            )
            up = jnp.dot(
                xs_buf[expert], gu_buf[expert, tile, 1], preferred_element_type=jnp.float32
            )
            value = gate / (1.0 + jnp.exp(-gate)) * up
            hid_buf[:, tile * TILE : (tile + 1) * TILE] = value.astype(jnp.bfloat16)
        weight_copies[expert][2 * tiles].wait()
        for column in range(0, width, 2 * TILE):
            served_buf[expert, :, column : column + 2 * TILE] = jnp.dot(
                hid_buf[...],
                dn_buf[expert, :, column : column + 2 * TILE],
                preferred_element_type=jnp.float32,
            ).astype(jnp.bfloat16)

    out_copies = []
    for group in range(groups):
        for column in range(0, width, 2 * TILE):
            total = None
            for expert in range(2):
                placed = jnp.dot(
                    place_ref[expert, first + group],
                    served_buf[expert, pl.ds(group * slots, slots), column : column + 2 * TILE],
                    preferred_element_type=jnp.float32,
                )
                term = placed * share_ref[first + group, :, expert : expert + 1]
                total = term if total is None else total + term
            y_buf[group, :, column : column + 2 * TILE] = total.astype(jnp.bfloat16)
        cut = group_rows // cuts[group]
        for number in range(2 * cuts[group]):
            row, side = divmod(number, 2)
            done = len(out_copies)
            copy = pltpu.make_async_copy(
                y_buf.at[group, pl.ds(row * cut, cut), pl.ds(side * half, half)],
                out_refs[done],
                y_sem.at[done],
            )
            copy.start()
            out_copies.append(copy)
    for copy in out_copies:
        copy.wait()


def run_experts(first, pieces, cuts, pick, place, share, weights):
    group_rows, slots = place.shape[2:]
    groups = len(pieces)
    hidden, width = weights[2].shape
    tiles = hidden // TILE
    spots = [
        (group, row, column) for group, held in enumerate(pieces) for row, column, _ in held
    ]
    arrays = [array for held in pieces for _, _, array in held]
    anywhere = pl.BlockSpec(memory_space=pl.ANY)
    stored = pl.BlockSpec(memory_space=pltpu.HBM)
    inside = pl.BlockSpec(memory_space=pltpu.VMEM)
    outs = pl.pallas_call(
        lambda *refs: expert_kernel(first, spots, cuts, *refs),
        out_shape=[
            jax.ShapeDtypeStruct((group_rows // cut, width // 2), jnp.bfloat16)
            for cut in cuts
            for _ in range(2 * cut)
        ],
        in_specs=[inside] * 3 + [stored] * 4 + [anywhere] * len(arrays),
        out_specs=[anywhere] * (2 * sum(cuts)),
        scratch_shapes=[
            pltpu.VMEM((groups, group_rows, width), jnp.bfloat16),
            pltpu.VMEM((2, groups * slots, width), jnp.bfloat16),
            pltpu.VMEM((2, tiles, 2, width, TILE), jnp.bfloat16),
            pltpu.VMEM((2, hidden, width), jnp.bfloat16),
            pltpu.VMEM((groups * slots, hidden), jnp.bfloat16),
            pltpu.VMEM((2, groups * slots, width), jnp.bfloat16),
            pltpu.VMEM((groups, group_rows, width), jnp.bfloat16),
            pltpu.SemaphoreType.DMA((len(arrays),)),
            pltpu.SemaphoreType.DMA((2, 2 * tiles + 1)),
            pltpu.SemaphoreType.DMA((2 * sum(cuts),)),
        ],
        compiler_params=pltpu.CompilerParams(vmem_limit_bytes=(28 + 6 * group_rows // 256) * 1024 * 1024),
        cost_estimate=pl.CostEstimate(
            flops=12 * groups * slots * width * hidden,
            bytes_accessed=12 * width * hidden + 4 * groups * group_rows * width,
            transcendentals=2 * groups * slots * hidden,
        ),
        name="experts",
    )(pick, place, share, *weights, *arrays)
    return list(zip(outs[0::2], outs[1::2]))


def per_device(
    hidden_in,
    attn_gain,
    w_query,
    w_keyval,
    q_gain,
    k_gain,
    w_out,
    moe_gain,
    expert_ids,
    gate_fixed,
    w_gateup,
    w_down,
):
    tokens = hidden_in[0].astype(jnp.float32)
    row_count, model_width = tokens.shape
    head_dim = q_gain.shape[0]
    local_heads = w_query.shape[1] // head_dim
    kv_heads = w_keyval.shape[2] // head_dim
    group_size = local_heads * lax.axis_size("rep") // kv_heads
    rep_index = lax.axis_index("rep")
    kv_width = kv_heads * head_dim
    top_count = expert_ids.shape[2]
    expert_count = lax.axis_size(EVERY)

    normed, own_payload = prepare(
        hidden_in[0], attn_gain, w_keyval, k_gain, expert_ids[0], gate_fixed[0]
    )
    across_rows = swap(normed, "rep", ACROSS)
    line = jnp.concatenate(
        [own_payload] + [swap(own_payload, "seq", bits) for bits in range(1, lax.axis_size("seq"))], axis=0
    )
    pair_rows = swap(ready(normed, line)[0], "rep", PAIR)
    corner_rows = swap(across_rows, "rep", PAIR)
    line_routes = line[:, 2 * kv_width :]

    def head_kv(rep):
        index = rep * local_heads // group_size * head_dim
        return [
            lax.dynamic_slice_in_dim(line, index, head_dim, 1),
            lax.dynamic_slice_in_dim(line, kv_width + index, head_dim, 1),
        ]

    sent = jnp.concatenate(head_kv(rep_index ^ ACROSS) + [line_routes], axis=1)
    sent, across_rows = ready(sent, across_rows)
    across = swap(sent, "rep", ACROSS)
    half_kv = jnp.concatenate(
        [jnp.concatenate(head_kv(rep_index), axis=1), across[:, : 2 * head_dim]], axis=0
    )
    pair_kv = swap(half_kv, "rep", PAIR)
    both_routes = jnp.stack([line_routes, across[:, 2 * head_dim :]])
    far_routes = swap(both_routes, "role", 1)
    coded = jnp.concatenate([both_routes[1:], far_routes[:1], far_routes[1:], both_routes[:1]])
    queries = make_queries([normed, across_rows, pair_rows, corner_rows], w_query, q_gain)
    kept, leaving = attend(queries, half_kv, pair_kv, w_out, head_dim)
    leaving, own_dn = ready(swap(leaving, "rep", PAIR), w_down[0])
    halves = kept + leaving.astype(jnp.float32)
    far_dn, far_gu = swap(own_dn, "rep", PAIR), swap(w_gateup[0], "rep", PAIR)
    far_sum = halves[row_count:].astype(jnp.bfloat16)
    across_sum, coded, far_dn, far_gu = ready(
        swap(far_sum, "rep", ACROSS), coded, far_dn, far_gu
    )
    attended = halves[:row_count] + across_sum.astype(jnp.float32)
    mixed = tokens + attended

    moe_in = rms_rows(mixed, moe_gain).astype(jnp.bfloat16)

    capacity = max(2, 7 * row_count * top_count // (4 * expert_count))
    slots = -(-capacity * (coded.shape[1] // row_count) // 16) * 16
    rows, tables = spread_rows(
        moe_in,
        coded,
        lambda codes: make_tables(codes, lax.axis_index(EVERY), slots, top_count),
    )
    weights = [
        pltpu.with_memory_space_constraint(one, pltpu.HBM)
        for one in (w_gateup[0], far_gu, w_down[0], far_dn)
    ]

    tables = (*tables, weights)
    by_rep, by_role = run_experts(0, rows[:2], (1, 1), *tables)
    rep_low, rep_high, role_low, role_high, *held = ready(
        *by_rep, *by_role, *(array for _, _, array in rows[2])
    )
    by_rep, by_role = (rep_low, rep_high), (role_low, role_high)
    pieces = [(row, column, array) for (row, column, _), array in zip(rows[2], held)]
    *corner, near = run_experts(2, [pieces, rows[3]], (2, 1), *tables)
    routed = collect_rows(row_count, near, by_rep, by_role, corner)
    return (mixed + routed).astype(jnp.bfloat16)[None]


def solution(mesh):
    placed = (
        P("role", ("seq", "rep"), None),
        P(),
        P(None, "rep"),
        P(),
        P(),
        P(),
        P("rep", None),
        P(),
        P("role", ("seq", "rep"), None),
        P("role", ("seq", "rep"), None),
        P(("role", "seq", "rep"), None, None),
        P(("role", "seq", "rep"), None, None),
    )
    return jax.shard_map(
        per_device,
        mesh=mesh,
        in_specs=placed,
        out_specs=P("role", ("seq", "rep"), None),
        check_vma=False,
    )
```

```python
import jax
import jax.numpy as jnp
from jax import lax
from jax.experimental import pallas as pl
from jax.experimental.pallas import tpu as pltpu
from jax.sharding import PartitionSpec as P

EVERY = ("role", "seq", "rep")
PAIR = 1
ACROSS = 2
TILE = 256
LANES = 128


def rms_rows(values_in, gain_vec):
    return (
        values_in
        * lax.rsqrt(jnp.mean(values_in * values_in, axis=-1, keepdims=True) + 1e-06)
        * gain_vec
    )


def swap(block, axis, bits):
    size = lax.axis_size(axis)
    return lax.ppermute(block, axis, [(i, i ^ bits) for i in range(size)])


def seq_bits():
    size = lax.axis_size("seq")
    return [1 << place for place in reversed(range(size.bit_length() - 1))]


def ready(*arrays):
    return lax.optimization_barrier(arrays)


def pack_kernel(*refs):
    low_ref, high_ref = refs[-2:]
    count = len(refs) // 2 - 1
    half = low_ref.shape[1]
    start = 0
    for rep_ref, role_ref in zip(refs[:count], refs[count:-2]):
        rows = pl.ds(start, rep_ref.shape[0])
        low_ref[rows] = rep_ref[:, :half]
        high_ref[rows] = role_ref[:, half:]
        start += rep_ref.shape[0]


def pack_corners(by_rep, by_role):
    rows, width = sum(part.shape[0] for part in by_rep), by_rep[0].shape[1]
    half = jax.ShapeDtypeStruct((rows, width // 2), jnp.bfloat16)
    return pl.pallas_call(
        pack_kernel,
        out_shape=[half, half],
        compiler_params=pltpu.CompilerParams(vmem_limit_bytes=(4 + rows // 64) * 1024 * 1024),
        cost_estimate=pl.CostEstimate(
            flops=0, bytes_accessed=4 * rows * width, transcendentals=0
        ),
        name="pack_corners",
    )(*by_rep, *by_role)


def spread_rows(own, coded, tables_of):
    rows, half = own.shape[0], own.shape[1] // 2

    def both_ways(part):
        return swap(part, "rep", ACROSS), swap(part, "role", 1)

    blocks = {0: own}
    for bits in seq_bits():
        blocks |= {place ^ bits: swap(block, "seq", bits) for place, block in blocks.items()}
    middle = [blocks[place] for place in range(2, len(blocks) - 1)]
    middle = jnp.concatenate(middle, axis=0) if len(middle) > 1 else middle[0]
    parts = [own, blocks[1], middle, blocks[len(blocks) - 1]]
    parts[2], coded, *outer = ready(parts[2], coded, *both_ways(own))
    parts[3], *early = ready(parts[3], *both_ways(parts[1]), *tables_of(coded))
    by_rep, by_role = zip(outer, early[:2], both_ways(parts[2]), both_ways(parts[3]))
    tables = early[2:]
    low, high = pack_corners(by_rep, by_role)
    corner_low, corner_high = swap(low, "role", 1), swap(high, "rep", ACROSS)
    starts = (0, rows, 2 * rows, 2 * rows + middle.shape[0])
    groups = [
        [(start, 0, part) for start, part in zip(starts, held)]
        for held in (by_rep, by_role, parts)
    ]
    groups.insert(2, [(0, 0, corner_low), (0, half, corner_high)])
    return groups, tables


def added(first, second):
    return (first.astype(jnp.float32) + second.astype(jnp.float32)).astype(jnp.bfloat16)


def collect_rows(row_count, near, by_rep, by_role, corner):
    straight_low = swap(by_role[0], "role", 1)
    straight_high = swap(by_rep[1], "rep", ACROSS)
    straight_low, straight_high, near_low, near_high, *corner = ready(
        straight_low, straight_high, *near, *corner[0], *corner[1]
    )
    cut = near_low.shape[0] // 2
    halves = slice(0, cut), slice(cut, None)

    def merged(rows, turned_low, turned_high):
        return jnp.concatenate(
            [
                base[rows].astype(jnp.float32)
                + first[rows].astype(jnp.float32)
                + second.astype(jnp.float32)
                for base, first, second in (
                    (near_low, straight_low, turned_low),
                    (near_high, straight_high, turned_high),
                )
            ],
            axis=1,
        )

    def corners(number):
        low, high = corner[2 * number : 2 * number + 2]
        return swap(low, "role", 1), swap(high, "rep", ACROSS)

    def sums(number, corner_low, corner_high):
        rows = halves[number]
        return added(by_rep[0][rows], corner_low), added(by_role[1][rows], corner_high)

    def turned(low, high):
        return swap(low, "rep", ACROSS), swap(high, "role", 1)

    far_corner, beside_corner = corners(1), corners(0)
    *far, corner_low, corner_high = ready(*turned(*sums(1, *far_corner)), *beside_corner)
    upper = merged(halves[1], *far)
    *near_sums, upper = ready(*sums(0, corner_low, corner_high), upper)
    lower = merged(halves[0], *turned(*near_sums))
    top_bits, *low_bits = seq_bits()

    def folded(rows):
        for bits in reversed(low_bits):
            pairs = rows.reshape(-1, 2, row_count, rows.shape[1])
            leaving = pairs[:, 1].astype(jnp.bfloat16).reshape(-1, rows.shape[1])
            kept = pairs[:, 0].reshape(-1, rows.shape[1]).astype(jnp.float32)
            rows = kept + swap(leaving, "seq", bits).astype(jnp.float32)
        return rows

    upper = folded(upper).astype(jnp.bfloat16)
    return folded(lower) + swap(upper, "seq", top_bits).astype(jnp.float32)


def prepare_kernel(*refs):
    tokens_in, gain_in, kv_in, k_gain_in, ids_in, gates_in, normed_ref, out_ref = refs[:8]
    held, sem = refs[8:14], refs[14]
    sources = (tokens_in, gain_in, kv_in, k_gain_in, ids_in, gates_in)
    copies = [
        pltpu.make_async_copy(src, dst, sem.at[number])
        for number, (src, dst) in enumerate(zip(sources, held))
    ]
    for copy in copies:
        copy.start()
    for copy in copies:
        copy.wait()
    tokens_ref, gain_ref, kv_ref, k_gain_ref, ids_ref, gates_ref = held
    normed = rms_rows(tokens_ref[...].astype(jnp.float32), gain_ref[...]).astype(jnp.bfloat16)
    normed_ref[...] = normed
    kv_width, head_dim = kv_ref.shape[2], k_gain_ref.shape[1]
    keys = jnp.dot(normed, kv_ref[0], preferred_element_type=jnp.float32)
    for start in range(0, kv_width, head_dim):
        head = rms_rows(keys[:, start : start + head_dim], k_gain_ref[...])
        out_ref[:, start : start + head_dim] = head.astype(jnp.bfloat16)
    values = jnp.dot(normed, kv_ref[1], preferred_element_type=jnp.float32)
    out_ref[:, kv_width : 2 * kv_width] = values.astype(jnp.bfloat16)
    coded = jnp.concatenate([ids_ref[...], gates_ref[...] // 64, gates_ref[...] % 64], axis=0)
    count = coded.shape[0]
    spread = lax.broadcasted_iota(jnp.int32, (count, LANES), 0)
    spread = spread == lax.broadcasted_iota(jnp.int32, (count, LANES), 1)
    out_ref[:, 2 * kv_width :] = lax.dot_general(
        coded.astype(jnp.float32).astype(jnp.bfloat16),
        spread.astype(jnp.float32).astype(jnp.bfloat16),
        (((0,), (0,)), ((), ())),
        preferred_element_type=jnp.float32,
    ).astype(jnp.bfloat16)


def prepare(tokens, attn_gain, w_keyval, k_gain, ids, gates):
    rows, width = tokens.shape
    operands = [
        pltpu.with_memory_space_constraint(one, pltpu.HBM)
        for one in (tokens, attn_gain[None], w_keyval, k_gain[None], ids.T, gates.T)
    ]
    return pl.pallas_call(
        prepare_kernel,
        out_shape=[
            jax.ShapeDtypeStruct((rows, width), jnp.bfloat16),
            jax.ShapeDtypeStruct((rows, 2 * w_keyval.shape[2] + LANES), jnp.bfloat16),
        ],
        in_specs=[pl.BlockSpec(memory_space=pltpu.HBM)] * len(operands),
        scratch_shapes=[pltpu.VMEM(one.shape, one.dtype) for one in operands]
        + [pltpu.SemaphoreType.DMA((len(operands),))],
        compiler_params=pltpu.CompilerParams(vmem_limit_bytes=8 * 1024 * 1024),
        cost_estimate=pl.CostEstimate(
            flops=4 * rows * width * w_keyval.shape[2],
            bytes_accessed=4 * width * w_keyval.shape[2] + 4 * rows * width,
            transcendentals=rows,
        ),
        name="prepare",
    )(*operands)


def queries_kernel(first_ref, second_ref, third_ref, fourth_ref, weight_ref, gain_ref, out_ref):
    rows, head_dim = first_ref.shape[0], gain_ref.shape[1]
    refs = (first_ref, second_ref, third_ref, fourth_ref)
    held = jnp.concatenate([ref[...] for ref in refs], axis=0)
    raw = jnp.dot(held, weight_ref[...], preferred_element_type=jnp.float32)
    for start in range(0, weight_ref.shape[1], head_dim):
        head = rms_rows(raw[:, start : start + head_dim], gain_ref[...])
        out_ref[:, start : start + head_dim] = head.astype(jnp.bfloat16)


def make_queries(blocks, w_query, q_gain):
    rows, width = len(blocks) * blocks[0].shape[0], w_query.shape[1]
    return pl.pallas_call(
        queries_kernel,
        out_shape=jax.ShapeDtypeStruct((rows, width), jnp.bfloat16),
        compiler_params=pltpu.CompilerParams(vmem_limit_bytes=8 * 1024 * 1024),
        cost_estimate=pl.CostEstimate(
            flops=2 * rows * width * w_query.shape[0],
            bytes_accessed=2 * width * w_query.shape[0],
            transcendentals=rows,
        ),
        name="queries",
    )(*blocks, w_query, q_gain[None])


def attend_kernel(head_dim, query_ref, near_ref, far_ref, weight_ref, kept_ref, leaving_ref, held_ref):
    keys = [ref[:, :head_dim] for ref in (near_ref, far_ref)]
    values = [ref[:, head_dim:] for ref in (near_ref, far_ref)]
    for start in range(0, query_ref.shape[1], head_dim):
        query = query_ref[:, start : start + head_dim]
        scores = [
            lax.dot_general(
                query, key, (((1,), (1,)), ((), ())), preferred_element_type=jnp.float32
            )
            * head_dim ** (-0.5)
            for key in keys
        ]
        row_max = jnp.maximum(
            jnp.max(scores[0], axis=1, keepdims=True), jnp.max(scores[1], axis=1, keepdims=True)
        )
        denom, total = 0.0, 0.0
        for score, value in zip(scores, values):
            weights = jnp.exp(score - row_max)
            denom = denom + jnp.sum(weights, axis=1, keepdims=True)
            total = total + jnp.dot(
                weights.astype(jnp.bfloat16), value, preferred_element_type=jnp.float32
            )
        held_ref[:, start : start + head_dim] = (total / denom).astype(jnp.bfloat16)
    cut = kept_ref.shape[0]
    for column in range(0, weight_ref.shape[1], 2 * TILE):
        columns = slice(column, column + 2 * TILE)
        partial = jnp.dot(held_ref[...], weight_ref[:, columns], preferred_element_type=jnp.float32)
        kept_ref[:, columns] = partial[:cut]
        leaving_ref[:, columns] = partial[cut:].astype(jnp.bfloat16)


def attend(queries, near_kv, far_kv, w_out, head_dim):
    rows, width = queries.shape
    keys = 2 * near_kv.shape[0]
    half = (rows // 2, w_out.shape[1])
    return pl.pallas_call(
        lambda *refs: attend_kernel(head_dim, *refs),
        out_shape=[
            jax.ShapeDtypeStruct(half, jnp.float32),
            jax.ShapeDtypeStruct(half, jnp.bfloat16),
        ],
        scratch_shapes=[pltpu.VMEM((rows, width), jnp.bfloat16)],
        compiler_params=pltpu.CompilerParams(vmem_limit_bytes=12 * 1024 * 1024),
        cost_estimate=pl.CostEstimate(
            flops=4 * rows * width * keys + 2 * rows * width * w_out.shape[1],
            bytes_accessed=2 * width * w_out.shape[1] + 4 * rows * w_out.shape[1],
            transcendentals=rows * keys * width // head_dim,
        ),
        name="attend",
    )(queries, near_kv, far_kv, w_out)


def tables_kernel(top_count, expert_ref, coded_ref, pick_ref, place_ref, share_ref):
    groups, rows, lanes = coded_ref.shape
    slots = place_ref.shape[3]
    lane = lax.broadcasted_iota(jnp.int32, (rows, lanes), 1)
    source = lax.broadcasted_iota(jnp.int32, (lanes, lanes), 0)
    target = lax.broadcasted_iota(jnp.int32, (lanes, lanes), 1)
    joined = jnp.where(source == target + top_count, 64.0, 0.0)
    joined = joined + jnp.where(source == target + 2 * top_count, 1.0, 0.0)
    joined = jnp.where(target < top_count, joined, 0.0).astype(jnp.bfloat16)
    first = lax.broadcasted_iota(jnp.int32, (rows, rows), 0)
    second = lax.broadcasted_iota(jnp.int32, (rows, rows), 1)
    later = jnp.where(first < second, 1.0, 0.0).astype(jnp.bfloat16)
    earlier = jnp.where(second < first, 1.0, 0.0).astype(jnp.bfloat16)
    ones = jnp.ones((8, lanes), jnp.bfloat16)
    slot_row = lax.broadcasted_iota(jnp.int32, (slots, rows), 0).astype(jnp.float32)
    slot_lane = lax.broadcasted_iota(jnp.int32, (rows, slots), 1).astype(jnp.float32)
    for group in range(groups):
        coded = coded_ref[group]
        gates = jnp.dot(coded, joined, preferred_element_type=jnp.float32)
        gate_sum = jnp.sum(gates, axis=1, keepdims=True)
        named = coded.astype(jnp.float32).astype(jnp.int32)
        for number in range(2):
            expert = expert_ref[0] ^ (number * PAIR)
            hits = jnp.where((named == expert) & (lane < top_count), 1.0, 0.0)
            share_ref[group, :, number : number + 1] = (
                jnp.sum(hits * gates, axis=1, keepdims=True) / gate_sum
            )
            hit = jnp.sum(hits, axis=1, keepdims=True)
            held = jnp.broadcast_to(hit, (rows, lanes)).astype(jnp.bfloat16)
            rank = jnp.dot(earlier, held, preferred_element_type=jnp.float32)[:, :1]
            rank = jnp.where(hit > 0.0, rank, -1.0)
            place_ref[number, group] = jnp.where(rank == slot_lane, 1.0, 0.0).astype(jnp.bfloat16)
            hit_row = lax.dot_general(
                ones,
                hits.astype(jnp.bfloat16),
                (((1,), (1,)), ((), ())),
                preferred_element_type=jnp.float32,
            )
            rank_row = jnp.dot(
                hit_row.astype(jnp.bfloat16), later, preferred_element_type=jnp.float32
            )
            rank_row = jnp.where(hit_row > 0.0, rank_row, -1.0)[:1]
            pick_ref[group, number * slots : (number + 1) * slots] = jnp.where(
                rank_row == slot_row, 1.0, 0.0
            ).astype(jnp.bfloat16)


def make_tables(coded, expert, slots, top_count):
    groups, rows, lanes = coded.shape
    return pl.pallas_call(
        lambda *refs: tables_kernel(top_count, *refs),
        out_shape=[
            jax.ShapeDtypeStruct((groups, 2 * slots, rows), jnp.bfloat16),
            jax.ShapeDtypeStruct((2, groups, rows, slots), jnp.bfloat16),
            jax.ShapeDtypeStruct((groups, rows, 2), jnp.float32),
        ],
        in_specs=[
            pl.BlockSpec(memory_space=pltpu.SMEM),
            pl.BlockSpec(memory_space=pltpu.VMEM),
        ],
        compiler_params=pltpu.CompilerParams(vmem_limit_bytes=24 * 1024 * 1024),
        cost_estimate=pl.CostEstimate(
            flops=4 * groups * rows * rows * lanes,
            bytes_accessed=8 * groups * rows * slots,
            transcendentals=0,
        ),
        name="tables",
    )(expert.astype(jnp.int32)[None], coded)


def expert_kernel(first, spots, cuts, *refs):
    pick_ref, place_ref, share_ref, own_gu_ref, far_gu_ref, own_dn_ref, far_dn_ref = refs[:7]
    group_rows, slots = place_ref.shape[2:]
    groups = len(cuts)
    piece_refs = refs[7 : 7 + len(spots)]
    out_refs = refs[7 + len(spots) : 7 + len(spots) + 2 * sum(cuts)]
    xs_buf, gu_buf, dn_buf, hid_buf, served_buf, y_buf, w_sem, y_sem = refs[
        7 + len(spots) + len(out_refs) :
    ]
    width = xs_buf.shape[2]
    half = width // 2
    hidden = own_dn_ref.shape[0]
    tiles = hidden // TILE

    weight_copies = []
    for expert, (gu_ref, dn_ref) in enumerate(((own_gu_ref, own_dn_ref), (far_gu_ref, far_dn_ref))):
        mine = []
        for tile in range(tiles):
            for side in range(2):
                mine.append(
                    pltpu.make_async_copy(
                        gu_ref.at[:, pl.ds(side * hidden + tile * TILE, TILE)],
                        gu_buf.at[expert, tile, side],
                        w_sem.at[expert, 2 * tile + side],
                    )
                )
        mine.append(pltpu.make_async_copy(dn_ref, dn_buf.at[expert], w_sem.at[expert, 2 * tiles]))
        weight_copies.append(mine)
    for mine in weight_copies:
        for copy in mine:
            copy.start()

    for group in range(groups):
        for column in range(0, width, half):
            held = [
                piece[:, column - start : column - start + half]
                for (where, _, start), piece in zip(spots, piece_refs)
                if where == group and start <= column < start + piece.shape[1]
            ]
            chosen = jnp.dot(
                pick_ref[first + group],
                jnp.concatenate(held, axis=0),
                preferred_element_type=jnp.float32,
            ).astype(jnp.bfloat16)
            rows = pl.ds(group * slots, slots)
            xs_buf[0, rows, column : column + half] = chosen[:slots]
            xs_buf[1, rows, column : column + half] = chosen[slots:]

    for expert in range(2):
        for tile in range(tiles):
            weight_copies[expert][2 * tile].wait()
            weight_copies[expert][2 * tile + 1].wait()
            gate = jnp.dot(
                xs_buf[expert], gu_buf[expert, tile, 0], preferred_element_type=jnp.float32
            )
            up = jnp.dot(
                xs_buf[expert], gu_buf[expert, tile, 1], preferred_element_type=jnp.float32
            )
            value = gate / (1.0 + jnp.exp(-gate)) * up
            hid_buf[:, tile * TILE : (tile + 1) * TILE] = value.astype(jnp.bfloat16)
        weight_copies[expert][2 * tiles].wait()
        for column in range(0, width, 2 * TILE):
            served_buf[expert, :, column : column + 2 * TILE] = jnp.dot(
                hid_buf[...],
                dn_buf[expert, :, column : column + 2 * TILE],
                preferred_element_type=jnp.float32,
            ).astype(jnp.bfloat16)

    out_copies = []
    for group in range(groups):
        for column in range(0, width, 2 * TILE):
            total = None
            for expert in range(2):
                placed = jnp.dot(
                    place_ref[expert, first + group],
                    served_buf[expert, pl.ds(group * slots, slots), column : column + 2 * TILE],
                    preferred_element_type=jnp.float32,
                )
                term = placed * share_ref[first + group, :, expert : expert + 1]
                total = term if total is None else total + term
            y_buf[group, :, column : column + 2 * TILE] = total.astype(jnp.bfloat16)
        cut = group_rows // cuts[group]
        for number in range(2 * cuts[group]):
            row, side = divmod(number, 2)
            done = len(out_copies)
            copy = pltpu.make_async_copy(
                y_buf.at[group, pl.ds(row * cut, cut), pl.ds(side * half, half)],
                out_refs[done],
                y_sem.at[done],
            )
            copy.start()
            out_copies.append(copy)
    for copy in out_copies:
        copy.wait()


def run_experts(first, pieces, cuts, pick, place, share, weights):
    group_rows, slots = place.shape[2:]
    groups = len(pieces)
    hidden, width = weights[2].shape
    tiles = hidden // TILE
    spots = [
        (group, row, column) for group, held in enumerate(pieces) for row, column, _ in held
    ]
    arrays = [array for held in pieces for _, _, array in held]
    anywhere = pl.BlockSpec(memory_space=pl.ANY)
    stored = pl.BlockSpec(memory_space=pltpu.HBM)
    inside = pl.BlockSpec(memory_space=pltpu.VMEM)
    outs = pl.pallas_call(
        lambda *refs: expert_kernel(first, spots, cuts, *refs),
        out_shape=[
            jax.ShapeDtypeStruct((group_rows // cut, width // 2), jnp.bfloat16)
            for cut in cuts
            for _ in range(2 * cut)
        ],
        in_specs=[inside] * 3 + [stored] * 4 + [inside] * len(arrays),
        out_specs=[anywhere] * (2 * sum(cuts)),
        scratch_shapes=[
            pltpu.VMEM((2, groups * slots, width), jnp.bfloat16),
            pltpu.VMEM((2, tiles, 2, width, TILE), jnp.bfloat16),
            pltpu.VMEM((2, hidden, width), jnp.bfloat16),
            pltpu.VMEM((groups * slots, hidden), jnp.bfloat16),
            pltpu.VMEM((2, groups * slots, width), jnp.bfloat16),
            pltpu.VMEM((groups, group_rows, width), jnp.bfloat16),
            pltpu.SemaphoreType.DMA((2, 2 * tiles + 1)),
            pltpu.SemaphoreType.DMA((2 * sum(cuts),)),
        ],
        compiler_params=pltpu.CompilerParams(vmem_limit_bytes=(28 + 6 * group_rows // 256) * 1024 * 1024),
        cost_estimate=pl.CostEstimate(
            flops=12 * groups * slots * width * hidden,
            bytes_accessed=12 * width * hidden + 4 * groups * group_rows * width,
            transcendentals=2 * groups * slots * hidden,
        ),
        name="experts",
    )(pick, place, share, *weights, *arrays)
    return list(zip(outs[0::2], outs[1::2]))


def per_device(
    hidden_in,
    attn_gain,
    w_query,
    w_keyval,
    q_gain,
    k_gain,
    w_out,
    moe_gain,
    expert_ids,
    gate_fixed,
    w_gateup,
    w_down,
):
    tokens = hidden_in[0].astype(jnp.float32)
    row_count, model_width = tokens.shape
    head_dim = q_gain.shape[0]
    local_heads = w_query.shape[1] // head_dim
    kv_heads = w_keyval.shape[2] // head_dim
    group_size = local_heads * lax.axis_size("rep") // kv_heads
    rep_index = lax.axis_index("rep")
    kv_width = kv_heads * head_dim
    top_count = expert_ids.shape[2]
    expert_count = lax.axis_size(EVERY)

    normed, own_payload = prepare(
        hidden_in[0], attn_gain, w_keyval, k_gain, expert_ids[0], gate_fixed[0]
    )
    across_rows = swap(normed, "rep", ACROSS)
    line = jnp.concatenate(
        [own_payload] + [swap(own_payload, "seq", bits) for bits in range(1, lax.axis_size("seq"))], axis=0
    )
    pair_rows = swap(ready(normed, line)[0], "rep", PAIR)
    corner_rows = swap(across_rows, "rep", PAIR)
    line_routes = line[:, 2 * kv_width :]

    def head_kv(rep):
        index = rep * local_heads // group_size * head_dim
        return [
            lax.dynamic_slice_in_dim(line, index, head_dim, 1),
            lax.dynamic_slice_in_dim(line, kv_width + index, head_dim, 1),
        ]

    sent = jnp.concatenate(head_kv(rep_index ^ ACROSS) + [line_routes], axis=1)
    sent, across_rows = ready(sent, across_rows)
    across = swap(sent, "rep", ACROSS)
    half_kv = jnp.concatenate(
        [jnp.concatenate(head_kv(rep_index), axis=1), across[:, : 2 * head_dim]], axis=0
    )
    pair_kv = swap(half_kv, "rep", PAIR)
    both_routes = jnp.stack([line_routes, across[:, 2 * head_dim :]])
    far_routes = swap(both_routes, "role", 1)
    coded = jnp.concatenate([both_routes[1:], far_routes[:1], far_routes[1:], both_routes[:1]])
    queries = make_queries([normed, across_rows, pair_rows, corner_rows], w_query, q_gain)
    kept, leaving = attend(queries, half_kv, pair_kv, w_out, head_dim)
    leaving, own_dn = ready(swap(leaving, "rep", PAIR), w_down[0])
    halves = kept + leaving.astype(jnp.float32)
    far_dn, far_gu = swap(own_dn, "rep", PAIR), swap(w_gateup[0], "rep", PAIR)
    far_sum = halves[row_count:].astype(jnp.bfloat16)
    across_sum, coded, far_dn, far_gu = ready(
        swap(far_sum, "rep", ACROSS), coded, far_dn, far_gu
    )
    attended = halves[:row_count] + across_sum.astype(jnp.float32)
    mixed = tokens + attended

    moe_in = rms_rows(mixed, moe_gain).astype(jnp.bfloat16)

    capacity = max(2, 7 * row_count * top_count // (4 * expert_count))
    slots = -(-capacity * (coded.shape[1] // row_count) // 16) * 16
    rows, tables = spread_rows(
        moe_in,
        coded,
        lambda codes: make_tables(codes, lax.axis_index(EVERY), slots, top_count),
    )
    weights = [
        pltpu.with_memory_space_constraint(one, pltpu.HBM)
        for one in (w_gateup[0], far_gu, w_down[0], far_dn)
    ]

    tables = (*tables, weights)
    by_rep, by_role = run_experts(0, rows[:2], (1, 1), *tables)
    rep_low, rep_high, role_low, role_high, *held = ready(
        *by_rep, *by_role, *(array for _, _, array in rows[2])
    )
    by_rep, by_role = (rep_low, rep_high), (role_low, role_high)
    pieces = [(row, column, array) for (row, column, _), array in zip(rows[2], held)]
    *corner, near = run_experts(2, [pieces, rows[3]], (2, 1), *tables)
    routed = collect_rows(row_count, near, by_rep, by_role, corner)
    return (mixed + routed).astype(jnp.bfloat16)[None]


def solution(mesh):
    placed = (
        P("role", ("seq", "rep"), None),
        P(),
        P(None, "rep"),
        P(),
        P(),
        P(),
        P("rep", None),
        P(),
        P("role", ("seq", "rep"), None),
        P("role", ("seq", "rep"), None),
        P(("role", "seq", "rep"), None, None),
        P(("role", "seq", "rep"), None, None),
    )
    return jax.shard_map(
        per_device,
        mesh=mesh,
        in_specs=placed,
        out_specs=P("role", ("seq", "rep"), None),
        check_vma=False,
    )
```
